32 devices in a mesh: slab: 8 (over z, y), mode: 4 (over x, core).
Axes of the slice: x: 2, y: 2, z: 4, core: 2. Of those that a mesh axis runs over, the one named last changes fastest.
Arguments:
- incoming_occupation: float32 [256, 64, 16, 128], P('mode', 'slab'), may hold values from 0.25 to 1.75
- crystal_kelvin_given: float32 [64, 16, 128], P('slab'), may hold values from 0.5 to 1.5
- generating_region_flag: int32 [64, 16, 128], P('slab'), may hold values 0 or 1
- ordinate_label_array: int32 [256], P('mode'), may hold values from 0 to 255, each once
- spectral_group_velocity: float32 [8], replicated, may hold values from 0.5 to 1
- spectral_scatter_rate: float32 [8], replicated, may hold values from 0.0003 to 0.03
- spectral_storage_factor: float32 [8], replicated, may hold values from 0.5 to 2
- spectral_quartic_threshold: float32 [8], replicated, may hold values from 0.4 to 1
- spectral_generation_rate: float32 [8], replicated, may hold values from 0.005 to 0.05
Outputs:
- energy_out: float32 [256, 64, 16, 128], P('mode', 'slab')
- temp_out: float32 [64, 16, 128], P('slab')
The draws below stay inside these ranges and needn't reach their ends.
Inputs may be any that keep to these rules, and one draw needn't show every extreme that they name: `ordinate_label_array`: each of the 256 mode numbers stands in exactly one slot.
All inputs are finite; a program needn't handle non-finite values. No bound on the sum of `generating_region_flag` on one device may be relied on, other than what follows from the above.
Results may differ from the reference program's by a relative error of at most 0.0003.
Values sent between devices are 32-bit elements; how exact they have to be, the bound alone decides.
No kernel may reach another device: no remote copies, remote signals or barrier semaphores. Data moves between devices by JAX's collectives and lax.ppermute only.
A program may use at most 128 MiB of HBM per device.

```python
import math
import jax
import jax.numpy as jnp
from jax import lax

FREQ_GROUPS = 8
DIRS = 32
MODES = 256
Y_EXTENT = 16
Z_EXTENT = 128
ITERS = 3
NEWTON = 4
X_EXTENT = 64


def set_ends(drawn, rng, smallest, top_value):
    dims = drawn.shape
    place = [jax.random.randint(jax.random.fold_in(rng, axis), (), 0, dims[axis]) for axis in range(len(dims))]
    drawn = drawn.at[tuple(place)].set(smallest)
    longest = dims.index(max(dims))
    place[longest] = (place[longest] + 1) % dims[longest]
    return drawn.at[tuple(place)].set(top_value)


def shard_levels(stream_key, extent, pieces, low, top_value):
    gain, own = 1.0, jax.random.fold_in(stream_key, 6)
    for axis_at, shards_of in pieces:
        draws = jnp.exp(jax.random.uniform(jax.random.fold_in(own, axis_at), (shards_of,), jnp.float32, low / len(pieces), top_value / len(pieces)))
        gain = gain * jnp.repeat(draws, extent[axis_at] // shards_of).reshape([-1 if axis == axis_at else 1 for axis in range(len(extent))])
    return gain


def setup_inputs(seed: int = 0) -> dict:
    seeds = jax.random.split(jax.random.key(seed), 10)
    return {
        "incoming_occupation": jnp.clip(0.25 + 1.5 * jax.random.uniform(seeds[0], (MODES, X_EXTENT, Y_EXTENT, Z_EXTENT), jnp.float32) ** shard_levels(seeds[0], (MODES, X_EXTENT, Y_EXTENT, Z_EXTENT), ((0, 4), (1, 8)), -0.2, 0.2), 0.25, 1.75),
        "crystal_kelvin_given": jnp.clip(0.5 + 1.0 * jax.random.uniform(seeds[1], (X_EXTENT, Y_EXTENT, Z_EXTENT), jnp.float32) ** shard_levels(seeds[1], (X_EXTENT, Y_EXTENT, Z_EXTENT), ((0, 8),), -0.2, 0.2), 0.5, 1.5),
        "generating_region_flag": set_ends((jax.random.randint(seeds[2], (X_EXTENT, Y_EXTENT, Z_EXTENT), 0, 4) < 1).astype(jnp.int32), jax.random.fold_in(seeds[2], 1), 0, 1),
        "ordinate_label_array": jax.random.permutation(seeds[3], MODES).astype(jnp.int32),
        "spectral_group_velocity": jnp.clip(jnp.exp(jax.random.uniform(seeds[4], (FREQ_GROUPS,), jnp.float32, math.log(0.5), math.log(1.0))), 0.5, 1.0),
        "spectral_scatter_rate": jnp.clip(jnp.exp(jax.random.uniform(seeds[5], (FREQ_GROUPS,), jnp.float32, math.log(0.0003), math.log(0.03))), 0.0003, 0.03),
        "spectral_storage_factor": jnp.clip(jnp.exp(jax.random.uniform(seeds[6], (FREQ_GROUPS,), jnp.float32, math.log(0.5), math.log(2.0))), 0.5, 2.0),
        "spectral_quartic_threshold": jnp.clip(jnp.exp(jax.random.uniform(seeds[7], (FREQ_GROUPS,), jnp.float32, math.log(0.4), math.log(1.0))), 0.4, 1.0),
        "spectral_generation_rate": jnp.clip(jnp.exp(jax.random.uniform(seeds[8], (FREQ_GROUPS,), jnp.float32, math.log(0.005), math.log(0.05))), 0.005, 0.05),
    }


PSEUDO_RATE = 0.03

def spectral_entry(indicator_matrix, values):
    return lax.optimization_barrier(jnp.sum(indicator_matrix * values[None, :], axis=1))

def broadcast_spectral(values):
    return values[:, None, None, None]

def entry_amounts(gathered_entries, spectral_group_velocity, spectral_scatter_rate, spectral_storage_factor, spectral_quartic_threshold, spectral_generation_rate):
    spectral_ordinal = gathered_entries // DIRS
    direction = gathered_entries % DIRS
    indicator_matrix = (spectral_ordinal[:, None] == jnp.arange(FREQ_GROUPS, dtype=jnp.int32)[None, :]).astype(spectral_group_velocity.dtype)
    group_speed = spectral_entry(indicator_matrix, spectral_group_velocity)
    relax_rate = spectral_entry(indicator_matrix, spectral_scatter_rate)
    heat_scale = spectral_entry(indicator_matrix, spectral_storage_factor)
    threshold_factor = spectral_entry(indicator_matrix, spectral_quartic_threshold)
    source_rate = spectral_entry(indicator_matrix, spectral_generation_rate)
    polar_level = direction % 4
    cosine = jnp.where(polar_level == 0, 0.99995, jnp.where(polar_level == 1, 0.9999, jnp.where(polar_level == 2, -0.9999, -0.99995))).astype(spectral_group_velocity.dtype)
    sine_part = jnp.sqrt(1.0 - cosine * cosine)
    azimuth = ((direction // 4).astype(spectral_group_velocity.dtype) + 0.5) * (2.0 * math.pi / (DIRS // 4))
    velocity_x = group_speed * cosine
    velocity_y = group_speed * sine_part * jnp.cos(azimuth)
    velocity_z = group_speed * sine_part * jnp.sin(azimuth)
    diagonal = jnp.abs(velocity_x) + jnp.abs(velocity_y) + jnp.abs(velocity_z) + relax_rate + PSEUDO_RATE
    decay_ratio = jnp.abs(velocity_x) / diagonal
    wall_value = heat_scale * (1.0 + 1.0 / (4.0 * threshold_factor ** 3))
    return (velocity_x, velocity_y, velocity_z, relax_rate, heat_scale, threshold_factor, source_rate, diagonal, decay_ratio, wall_value)

def transport_forcing(mode_group_internal, crystal_kelvin, generating_region_flag, entry_location):
    velocity_y = entry_location[1]
    velocity_z = entry_location[2]
    upwind_y = jnp.where(broadcast_spectral(velocity_y) > 0, jnp.roll(mode_group_internal, 1, 2), jnp.roll(mode_group_internal, -1, 2))
    upwind_z = jnp.where(broadcast_spectral(velocity_z) > 0, jnp.roll(mode_group_internal, 1, 3), jnp.roll(mode_group_internal, -1, 3))
    conservation_residual = broadcast_spectral(entry_location[4]) * (crystal_kelvin + crystal_kelvin ** 4 / (4.0 * broadcast_spectral(entry_location[5]) ** 3))
    heating = broadcast_spectral(entry_location[6]) * generating_region_flag.astype(mode_group_internal.dtype)
    gathered = PSEUDO_RATE * mode_group_internal + broadcast_spectral(entry_location[3]) * conservation_residual + heating
    gathered = gathered + broadcast_spectral(jnp.abs(velocity_y)) * upwind_y + broadcast_spectral(jnp.abs(velocity_z)) * upwind_z
    return gathered / broadcast_spectral(entry_location[7])

def root_finding_correction(volumetric_internal, crystal_kelvin, spectral_storage_factor, spectral_quartic_threshold):
    for newton_step in range(NEWTON):
        third_power_kelvin = crystal_kelvin ** 3
        present_iterate = -volumetric_internal
        residual_derivative = jnp.zeros_like(volumetric_internal)
        for spectral_ordinal in range(FREQ_GROUPS):
            threshold_third_power = spectral_quartic_threshold[spectral_ordinal] ** 3
            present_iterate = present_iterate + spectral_storage_factor[spectral_ordinal] * (crystal_kelvin + crystal_kelvin * third_power_kelvin / (4.0 * threshold_third_power))
            residual_derivative = residual_derivative + spectral_storage_factor[spectral_ordinal] * (1.0 + third_power_kelvin / threshold_third_power)
        crystal_kelvin = crystal_kelvin - present_iterate / residual_derivative
    return crystal_kelvin

def march_tile_once(mode_group_internal, gathered_entries, crystal_kelvin, generating_region_flag, model_settings):
    entry_location = entry_amounts(gathered_entries, *model_settings)
    equilibrium_reemission = transport_forcing(mode_group_internal, crystal_kelvin, generating_region_flag, entry_location)
    forward = broadcast_spectral(entry_location[0]) > 0
    flipped = jnp.where(forward, equilibrium_reemission, equilibrium_reemission[:, ::-1])
    ratio_plane = entry_location[8][:, None, None]
    start_layer = entry_location[9][:, None, None] * jnp.ones((mode_group_internal.shape[0], mode_group_internal.shape[2], mode_group_internal.shape[3]), mode_group_internal.dtype)

    def advance(incoming_layer, layer):
        following = ratio_plane * incoming_layer + layer
        return (following, following)
    last_layer, layers = lax.scan(advance, start_layer, jnp.moveaxis(flipped, 1, 0))
    swept_energy = jnp.moveaxis(layers, 0, 1)
    return jnp.where(forward, swept_energy, swept_energy[:, ::-1])

def reference(incoming_occupation, crystal_kelvin_given, generating_region_flag, ordinate_label_array, spectral_group_velocity, spectral_scatter_rate, spectral_storage_factor, spectral_quartic_threshold, spectral_generation_rate):
    model_settings = (spectral_group_velocity, spectral_scatter_rate, spectral_storage_factor, spectral_quartic_threshold, spectral_generation_rate)
    block_count = MODES // 32
    mode_group_internal = incoming_occupation
    crystal_kelvin = crystal_kelvin_given
    for iteration in range(ITERS):

        def one_block(twofold_result):
            return march_tile_once(twofold_result[0], twofold_result[1], crystal_kelvin, generating_region_flag, model_settings)
        mode_group_internal = lax.map(one_block, (mode_group_internal.reshape(block_count, 32, X_EXTENT, Y_EXTENT, Z_EXTENT), ordinate_label_array.reshape(block_count, 32)))
        mode_group_internal = mode_group_internal.reshape(MODES, X_EXTENT, Y_EXTENT, Z_EXTENT)
        volumetric_internal = lax.optimization_barrier(jnp.sum(mode_group_internal, axis=0)) / DIRS
        crystal_kelvin = root_finding_correction(volumetric_internal, crystal_kelvin, spectral_storage_factor, spectral_quartic_threshold)
    return (mode_group_internal, crystal_kelvin)
```

```python
import functools
import math

import jax
import jax.numpy as jnp
import numpy as np
from jax import lax
from jax.experimental import pallas as pl
from jax.experimental.pallas import tpu as pltpu
from jax.sharding import PartitionSpec as P

FREQ_GROUPS = 8
DIRS = 32
ITERS = 3
NEWTON = 4
PSEUDO_RATE = 0.03

SELF, UPY, UPZ, THERM, QUART, HEAT, RATIO, COMPOSITE, WALL = range(9)
FORWARD, SHIFT_Y, SHIFT_Z = range(3)

SMEM = pl.BlockSpec(memory_space=pltpu.SMEM)


def slot_tables(labels, speed, rate, storage, threshold, generation, depth, width_y, width_z):
    band = labels // DIRS
    direction = labels % DIRS
    of_band = (band[None, :] == jnp.arange(FREQ_GROUPS, dtype=jnp.int32)[:, None]).astype(jnp.float32)
    speed, rate, storage, threshold, generation = (
        jnp.sum(of_band * value[:, None], axis=0)
        for value in (speed, rate, storage, threshold, generation)
    )
    polar = direction % 4
    cosine = jnp.where((polar == 0) | (polar == 3), np.float32(0.99995), np.float32(0.9999))
    sine = jnp.sqrt(1.0 - cosine * cosine)
    azimuth = ((direction // 4).astype(jnp.float32) + 0.5) * (2.0 * math.pi / (DIRS // 4))
    vy = speed * sine * jnp.cos(azimuth)
    vz = speed * sine * jnp.sin(azimuth)
    vx = speed * cosine
    diagonal = vx + jnp.abs(vy) + jnp.abs(vz) + rate + PSEUDO_RATE
    quartic = 1.0 / (4.0 * threshold**3)
    ratio = vx / diagonal
    composite = ratio
    for _ in range(int(math.log2(depth))):
        composite = composite * composite
    therm = rate * storage / diagonal
    floats = jnp.stack(
        [
            PSEUDO_RATE / diagonal,
            jnp.abs(vy) / diagonal,
            jnp.abs(vz) / diagonal,
            therm,
            therm * quartic,
            generation / diagonal,
            ratio,
            composite,
            storage * (1.0 + quartic),
        ]
    )
    ints = jnp.stack(
        [
            (polar < 2).astype(jnp.int32),
            jnp.where(vy > 0, 1, width_y - 1).astype(jnp.int32),
            jnp.where(vz > 0, 1, width_z - 1).astype(jnp.int32),
        ]
    )
    return floats, ints


def newton(density, kelvin, linear, quart):
    for _ in range(NEWTON):
        cube = kelvin * kelvin * kelvin
        residual = linear * kelvin + quart * (kelvin * cube) - density
        kelvin = kelvin - residual / (linear + 4.0 * quart * cube)
    return kelvin


def sweep_body(block, depth, floats, ints, first, energy, incoming, kelvin, quartic, heat, swept, outgoing):
    base = pl.program_id(0) * block

    def one_slot(i, carry):
        s = base + i
        forward = ints[FORWARD, s]
        start = jnp.where(forward == 1, 0, depth - 1)
        step = jnp.where(forward == 1, 1, -1)
        shift_y, shift_z = ints[SHIFT_Y, s], ints[SHIFT_Z, s]
        c_self, c_y, c_z = floats[SELF, s], floats[UPY, s], floats[UPZ, s]
        c_t, c_q, c_h = floats[THERM, s], floats[QUART, s], floats[HEAT, s]
        ratio = floats[RATIO, s]
        total = None
        fading = None if first else incoming[i]
        for j in range(depth):
            x = start + step * j
            value = energy[i, x]
            if not first:
                fading = ratio * fading
                value = value + fading
            source = (
                c_self * value
                + c_y * pltpu.roll(value, shift_y, 0)
                + c_z * pltpu.roll(value, shift_z, 1)
                + c_t * kelvin[x]
                + c_q * quartic[x]
                + c_h * heat[x]
            )
            total = source if total is None else ratio * total + source
            swept[i, x] = total
        outgoing[i] = total
        return carry

    lax.fori_loop(0, block, one_slot, 0)


def first_kernel(block, depth, floats, ints, energy, kelvin, flag, swept, outgoing, quartic, heat):
    @pl.when(pl.program_id(0) == 0)
    def _():
        square = kelvin[...] * kelvin[...]
        quartic[...] = square * square
        heat[...] = flag[...].astype(jnp.float32)

    sweep_body(block, depth, floats, ints, True, energy, None, kelvin, quartic, heat, swept, outgoing)


def next_kernel(
    block, depth, parts, floats, ints, sums, energy, incoming, before, flag, *rest
):
    densities, (swept, outgoing, kelvin, quartic, heat) = rest[:parts], rest[parts:]

    @pl.when(pl.program_id(0) == 0)
    def _():
        now = newton(add_up(densities) * (1.0 / DIRS), before[...], sums[0], sums[1])
        kelvin[...] = now
        square = now * now
        quartic[...] = square * square
        heat[...] = flag[...].astype(jnp.float32)

    sweep_body(block, depth, floats, ints, False, energy, incoming, kelvin, quartic, heat, swept, outgoing)


def add_up(refs):
    values = [ref[...] for ref in refs]
    while len(values) > 1:
        values = [a + b for a, b in zip(values[::2], values[1::2])]
    return values[0]


def density_kernel(block, depth, final, floats, ints, swept, incoming, *outs):
    density = outs[-1]

    @pl.when(pl.program_id(0) == 0)
    def _():
        density[...] = jnp.zeros_like(density)

    base = pl.program_id(0) * block

    def one_slot(i, carry):
        s = base + i
        forward = ints[FORWARD, s]
        start = jnp.where(forward == 1, 0, depth - 1)
        step = jnp.where(forward == 1, 1, -1)
        ratio = floats[RATIO, s]
        fading = incoming[i]
        for j in range(depth):
            x = start + step * j
            fading = ratio * fading
            value = swept[i, x] + fading
            if final:
                outs[0][i, x] = value
            density[x] += value
        return carry

    lax.fori_loop(0, block, one_slot, 0)


def newton_kernel(sums, before, *rest):
    densities, kelvin = rest[:-1], rest[-1]
    kelvin[...] = newton(add_up(densities) * (1.0 / DIRS), before[...], sums[0], sums[1])


def scan_kernel(own, slabs, home, floats, ints, outgoing, incoming):
    base = home[0] * own

    def one_slot(i, carry):
        s = base + i
        forward = ints[FORWARD, s]
        start = jnp.where(forward == 1, 0, slabs - 1)
        step = jnp.where(forward == 1, 1, -1)
        composite = floats[COMPOSITE, s]
        entering = jnp.full(outgoing.shape[2:], floats[WALL, s], jnp.float32)
        for j in range(slabs):
            k = start + step * j
            incoming[k, i] = entering
            if j < slabs - 1:
                entering = composite * entering + outgoing[k, i]
        return carry

    lax.fori_loop(0, own, one_slot, 0)


def local(incoming_occupation, crystal_kelvin_given, generating_region_flag, labels, speed, rate, storage, threshold, generation):
    slots, depth, width_y, width_z = incoming_occupation.shape
    slabs, modes = lax.axis_size("slab"), lax.axis_size("mode")
    own = slots // slabs
    block = 8
    grid = (slots // block,)
    plane = (width_y, width_z)
    home = lax.axis_index("slab").astype(jnp.int32).reshape(1)
    floats, ints = slot_tables(labels, speed, rate, storage, threshold, generation, depth, width_y, width_z)
    sums = jnp.stack([jnp.sum(storage), jnp.sum(storage / (4.0 * threshold**3))])

    slot_block = pl.BlockSpec((block, depth, *plane), lambda i: (i, 0, 0, 0))
    face_block = pl.BlockSpec((block, *plane), lambda i: (i, 0, 0))
    cells = pl.BlockSpec((depth, *plane), lambda i: (0, 0, 0))
    energy_shape = jax.ShapeDtypeStruct((slots, depth, *plane), jnp.float32)
    face_shape = jax.ShapeDtypeStruct((slots, *plane), jnp.float32)
    cell_shape = jax.ShapeDtypeStruct((depth, *plane), jnp.float32)
    cell_scratch = pltpu.VMEM((depth, *plane), jnp.float32)
    params = pltpu.CompilerParams(vmem_limit_bytes=40 * 1024 * 1024)

    def exchange(outgoing):
        gathered = lax.all_to_all(outgoing.reshape(slabs, own, *plane), "slab", 0, 0)
        incoming = pl.pallas_call(
            functools.partial(scan_kernel, own, slabs),
            in_specs=[SMEM, SMEM, SMEM, pl.BlockSpec(memory_space=pltpu.VMEM)],
            out_specs=pl.BlockSpec(memory_space=pltpu.VMEM),
            out_shape=jax.ShapeDtypeStruct((slabs, own, *plane), jnp.float32),
            compiler_params=params,
            name="slab_scan",
        )(home, floats, ints, gathered)
        return lax.all_to_all(incoming, "slab", 0, 0).reshape(slots, *plane)

    def spread(density):
        return [density] + [
            lax.ppermute(density, "mode", [(i, i ^ by) for i in range(modes)]) for by in range(1, modes)
        ]

    kelvin = crystal_kelvin_given
    swept, outgoing = pl.pallas_call(
        functools.partial(first_kernel, block, depth),
        grid=grid,
        in_specs=[SMEM, SMEM, slot_block, cells, cells],
        out_specs=[slot_block, face_block],
        out_shape=[energy_shape, face_shape],
        scratch_shapes=[cell_scratch, cell_scratch],
        compiler_params=params,
        name="first_sweep",
    )(floats, ints, incoming_occupation, kelvin, generating_region_flag)
    for _ in range(ITERS - 1):
        incoming = exchange(outgoing)
        density = pl.pallas_call(
            functools.partial(density_kernel, block, depth, False),
            grid=grid,
            in_specs=[SMEM, SMEM, slot_block, face_block],
            out_specs=cells,
            out_shape=cell_shape,
            compiler_params=params,
            name="density",
        )(floats, ints, swept, incoming)
        swept, outgoing, kelvin = pl.pallas_call(
            functools.partial(next_kernel, block, depth, modes),
            grid=grid,
            in_specs=[SMEM, SMEM, SMEM, slot_block, face_block, cells, cells] + [cells] * modes,
            out_specs=[slot_block, face_block, cells],
            out_shape=[energy_shape, face_shape, cell_shape],
            scratch_shapes=[cell_scratch, cell_scratch],
            compiler_params=params,
            name="next_sweep",
        )(floats, ints, sums, swept, incoming, kelvin, generating_region_flag, *spread(density))
    incoming = exchange(outgoing)
    energy, density = pl.pallas_call(
        functools.partial(density_kernel, block, depth, True),
        grid=grid,
        in_specs=[SMEM, SMEM, slot_block, face_block],
        out_specs=[slot_block, cells],
        out_shape=[energy_shape, cell_shape],
        compiler_params=params,
        name="final_energy",
    )(floats, ints, swept, incoming)
    kelvin = pl.pallas_call(
        newton_kernel,
        in_specs=[SMEM] + [pl.BlockSpec(memory_space=pltpu.VMEM)] * (modes + 1),
        out_specs=pl.BlockSpec(memory_space=pltpu.VMEM),
        out_shape=cell_shape,
        compiler_params=params,
        name="final_kelvin",
    )(sums, kelvin, *spread(density))
    return energy, kelvin


def solution(mesh):
    return jax.shard_map(
        local,
        mesh=mesh,
        in_specs=(
            P("mode", "slab", None, None),
            P("slab", None, None),
            P("slab", None, None),
            P("mode"),
            P(),
            P(),
            P(),
            P(),
            P(),
        ),
        out_specs=(P("mode", "slab", None, None), P("slab", None, None)),
        check_vma=False,
    )
```

```python
import functools
import math

import jax
import jax.numpy as jnp
import numpy as np
from jax import lax
from jax.experimental import pallas as pl
from jax.experimental.pallas import tpu as pltpu
from jax.sharding import PartitionSpec as P

FREQ_GROUPS = 8
DIRS = 32
ITERS = 3
NEWTON = 4
PSEUDO_RATE = 0.03
GROUP = 4
COSINES = (np.float32(0.99995), np.float32(0.9999))

SELF, UPY, UPZ, RATIO, WALL, FULL, FULL_N, FULL_T, FULL_GROUP = range(9)
FORWARD, SHIFT_Y, SHIFT_Z, EDGE_Y, KIND = range(5)
SLAB, MODE = range(2)

SMEM = pl.BlockSpec(memory_space=pltpu.SMEM)
VMEM = pl.BlockSpec(memory_space=pltpu.VMEM)
PARAMS = pltpu.CompilerParams(vmem_limit_bytes=48 * 1024 * 1024)


def diagonal_of(speed, rate, cosine):
    sine = jnp.sqrt(1.0 - cosine * cosine)
    across = np.float32(math.cos(math.pi / 8) + math.sin(math.pi / 8))
    return speed * (cosine + sine * across) + rate + PSEUDO_RATE


def slot_tables(labels, speed, rate, storage, threshold, slab, slabs, depth, width_y, width_z):
    band = labels // DIRS
    direction = labels % DIRS
    of_band = (band[None, :] == jnp.arange(FREQ_GROUPS, dtype=jnp.int32)[:, None]).astype(jnp.float32)
    speed, rate, storage, threshold = (
        jnp.sum(of_band * value[:, None], axis=0) for value in (speed, rate, storage, threshold)
    )
    polar = direction % 4
    outer = (polar == 0) | (polar == 3)
    forward = polar < 2
    cosine = jnp.where(outer, COSINES[0], COSINES[1])
    sine = jnp.sqrt(1.0 - cosine * cosine)
    azimuth = ((direction // 4).astype(jnp.float32) + 0.5) * (2.0 * math.pi / (DIRS // 4))
    vy = speed * sine * jnp.cos(azimuth)
    vz = speed * sine * jnp.sin(azimuth)
    diagonal = diagonal_of(speed, rate, cosine)
    ratio = speed * cosine / diagonal
    full = lax.integer_pow(ratio, depth)
    at_wall = jnp.where(forward, slab == 0, slab == slabs - 1)
    wall = storage * (1.0 + 1.0 / (4.0 * threshold**3))
    floats = jnp.stack(
        [
            PSEUDO_RATE / diagonal,
            jnp.abs(vy) / diagonal,
            jnp.abs(vz) / diagonal,
            ratio,
            jnp.where(at_wall, wall, 0.0),
            full,
            depth * full,
            (depth * (depth + 1) // 2) * full,
            lax.integer_pow(full, GROUP),
        ]
    )
    ints = jnp.stack(
        [
            forward.astype(jnp.int32),
            jnp.where(vy > 0, 1, 7).astype(jnp.int32),
            jnp.where(vz > 0, 1, width_z - 1).astype(jnp.int32),
            jnp.where(vy > 0, 0, 7).astype(jnp.int32),
            2 * band + jnp.where(outer, 0, 1),
        ]
    )
    x = jnp.arange(slabs * depth, dtype=jnp.int32)[:, None]
    past = jnp.where(forward[None, :], x - (slab * depth + depth - 1), slab * depth - x)
    n = past.astype(jnp.float32)
    weight = jnp.where(past > 0, jnp.power(ratio[None, :], jnp.maximum(n, 0.0)), 0.0)
    return floats, ints, jnp.concatenate([weight, n * weight, (0.5 * n * (n + 1.0)) * weight], axis=1)


def kind_table(speed, rate, storage, threshold, generation):
    rows = []
    for cosine in COSINES:
        diagonal = diagonal_of(speed, rate, cosine)
        therm = rate * storage / diagonal
        rows.append(jnp.stack([therm, therm / (4.0 * threshold**3), generation / diagonal]))
    return jnp.stack(rows, axis=2).reshape(3, 2 * FREQ_GROUPS)


def newton(density, kelvin, linear, quart):
    for _ in range(NEWTON):
        cube = kelvin * kelvin * kelvin
        residual = linear * kelvin + quart * (kelvin * cube) - density
        kelvin = kelvin - residual / (linear + 4.0 * quart * cube)
    return kelvin


def add_up(refs):
    values = [ref[...] for ref in refs]
    while len(values) > 1:
        values = [a + b for a, b in zip(values[::2], values[1::2])]
    return values[0]


def stencil(low, high, c_self, c_y, c_z, shift_y, shift_z, at_edge):
    turned_low, turned_high = pltpu.roll(low, shift_y, 0), pltpu.roll(high, shift_y, 0)
    up_low = jnp.where(at_edge, turned_high, turned_low)
    up_high = jnp.where(at_edge, turned_low, turned_high)
    return (
        c_self * low + c_y * up_low + c_z * pltpu.roll(low, shift_z, 1),
        c_self * high + c_y * up_high + c_z * pltpu.roll(high, shift_z, 1),
    )


def sweep_kernel(which, sizes, *refs):
    block, blocks, depth, width_y, slots, modes, group = sizes
    refs = list(refs)
    take = lambda count: [refs.pop(0) for _ in range(count)]
    meta, floats, ints, kinds, energy, flag, matrix = take(7)
    kelvins = take(1 if which == 1 else modes)
    older = take(which - 1)
    (swept,) = take(1)
    if which == 1:
        stencil_one, stencil_two, quarter = take(3)
    elif which == 2:
        (stencil_one,) = take(1)
    faces = take(group)
    shares = take(modes)
    outgoing, density, sources, kelvin = take(4)
    own = slots // group
    rows = width_y // modes
    step = pl.program_id(0)
    slab, mode = meta[SLAB], meta[MODE]

    @pl.when(step == 0)
    def _():
        if which == 1:
            kelvin[...] = kelvins[0][...]
            for yy in range(rows):
                quarter[:, yy * 128 : (yy + 1) * 128] = kelvin[pl.ds(mode * rows + yy, depth, stride=width_y), :]
        else:
            for by in range(modes):
                for yy in range(rows):
                    y = (mode ^ by) * rows + yy
                    kelvin[pl.ds(y, depth, stride=width_y), :] = kelvins[by][:, yy * 128 : (yy + 1) * 128]
        density[...] = jnp.zeros_like(density)

        def one_cell_row(x, carry):
            at = pl.ds(x * width_y, width_y)
            t = kelvin[at, :]
            square = t * t
            fourth = square * square
            heat = flag[at, :].astype(jnp.float32)
            for kind in range(2 * FREQ_GROUPS):
                sources[kind, at, :] = kinds[0, kind] * t + kinds[1, kind] * fourth + kinds[2, kind] * heat
            return carry

        lax.fori_loop(0, depth, one_cell_row, 0)

    row = lax.broadcasted_iota(jnp.int32, (8, 128), 0)

    def one_slot(i, carry):
        s = step * block + i
        forward = ints[FORWARD, s]
        start = jnp.where(forward == 1, 0, depth - 1)
        stride = jnp.where(forward == 1, 1, -1)
        c_self, c_y, c_z, ratio = floats[SELF, s], floats[UPY, s], floats[UPZ, s], floats[RATIO, s]
        kind = ints[KIND, s]
        at_edge = row == ints[EDGE_Y, s]
        apply = lambda low, high: stencil(low, high, c_self, c_y, c_z, ints[SHIFT_Y, s], ints[SHIFT_Z, s], at_edge)
        total_low = total_high = jnp.full((8, 128), floats[WALL, s], jnp.float32)
        for j in range(depth):
            at = (start + stride * j) * 16
            at_low, at_high = pl.ds(at, 8), pl.ds(at + 8, 8)
            low, high = apply(energy[i, at_low, :], energy[i, at_high, :])
            total_low = ratio * total_low + (low + sources[kind, at_low, :])
            total_high = ratio * total_high + (high + sources[kind, at_high, :])
            swept[i, at_low, :] = total_low
            swept[i, at_high, :] = total_high
            density[at_low, :] += total_low
            density[at_high, :] += total_high
        at_low, at_high = pl.ds(s * 16, 8), pl.ds(s * 16 + 8, 8)
        outgoing[at_low, :] = total_low
        outgoing[at_high, :] = total_high
        if which < ITERS:
            low, high = apply(total_low, total_high)
            stencil_one[at_low, :] = low
            stencil_one[at_high, :] = high
        if which == 1:
            low, high = apply(low, high)
            stencil_two[at_low, :] = low
            stencil_two[at_high, :] = high
        return carry

    lax.fori_loop(0, block, one_slot, 0, unroll=2)

    @pl.when(step == blocks - 1)
    def _():
        face = stencil_two if which == 1 else stencil_one if which == 2 else outgoing
        for by in range(group):
            faces[by][...] = face[pl.ds(((slab % group) ^ by) * own * 16, own * 16), :]
        planes = [outgoing] + older
        home = pl.ds(slab * depth, depth)
        for by in range(modes):
            ys = [(mode ^ by) * rows + yy for yy in range(rows)]
            total = None
            for index, plane in enumerate(planes):
                right = jnp.concatenate([plane[pl.ds(y, slots, stride=width_y), :] for y in ys], axis=1)
                term = jnp.dot(
                    matrix[:, index * slots : (index + 1) * slots],
                    right,
                    precision=lax.Precision.HIGHEST,
                    preferred_element_type=jnp.float32,
                )
                total = term if total is None else total + term
            shares[by][...] = total
            shares[by][home, :] += jnp.concatenate([density[pl.ds(y, depth, stride=width_y), :] for y in ys], axis=1)


def partial_kernel(slabs, depth, modes, meta, *refs):
    shares, outs, total = refs[:modes], refs[modes:-1], refs[-1]
    total[...] = add_up(shares)
    for by in range(slabs):
        outs[by][...] = total[pl.ds((meta[SLAB] ^ by) * depth, depth), :]


def newton_kernel(sums, before, *rest):
    parts, kelvin = rest[:-1], rest[-1]
    kelvin[...] = newton(add_up(parts) * (1.0 / DIRS), before[...], sums[0], sums[1])


def compose_kernel(own, group, earlier, meta, floats, ints, *refs):
    refs = list(refs)
    received, entered = refs[:group], refs[group : group + earlier]
    composite, effective = refs[group + earlier :]
    place = meta[SLAB] % group
    for by in range(group):
        effective[place ^ by] = received[by][...]

    def one_slot(i, carry):
        s = place * own + i
        forward = ints[FORWARD, s]
        start = jnp.where(forward == 1, 0, group - 1)
        stride = jnp.where(forward == 1, 1, -1)
        at = pl.ds(i * 16, 16)
        total = jnp.zeros((16, 128), jnp.float32)
        for j in range(group):
            k = start + stride * j
            value = effective[k, at, :]
            if earlier:
                for back in range(earlier):
                    value += floats[FULL_N + back, s] * entered[earlier - 1 - back][k, at, :]
                effective[k, at, :] = value
            total = floats[FULL, s] * total + value
        composite[at, :] = total
        return carry

    lax.fori_loop(0, own, one_slot, 0)


def enter_kernel(own, group, groups, meta, floats, ints, effective, *refs):
    composites, (entered, *outs, ordered) = refs[:groups], refs[groups:]
    slab = meta[SLAB]
    place, mine = slab % group, slab // group
    for by in range(groups):
        ordered[mine ^ by] = composites[by][...]

    def one_slot(i, carry):
        s = place * own + i
        forward = ints[FORWARD, s]
        start = jnp.where(forward == 1, 0, group - 1)
        stride = jnp.where(forward == 1, 1, -1)
        begin = jnp.where(forward == 1, 0, groups - 1)
        ahead = jnp.where(forward == 1, mine, groups - 1 - mine)
        at = pl.ds(i * 16, 16)
        total = jnp.zeros((16, 128), jnp.float32)
        for g in range(groups - 1):
            later = floats[FULL_GROUP, s] * total + ordered[begin + stride * g, at, :]
            total = jnp.where(g < ahead, later, total)
        for j in range(group):
            k = start + stride * j
            entered[k, at, :] = total
            if j < group - 1:
                total = floats[FULL, s] * total + effective[k, at, :]
        return carry

    lax.fori_loop(0, own, one_slot, 0)
    for by in range(group):
        outs[by][...] = entered[place ^ by]


def final_kernel(block, depth, width_y, own, group, modes, meta, floats, ints, swept, *refs):
    planes = [refs[index * group : (index + 1) * group] for index in range(ITERS)]
    kelvins = refs[ITERS * group : ITERS * group + modes]
    energy, kelvin, *ordered = refs[ITERS * group + modes :]
    step = pl.program_id(0)
    place = meta[SLAB] % group
    rows = width_y // modes

    @pl.when(step == 0)
    def _():
        for index in range(ITERS):
            for by in range(group):
                ordered[index][pl.ds((place ^ by) * own * 16, own * 16), :] = planes[index][by][...]
        for by in range(modes):
            for yy in range(rows):
                y = (meta[MODE] ^ by) * rows + yy
                kelvin[pl.ds(y, depth, stride=width_y), :] = kelvins[by][:, yy * 128 : (yy + 1) * 128]

    def one_slot(i, carry):
        s = step * block + i
        forward = ints[FORWARD, s]
        start = jnp.where(forward == 1, 0, depth - 1)
        stride = jnp.where(forward == 1, 1, -1)
        ratio = floats[RATIO, s]
        at = pl.ds(s * 16, 16)
        first, second, third = (ref[at, :] for ref in ordered)
        for j in range(depth):
            first = ratio * first
            second = ratio * second + first
            third = ratio * third + second
            here = pl.ds((start + stride * j) * 16, 16)
            energy[i, here, :] = swept[i, here, :] + third
        return carry

    lax.fori_loop(0, block, one_slot, 0, unroll=2)


def local(incoming_occupation, crystal_kelvin_given, generating_region_flag, labels, speed, rate, storage, threshold, generation):
    slots, depth, width_y, width_z = incoming_occupation.shape
    slabs, modes = lax.axis_size("slab"), lax.axis_size("mode")
    group, groups = GROUP, slabs // GROUP
    own = slots // group
    lanes = width_y // modes * width_z
    block = 8
    blocks = slots // block
    slab = lax.axis_index("slab").astype(jnp.int32)
    mode = lax.axis_index("mode").astype(jnp.int32)
    meta = jnp.stack([slab, mode])
    floats, ints, matrix = slot_tables(labels, speed, rate, storage, threshold, slab, slabs, depth, width_y, width_z)
    kinds = kind_table(speed, rate, storage, threshold, generation)
    sums = jnp.stack([jnp.sum(storage), jnp.sum(storage / (4.0 * threshold**3))])

    def shape(*dims):
        return jax.ShapeDtypeStruct(dims, jnp.float32)

    def whole(*dims):
        return pl.BlockSpec(dims, lambda i: (0,) * len(dims))

    def swap(array, axis, by):
        size = lax.axis_size(axis)
        return lax.ppermute(array, axis, [(i, i ^ by) for i in range(size)])

    cells = depth * width_y
    slot_block = pl.BlockSpec((block, cells, width_z), lambda i: (i, 0, 0))
    face_rows = own * width_y

    def sweep(which, energy, kelvins, older):
        outs = [(slot_block, shape(slots, cells, width_z))]
        plane = (whole(slots * width_y, width_z), shape(slots * width_y, width_z))
        if which == 1:
            outs += [plane, plane, (whole(depth, lanes), shape(depth, lanes))]
        elif which == 2:
            outs += [plane]
        outs += [(whole(face_rows, width_z), shape(face_rows, width_z))] * group
        outs += [(whole(slabs * depth, lanes), shape(slabs * depth, lanes))] * modes
        results = pl.pallas_call(
            functools.partial(sweep_kernel, which, (block, blocks, depth, width_y, slots, modes, group)),
            grid=(blocks,),
            in_specs=[SMEM] * 4
            + [slot_block, whole(cells, width_z), whole(slabs * depth, ITERS * slots)]
            + [whole(*k.shape) for k in kelvins]
            + [whole(slots * width_y, width_z)] * len(older),
            out_specs=[spec for spec, _ in outs],
            out_shape=[of for _, of in outs],
            scratch_shapes=[
                pltpu.VMEM((slots * width_y, width_z), jnp.float32),
                pltpu.VMEM((cells, width_z), jnp.float32),
                pltpu.VMEM((2 * FREQ_GROUPS, cells, width_z), jnp.float32),
                pltpu.VMEM((cells, width_z), jnp.float32),
            ],
            compiler_params=PARAMS,
            name=f"sweep_{which}",
        )(meta, floats, ints, kinds, energy, flag, matrix, *kelvins, *older)
        return results[: -group - modes], results[-group - modes : -modes], results[-modes:]

    def solve(shares, before):
        shares = [shares[0]] + [swap(shares[by], "mode", by) for by in range(1, modes)]
        parts = pl.pallas_call(
            functools.partial(partial_kernel, slabs, depth, modes),
            in_specs=[SMEM] + [VMEM] * modes,
            out_specs=[VMEM] * slabs,
            out_shape=[shape(depth, lanes)] * slabs,
            scratch_shapes=[pltpu.VMEM((slabs * depth, lanes), jnp.float32)],
            compiler_params=PARAMS,
            name="density_parts",
        )(meta, *shares)
        parts = [parts[0]] + [swap(parts[by], "slab", by) for by in range(1, slabs)]
        quarter = pl.pallas_call(
            newton_kernel,
            in_specs=[SMEM] + [VMEM] * (slabs + 1),
            out_specs=VMEM,
            out_shape=shape(depth, lanes),
            compiler_params=PARAMS,
            name="newton",
        )(sums, before, *parts)
        return quarter, [quarter] + [swap(quarter, "mode", by) for by in range(1, modes)]

    def exchange(faces, before):
        received = [faces[0]] + [swap(faces[by], "slab", by) for by in range(1, group)]
        composite, effective = pl.pallas_call(
            functools.partial(compose_kernel, own, group, len(before)),
            in_specs=[SMEM] * 3 + [VMEM] * (group + len(before)),
            out_specs=[VMEM] * 2,
            out_shape=[shape(face_rows, width_z), shape(group, face_rows, width_z)],
            compiler_params=PARAMS,
            name="compose",
        )(meta, floats, ints, *received, *before)
        composites = [composite] + [swap(composite, "slab", by * group) for by in range(1, groups)]
        entered, *outs = pl.pallas_call(
            functools.partial(enter_kernel, own, group, groups),
            in_specs=[SMEM] * 3 + [VMEM] * (1 + groups),
            out_specs=[VMEM] * (1 + group),
            out_shape=[shape(group, face_rows, width_z)] + [shape(face_rows, width_z)] * group,
            scratch_shapes=[pltpu.VMEM((groups, face_rows, width_z), jnp.float32)],
            compiler_params=PARAMS,
            name="enter",
        )(meta, floats, ints, effective, *composites)
        return entered, [outs[0]] + [swap(outs[by], "slab", by) for by in range(1, group)]

    flag = generating_region_flag.reshape(cells, width_z)
    energy = incoming_occupation.reshape(slots, cells, width_z)
    kelvins = [crystal_kelvin_given.reshape(cells, width_z)]

    (energy, once, twice, quarter), faces, shares = sweep(1, energy, kelvins, [])
    quarter, kelvins = solve(shares, quarter)
    entered_one, planes_one = exchange(faces, [])

    (energy, once_two), faces, shares = sweep(2, energy, kelvins, [once])
    quarter, kelvins = solve(shares, quarter)
    entered_two, planes_two = exchange(faces, [entered_one])

    (energy,), faces, shares = sweep(3, energy, kelvins, [once_two, twice])
    quarter, kelvins = solve(shares, quarter)
    _, planes_three = exchange(faces, [entered_one, entered_two])

    energy, kelvin = pl.pallas_call(
        functools.partial(final_kernel, block, depth, width_y, own, group, modes),
        grid=(blocks,),
        in_specs=[SMEM] * 3
        + [slot_block]
        + [whole(face_rows, width_z)] * (ITERS * group)
        + [whole(depth, lanes)] * modes,
        out_specs=[slot_block, whole(cells, width_z)],
        out_shape=[shape(slots, cells, width_z), shape(cells, width_z)],
        scratch_shapes=[pltpu.VMEM((slots * width_y, width_z), jnp.float32)] * ITERS,
        compiler_params=PARAMS,
        name="final_energy",
    )(meta, floats, ints, energy, *planes_one, *planes_two, *planes_three, *kelvins)
    return energy.reshape(slots, depth, width_y, width_z), kelvin.reshape(depth, width_y, width_z)


def solution(mesh):
    return jax.shard_map(
        local,
        mesh=mesh,
        in_specs=(
            P("mode", "slab", None, None),
            P("slab", None, None),
            P("slab", None, None),
            P("mode"),
            P(),
            P(),
            P(),
            P(),
            P(),
        ),
        out_specs=(P("mode", "slab", None, None), P("slab", None, None)),
        check_vma=False,
    )
```

```python
import functools
import math

import jax
import jax.numpy as jnp
import numpy as np
from jax import lax
from jax.experimental import pallas as pl
from jax.experimental.pallas import tpu as pltpu
from jax.sharding import PartitionSpec as P

FREQ_GROUPS = 8
DIRS = 32
ITERS = 3
NEWTON = 4
PSEUDO_RATE = 0.03
GROUP = 4
COSINES = (np.float32(0.99995), np.float32(0.9999))

SELF, UPY, UPZ, RATIO, WALL, FULL, FULL_N, FULL_T, FULL_GROUP = range(9)
FORWARD, SHIFT_Y, SHIFT_Z, EDGE_Y, KIND = range(5)
SLAB, MODE = range(2)

SMEM = pl.BlockSpec(memory_space=pltpu.SMEM)
VMEM = pl.BlockSpec(memory_space=pltpu.VMEM)
PARAMS = pltpu.CompilerParams(vmem_limit_bytes=48 * 1024 * 1024)


def diagonal_of(speed, rate, cosine):
    sine = jnp.sqrt(1.0 - cosine * cosine)
    across = np.float32(math.cos(math.pi / 8) + math.sin(math.pi / 8))
    return speed * (cosine + sine * across) + rate + PSEUDO_RATE


def slot_tables(labels, speed, rate, storage, threshold, slab, slabs, depth, width_y, width_z):
    band = labels // DIRS
    direction = labels % DIRS
    of_band = (band[None, :] == jnp.arange(FREQ_GROUPS, dtype=jnp.int32)[:, None]).astype(jnp.float32)
    speed, rate, storage, threshold = (
        jnp.sum(of_band * value[:, None], axis=0) for value in (speed, rate, storage, threshold)
    )
    polar = direction % 4
    outer = (polar == 0) | (polar == 3)
    forward = polar < 2
    cosine = jnp.where(outer, COSINES[0], COSINES[1])
    sine = jnp.sqrt(1.0 - cosine * cosine)
    azimuth = ((direction // 4).astype(jnp.float32) + 0.5) * (2.0 * math.pi / (DIRS // 4))
    vy = speed * sine * jnp.cos(azimuth)
    vz = speed * sine * jnp.sin(azimuth)
    diagonal = diagonal_of(speed, rate, cosine)
    ratio = speed * cosine / diagonal
    full = lax.integer_pow(ratio, depth)
    at_wall = jnp.where(forward, slab == 0, slab == slabs - 1)
    wall = storage * (1.0 + 1.0 / (4.0 * threshold**3))
    floats = jnp.stack(
        [
            PSEUDO_RATE / diagonal,
            jnp.abs(vy) / diagonal,
            jnp.abs(vz) / diagonal,
            ratio,
            jnp.where(at_wall, wall, 0.0),
            full,
            depth * full,
            (depth * (depth + 1) // 2) * full,
            lax.integer_pow(full, GROUP),
        ]
    )
    ints = jnp.stack(
        [
            forward.astype(jnp.int32),
            jnp.where(vy > 0, 1, 7).astype(jnp.int32),
            jnp.where(vz > 0, 1, width_z - 1).astype(jnp.int32),
            jnp.where(vy > 0, 0, 7).astype(jnp.int32),
            2 * band + jnp.where(outer, 0, 1),
        ]
    )
    x = jnp.arange(slabs * depth, dtype=jnp.int32)[:, None]
    past = jnp.where(forward[None, :], x - (slab * depth + depth - 1), slab * depth - x)
    n = past.astype(jnp.float32)
    weight = jnp.where(past > 0, jnp.power(ratio[None, :], jnp.maximum(n, 0.0)), 0.0)
    return floats, ints, jnp.concatenate([weight, n * weight, (0.5 * n * (n + 1.0)) * weight], axis=1)


def kind_table(speed, rate, storage, threshold, generation):
    rows = []
    for cosine in COSINES:
        diagonal = diagonal_of(speed, rate, cosine)
        therm = rate * storage / diagonal
        rows.append(jnp.stack([therm, therm / (4.0 * threshold**3), generation / diagonal]))
    return jnp.stack(rows, axis=2).reshape(3, 2 * FREQ_GROUPS)


def newton(density, kelvin, linear, quart):
    for _ in range(NEWTON):
        cube = kelvin * kelvin * kelvin
        residual = linear * kelvin + quart * (kelvin * cube) - density
        kelvin = kelvin - residual / (linear + 4.0 * quart * cube)
    return kelvin


def stencil(low, high, c_self, c_y, c_z, shift_y, shift_z, at_edge):
    turned_low, turned_high = pltpu.roll(low, shift_y, 0), pltpu.roll(high, shift_y, 0)
    up_low = jnp.where(at_edge, turned_high, turned_low)
    up_high = jnp.where(at_edge, turned_low, turned_high)
    return (
        c_self * low + c_y * up_low + c_z * pltpu.roll(low, shift_z, 1),
        c_self * high + c_y * up_high + c_z * pltpu.roll(high, shift_z, 1),
    )


def sweep_kernel(which, sizes, *refs):
    block, blocks, depth, width_y, slots, modes = sizes
    refs = list(refs)
    take = lambda count: [refs.pop(0) for _ in range(count)]
    meta, floats, ints, kinds, energy, flag, matrix, given = take(8)
    older = take(which - 1)
    swept, shares = take(2)
    if which == 1:
        stencil_one, stencil_two, quarter = take(3)
    elif which == 2:
        (stencil_one,) = take(1)
    else:
        (outgoing,) = take(1)
    if which < ITERS:
        (outgoing,) = take(1)
    density, sources, kelvin = take(3)
    rows = width_y // modes
    step = pl.program_id(0)

    @pl.when(step == 0)
    def _():
        if which == 1:
            kelvin[...] = given[...]
            for yy in range(rows):
                y = meta[MODE] * rows + yy
                quarter[:, yy * 128 : (yy + 1) * 128] = kelvin[pl.ds(y, depth, stride=width_y), :]
        else:
            for y in range(width_y):
                lane = (y % rows) * 128
                kelvin[pl.ds(y, depth, stride=width_y), :] = given[y // rows, :, lane : lane + 128]
        density[...] = jnp.zeros_like(density)

        def one_cell_row(x, carry):
            at = pl.ds(x * width_y, width_y)
            t = kelvin[at, :]
            square = t * t
            fourth = square * square
            heat = flag[at, :].astype(jnp.float32)
            for kind in range(2 * FREQ_GROUPS):
                sources[kind, at, :] = kinds[0, kind] * t + kinds[1, kind] * fourth + kinds[2, kind] * heat
            return carry

        lax.fori_loop(0, depth, one_cell_row, 0)

    row = lax.broadcasted_iota(jnp.int32, (8, 128), 0)

    def one_slot(i, sums):
        s = step * block + i
        forward = ints[FORWARD, s] == 1
        c_self, c_y, c_z, ratio = floats[SELF, s], floats[UPY, s], floats[UPZ, s], floats[RATIO, s]
        kind, shift_y, shift_z = ints[KIND, s], ints[SHIFT_Y, s], ints[SHIFT_Z, s]
        at_edge = row == ints[EDGE_Y, s]
        apply = lambda low, high: stencil(low, high, c_self, c_y, c_z, shift_y, shift_z, at_edge)
        layers = []
        for x in range(depth):
            at = x * 16
            low, high = apply(energy[i, at : at + 8, :], energy[i, at + 8 : at + 16, :])
            layers.append((low + sources[kind, at : at + 8, :], high + sources[kind, at + 8 : at + 16, :]))
        faces, sums = [], list(sums)
        for half in range(2):
            values = [layer[half] for layer in layers]
            values = [jnp.where(forward, a, b) for a, b in zip(values, values[::-1])]
            total = jnp.full((8, 128), floats[WALL, s], jnp.float32)
            for j in range(depth):
                total = ratio * total + values[j]
                values[j] = total
            faces.append(total)
            values = [jnp.where(forward, a, b) for a, b in zip(values, values[::-1])]
            for x in range(depth):
                at = x * 16 + half * 8
                swept[i, at : at + 8, :] = values[x]
                sums[2 * x + half] = sums[2 * x + half] + values[x]
        at_low, at_high = pl.ds(s * 16, 8), pl.ds(s * 16 + 8, 8)
        low, high = faces
        outgoing[at_low, :] = low
        outgoing[at_high, :] = high
        if which < ITERS:
            low, high = apply(low, high)
            stencil_one[at_low, :] = low
            stencil_one[at_high, :] = high
        if which == 1:
            low, high = apply(low, high)
            stencil_two[at_low, :] = low
            stencil_two[at_high, :] = high
        return tuple(sums)

    sums = lax.fori_loop(0, block, one_slot, (jnp.zeros((8, 128), jnp.float32),) * (2 * depth), unroll=4)
    for part in range(2 * depth):
        density[part * 8 : part * 8 + 8, :] += sums[part]

    @pl.when(step == blocks - 1)
    def _():
        planes = [outgoing] + older
        home = pl.ds(meta[SLAB] * depth, depth)
        for at in range(modes):
            ys = [at * rows + yy for yy in range(rows)]
            total = None
            for index, plane in enumerate(planes):
                right = jnp.concatenate([plane[pl.ds(y, slots, stride=width_y), :] for y in ys], axis=1)
                term = jnp.dot(
                    matrix[:, index * slots : (index + 1) * slots],
                    right,
                    precision=lax.Precision.HIGHEST,
                    preferred_element_type=jnp.float32,
                )
                total = term if total is None else total + term
            shares[at] = total
            shares[at, home, :] += jnp.concatenate([density[pl.ds(y, depth, stride=width_y), :] for y in ys], axis=1)


def add_up(ref):
    values = [ref[index] for index in range(ref.shape[0])]
    while len(values) > 1:
        values = [a + b for a, b in zip(values[::2], values[1::2])]
    return values[0]


def partial_kernel(depth, shares, parts):
    total = add_up(shares)
    for slab in range(parts.shape[0]):
        parts[slab] = total[slab * depth : (slab + 1) * depth]


def newton_kernel(sums, before, parts, kelvin, copies):
    now = newton(add_up(parts) * (1.0 / DIRS), before[...], sums[0], sums[1])
    kelvin[...] = now
    for index in range(copies.shape[0]):
        copies[index] = now


def compose_kernel(own, group, earlier, meta, floats, ints, received, *refs):
    entered, composite = refs[:earlier], refs[earlier]
    effective = refs[earlier + 1] if earlier else None
    base = meta[SLAB] % group * own

    def one_slot(i, carry):
        s = base + i
        forward = ints[FORWARD, s] == 1
        at = pl.ds(i * 16, 16)
        values = []
        for k in range(group):
            value = received[k, at, :]
            for back in range(earlier):
                value += floats[FULL_N + back, s] * entered[earlier - 1 - back][k, at, :]
            if earlier:
                effective[k, at, :] = value
            values.append(value)
        values = [jnp.where(forward, a, b) for a, b in zip(values, values[::-1])]
        total = values[0]
        for value in values[1:]:
            total = floats[FULL, s] * total + value
        composite[at, :] = total
        return carry

    lax.fori_loop(0, own, one_slot, 0, unroll=4)


def enter_kernel(own, group, groups, meta, floats, ints, effective, *refs):
    composites, (entered, ordered) = refs[:groups], refs[groups:]
    slab = meta[SLAB]
    place, mine = slab % group, slab // group
    for by in range(groups):
        ordered[mine ^ by] = composites[by][...]

    def one_slot(i, carry):
        s = place * own + i
        forward = ints[FORWARD, s] == 1
        begin = jnp.where(forward, 0, groups - 1)
        stride = jnp.where(forward, 1, -1)
        ahead = jnp.where(forward, mine, groups - 1 - mine)
        at = pl.ds(i * 16, 16)
        total = jnp.zeros((16, 128), jnp.float32)
        for g in range(groups - 1):
            later = floats[FULL_GROUP, s] * total + ordered[begin + stride * g, at, :]
            total = jnp.where(g < ahead, later, total)
        values = [effective[k, at, :] for k in range(group)]
        values = [jnp.where(forward, a, b) for a, b in zip(values, values[::-1])]
        inflow = [total]
        for value in values[:-1]:
            total = floats[FULL, s] * total + value
            inflow.append(total)
        for k in range(group):
            entered[k, at, :] = jnp.where(forward, inflow[k], inflow[group - 1 - k])
        return carry

    lax.fori_loop(0, own, one_slot, 0, unroll=4)


def final_kernel(block, depth, width_y, modes, floats, ints, swept, first, second, third, kelvins, energy, kelvin):
    step = pl.program_id(0)
    rows = width_y // modes

    @pl.when(step == 0)
    def _():
        for y in range(width_y):
            lane = (y % rows) * 128
            kelvin[pl.ds(y, depth, stride=width_y), :] = kelvins[y // rows, :, lane : lane + 128]

    def one_slot(i, carry):
        s = step * block + i
        forward = ints[FORWARD, s] == 1
        ratio = floats[RATIO, s]
        at = pl.ds(s * 16, 16)
        a, b, c = first[at, :], second[at, :], third[at, :]
        values = []
        for j in range(depth):
            a = ratio * a
            b = ratio * b + a
            c = ratio * c + b
            values.append(c)
        for x in range(depth):
            here = slice(x * 16, x * 16 + 16)
            energy[i, here, :] = swept[i, here, :] + jnp.where(forward, values[x], values[depth - 1 - x])
        return carry

    lax.fori_loop(0, block, one_slot, 0, unroll=4)


def local(incoming_occupation, crystal_kelvin_given, generating_region_flag, labels, speed, rate, storage, threshold, generation):
    slots, depth, width_y, width_z = incoming_occupation.shape
    slabs, modes = lax.axis_size("slab"), lax.axis_size("mode")
    group, groups = GROUP, slabs // GROUP
    own = slots // group
    lanes = width_y // modes * width_z
    block = 8
    blocks = slots // block
    slab = lax.axis_index("slab").astype(jnp.int32)
    meta = jnp.stack([slab, lax.axis_index("mode").astype(jnp.int32)])
    floats, ints, matrix = slot_tables(labels, speed, rate, storage, threshold, slab, slabs, depth, width_y, width_z)
    kinds = kind_table(speed, rate, storage, threshold, generation)
    sums = jnp.stack([jnp.sum(storage), jnp.sum(storage / (4.0 * threshold**3))])

    def shape(*dims):
        return jax.ShapeDtypeStruct(dims, jnp.float32)

    def whole(*dims):
        return pl.BlockSpec(dims, lambda i: (0,) * len(dims))

    cells = depth * width_y
    slot_block = pl.BlockSpec((block, cells, width_z), lambda i: (i, 0, 0))
    face_rows = own * width_y
    members = [list(range(g * group, (g + 1) * group)) for g in range(groups)]
    near = functools.partial(lax.all_to_all, axis_name="slab", split_axis=0, concat_axis=0, axis_index_groups=members)
    over = lambda array, axis: lax.all_to_all(array, axis, 0, 0)

    def sweep(which, energy, kelvin, older):
        plane = (whole(slots * width_y, width_z), shape(slots * width_y, width_z))
        outs = [(slot_block, shape(slots, cells, width_z))]
        outs += [(whole(modes, slabs * depth, lanes), shape(modes, slabs * depth, lanes))]
        if which == 1:
            outs += [plane, plane, (whole(depth, lanes), shape(depth, lanes))]
        else:
            outs += [plane]
        face = [pltpu.VMEM((slots * width_y, width_z), jnp.float32)] if which < ITERS else []
        return pl.pallas_call(
            functools.partial(sweep_kernel, which, (block, blocks, depth, width_y, slots, modes)),
            grid=(blocks,),
            in_specs=[SMEM] * 4
            + [slot_block, whole(cells, width_z), whole(slabs * depth, ITERS * slots), whole(*kelvin.shape)]
            + [whole(slots * width_y, width_z)] * len(older),
            out_specs=[spec for spec, _ in outs],
            out_shape=[of for _, of in outs],
            scratch_shapes=face
            + [
                pltpu.VMEM((cells, width_z), jnp.float32),
                pltpu.VMEM((2 * FREQ_GROUPS, cells, width_z), jnp.float32),
                pltpu.VMEM((cells, width_z), jnp.float32),
            ],
            compiler_params=PARAMS,
            name=f"sweep_{which}",
        )(meta, floats, ints, kinds, energy, flag, matrix, kelvin, *older)

    def solve(shares, before):
        parts = pl.pallas_call(
            functools.partial(partial_kernel, depth),
            in_specs=[VMEM],
            out_specs=VMEM,
            out_shape=shape(slabs, depth, lanes),
            compiler_params=PARAMS,
            name="density_parts",
        )(over(shares, "mode"))
        quarter, copies = pl.pallas_call(
            newton_kernel,
            in_specs=[SMEM, VMEM, VMEM],
            out_specs=[VMEM, VMEM],
            out_shape=[shape(depth, lanes), shape(modes, depth, lanes)],
            compiler_params=PARAMS,
            name="newton",
        )(sums, before, over(parts, "slab"))
        return quarter, over(copies, "mode")

    def exchange(face, before):
        received = near(face.reshape(group, face_rows, width_z))
        blocked = shape(group, face_rows, width_z)
        composite, *effective = pl.pallas_call(
            functools.partial(compose_kernel, own, group, len(before)),
            in_specs=[SMEM] * 3 + [VMEM] * (1 + len(before)),
            out_specs=[VMEM] * (2 if before else 1),
            out_shape=[shape(face_rows, width_z)] + ([blocked] if before else []),
            compiler_params=PARAMS,
            name="compose",
        )(meta, floats, ints, received, *before)
        composites = [composite] + [
            lax.ppermute(composite, "slab", [(i, i ^ (by * group)) for i in range(slabs)]) for by in range(1, groups)
        ]
        entered = pl.pallas_call(
            functools.partial(enter_kernel, own, group, groups),
            in_specs=[SMEM] * 3 + [VMEM] * (1 + groups),
            out_specs=VMEM,
            out_shape=blocked,
            scratch_shapes=[pltpu.VMEM((groups, face_rows, width_z), jnp.float32)],
            compiler_params=PARAMS,
            name="enter",
        )(meta, floats, ints, effective[0] if before else received, *composites)
        return entered, near(entered).reshape(slots * width_y, width_z)

    flag = generating_region_flag.reshape(cells, width_z)
    energy = incoming_occupation.reshape(slots, cells, width_z)

    energy, shares, once, twice, quarter = sweep(1, energy, crystal_kelvin_given.reshape(cells, width_z), [])
    quarter, kelvin = solve(shares, quarter)
    entered_one, plane_one = exchange(twice, [])

    energy, shares, once_two = sweep(2, energy, kelvin, [once])
    quarter, kelvin = solve(shares, quarter)
    entered_two, plane_two = exchange(once_two, [entered_one])

    energy, shares, outgoing = sweep(3, energy, kelvin, [once_two, twice])
    quarter, kelvin = solve(shares, quarter)
    _, plane_three = exchange(outgoing, [entered_one, entered_two])

    energy, kelvin = pl.pallas_call(
        functools.partial(final_kernel, block, depth, width_y, modes),
        grid=(blocks,),
        in_specs=[SMEM] * 2
        + [slot_block]
        + [whole(slots * width_y, width_z)] * ITERS
        + [whole(modes, depth, lanes)],
        out_specs=[slot_block, whole(cells, width_z)],
        out_shape=[shape(slots, cells, width_z), shape(cells, width_z)],
        compiler_params=PARAMS,
        name="final_energy",
    )(floats, ints, energy, plane_one, plane_two, plane_three, kelvin)
    return energy.reshape(slots, depth, width_y, width_z), kelvin.reshape(depth, width_y, width_z)


def solution(mesh):
    return jax.shard_map(
        local,
        mesh=mesh,
        in_specs=(
            P("mode", "slab", None, None),
            P("slab", None, None),
            P("slab", None, None),
            P("mode"),
            P(),
            P(),
            P(),
            P(),
            P(),
        ),
        out_specs=(P("mode", "slab", None, None), P("slab", None, None)),
        check_vma=False,
    )
```

```python
import functools
import math

import jax
import jax.numpy as jnp
import numpy as np
from jax import lax
from jax.experimental import pallas as pl
from jax.experimental.pallas import tpu as pltpu
from jax.sharding import PartitionSpec as P

FREQ_GROUPS = 8
DIRS = 32
ITERS = 3
NEWTON = 4
PSEUDO_RATE = 0.03
GROUP = 4
COSINES = (np.float32(0.99995), np.float32(0.9999))

SELF, UPY, UPZ, RATIO, WALL, FULL, FULL_N, FULL_T, FULL_GROUP, WARM = range(10)
FORWARD, SHIFT_Y, SHIFT_Z, EDGE_Y, KIND = range(5)
THERM, QUART, HEAT, DECAY, STAY, AROUND = range(6)
KINDS = 2 * FREQ_GROUPS
SLAB, MODE = range(2)

SMEM = pl.BlockSpec(memory_space=pltpu.SMEM)
VMEM = pl.BlockSpec(memory_space=pltpu.VMEM)
PARAMS = pltpu.CompilerParams(vmem_limit_bytes=48 * 1024 * 1024)
ACROSS = math.cos(math.pi / 8) + math.sin(math.pi / 8)


def diagonal_of(speed, rate, cosine):
    sine = jnp.sqrt(1.0 - cosine * cosine)
    return speed * (cosine + sine * np.float32(ACROSS)) + rate + PSEUDO_RATE


def slot_tables(labels, speed, rate, storage, threshold, generation, slab, slabs, depth, width_z):
    band = labels // DIRS
    direction = labels % DIRS
    of_band = (band[None, :] == jnp.arange(FREQ_GROUPS, dtype=jnp.int32)[:, None]).astype(jnp.float32)
    speed, rate, storage, threshold, generation = (
        jnp.sum(of_band * value[:, None], axis=0) for value in (speed, rate, storage, threshold, generation)
    )
    polar = direction % 4
    outer = (polar == 0) | (polar == 3)
    forward = polar < 2
    cosine = jnp.where(outer, COSINES[0], COSINES[1])
    sine = jnp.sqrt(1.0 - cosine * cosine)
    azimuth = ((direction // 4).astype(jnp.float32) + 0.5) * (2.0 * math.pi / (DIRS // 4))
    vy = speed * sine * jnp.cos(azimuth)
    vz = speed * sine * jnp.sin(azimuth)
    diagonal = diagonal_of(speed, rate, cosine)
    ratio = speed * cosine / diagonal
    full = lax.integer_pow(ratio, depth)
    at_wall = jnp.where(forward, slab == 0, slab == slabs - 1)
    wall = storage * (1.0 + 1.0 / (4.0 * threshold**3))
    floats = jnp.stack(
        [
            PSEUDO_RATE / diagonal,
            jnp.abs(vy) / diagonal,
            jnp.abs(vz) / diagonal,
            ratio,
            jnp.where(at_wall, wall, 0.0),
            full,
            depth * full,
            (depth * (depth + 1) // 2) * full,
            lax.integer_pow(full, GROUP),
            generation / diagonal,
        ]
    )
    ints = jnp.stack(
        [
            forward.astype(jnp.int32),
            jnp.where(vy > 0, 1, 7).astype(jnp.int32),
            jnp.where(vz > 0, 1, width_z - 1).astype(jnp.int32),
            jnp.where(vy > 0, 0, 7).astype(jnp.int32),
            2 * band + jnp.where(outer, 0, 1),
        ]
    )
    x = jnp.arange(slabs * depth, dtype=jnp.int32)[:, None]
    past = jnp.where(forward[None, :], x - (slab * depth + depth - 1), slab * depth - x)
    n = past.astype(jnp.float32)
    weight = jnp.where(past > 0, jnp.power(ratio[None, :], jnp.maximum(n, 0.0)), 0.0)
    return floats, ints, jnp.concatenate([weight, n * weight, (0.5 * n * (n + 1.0)) * weight], axis=1)


def kind_table(speed, rate, storage, threshold, generation):
    rows = []
    for cosine in COSINES:
        diagonal = diagonal_of(speed, rate, cosine)
        therm = rate * storage / diagonal
        quart = therm / (4.0 * threshold**3)
        across = jnp.sqrt(1.0 - cosine * cosine) * np.float32(2.0 * ACROSS)
        rows.append(
            jnp.stack(
                [
                    therm,
                    quart,
                    generation / diagonal,
                    speed * cosine / diagonal,
                    (DIRS // 4) * PSEUDO_RATE / diagonal,
                    across * speed / diagonal,
                ]
            )
        )
    return jnp.stack(rows, axis=2).reshape(6, KINDS)


def heat_matrices(kinds, slab, slabs, depth):
    cells = slabs * depth
    there = jnp.arange(cells, dtype=jnp.int32)
    decay = kinds[DECAY][:, None, None]
    per_cell = (DIRS // 4) / DIRS

    def side_by_side(weight, factor):
        sums = [jnp.sum((factor * kinds[row])[:, None, None] * weight, axis=0) for row in (THERM, QUART)]
        return jnp.concatenate(sums, axis=1)

    def between(here):
        far = jnp.abs(here[:, None] - there[None, :])
        n = far.astype(jnp.float32)
        return n, jnp.power(decay, n[None]) * jnp.where(far == 0, 2.0, 1.0)[None]

    _, everywhere = between(there)
    n, home = between(slab * depth + jnp.arange(depth, dtype=jnp.int32))
    twice = home * (n + 1.0)[None]
    one = jnp.full((KINDS,), per_cell, jnp.float32)
    once = side_by_side(home, one)
    stay = side_by_side(twice, kinds[STAY] / DIRS)
    around = side_by_side(twice, kinds[AROUND] / DIRS)
    before = jnp.stack([slab * depth - 1 - there, there - (slab + 1) * depth])
    n = before.astype(jnp.float32)[:, None, :]
    power = jnp.power(kinds[DECAY][None, :, None], jnp.maximum(n, 0.0))
    inflow = jnp.where(before[:, None, :] >= 0, power, 0.0)
    inflow = jnp.concatenate(
        [inflow * kinds[THERM][None, :, None], inflow * kinds[QUART][None, :, None]], axis=2
    )
    longer = inflow * (jnp.concatenate([n, n], axis=2) + 1.0)
    inflow, longer = (value.reshape(2 * KINDS, 2 * cells) for value in (inflow, longer))
    return (
        side_by_side(everywhere, one),
        jnp.concatenate([inflow, longer, stay, around], axis=0),
        jnp.concatenate([inflow, once], axis=0),
    )


def newton(density, kelvin, linear, quart):
    for _ in range(NEWTON):
        cube = kelvin * kelvin * kelvin
        residual = linear * kelvin + quart * (kelvin * cube) - density
        kelvin = kelvin - residual / (linear + 4.0 * quart * cube)
    return kelvin


def exact_dot(left, right):
    return jnp.dot(left, right, precision=lax.Precision.HIGHEST, preferred_element_type=jnp.float32)


def fourth(value):
    square = value * value
    return square * square


def add_up(values):
    while len(values) > 1:
        values = [a + b for a, b in zip(values[::2], values[1::2])]
    return values[0]


def stencil(low, high, c_self, c_y, c_z, shift_y, shift_z, at_edge):
    turned_low, turned_high = pltpu.roll(low, shift_y, 0), pltpu.roll(high, shift_y, 0)
    up_low = jnp.where(at_edge, turned_high, turned_low)
    up_high = jnp.where(at_edge, turned_low, turned_high)
    return (
        c_self * low + c_y * up_low + c_z * pltpu.roll(low, shift_z, 1),
        c_self * high + c_y * up_high + c_z * pltpu.roll(high, shift_z, 1),
    )


def course(ints, s, depth):
    forward = ints[FORWARD, s] == 1
    return jnp.where(forward, 0, depth - 1), jnp.where(forward, 1, -1)


def slot_stencil(floats, ints, s, row):
    at_edge = row == ints[EDGE_Y, s]
    c_self, c_y, c_z = floats[SELF, s], floats[UPY, s], floats[UPZ, s]
    shift_y, shift_z = ints[SHIFT_Y, s], ints[SHIFT_Z, s]
    return lambda low, high: stencil(low, high, c_self, c_y, c_z, shift_y, shift_z, at_edge)


def rows_of(s):
    at = pl.multiple_of(s * 16, 16)
    return pl.ds(at, 8), pl.ds(at + 8, 8)


def sweeps_kernel(sizes, meta, floats, ints, kinds, energy, flag, given, matrix, swept, quarter, *rest):
    block, blocks, depth, width_y, slots, modes, group = sizes
    faces, rest = rest[:group], rest[group:]
    keep, send, *planes, density, flat, sources, heat = rest
    out_one, turn_one, turn_two, out_two, turn_late, out_three = planes
    rows, own = width_y // modes, slots // group
    step = pl.program_id(0)
    slab, mode = meta[SLAB], meta[MODE]

    @pl.when(step == 0)
    def _():
        for yy in range(rows):
            quarter[:, yy * 128 : (yy + 1) * 128] = given[pl.ds(mode * rows + yy, depth, stride=width_y), :]
        density[...] = jnp.zeros_like(density)

        def one_layer(x, carry):
            at = pl.ds(pl.multiple_of(x * 16, 16), 16)
            t = given[at, :]
            power = fourth(t)
            hot = flag[at, :].astype(jnp.float32)
            heat[x] = hot
            for kind in range(KINDS):
                sources[kind, x] = kinds[THERM, kind] * t + kinds[QUART, kind] * power + kinds[HEAT, kind] * hot
            return carry

        lax.fori_loop(0, depth, one_layer, 0)

    row = lax.broadcasted_iota(jnp.int32, (8, 128), 0)

    def one_slot(i, carry):
        s = step * block + i
        start, stride = course(ints, s, depth)
        side = 1 - ints[FORWARD, s]
        ratio, warm, kind = floats[RATIO, s], floats[WARM, s], ints[KIND, s]
        apply = slot_stencil(floats, ints, s, row)
        xs = [start + stride * j for j in range(depth)]
        layers = [(energy[i, x, :8, :], energy[i, x, 8:, :]) for x in xs]
        last = []
        for turn in range(ITERS):
            total_low = total_high = jnp.full((8, 128), floats[WALL, s], jnp.float32)
            for j, x in enumerate(xs):
                low, high = apply(*layers[j])
                if turn == 0:
                    low, high = low + sources[kind, x, :8, :], high + sources[kind, x, 8:, :]
                else:
                    low, high = low + warm * heat[x, :8, :], high + warm * heat[x, 8:, :]
                total_low = ratio * total_low + low
                total_high = ratio * total_high + high
                layers[j] = (total_low, total_high)
                density[turn, side, j, :8, :] += total_low
                density[turn, side, j, 8:, :] += total_high
                if turn == ITERS - 1:
                    swept[i, x, :8, :] = total_low
                    swept[i, x, 8:, :] = total_high
            last.append((total_low, total_high))
        turned = apply(*last[0])
        at_low, at_high = rows_of(s)
        values = (last[0], turned, apply(*turned), last[1], apply(*last[1]), last[2])
        for plane, (low, high) in zip(planes, values):
            plane[at_low, :] = low
            plane[at_high, :] = high
        return carry

    lax.fori_loop(0, block, one_slot, 0, unroll=2)

    @pl.when(step == blocks - 1)
    def _():
        for by in range(group):
            at = pl.ds(pl.multiple_of(((slab % group) ^ by) * own * 16, 16), own * 16)
            for index, plane in enumerate((turn_two, turn_late, out_three)):
                faces[by][index] = plane[at, :]
        for turn in range(ITERS):
            for x in range(depth):
                flat[turn, x * 16 : x * 16 + 16, :] = density[turn, 0, x] + density[turn, 1, depth - 1 - x]
        home = pl.ds(pl.multiple_of(slab * depth, 8), depth)
        for by in range(modes):
            ys = [(mode ^ by) * rows + yy for yy in range(rows)]
            pick = lambda plane, count: jnp.concatenate([plane[pl.ds(y, count, stride=width_y), :] for y in ys], axis=1)
            one, two = pick(turn_one, slots), pick(turn_late, slots)
            rights = (
                pick(out_one, slots),
                jnp.concatenate([pick(out_two, slots), one], axis=0),
                jnp.concatenate([pick(out_three, slots), two, pick(turn_two, slots)], axis=0),
            )
            target = (send if by % 2 else keep).at[by // 2]
            for turn, right in enumerate(rights):
                target[turn] = exact_dot(matrix[:, : (turn + 1) * slots], right)
                target[turn, home, :] += pick(flat.at[turn], depth)


def split_kernel(mine, other, keep, send):
    for index in range(mine.shape[0]):
        target = send if index % 2 else keep
        target[index // 2] = mine[index] + other[index]


def parts_kernel(depth, mine, other, parts):
    for turn in range(ITERS):
        total = mine[0, turn] + other[0, turn]
        for slab in range(parts.shape[0]):
            parts[slab, turn] = total[slab * depth : (slab + 1) * depth]


def totals_kernel(parts, before, copies, late):
    slabs = parts.shape[0]
    one, two, three = (
        add_up([parts[slab, turn] for slab in range(slabs)]) * (1.0 / DIRS) for turn in range(ITERS)
    )
    late[...] = three
    for slab in range(slabs):
        copies[slab, 0] = one
        copies[slab, 1] = two
        copies[slab, 2] = before[...]


def kelvins_kernel(depth, sums, gathered, late, matrix, packed):
    slabs = gathered.shape[0]
    cells = slabs * depth
    one, two, before = (
        jnp.concatenate([gathered[slab, index] for slab in range(slabs)], axis=0) for index in range(3)
    )
    kelvin = newton(one, before, sums[0], sums[1])
    packed[:cells, :] = kelvin
    two = two + exact_dot(matrix[...], jnp.concatenate([kelvin, fourth(kelvin)], axis=0))
    packed[cells : 2 * cells, :] = newton(two, kelvin, sums[0], sums[1])
    packed[2 * cells :, :] = late[...]


def compose_kernel(own, group, meta, floats, ints, *refs):
    received, (composite, effective, ordered) = refs[:group], refs[group:]
    place = meta[SLAB] % group
    for by in range(group):
        ordered[place ^ by] = received[by][...]

    def one_slot(i, carry):
        s = place * own + i
        start, stride = course(ints, s, group)
        full, full_n, full_t = floats[FULL, s], floats[FULL_N, s], floats[FULL_T, s]
        at = pl.ds(pl.multiple_of(i * 16, 16), 16)
        one = two = three = jnp.zeros((16, 128), jnp.float32)
        for j in range(group):
            k = start + stride * j
            three = full * three + full_n * two + full_t * one + ordered[k, 2, at, :]
            two = full * two + full_n * one + ordered[k, 1, at, :]
            one = full * one + ordered[k, 0, at, :]
        for index, value in enumerate((one, two, three)):
            composite[index, at, :] = value
        return carry

    lax.fori_loop(0, own, one_slot, 0, unroll=4)
    effective[...] = ordered[...]


def enter_kernel(own, group, groups, depth, meta, floats, ints, effective, *refs):
    composites, rest = refs[:groups], refs[groups:]
    outs, (ordered, entered) = rest[:group], rest[group:]
    slab = meta[SLAB]
    place, mine = slab % group, slab // group
    for by in range(groups):
        ordered[mine ^ by] = composites[by][...]
    span = depth * group

    def one_slot(i, carry):
        s = place * own + i
        start, stride = course(ints, s, group)
        begin, leap = course(ints, s, groups)
        ahead = jnp.where(ints[FORWARD, s] == 1, mine, groups - 1 - mine)
        at = pl.ds(pl.multiple_of(i * 16, 16), 16)

        def push(values, full, full_n, full_t, added):
            one, two, three = values
            return (
                full * one + added[0],
                full * two + full_n * one + added[1],
                full * three + full_n * two + full_t * one + added[2],
            )

        values = (jnp.zeros((16, 128), jnp.float32),) * 3
        whole = floats[FULL_GROUP, s]
        for g in range(groups - 1):
            index = begin + leap * g
            added = [ordered[index, plane, at, :] for plane in range(3)]
            later = push(values, whole, span * whole, (span * (span + 1) // 2) * whole, added)
            values = tuple(jnp.where(g < ahead, a, b) for a, b in zip(later, values))
        full, full_n, full_t = floats[FULL, s], floats[FULL_N, s], floats[FULL_T, s]
        for j in range(group):
            k = start + stride * j
            for plane in range(3):
                entered[k, plane, at, :] = values[plane]
            if j < group - 1:
                values = push(values, full, full_n, full_t, [effective[k, plane, at, :] for plane in range(3)])
        return carry

    lax.fori_loop(0, own, one_slot, 0, unroll=2)
    for by in range(group):
        outs[by][...] = entered[place ^ by]


def final_kernel(sizes, order, meta, floats, ints, kinds, sums, swept, *refs):
    block, depth, width_y, width_z, slots, slabs, modes, group = sizes
    received, refs = refs[:group], refs[group:]
    packs, refs = refs[:modes], refs[modes:]
    first_matrix, second_matrix, energy, kelvin, *refs = refs
    warm_one, warm_two, late, enter_one, enter_long, enter_two, second, added, own_one, own_two, *ordered = refs
    step = pl.program_id(0)
    slab, mode = meta[SLAB], meta[MODE]
    own, lanes, cells = slots // group, width_y // modes * width_z, slabs * depth

    @pl.when(step == 0)
    def _():
        for by in range(group):
            at = pl.ds(pl.multiple_of(((slab % group) ^ by) * own * 16, 16), own * 16)
            for index in range(ITERS):
                ordered[index][at, :] = received[by][index]
        for pack, by in zip(packs, order):
            at = pl.ds(pl.multiple_of((mode ^ by) * lanes, 128), lanes)
            warm_one[:, at] = pack[:cells, :]
            warm_two[:, at] = pack[cells : 2 * cells, :]
            late[:, at] = pack[2 * cells :, :]
        home = pl.ds(pl.multiple_of(slab * depth, 8), depth)
        chunk = 4
        plain, around = [], []
        for c in range(width_y // chunk):
            at = slice(c * chunk * 128, (c + 1) * chunk * 128)
            one, two = warm_one[:, at], warm_two[:, at]
            one = exact_dot(first_matrix[...], jnp.concatenate([one, fourth(one)], axis=0))
            two = exact_dot(second_matrix[...], jnp.concatenate([two, fourth(two)], axis=0))
            for yy in range(chunk):
                y, lane = c * chunk + yy, slice(yy * 128, (yy + 1) * 128)
                scattered = pl.ds(y, 2 * KINDS, stride=width_y)
                enter_one[scattered, :] = one[: 2 * KINDS, lane]
                enter_long[scattered, :] = one[2 * KINDS : 4 * KINDS, lane]
                enter_two[scattered, :] = two[: 2 * KINDS, lane]
                plain.append(one[4 * KINDS : 4 * KINDS + depth, lane] + two[2 * KINDS :, lane])
                around.append(one[4 * KINDS + depth :, lane])
        for y in range(width_y):
            lane = slice(y * 128, (y + 1) * 128)
            near = around[y - 1] + around[(y + 1) % width_y]
            near = near + (pltpu.roll(around[y], 1, 1) + pltpu.roll(around[y], width_z - 1, 1))
            density = late[:, lane] + plain[y] + near
            scattered = pl.ds(y, depth, stride=width_y)
            now = warm_two[home, lane]
            kelvin[scattered, :] = newton(density, now, sums[0], sums[1])
            own_one[scattered, :] = warm_one[home, lane]
            own_two[scattered, :] = now

        def one_kind(kind, carry):
            therm, quart, decay = kinds[THERM, kind], kinds[QUART, kind], kinds[DECAY, kind]
            at = pl.ds(pl.multiple_of(kind * 16, 16), 16)
            back_at = pl.ds(pl.multiple_of((kind + KINDS) * 16, 16), 16)
            layers = []
            for x in range(depth):
                here = slice(x * 16, x * 16 + 16)
                t, u = own_one[here, :], own_two[here, :]
                layers.append(therm * t + quart * fourth(t))
                added[kind, x] = therm * u + quart * fourth(u)
            up, down = enter_one[at, :], enter_one[back_at, :]
            for j in range(depth):
                up = decay * up + layers[j]
                down = decay * down + layers[depth - 1 - j]
                second[kind, j] = up
                second[kind + KINDS, j] = down
            return carry

        lax.fori_loop(0, KINDS, one_kind, 0)

    row = lax.broadcasted_iota(jnp.int32, (8, 128), 0)

    def one_slot(i, carry):
        s = step * block + i
        start, stride = course(ints, s, depth)
        ratio, kind = floats[RATIO, s], ints[KIND, s]
        sided = kind + KINDS * (1 - ints[FORWARD, s])
        apply = slot_stencil(floats, ints, s, row)
        at, kind_at = rows_of(s), rows_of(sided)
        one, two, three = ([ref[half, :] for half in at] for ref in ordered)
        longer = apply(*(enter_long[half, :] for half in kind_at))
        three = [a + b + enter_two[half, :] for a, b, half in zip(three, longer, kind_at)]
        for j in range(depth):
            x = start + stride * j
            fresh = apply(second[sided, j, :8, :], second[sided, j, 8:, :])
            for half, here in enumerate((slice(0, 8), slice(8, 16))):
                one[half] = ratio * one[half]
                two[half] = ratio * two[half] + one[half]
                three[half] = ratio * three[half] + (fresh[half] + added[kind, x, here, :] + two[half])
                energy[i, x, here, :] = swept[i, x, here, :] + three[half]
        return carry

    lax.fori_loop(0, block, one_slot, 0, unroll=2)


def local(incoming_occupation, crystal_kelvin_given, generating_region_flag, labels, speed, rate, storage, threshold, generation):
    slots, depth, width_y, width_z = incoming_occupation.shape
    slabs, modes = lax.axis_size("slab"), lax.axis_size("mode")
    group, groups = GROUP, slabs // GROUP
    own = slots // group
    lanes = width_y // modes * width_z
    block = 8
    blocks = slots // block
    cells, all_x = depth * width_y, slabs * depth
    face_rows = own * width_y
    slab = lax.axis_index("slab").astype(jnp.int32)
    meta = jnp.stack([slab, lax.axis_index("mode").astype(jnp.int32)])
    floats, ints, matrix = slot_tables(labels, speed, rate, storage, threshold, generation, slab, slabs, depth, width_z)
    kinds = kind_table(speed, rate, storage, threshold, generation)
    everywhere, first_matrix, second_matrix = heat_matrices(kinds, slab, slabs, depth)
    sums = jnp.stack([jnp.sum(storage), jnp.sum(storage / (4.0 * threshold**3))])

    def shape(*dims):
        return jax.ShapeDtypeStruct(dims, jnp.float32)

    def whole(*dims):
        return pl.BlockSpec(dims, lambda i: (0,) * len(dims))

    def scratch(*dims):
        return pltpu.VMEM(dims, jnp.float32)

    def swap(array, axis, by):
        return lax.ppermute(array, axis, [(i, i ^ by) for i in range(lax.axis_size(axis))])

    def call(kernel, name, in_specs, out_shapes, *args, scratches=()):
        return pl.pallas_call(
            kernel,
            in_specs=in_specs,
            out_specs=[VMEM] * len(out_shapes),
            out_shape=out_shapes,
            scratch_shapes=list(scratches),
            compiler_params=PARAMS,
            name=name,
        )(*args)

    slot_block = pl.BlockSpec((block, depth, width_y, width_z), lambda i: (i, 0, 0, 0))
    slot_shape = shape(slots, depth, width_y, width_z)
    face = (3, face_rows, width_z)
    half = (modes // 2, ITERS, all_x, lanes)
    swept, quarter, *rest = pl.pallas_call(
        functools.partial(sweeps_kernel, (block, blocks, depth, width_y, slots, modes, group)),
        grid=(blocks,),
        in_specs=[SMEM] * 4 + [slot_block, whole(cells, width_z), whole(cells, width_z), whole(all_x, ITERS * slots)],
        out_specs=[slot_block, whole(depth, lanes)] + [whole(*face)] * group + [whole(*half)] * 2,
        out_shape=[slot_shape, shape(depth, lanes)] + [shape(*face)] * group + [shape(*half)] * 2,
        scratch_shapes=[scratch(slots * width_y, width_z)] * 6
        + [
            scratch(ITERS, 2, depth, width_y, width_z),
            scratch(ITERS, cells, width_z),
            scratch(KINDS, depth, width_y, width_z),
            scratch(depth, width_y, width_z),
        ],
        compiler_params=PARAMS,
        name="sweeps",
    )(
        meta,
        floats,
        ints,
        kinds,
        incoming_occupation,
        generating_region_flag.reshape(cells, width_z),
        crystal_kelvin_given.reshape(cells, width_z),
        matrix,
    )
    faces, (keep, send) = rest[:group], rest[group:]

    by = 1
    other = swap(send, "mode", by)
    received = [faces[0]] + [swap(faces[index], "slab", index) for index in range(1, group)]
    while 2 * by < modes:
        by *= 2
        now = (modes // (2 * by), ITERS, all_x, lanes)
        keep, send = call(split_kernel, "density_split", [VMEM] * 2, [shape(*now)] * 2, keep, other)
        other = swap(send, "mode", by)
    piece = (slabs, ITERS, depth, lanes)
    (parts,) = call(functools.partial(parts_kernel, depth), "density_parts", [VMEM] * 2, [shape(*piece)], keep, other)
    parts = lax.all_to_all(parts, "slab", 0, 0)
    copies, late = call(totals_kernel, "density_totals", [VMEM] * 2, [shape(*piece), shape(depth, lanes)], parts, quarter)
    gathered = lax.all_to_all(copies, "slab", 0, 0)
    pack_shape = shape(2 * all_x + depth, lanes)
    (packed,) = call(
        functools.partial(kelvins_kernel, depth), "kelvins", [SMEM] + [VMEM] * 3, [pack_shape], sums, gathered, late, everywhere
    )
    packs, order = [packed], [0]
    while by:
        packs = packs + [swap(pack, "mode", by) for pack in packs]
        order = order + [index ^ by for index in order]
        by //= 2

    composite, effective = call(
        functools.partial(compose_kernel, own, group),
        "compose",
        [SMEM] * 3 + [VMEM] * group,
        [shape(*face), shape(group, *face)],
        meta,
        floats,
        ints,
        *received,
        scratches=[scratch(group, *face)],
    )
    composites = [composite] + [swap(composite, "slab", index * group) for index in range(1, groups)]
    entering = call(
        functools.partial(enter_kernel, own, group, groups, depth),
        "enter",
        [SMEM] * 3 + [VMEM] * (1 + groups),
        [shape(*face)] * group,
        meta,
        floats,
        ints,
        effective,
        *composites,
        scratches=[scratch(groups, *face), scratch(group, *face)],
    )
    entering = [entering[0]] + [swap(entering[index], "slab", index) for index in range(1, group)]

    energy, kelvin = pl.pallas_call(
        functools.partial(final_kernel, (block, depth, width_y, width_z, slots, slabs, modes, group), order),
        grid=(blocks,),
        in_specs=[SMEM] * 5
        + [slot_block]
        + [whole(*face)] * group
        + [whole(*pack_shape.shape)] * modes
        + [whole(*first_matrix.shape), whole(*second_matrix.shape)],
        out_specs=[slot_block, whole(cells, width_z)],
        out_shape=[slot_shape, shape(cells, width_z)],
        scratch_shapes=[scratch(all_x, width_y * width_z)] * 2
        + [scratch(depth, width_y * width_z)]
        + [scratch(2 * KINDS * width_y, width_z)] * 3
        + [scratch(2 * KINDS, depth, width_y, width_z), scratch(KINDS, depth, width_y, width_z)]
        + [scratch(cells, width_z)] * 2
        + [scratch(slots * width_y, width_z)] * 3,
        compiler_params=PARAMS,
        name="final_energy",
    )(meta, floats, ints, kinds, sums, swept, *entering, *packs, first_matrix, second_matrix)
    return energy, kelvin.reshape(depth, width_y, width_z)


def solution(mesh):
    return jax.shard_map(
        local,
        mesh=mesh,
        in_specs=(
            P("mode", "slab", None, None),
            P("slab", None, None),
            P("slab", None, None),
            P("mode"),
            P(),
            P(),
            P(),
            P(),
            P(),
        ),
        out_specs=(P("mode", "slab", None, None), P("slab", None, None)),
        check_vma=False,
    )
```

```python
import functools
import math

import jax
import jax.numpy as jnp
import numpy as np
from jax import lax
from jax.experimental import pallas as pl
from jax.experimental.pallas import tpu as pltpu
from jax.sharding import PartitionSpec as P

FREQ_GROUPS = 8
DIRS = 32
ITERS = 3
NEWTON = 4
PSEUDO_RATE = 0.03
GROUP = 4
COSINES = (np.float32(0.99995), np.float32(0.9999))

SELF, UPY, UPZ, RATIO, WALL, FULL, FULL_N, FULL_T, FULL_GROUP, WARM = range(10)
FORWARD, SHIFT_Y, SHIFT_Z, EDGE_Y, KIND = range(5)
THERM, QUART, HEAT, DECAY, STAY, AROUND = range(6)
KINDS = 2 * FREQ_GROUPS
SLAB, MODE = range(2)

SMEM = pl.BlockSpec(memory_space=pltpu.SMEM)
VMEM = pl.BlockSpec(memory_space=pltpu.VMEM)
PARAMS = pltpu.CompilerParams(vmem_limit_bytes=48 * 1024 * 1024)
ACROSS = math.cos(math.pi / 8) + math.sin(math.pi / 8)


def diagonal_of(speed, rate, cosine):
    sine = jnp.sqrt(1.0 - cosine * cosine)
    return speed * (cosine + sine * np.float32(ACROSS)) + rate + PSEUDO_RATE


def slot_tables(labels, speed, rate, storage, threshold, generation, slab, slabs, depth, width_z):
    band = labels // DIRS
    direction = labels % DIRS
    of_band = (band[None, :] == jnp.arange(FREQ_GROUPS, dtype=jnp.int32)[:, None]).astype(jnp.float32)
    speed, rate, storage, threshold, generation = (
        jnp.sum(of_band * value[:, None], axis=0) for value in (speed, rate, storage, threshold, generation)
    )
    polar = direction % 4
    outer = (polar == 0) | (polar == 3)
    forward = polar < 2
    cosine = jnp.where(outer, COSINES[0], COSINES[1])
    sine = jnp.sqrt(1.0 - cosine * cosine)
    azimuth = ((direction // 4).astype(jnp.float32) + 0.5) * (2.0 * math.pi / (DIRS // 4))
    vy = speed * sine * jnp.cos(azimuth)
    vz = speed * sine * jnp.sin(azimuth)
    diagonal = diagonal_of(speed, rate, cosine)
    ratio = speed * cosine / diagonal
    full = lax.integer_pow(ratio, depth)
    at_wall = jnp.where(forward, slab == 0, slab == slabs - 1)
    wall = storage * (1.0 + 1.0 / (4.0 * threshold**3))
    floats = jnp.stack(
        [
            PSEUDO_RATE / diagonal,
            jnp.abs(vy) / diagonal,
            jnp.abs(vz) / diagonal,
            ratio,
            jnp.where(at_wall, wall, 0.0),
            full,
            depth * full,
            (depth * (depth + 1) // 2) * full,
            lax.integer_pow(full, GROUP),
            generation / diagonal,
        ]
    )
    ints = jnp.stack(
        [
            forward.astype(jnp.int32),
            jnp.where(vy > 0, 1, 7).astype(jnp.int32),
            jnp.where(vz > 0, 1, width_z - 1).astype(jnp.int32),
            jnp.where(vy > 0, 0, 7).astype(jnp.int32),
            2 * band + jnp.where(outer, 0, 1),
        ]
    )
    x = jnp.arange(slabs * depth, dtype=jnp.int32)[:, None]
    by_half = lambda value: value.reshape(GROUP, 2, -1).transpose(1, 0, 2).reshape(1, -1)
    past = jnp.where(by_half(forward), x - (slab * depth + depth - 1), slab * depth - x)
    n = past.astype(jnp.float32)
    weight = jnp.where(past > 0, jnp.power(by_half(ratio), jnp.maximum(n, 0.0)), 0.0)
    return floats, ints, jnp.concatenate([weight, n * weight, (0.5 * n * (n + 1.0)) * weight], axis=1)


def kind_table(speed, rate, storage, threshold, generation):
    rows = []
    for cosine in COSINES:
        diagonal = diagonal_of(speed, rate, cosine)
        therm = rate * storage / diagonal
        quart = therm / (4.0 * threshold**3)
        across = jnp.sqrt(1.0 - cosine * cosine) * np.float32(2.0 * ACROSS)
        rows.append(
            jnp.stack(
                [
                    therm,
                    quart,
                    generation / diagonal,
                    speed * cosine / diagonal,
                    (DIRS // 4) * PSEUDO_RATE / diagonal,
                    across * speed / diagonal,
                ]
            )
        )
    return jnp.stack(rows, axis=2).reshape(6, KINDS)


def heat_matrices(kinds, slab, slabs, depth):
    cells = slabs * depth
    there = jnp.arange(cells, dtype=jnp.int32)
    decay = kinds[DECAY][:, None, None]
    per_cell = (DIRS // 4) / DIRS

    def side_by_side(weight, factor):
        sums = [jnp.sum((factor * kinds[row])[:, None, None] * weight, axis=0) for row in (THERM, QUART)]
        return jnp.concatenate(sums, axis=1)

    def between(here):
        far = jnp.abs(here[:, None] - there[None, :])
        n = far.astype(jnp.float32)
        return n, jnp.power(decay, n[None]) * jnp.where(far == 0, 2.0, 1.0)[None]

    _, everywhere = between(there)
    n, home = between(slab * depth + jnp.arange(depth, dtype=jnp.int32))
    twice = home * (n + 1.0)[None]
    one = jnp.full((KINDS,), per_cell, jnp.float32)
    once = side_by_side(home, one)
    stay = side_by_side(twice, kinds[STAY] / DIRS)
    around = side_by_side(twice, kinds[AROUND] / DIRS)
    before = jnp.stack([slab * depth - 1 - there, there - (slab + 1) * depth])
    n = before.astype(jnp.float32)[:, None, :]
    power = jnp.power(kinds[DECAY][None, :, None], jnp.maximum(n, 0.0))
    inflow = jnp.where(before[:, None, :] >= 0, power, 0.0)
    inflow = jnp.concatenate(
        [inflow * kinds[THERM][None, :, None], inflow * kinds[QUART][None, :, None]], axis=2
    )
    longer = inflow * (jnp.concatenate([n, n], axis=2) + 1.0)
    inflow, longer = (value.reshape(2 * KINDS, 2 * cells) for value in (inflow, longer))
    return (
        side_by_side(everywhere, one),
        jnp.concatenate([inflow, longer, stay, around], axis=0),
        jnp.concatenate([inflow, once], axis=0),
    )


def newton(density, kelvin, linear, quart):
    for _ in range(NEWTON):
        cube = kelvin * kelvin * kelvin
        residual = linear * kelvin + quart * (kelvin * cube) - density
        kelvin = kelvin - residual / (linear + 4.0 * quart * cube)
    return kelvin


def exact_dot(left, right):
    return jnp.dot(left, right, precision=lax.Precision.HIGHEST, preferred_element_type=jnp.float32)


def fourth(value):
    square = value * value
    return square * square


def add_up(values):
    while len(values) > 1:
        values = [a + b for a, b in zip(values[::2], values[1::2])]
    return values[0]


def stencil(low, high, c_self, c_y, c_z, shift_y, shift_z, at_edge):
    turned_low, turned_high = pltpu.roll(low, shift_y, 0), pltpu.roll(high, shift_y, 0)
    up_low = jnp.where(at_edge, turned_high, turned_low)
    up_high = jnp.where(at_edge, turned_low, turned_high)
    return (
        c_self * low + c_y * up_low + c_z * pltpu.roll(low, shift_z, 1),
        c_self * high + c_y * up_high + c_z * pltpu.roll(high, shift_z, 1),
    )


def course(ints, s, depth):
    forward = ints[FORWARD, s] == 1
    return jnp.where(forward, 0, depth - 1), jnp.where(forward, 1, -1)


def slot_stencil(floats, ints, s, row):
    at_edge = row == ints[EDGE_Y, s]
    c_self, c_y, c_z = floats[SELF, s], floats[UPY, s], floats[UPZ, s]
    shift_y, shift_z = ints[SHIFT_Y, s], ints[SHIFT_Z, s]
    return lambda low, high: stencil(low, high, c_self, c_y, c_z, shift_y, shift_z, at_edge)


def rows_of(s):
    at = pl.multiple_of(s * 16, 16)
    return pl.ds(at, 8), pl.ds(at + 8, 8)


def sweeps_kernel(half, sizes, *refs):
    block, depth, width_y, modes, group = sizes
    refs = list(refs)
    take = lambda count: [refs.pop(0) for _ in range(count)]
    meta, floats, ints, kinds, energy, flag, given = take(7)
    if half:
        matrix, *older, older_density = take(8)
    (swept,) = take(1)
    faces = take(group)
    if half:
        keep, send = take(2)
        planes = take(6)
        flat, density, sources, heat = take(4)
    else:
        (quarter,) = take(1)
        planes = take(6)
        flat, density, sources, heat = take(4)
    rows = width_y // modes
    step = pl.program_id(0)
    slab, mode = meta[SLAB], meta[MODE]

    @pl.when(step == 0)
    def _():
        if not half:
            for yy in range(rows):
                quarter[:, yy * 128 : (yy + 1) * 128] = given[pl.ds(mode * rows + yy, depth, stride=width_y), :]
        density[...] = jnp.zeros_like(density)

        def one_layer(x, carry):
            at = pl.ds(pl.multiple_of(x * 16, 16), 16)
            t = given[at, :]
            power = fourth(t)
            hot = flag[at, :].astype(jnp.float32)
            heat[x] = hot
            for kind in range(KINDS):
                sources[kind, x] = kinds[THERM, kind] * t + kinds[QUART, kind] * power + kinds[HEAT, kind] * hot
            return carry

        lax.fori_loop(0, depth, one_layer, 0)

    row = lax.broadcasted_iota(jnp.int32, (8, 128), 0)

    def one_slot(i, carry):
        s = (2 * step + half) * block + i
        start, stride = course(ints, s, depth)
        side = 1 - ints[FORWARD, s]
        ratio, warm, kind = floats[RATIO, s], floats[WARM, s], ints[KIND, s]
        apply = slot_stencil(floats, ints, s, row)
        xs = [start + stride * j for j in range(depth)]
        layers = [(energy[i, x, :8, :], energy[i, x, 8:, :]) for x in xs]
        last = []
        for turn in range(ITERS):
            total_low = total_high = jnp.full((8, 128), floats[WALL, s], jnp.float32)
            for j, x in enumerate(xs):
                low, high = apply(*layers[j])
                if turn == 0:
                    low, high = low + sources[kind, x, :8, :], high + sources[kind, x, 8:, :]
                else:
                    low, high = low + warm * heat[x, :8, :], high + warm * heat[x, 8:, :]
                total_low = ratio * total_low + low
                total_high = ratio * total_high + high
                layers[j] = (total_low, total_high)
                density[turn, side, j, :8, :] += total_low
                density[turn, side, j, 8:, :] += total_high
                if turn == ITERS - 1:
                    swept[i, x, :8, :] = total_low
                    swept[i, x, 8:, :] = total_high
            last.append((total_low, total_high))
        turned = apply(*last[0])
        at_low, at_high = rows_of(step * block + i)
        values = (last[0], turned, apply(*turned), last[1], apply(*last[1]), last[2])
        for plane, (low, high) in zip(planes, values):
            plane[at_low, :] = low
            plane[at_high, :] = high
        return carry

    lax.fori_loop(0, block, one_slot, 0, unroll=2)

    @pl.when(step == group - 1)
    def _():
        _, turn_one, turn_two, _, turn_late, out_three = planes
        for by in range(group):
            at = pl.ds(pl.multiple_of(((slab % group) ^ by) * block * 16, 16), block * 16)
            for index, plane in enumerate((turn_two, turn_late, out_three)):
                faces[by][index] = plane[at, :]
        for turn in range(ITERS):
            for x in range(depth):
                at = slice(x * 16, x * 16 + 16)
                total = density[turn, 0, x] + density[turn, 1, depth - 1 - x]
                flat[turn, at, :] = total + older_density[turn, at, :] if half else total
        if not half:
            return
        home = pl.ds(pl.multiple_of(slab * depth, 8), depth)
        slots = 2 * group * block
        for by in range(modes):
            ys = [(mode ^ by) * rows + yy for yy in range(rows)]
            pick = lambda plane, count: jnp.concatenate([plane[pl.ds(y, count, stride=width_y), :] for y in ys], axis=1)
            out_one, turn_one, turn_two, out_two, turn_late, out_three = (
                [pick(before, slots // 2), pick(plane, slots // 2)] for before, plane in zip(older, planes)
            )
            rights = (out_one, out_two + turn_one, out_three + turn_late + turn_two)
            target = (send if by % 2 else keep).at[by // 2]
            for turn, right in enumerate(rights):
                target[turn] = exact_dot(matrix[:, : (turn + 1) * slots], jnp.concatenate(right, axis=0))
                target[turn, home, :] += pick(flat.at[turn], depth)


def split_kernel(mine, other, keep, send):
    for index in range(mine.shape[0]):
        target = send if index % 2 else keep
        target[index // 2] = mine[index] + other[index]


def parts_kernel(depth, mine, other, parts):
    for turn in range(ITERS):
        total = mine[0, turn] + other[0, turn]
        for slab in range(parts.shape[0]):
            parts[slab, turn] = total[slab * depth : (slab + 1) * depth]


def totals_kernel(sums, parts, before, copies, late):
    slabs = parts.shape[0]
    one, two, three = (
        add_up([parts[slab, turn] for slab in range(slabs)]) * (1.0 / DIRS) for turn in range(ITERS)
    )
    late[...] = three
    kelvin = newton(one, before[...], sums[0], sums[1])
    for slab in range(slabs):
        copies[slab, 0] = kelvin
        copies[slab, 1] = two


def kelvins_kernel(depth, sums, gathered, late, matrix, packed):
    slabs = gathered.shape[0]
    cells = slabs * depth
    kelvin, two = (jnp.concatenate([gathered[slab, index] for slab in range(slabs)], axis=0) for index in range(2))
    packed[:cells, :] = kelvin
    two = two + exact_dot(matrix[...], jnp.concatenate([kelvin, fourth(kelvin)], axis=0))
    packed[cells : 2 * cells, :] = newton(two, kelvin, sums[0], sums[1])
    packed[2 * cells :, :] = late[...]


def compose_kernel(half, block, group, meta, floats, ints, *refs):
    received, (composite, effective, ordered) = refs[:group], refs[group:]
    place = meta[SLAB] % group
    for by in range(group):
        ordered[place ^ by] = received[by][...]

    def one_slot(i, carry):
        s = (2 * place + half) * block + i
        start, stride = course(ints, s, group)
        full, full_n, full_t = floats[FULL, s], floats[FULL_N, s], floats[FULL_T, s]
        at = pl.ds(pl.multiple_of(i * 16, 16), 16)
        one = two = three = jnp.zeros((16, 128), jnp.float32)
        for j in range(group):
            k = start + stride * j
            three = full * three + full_n * two + full_t * one + ordered[k, 2, at, :]
            two = full * two + full_n * one + ordered[k, 1, at, :]
            one = full * one + ordered[k, 0, at, :]
        for index, value in enumerate((one, two, three)):
            composite[index, at, :] = value
        return carry

    lax.fori_loop(0, block, one_slot, 0, unroll=4)
    effective[...] = ordered[...]


def enter_kernel(half, block, group, groups, depth, meta, floats, ints, effective, *refs):
    composites, rest = refs[:groups], refs[groups:]
    outs, (ordered, entered) = rest[:group], rest[group:]
    slab = meta[SLAB]
    place, mine = slab % group, slab // group
    for by in range(groups):
        ordered[mine ^ by] = composites[by][...]
    span = depth * group

    def one_slot(i, carry):
        s = (2 * place + half) * block + i
        start, stride = course(ints, s, group)
        begin, leap = course(ints, s, groups)
        ahead = jnp.where(ints[FORWARD, s] == 1, mine, groups - 1 - mine)
        at = pl.ds(pl.multiple_of(i * 16, 16), 16)

        def push(values, full, full_n, full_t, added):
            one, two, three = values
            return (
                full * one + added[0],
                full * two + full_n * one + added[1],
                full * three + full_n * two + full_t * one + added[2],
            )

        values = (jnp.zeros((16, 128), jnp.float32),) * 3
        whole = floats[FULL_GROUP, s]
        for g in range(groups - 1):
            index = begin + leap * g
            added = [ordered[index, plane, at, :] for plane in range(3)]
            later = push(values, whole, span * whole, (span * (span + 1) // 2) * whole, added)
            values = tuple(jnp.where(g < ahead, a, b) for a, b in zip(later, values))
        full, full_n, full_t = floats[FULL, s], floats[FULL_N, s], floats[FULL_T, s]
        for j in range(group):
            k = start + stride * j
            for plane in range(3):
                entered[k, plane, at, :] = values[plane]
            if j < group - 1:
                values = push(values, full, full_n, full_t, [effective[k, plane, at, :] for plane in range(3)])
        return carry

    lax.fori_loop(0, block, one_slot, 0, unroll=2)
    for by in range(group):
        outs[by][...] = entered[place ^ by]


def inflow_kernel(half, sizes, meta, floats, ints, swept, *refs):
    block, depth, group = sizes
    received, (energy, ordered) = refs[:group], refs[-2:]
    step = pl.program_id(0)

    @pl.when(step == 0)
    def _():
        for by in range(group):
            ordered[(meta[SLAB] % group) ^ by] = received[by][...]

    def one_slot(i, carry):
        s = (2 * step + half) * block + i
        start, stride = course(ints, s, depth)
        ratio = floats[RATIO, s]
        at = pl.ds(pl.multiple_of(i * 16, 16), 16)
        one, two, three = (ordered[step, plane, at, :] for plane in range(ITERS))
        for j in range(depth):
            x = start + stride * j
            one = ratio * one
            two = ratio * two + one
            three = ratio * three + two
            energy[i, x] = swept[i, x] + three
        return carry

    lax.fori_loop(0, block, one_slot, 0, unroll=4)


def final_kernel(sizes, order, meta, floats, ints, kinds, sums, inflown, *refs):
    block, depth, width_y, width_z, slabs, modes = sizes
    packs, refs = refs[:modes], refs[modes:]
    first_matrix, second_matrix, energy, kelvin, *refs = refs
    warm_one, warm_two, late, enter_one, enter_long, enter_two, second, added, own_one, own_two = refs
    step = pl.program_id(0)
    slab, mode = meta[SLAB], meta[MODE]
    lanes, cells = width_y // modes * width_z, slabs * depth

    @pl.when(step == 0)
    def _():
        for pack, by in zip(packs, order):
            at = pl.ds(pl.multiple_of((mode ^ by) * lanes, 128), lanes)
            warm_one[:, at] = pack[:cells, :]
            warm_two[:, at] = pack[cells : 2 * cells, :]
            late[:, at] = pack[2 * cells :, :]
        home = pl.ds(pl.multiple_of(slab * depth, 8), depth)
        chunk = 4
        plain, around = [], []
        for c in range(width_y // chunk):
            at = slice(c * chunk * 128, (c + 1) * chunk * 128)
            one, two = warm_one[:, at], warm_two[:, at]
            one = exact_dot(first_matrix[...], jnp.concatenate([one, fourth(one)], axis=0))
            two = exact_dot(second_matrix[...], jnp.concatenate([two, fourth(two)], axis=0))
            for yy in range(chunk):
                y, lane = c * chunk + yy, slice(yy * 128, (yy + 1) * 128)
                scattered = pl.ds(y, 2 * KINDS, stride=width_y)
                enter_one[scattered, :] = one[: 2 * KINDS, lane]
                enter_long[scattered, :] = one[2 * KINDS : 4 * KINDS, lane]
                enter_two[scattered, :] = two[: 2 * KINDS, lane]
                plain.append(one[4 * KINDS : 4 * KINDS + depth, lane] + two[2 * KINDS :, lane])
                around.append(one[4 * KINDS + depth :, lane])
        for y in range(width_y):
            lane = slice(y * 128, (y + 1) * 128)
            near = around[y - 1] + around[(y + 1) % width_y]
            near = near + (pltpu.roll(around[y], 1, 1) + pltpu.roll(around[y], width_z - 1, 1))
            density = late[:, lane] + plain[y] + near
            scattered = pl.ds(y, depth, stride=width_y)
            now = warm_two[home, lane]
            kelvin[scattered, :] = newton(density, now, sums[0], sums[1])
            own_one[scattered, :] = warm_one[home, lane]
            own_two[scattered, :] = now

        def one_kind(kind, carry):
            therm, quart, decay = kinds[THERM, kind], kinds[QUART, kind], kinds[DECAY, kind]
            for sided in (kind, kind + KINDS):
                at = pl.ds(pl.multiple_of(sided * 16, 16), 16)
                once, twice, new = enter_one[at, :], enter_long[at, :], enter_two[at, :]
                for j in range(depth):
                    x = j if sided is kind else depth - 1 - j
                    here = slice(x * 16, x * 16 + 16)
                    t, u = own_one[here, :], own_two[here, :]
                    once = decay * once + (therm * t + quart * fourth(t))
                    twice = decay * twice + once
                    new = decay * new + (therm * u + quart * fourth(u))
                    second[sided, x] = twice
                    added[sided, x] = new
            return carry

        lax.fori_loop(0, KINDS, one_kind, 0)

    row = lax.broadcasted_iota(jnp.int32, (8, 128), 0)

    def one_slot(i, carry):
        s = step * block + i
        sided = ints[KIND, s] + KINDS * (1 - ints[FORWARD, s])
        apply = slot_stencil(floats, ints, s, row)
        for x in range(depth):
            low, high = apply(second[sided, x, :8, :], second[sided, x, 8:, :])
            energy[i, x, :8, :] = inflown[i, x, :8, :] + (low + added[sided, x, :8, :])
            energy[i, x, 8:, :] = inflown[i, x, 8:, :] + (high + added[sided, x, 8:, :])
        return carry

    lax.fori_loop(0, block, one_slot, 0, unroll=2)


def local(incoming_occupation, crystal_kelvin_given, generating_region_flag, labels, speed, rate, storage, threshold, generation):
    slots, depth, width_y, width_z = incoming_occupation.shape
    slabs, modes = lax.axis_size("slab"), lax.axis_size("mode")
    group, groups = GROUP, slabs // GROUP
    lanes = width_y // modes * width_z
    block = slots // group // 2
    cells, all_x = depth * width_y, slabs * depth
    face_rows = block * width_y
    slab = lax.axis_index("slab").astype(jnp.int32)
    meta = jnp.stack([slab, lax.axis_index("mode").astype(jnp.int32)])
    floats, ints, matrix = slot_tables(labels, speed, rate, storage, threshold, generation, slab, slabs, depth, width_z)
    kinds = kind_table(speed, rate, storage, threshold, generation)
    everywhere, first_matrix, second_matrix = heat_matrices(kinds, slab, slabs, depth)
    sums = jnp.stack([jnp.sum(storage), jnp.sum(storage / (4.0 * threshold**3))])

    def shape(*dims):
        return jax.ShapeDtypeStruct(dims, jnp.float32)

    def whole(*dims):
        return pl.BlockSpec(dims, lambda i: (0,) * len(dims))

    def scratch(*dims):
        return pltpu.VMEM(dims, jnp.float32)

    def swap(array, axis, by):
        return lax.ppermute(array, axis, [(i, i ^ by) for i in range(lax.axis_size(axis))])

    def call(kernel, name, in_specs, out_shapes, *args, scratches=()):
        return pl.pallas_call(
            kernel,
            in_specs=in_specs,
            out_specs=[VMEM] * len(out_shapes),
            out_shape=out_shapes,
            scratch_shapes=list(scratches),
            compiler_params=PARAMS,
            name=name,
        )(*args)

    tied = lax.optimization_barrier
    slot_block = pl.BlockSpec((block, depth, width_y, width_z), lambda i: (i, 0, 0, 0))
    half_blocks = [pl.BlockSpec((block, depth, width_y, width_z), lambda i, h=h: (2 * i + h, 0, 0, 0)) for h in range(2)]
    slot_shape = shape(slots, depth, width_y, width_z)
    half_shape = shape(slots // 2, depth, width_y, width_z)
    face = (3, face_rows, width_z)
    share = (modes // 2, ITERS, all_x, lanes)
    plane = (slots // 2 * width_y, width_z)
    flat = (ITERS, cells, width_z)
    flag = generating_region_flag.reshape(cells, width_z)
    given = crystal_kelvin_given.reshape(cells, width_z)

    def sweeps(half, extra):
        outs = [(slot_block, half_shape)] + [(whole(*face), shape(*face))] * group
        scratches = []
        if half:
            outs += [(whole(*share), shape(*share))] * 2
            scratches = [scratch(*plane)] * 6 + [scratch(*flat)]
        else:
            outs += [(whole(*dims), shape(*dims)) for dims in [(depth, lanes)] + [plane] * 6 + [flat]]
        return pl.pallas_call(
            functools.partial(sweeps_kernel, half, (block, depth, width_y, modes, group)),
            grid=(group,),
            in_specs=[SMEM] * 4
            + [half_blocks[half], whole(cells, width_z), whole(cells, width_z)]
            + [whole(*array.shape) for array in extra],
            out_specs=[spec for spec, _ in outs],
            out_shape=[of for _, of in outs],
            scratch_shapes=scratches
            + [
                scratch(ITERS, 2, depth, width_y, width_z),
                scratch(KINDS, depth, width_y, width_z),
                scratch(depth, width_y, width_z),
            ],
            compiler_params=PARAMS,
            name=f"sweeps_{half}",
        )(meta, floats, ints, kinds, incoming_occupation, flag, given, *extra)

    def around_group(faces):
        return [faces[0]] + [swap(faces[index], "slab", index) for index in range(1, group)]

    def compose(half, received):
        return call(
            functools.partial(compose_kernel, half, block, group),
            f"compose_{half}",
            [SMEM] * 3 + [VMEM] * group,
            [shape(*face), shape(group, *face)],
            meta,
            floats,
            ints,
            *received,
            scratches=[scratch(group, *face)],
        )

    def across_groups(composite):
        return [composite] + [swap(composite, "slab", index * group) for index in range(1, groups)]

    def enter(half, effective, composites):
        return call(
            functools.partial(enter_kernel, half, block, group, groups, depth),
            f"enter_{half}",
            [SMEM] * 3 + [VMEM] * (1 + groups),
            [shape(*face)] * group,
            meta,
            floats,
            ints,
            effective,
            *composites,
            scratches=[scratch(groups, *face), scratch(group, *face)],
        )

    def add_inflow(half, swept, received, energy):
        return pl.pallas_call(
            functools.partial(inflow_kernel, half, (block, depth, group)),
            grid=(group,),
            in_specs=[SMEM] * 3
            + [slot_block]
            + [whole(*face)] * group
            + [pl.BlockSpec(memory_space=pl.ANY)] * len(energy),
            out_specs=half_blocks[half],
            out_shape=slot_shape,
            scratch_shapes=[scratch(group, *face)],
            input_output_aliases={4 + group: 0} if energy else {},
            compiler_params=PARAMS,
            name=f"inflow_{half}",
        )(meta, floats, ints, swept, *received, *energy)

    swept_0, *rest = sweeps(0, [])
    received_0 = around_group(rest[:group])
    quarter, *older = rest[group:]
    swept_1, *rest = sweeps(1, [matrix] + older)
    keep, send = rest[group:]

    by = 1
    other = swap(send, "mode", by)
    received_1 = around_group(rest[:group])
    while 2 * by < modes:
        by *= 2
        now = (modes // (2 * by), ITERS, all_x, lanes)
        keep, send = call(split_kernel, "density_split", [VMEM] * 2, [shape(*now)] * 2, keep, other)
        other = swap(send, "mode", by)
    composite_0, effective_0 = compose(0, received_0)
    other, composite_0 = tied((other, composite_0))
    composites_0 = across_groups(composite_0)
    (parts,) = call(
        functools.partial(parts_kernel, depth), "density_parts", [VMEM] * 2, [shape(slabs, ITERS, depth, lanes)], keep, other
    )
    composite_1, effective_1 = compose(1, received_1)
    parts, composite_1 = tied((parts, composite_1))
    parts = lax.all_to_all(parts, "slab", 0, 0)
    composites_1 = across_groups(composite_1)
    entering_0 = enter(0, effective_0, composites_0)
    parts, entering_0 = tied((parts, entering_0))
    copies, late = call(
        totals_kernel,
        "density_totals",
        [SMEM] + [VMEM] * 2,
        [shape(slabs, 2, depth, lanes), shape(depth, lanes)],
        sums,
        parts,
        quarter,
    )
    entering_0 = around_group(entering_0)
    entering_1 = enter(1, effective_1, composites_1)
    copies, entering_1 = tied((copies, entering_1))
    gathered = lax.all_to_all(copies, "slab", 0, 0)
    entering_1 = around_group(entering_1)
    pack_shape = shape(2 * all_x + depth, lanes)
    energy = add_inflow(0, swept_0, entering_0, [])
    gathered, energy = tied((gathered, energy))
    (packed,) = call(
        functools.partial(kelvins_kernel, depth), "kelvins", [SMEM] + [VMEM] * 3, [pack_shape], sums, gathered, late, everywhere
    )
    packs, order = [packed], [0]
    while by:
        packs = packs + [swap(pack, "mode", by) for pack in packs]
        order = order + [index ^ by for index in order]
        by //= 2
    energy = add_inflow(1, swept_1, entering_1, [energy])

    energy, kelvin = pl.pallas_call(
        functools.partial(final_kernel, (block, depth, width_y, width_z, slabs, modes), order),
        grid=(slots // block,),
        in_specs=[SMEM] * 5
        + [slot_block]
        + [whole(*pack_shape.shape)] * modes
        + [whole(*first_matrix.shape), whole(*second_matrix.shape)],
        out_specs=[slot_block, whole(cells, width_z)],
        out_shape=[slot_shape, shape(cells, width_z)],
        scratch_shapes=[scratch(all_x, width_y * width_z)] * 2
        + [scratch(depth, width_y * width_z)]
        + [scratch(2 * KINDS * width_y, width_z)] * 3
        + [scratch(2 * KINDS, depth, width_y, width_z)] * 2
        + [scratch(cells, width_z)] * 2,
        compiler_params=PARAMS,
        name="final_energy",
    )(meta, floats, ints, kinds, sums, energy, *packs, first_matrix, second_matrix)
    return energy, kelvin.reshape(depth, width_y, width_z)


def solution(mesh):
    return jax.shard_map(
        local,
        mesh=mesh,
        in_specs=(
            P("mode", "slab", None, None),
            P("slab", None, None),
            P("slab", None, None),
            P("mode"),
            P(),
            P(),
            P(),
            P(),
            P(),
        ),
        out_specs=(P("mode", "slab", None, None), P("slab", None, None)),
        check_vma=False,
    )
```

```python
import functools
import math

import jax
import jax.numpy as jnp
import numpy as np
from jax import lax
from jax.experimental import pallas as pl
from jax.experimental.pallas import tpu as pltpu
from jax.sharding import PartitionSpec as P

FREQ_GROUPS = 8
DIRS = 32
ITERS = 3
NEWTON = 4
PSEUDO_RATE = 0.03
GROUP = 4
COSINES = (np.float32(0.99995), np.float32(0.9999))

SELF, UPY, UPZ, RATIO, WALL, FULL, FULL_N, FULL_T, FULL_GROUP, WARM = range(10)
FORWARD, SHIFT_Y, SHIFT_Z, EDGE_Y, KIND = range(5)
THERM, QUART, HEAT, DECAY, STAY, AROUND = range(6)
KINDS = 2 * FREQ_GROUPS
SLAB, MODE = range(2)

SMEM = pl.BlockSpec(memory_space=pltpu.SMEM)
VMEM = pl.BlockSpec(memory_space=pltpu.VMEM)
PARAMS = pltpu.CompilerParams(vmem_limit_bytes=32 * 1024 * 1024)
LARGE = pltpu.CompilerParams(vmem_limit_bytes=60 * 1024 * 1024)
ACROSS = math.cos(math.pi / 8) + math.sin(math.pi / 8)


def diagonal_of(speed, rate, cosine):
    sine = jnp.sqrt(1.0 - cosine * cosine)
    return speed * (cosine + sine * np.float32(ACROSS)) + rate + PSEUDO_RATE


def slot_tables(labels, speed, rate, storage, threshold, generation, slab, slabs, depth, width_z):
    band = labels // DIRS
    direction = labels % DIRS
    of_band = (band[None, :] == jnp.arange(FREQ_GROUPS, dtype=jnp.int32)[:, None]).astype(jnp.float32)
    speed, rate, storage, threshold, generation = (
        jnp.sum(of_band * value[:, None], axis=0) for value in (speed, rate, storage, threshold, generation)
    )
    polar = direction % 4
    outer = (polar == 0) | (polar == 3)
    forward = polar < 2
    cosine = jnp.where(outer, COSINES[0], COSINES[1])
    sine = jnp.sqrt(1.0 - cosine * cosine)
    azimuth = ((direction // 4).astype(jnp.float32) + 0.5) * (2.0 * math.pi / (DIRS // 4))
    vy = speed * sine * jnp.cos(azimuth)
    vz = speed * sine * jnp.sin(azimuth)
    diagonal = diagonal_of(speed, rate, cosine)
    ratio = speed * cosine / diagonal
    full = lax.integer_pow(ratio, depth)
    at_wall = jnp.where(forward, slab == 0, slab == slabs - 1)
    wall = storage * (1.0 + 1.0 / (4.0 * threshold**3))
    floats = jnp.stack(
        [
            PSEUDO_RATE / diagonal,
            jnp.abs(vy) / diagonal,
            jnp.abs(vz) / diagonal,
            ratio,
            jnp.where(at_wall, wall, 0.0),
            full,
            depth * full,
            (depth * (depth + 1) // 2) * full,
            lax.integer_pow(full, GROUP),
            generation / diagonal,
        ]
    )
    ints = jnp.stack(
        [
            forward.astype(jnp.int32),
            jnp.where(vy > 0, 1, 7).astype(jnp.int32),
            jnp.where(vz > 0, 1, width_z - 1).astype(jnp.int32),
            jnp.where(vy > 0, 0, 7).astype(jnp.int32),
            2 * band + jnp.where(outer, 0, 1),
        ]
    )
    x = jnp.arange(slabs * depth, dtype=jnp.int32)[:, None]
    by_half = lambda value: value.reshape(GROUP, 2, -1).transpose(1, 0, 2).reshape(1, -1)
    past = jnp.where(by_half(forward), x - (slab * depth + depth - 1), slab * depth - x)
    n = past.astype(jnp.float32)
    weight = jnp.where(past > 0, jnp.power(by_half(ratio), jnp.maximum(n, 0.0)), 0.0)
    return floats, ints, jnp.concatenate([weight, n * weight, (0.5 * n * (n + 1.0)) * weight], axis=1)


def kind_table(speed, rate, storage, threshold, generation):
    rows = []
    for cosine in COSINES:
        diagonal = diagonal_of(speed, rate, cosine)
        therm = rate * storage / diagonal
        quart = therm / (4.0 * threshold**3)
        across = jnp.sqrt(1.0 - cosine * cosine) * np.float32(2.0 * ACROSS)
        rows.append(
            jnp.stack(
                [
                    therm,
                    quart,
                    generation / diagonal,
                    speed * cosine / diagonal,
                    (DIRS // 4) * PSEUDO_RATE / diagonal,
                    across * speed / diagonal,
                ]
            )
        )
    return jnp.stack(rows, axis=2).reshape(6, KINDS)


def heat_matrices(kinds, slab, slabs, depth):
    cells = slabs * depth
    there = jnp.arange(cells, dtype=jnp.int32)
    decay = kinds[DECAY][:, None, None]
    per_cell = (DIRS // 4) / DIRS

    def side_by_side(weight, factor):
        sums = [jnp.sum((factor * kinds[row])[:, None, None] * weight, axis=0) for row in (THERM, QUART)]
        return jnp.concatenate(sums, axis=1)

    def between(here):
        far = jnp.abs(here[:, None] - there[None, :])
        n = far.astype(jnp.float32)
        return n, jnp.power(decay, n[None]) * jnp.where(far == 0, 2.0, 1.0)[None]

    _, everywhere = between(there)
    n, home = between(slab * depth + jnp.arange(depth, dtype=jnp.int32))
    twice = home * (n + 1.0)[None]
    one = jnp.full((KINDS,), per_cell, jnp.float32)
    once = side_by_side(home, one)
    stay = side_by_side(twice, kinds[STAY] / DIRS)
    around = side_by_side(twice, kinds[AROUND] / DIRS)
    before = jnp.stack([slab * depth - 1 - there, there - (slab + 1) * depth])
    n = before.astype(jnp.float32)[:, None, :]
    power = jnp.power(kinds[DECAY][None, :, None], jnp.maximum(n, 0.0))
    inflow = jnp.where(before[:, None, :] >= 0, power, 0.0)
    inflow = jnp.concatenate(
        [inflow * kinds[THERM][None, :, None], inflow * kinds[QUART][None, :, None]], axis=2
    )
    longer = inflow * (jnp.concatenate([n, n], axis=2) + 1.0)
    inflow, longer = (value.reshape(2 * KINDS, 2 * cells) for value in (inflow, longer))
    return (
        side_by_side(everywhere, one),
        jnp.concatenate([inflow, longer, stay, around], axis=0),
        jnp.concatenate([inflow, once], axis=0),
    )


def newton(density, kelvin, linear, quart):
    for _ in range(NEWTON):
        cube = kelvin * kelvin * kelvin
        residual = linear * kelvin + quart * (kelvin * cube) - density
        kelvin = kelvin - residual / (linear + 4.0 * quart * cube)
    return kelvin


def exact_dot(left, right):
    return jnp.dot(left, right, precision=lax.Precision.HIGHEST, preferred_element_type=jnp.float32)


def fourth(value):
    square = value * value
    return square * square


def add_up(values):
    while len(values) > 1:
        values = [a + b for a, b in zip(values[::2], values[1::2])]
    return values[0]


def stencil(low, high, c_self, c_y, c_z, shift_y, shift_z, at_edge):
    turned_low, turned_high = pltpu.roll(low, shift_y, 0), pltpu.roll(high, shift_y, 0)
    up_low = jnp.where(at_edge, turned_high, turned_low)
    up_high = jnp.where(at_edge, turned_low, turned_high)
    return (
        c_self * low + c_y * up_low + c_z * pltpu.roll(low, shift_z, 1),
        c_self * high + c_y * up_high + c_z * pltpu.roll(high, shift_z, 1),
    )


def course(ints, s, depth):
    forward = ints[FORWARD, s] == 1
    return jnp.where(forward, 0, depth - 1), jnp.where(forward, 1, -1)


def slot_stencil(floats, ints, s, row):
    at_edge = row == ints[EDGE_Y, s]
    c_self, c_y, c_z = floats[SELF, s], floats[UPY, s], floats[UPZ, s]
    shift_y, shift_z = ints[SHIFT_Y, s], ints[SHIFT_Z, s]
    return lambda low, high: stencil(low, high, c_self, c_y, c_z, shift_y, shift_z, at_edge)


def rows_of(s):
    at = pl.multiple_of(s * 16, 16)
    return pl.ds(at, 8), pl.ds(at + 8, 8)


def sweeps_kernel(half, sizes, *refs):
    block, depth, width_y, modes, group = sizes
    refs = list(refs)
    take = lambda count: [refs.pop(0) for _ in range(count)]
    meta, floats, ints, kinds, energy, flag, given = take(7)
    if half:
        matrix, *older, older_density = take(8)
    (swept,) = take(1)
    faces = take(group)
    if half:
        keep, send = take(2)
        planes = take(6)
        flat, density, sources, heat = take(4)
    else:
        (quarter,) = take(1)
        planes = take(6)
        flat, density, sources, heat = take(4)
    rows = width_y // modes
    step = pl.program_id(0)
    slab, mode = meta[SLAB], meta[MODE]

    @pl.when(step == 0)
    def _():
        if not half:
            for yy in range(rows):
                quarter[:, yy * 128 : (yy + 1) * 128] = given[pl.ds(mode * rows + yy, depth, stride=width_y), :]
        density[...] = jnp.zeros_like(density)

        def one_layer(x, carry):
            at = pl.ds(pl.multiple_of(x * 16, 16), 16)
            t = given[at, :]
            power = fourth(t)
            hot = flag[at, :].astype(jnp.float32)
            heat[x] = hot
            for kind in range(KINDS):
                sources[kind, x] = kinds[THERM, kind] * t + kinds[QUART, kind] * power + kinds[HEAT, kind] * hot
            return carry

        lax.fori_loop(0, depth, one_layer, 0)

    row = lax.broadcasted_iota(jnp.int32, (8, 128), 0)

    def one_slot(i, carry):
        s = (2 * step + half) * block + i
        start, stride = course(ints, s, depth)
        side = 1 - ints[FORWARD, s]
        ratio, warm, kind = floats[RATIO, s], floats[WARM, s], ints[KIND, s]
        apply = slot_stencil(floats, ints, s, row)
        xs = [start + stride * j for j in range(depth)]
        layers = [(energy[i, x, :8, :], energy[i, x, 8:, :]) for x in xs]
        last = []
        for turn in range(ITERS):
            total_low = total_high = jnp.full((8, 128), floats[WALL, s], jnp.float32)
            for j, x in enumerate(xs):
                low, high = apply(*layers[j])
                if turn == 0:
                    low, high = low + sources[kind, x, :8, :], high + sources[kind, x, 8:, :]
                else:
                    low, high = low + warm * heat[x, :8, :], high + warm * heat[x, 8:, :]
                total_low = ratio * total_low + low
                total_high = ratio * total_high + high
                layers[j] = (total_low, total_high)
                density[turn, side, j, :8, :] += total_low
                density[turn, side, j, 8:, :] += total_high
                if turn == ITERS - 1:
                    swept[i, x, :8, :] = total_low
                    swept[i, x, 8:, :] = total_high
            last.append((total_low, total_high))
        turned = apply(*last[0])
        at_low, at_high = rows_of(step * block + i)
        values = (last[0], turned, apply(*turned), last[1], apply(*last[1]), last[2])
        for plane, (low, high) in zip(planes, values):
            plane[at_low, :] = low
            plane[at_high, :] = high
        return carry

    lax.fori_loop(0, block, one_slot, 0, unroll=2)

    @pl.when(step == group - 1)
    def _():
        _, turn_one, turn_two, _, turn_late, out_three = planes
        for by in range(group):
            at = pl.ds(pl.multiple_of(((slab % group) ^ by) * block * 16, 16), block * 16)
            for index, plane in enumerate((turn_two, turn_late, out_three)):
                faces[by][index] = plane[at, :]
        for turn in range(ITERS):
            for x in range(depth):
                at = slice(x * 16, x * 16 + 16)
                total = density[turn, 0, x] + density[turn, 1, depth - 1 - x]
                flat[turn, at, :] = total + older_density[turn, at, :] if half else total
        if not half:
            return
        home = pl.ds(pl.multiple_of(slab * depth, 8), depth)
        slots = 2 * group * block
        for by in range(modes):
            ys = [(mode ^ by) * rows + yy for yy in range(rows)]
            pick = lambda plane, count: jnp.concatenate([plane[pl.ds(y, count, stride=width_y), :] for y in ys], axis=1)
            out_one, turn_one, turn_two, out_two, turn_late, out_three = (
                [pick(before, slots // 2), pick(plane, slots // 2)] for before, plane in zip(older, planes)
            )
            rights = (out_one, out_two + turn_one, out_three + turn_late + turn_two)
            target = (send if by % 2 else keep).at[by // 2]
            for turn, right in enumerate(rights):
                target[turn] = exact_dot(matrix[:, : (turn + 1) * slots], jnp.concatenate(right, axis=0))
                target[turn, home, :] += pick(flat.at[turn], depth)


def split_kernel(mine, other, keep, send):
    for index in range(mine.shape[0]):
        target = send if index % 2 else keep
        target[index // 2] = mine[index] + other[index]


def parts_kernel(depth, mine, other, parts):
    for turn in range(ITERS):
        total = mine[0, turn] + other[0, turn]
        for slab in range(parts.shape[0]):
            parts[slab, turn] = total[slab * depth : (slab + 1) * depth]


def totals_kernel(sums, parts, before, copies, late):
    slabs = parts.shape[0]
    one, two, three = (
        add_up([parts[slab, turn] for slab in range(slabs)]) * (1.0 / DIRS) for turn in range(ITERS)
    )
    late[...] = three
    kelvin = newton(one, before[...], sums[0], sums[1])
    for slab in range(slabs):
        copies[slab, 0] = kelvin
        copies[slab, 1] = two


def kelvins_kernel(depth, sums, gathered, late, matrix, packed):
    slabs = gathered.shape[0]
    cells = slabs * depth
    kelvin, two = (jnp.concatenate([gathered[slab, index] for slab in range(slabs)], axis=0) for index in range(2))
    packed[:cells, :] = kelvin
    two = two + exact_dot(matrix[...], jnp.concatenate([kelvin, fourth(kelvin)], axis=0))
    packed[cells : 2 * cells, :] = newton(two, kelvin, sums[0], sums[1])
    packed[2 * cells :, :] = late[...]


def compose_kernel(half, block, group, meta, floats, ints, *refs):
    received, (composite, effective, ordered) = refs[:group], refs[group:]
    place = meta[SLAB] % group
    for by in range(group):
        ordered[place ^ by] = received[by][...]

    def one_slot(i, carry):
        s = (2 * place + half) * block + i
        start, stride = course(ints, s, group)
        full, full_n, full_t = floats[FULL, s], floats[FULL_N, s], floats[FULL_T, s]
        at = pl.ds(pl.multiple_of(i * 16, 16), 16)
        one = two = three = jnp.zeros((16, 128), jnp.float32)
        for j in range(group):
            k = start + stride * j
            three = full * three + full_n * two + full_t * one + ordered[k, 2, at, :]
            two = full * two + full_n * one + ordered[k, 1, at, :]
            one = full * one + ordered[k, 0, at, :]
        for index, value in enumerate((one, two, three)):
            composite[index, at, :] = value
        return carry

    lax.fori_loop(0, block, one_slot, 0, unroll=4)
    effective[...] = ordered[...]


def enter_kernel(half, block, group, groups, depth, meta, floats, ints, effective, *refs):
    composites, rest = refs[:groups], refs[groups:]
    outs, (ordered, entered) = rest[:group], rest[group:]
    slab = meta[SLAB]
    place, mine = slab % group, slab // group
    for by in range(groups):
        ordered[mine ^ by] = composites[by][...]
    span = depth * group

    def one_slot(i, carry):
        s = (2 * place + half) * block + i
        start, stride = course(ints, s, group)
        begin, leap = course(ints, s, groups)
        ahead = jnp.where(ints[FORWARD, s] == 1, mine, groups - 1 - mine)
        at = pl.ds(pl.multiple_of(i * 16, 16), 16)

        def push(values, full, full_n, full_t, added):
            one, two, three = values
            return (
                full * one + added[0],
                full * two + full_n * one + added[1],
                full * three + full_n * two + full_t * one + added[2],
            )

        values = (jnp.zeros((16, 128), jnp.float32),) * 3
        whole = floats[FULL_GROUP, s]
        for g in range(groups - 1):
            index = begin + leap * g
            added = [ordered[index, plane, at, :] for plane in range(3)]
            later = push(values, whole, span * whole, (span * (span + 1) // 2) * whole, added)
            values = tuple(jnp.where(g < ahead, a, b) for a, b in zip(later, values))
        full, full_n, full_t = floats[FULL, s], floats[FULL_N, s], floats[FULL_T, s]
        for j in range(group):
            k = start + stride * j
            for plane in range(3):
                entered[k, plane, at, :] = values[plane]
            if j < group - 1:
                values = push(values, full, full_n, full_t, [effective[k, plane, at, :] for plane in range(3)])
        return carry

    lax.fori_loop(0, block, one_slot, 0, unroll=2)
    for by in range(group):
        outs[by][...] = entered[place ^ by]


def inflow_kernel(half, sizes, meta, floats, ints, swept, *refs):
    block, depth, group = sizes
    received, (energy, ordered) = refs[:group], refs[-2:]
    step = pl.program_id(0)

    @pl.when(step == 0)
    def _():
        for by in range(group):
            ordered[(meta[SLAB] % group) ^ by] = received[by][...]

    def one_slot(i, carry):
        s = (2 * step + half) * block + i
        start, stride = course(ints, s, depth)
        ratio = floats[RATIO, s]
        at = pl.ds(pl.multiple_of(i * 16, 16), 16)
        one, two, three = (ordered[step, plane, at, :] for plane in range(ITERS))
        for j in range(depth):
            x = start + stride * j
            one = ratio * one
            two = ratio * two + one
            three = ratio * three + two
            energy[i, x] = swept[i, x] + three
        return carry

    lax.fori_loop(0, block, one_slot, 0, unroll=4)


def final_kernel(sizes, order, meta, floats, ints, kinds, sums, inflown, *refs):
    block, depth, width_y, width_z, slabs, modes = sizes
    packs, refs = refs[:modes], refs[modes:]
    first_matrix, second_matrix, energy, kelvin, *refs = refs
    warm_one, warm_two, late, enter_one, enter_long, enter_two, second, added, own_one, own_two = refs
    step = pl.program_id(0)
    slab, mode = meta[SLAB], meta[MODE]
    lanes, cells = width_y // modes * width_z, slabs * depth

    @pl.when(step == 0)
    def _():
        for pack, by in zip(packs, order):
            at = pl.ds(pl.multiple_of((mode ^ by) * lanes, 128), lanes)
            warm_one[:, at] = pack[:cells, :]
            warm_two[:, at] = pack[cells : 2 * cells, :]
            late[:, at] = pack[2 * cells :, :]
        home = pl.ds(pl.multiple_of(slab * depth, 8), depth)
        chunk = 4
        plain, around = [], []
        for c in range(width_y // chunk):
            at = slice(c * chunk * 128, (c + 1) * chunk * 128)
            one, two = warm_one[:, at], warm_two[:, at]
            one = exact_dot(first_matrix[...], jnp.concatenate([one, fourth(one)], axis=0))
            two = exact_dot(second_matrix[...], jnp.concatenate([two, fourth(two)], axis=0))
            for yy in range(chunk):
                y, lane = c * chunk + yy, slice(yy * 128, (yy + 1) * 128)
                scattered = pl.ds(y, 2 * KINDS, stride=width_y)
                enter_one[scattered, :] = one[: 2 * KINDS, lane]
                enter_long[scattered, :] = one[2 * KINDS : 4 * KINDS, lane]
                enter_two[scattered, :] = two[: 2 * KINDS, lane]
                plain.append(one[4 * KINDS : 4 * KINDS + depth, lane] + two[2 * KINDS :, lane])
                around.append(one[4 * KINDS + depth :, lane])
        for y in range(width_y):
            lane = slice(y * 128, (y + 1) * 128)
            near = around[y - 1] + around[(y + 1) % width_y]
            near = near + (pltpu.roll(around[y], 1, 1) + pltpu.roll(around[y], width_z - 1, 1))
            density = late[:, lane] + plain[y] + near
            scattered = pl.ds(y, depth, stride=width_y)
            now = warm_two[home, lane]
            kelvin[scattered, :] = newton(density, now, sums[0], sums[1])
            own_one[scattered, :] = warm_one[home, lane]
            own_two[scattered, :] = now

        def one_kind(kind, carry):
            therm, quart, decay = kinds[THERM, kind], kinds[QUART, kind], kinds[DECAY, kind]
            for sided in (kind, kind + KINDS):
                at = pl.ds(pl.multiple_of(sided * 16, 16), 16)
                once, twice, new = enter_one[at, :], enter_long[at, :], enter_two[at, :]
                for j in range(depth):
                    x = j if sided is kind else depth - 1 - j
                    here = slice(x * 16, x * 16 + 16)
                    t, u = own_one[here, :], own_two[here, :]
                    once = decay * once + (therm * t + quart * fourth(t))
                    twice = decay * twice + once
                    new = decay * new + (therm * u + quart * fourth(u))
                    second[sided, x] = twice
                    added[sided, x] = new
            return carry

        lax.fori_loop(0, KINDS, one_kind, 0)

    row = lax.broadcasted_iota(jnp.int32, (8, 128), 0)

    def one_slot(i, carry):
        s = step * block + i
        sided = ints[KIND, s] + KINDS * (1 - ints[FORWARD, s])
        apply = slot_stencil(floats, ints, s, row)
        for x in range(depth):
            low, high = apply(second[sided, x, :8, :], second[sided, x, 8:, :])
            energy[i, x, :8, :] = inflown[i, x, :8, :] + (low + added[sided, x, :8, :])
            energy[i, x, 8:, :] = inflown[i, x, 8:, :] + (high + added[sided, x, 8:, :])
        return carry

    lax.fori_loop(0, block, one_slot, 0, unroll=2)


def local(incoming_occupation, crystal_kelvin_given, generating_region_flag, labels, speed, rate, storage, threshold, generation):
    slots, depth, width_y, width_z = incoming_occupation.shape
    slabs, modes = lax.axis_size("slab"), lax.axis_size("mode")
    group, groups = GROUP, slabs // GROUP
    lanes = width_y // modes * width_z
    block = slots // group // 2
    cells, all_x = depth * width_y, slabs * depth
    face_rows = block * width_y
    slab = lax.axis_index("slab").astype(jnp.int32)
    meta = jnp.stack([slab, lax.axis_index("mode").astype(jnp.int32)])
    floats, ints, matrix = slot_tables(labels, speed, rate, storage, threshold, generation, slab, slabs, depth, width_z)
    kinds = kind_table(speed, rate, storage, threshold, generation)
    everywhere, first_matrix, second_matrix = heat_matrices(kinds, slab, slabs, depth)
    sums = jnp.stack([jnp.sum(storage), jnp.sum(storage / (4.0 * threshold**3))])

    def shape(*dims):
        return jax.ShapeDtypeStruct(dims, jnp.float32)

    def whole(*dims):
        return pl.BlockSpec(dims, lambda i: (0,) * len(dims))

    def scratch(*dims):
        return pltpu.VMEM(dims, jnp.float32)

    def swap(array, axis, by):
        return lax.ppermute(array, axis, [(i, i ^ by) for i in range(lax.axis_size(axis))])

    def call(kernel, name, in_specs, out_shapes, *args, scratches=()):
        return pl.pallas_call(
            kernel,
            in_specs=in_specs,
            out_specs=[VMEM] * len(out_shapes),
            out_shape=out_shapes,
            scratch_shapes=list(scratches),
            compiler_params=PARAMS,
            name=name,
        )(*args)

    tied = lax.optimization_barrier
    slot_block = pl.BlockSpec((block, depth, width_y, width_z), lambda i: (i, 0, 0, 0))
    half_blocks = [pl.BlockSpec((block, depth, width_y, width_z), lambda i, h=h: (2 * i + h, 0, 0, 0)) for h in range(2)]
    slot_shape = shape(slots, depth, width_y, width_z)
    half_shape = shape(slots // 2, depth, width_y, width_z)
    face = (3, face_rows, width_z)
    share = (modes // 2, ITERS, all_x, lanes)
    plane = (slots // 2 * width_y, width_z)
    flat = (ITERS, cells, width_z)
    flag = generating_region_flag.reshape(cells, width_z)
    given = crystal_kelvin_given.reshape(cells, width_z)

    def sweeps(half, extra):
        outs = [(slot_block, half_shape)] + [(whole(*face), shape(*face))] * group
        scratches = []
        if half:
            outs += [(whole(*share), shape(*share))] * 2
            scratches = [scratch(*plane)] * 6 + [scratch(*flat)]
        else:
            outs += [(whole(*dims), shape(*dims)) for dims in [(depth, lanes)] + [plane] * 6 + [flat]]
        return pl.pallas_call(
            functools.partial(sweeps_kernel, half, (block, depth, width_y, modes, group)),
            grid=(group,),
            in_specs=[SMEM] * 4
            + [half_blocks[half], whole(cells, width_z), whole(cells, width_z)]
            + [whole(*array.shape) for array in extra],
            out_specs=[spec for spec, _ in outs],
            out_shape=[of for _, of in outs],
            scratch_shapes=scratches
            + [
                scratch(ITERS, 2, depth, width_y, width_z),
                scratch(KINDS, depth, width_y, width_z),
                scratch(depth, width_y, width_z),
            ],
            compiler_params=LARGE,
            name=f"sweeps_{half}",
        )(meta, floats, ints, kinds, incoming_occupation, flag, given, *extra)

    def around_group(faces):
        return [faces[0]] + [swap(faces[index], "slab", index) for index in range(1, group)]

    def compose(half, received):
        return call(
            functools.partial(compose_kernel, half, block, group),
            f"compose_{half}",
            [SMEM] * 3 + [VMEM] * group,
            [shape(*face), shape(group, *face)],
            meta,
            floats,
            ints,
            *received,
            scratches=[scratch(group, *face)],
        )

    def across_groups(composite):
        return [composite] + [swap(composite, "slab", index * group) for index in range(1, groups)]

    def enter(half, effective, composites):
        return call(
            functools.partial(enter_kernel, half, block, group, groups, depth),
            f"enter_{half}",
            [SMEM] * 3 + [VMEM] * (1 + groups),
            [shape(*face)] * group,
            meta,
            floats,
            ints,
            effective,
            *composites,
            scratches=[scratch(groups, *face), scratch(group, *face)],
        )

    def add_inflow(half, swept, received, energy):
        return pl.pallas_call(
            functools.partial(inflow_kernel, half, (block, depth, group)),
            grid=(group,),
            in_specs=[SMEM] * 3
            + [slot_block]
            + [whole(*face)] * group
            + [pl.BlockSpec(memory_space=pl.ANY)] * len(energy),
            out_specs=half_blocks[half],
            out_shape=slot_shape,
            scratch_shapes=[scratch(group, *face)],
            input_output_aliases={4 + group: 0} if energy else {},
            compiler_params=LARGE,
            name=f"inflow_{half}",
        )(meta, floats, ints, swept, *received, *energy)

    swept_0, *rest = sweeps(0, [])
    received_0, (quarter, *older) = around_group(rest[:group]), rest[group:]
    swept_1, *rest = sweeps(1, [matrix] + older)
    faces_1, (keep, send), received_0 = tied((rest[:group], rest[group:], received_0))

    composite_0, effective_0 = compose(0, received_0)
    composites_0 = across_groups(composite_0)
    by = 1
    other = swap(send, "mode", by)
    received_1 = around_group(faces_1)
    while 2 * by < modes:
        by *= 2
        now = (modes // (2 * by), ITERS, all_x, lanes)
        keep, send = call(split_kernel, "density_split", [VMEM] * 2, [shape(*now)] * 2, keep, other)
        other = swap(send, "mode", by)
    other, received_1, composites_0 = tied((other, received_1, composites_0))

    (parts,) = call(
        functools.partial(parts_kernel, depth), "density_parts", [VMEM] * 2, [shape(slabs, ITERS, depth, lanes)], keep, other
    )
    entering_0 = around_group(enter(0, effective_0, composites_0))
    composite_1, effective_1 = compose(1, received_1)
    composites_1 = across_groups(composite_1)
    parts = lax.all_to_all(parts, "slab", 0, 0)
    parts, entering_0, composites_1 = tied((parts, entering_0, composites_1))

    copies, late = call(
        totals_kernel,
        "density_totals",
        [SMEM] + [VMEM] * 2,
        [shape(slabs, 2, depth, lanes), shape(depth, lanes)],
        sums,
        parts,
        quarter,
    )
    entering_1 = around_group(enter(1, effective_1, composites_1))
    gathered = lax.all_to_all(copies, "slab", 0, 0)
    energy = add_inflow(0, swept_0, entering_0, [])
    gathered, entering_1, energy = tied((gathered, entering_1, energy))

    pack_shape = shape(2 * all_x + depth, lanes)
    (packed,) = call(
        functools.partial(kelvins_kernel, depth), "kelvins", [SMEM] + [VMEM] * 3, [pack_shape], sums, gathered, late, everywhere
    )
    packs, order = [packed], [0]
    while by:
        packs = packs + [swap(pack, "mode", by) for pack in packs]
        order = order + [index ^ by for index in order]
        by //= 2
    energy = add_inflow(1, swept_1, entering_1, [energy])

    energy, kelvin = pl.pallas_call(
        functools.partial(final_kernel, (block, depth, width_y, width_z, slabs, modes), order),
        grid=(slots // block,),
        in_specs=[SMEM] * 5
        + [slot_block]
        + [whole(*pack_shape.shape)] * modes
        + [whole(*first_matrix.shape), whole(*second_matrix.shape)],
        out_specs=[slot_block, whole(cells, width_z)],
        out_shape=[slot_shape, shape(cells, width_z)],
        scratch_shapes=[scratch(all_x, width_y * width_z)] * 2
        + [scratch(depth, width_y * width_z)]
        + [scratch(2 * KINDS * width_y, width_z)] * 3
        + [scratch(2 * KINDS, depth, width_y, width_z)] * 2
        + [scratch(cells, width_z)] * 2,
        compiler_params=LARGE,
        name="final_energy",
    )(meta, floats, ints, kinds, sums, energy, *packs, first_matrix, second_matrix)
    return energy, kelvin.reshape(depth, width_y, width_z)


def solution(mesh):
    return jax.shard_map(
        local,
        mesh=mesh,
        in_specs=(
            P("mode", "slab", None, None),
            P("slab", None, None),
            P("slab", None, None),
            P("mode"),
            P(),
            P(),
            P(),
            P(),
            P(),
        ),
        out_specs=(P("mode", "slab", None, None), P("slab", None, None)),
        check_vma=False,
    )
```

```python
import functools
import math

import jax
import jax.numpy as jnp
import numpy as np
from jax import lax
from jax.experimental import pallas as pl
from jax.experimental.pallas import tpu as pltpu
from jax.sharding import PartitionSpec as P

FREQ_GROUPS = 8
DIRS = 32
ITERS = 3
NEWTON = 4
PSEUDO_RATE = 0.03
GROUP = 4
COSINES = (np.float32(0.99995), np.float32(0.9999))

SELF, UPY, UPZ, RATIO, WALL, FULL, FULL_N, FULL_T, FULL_GROUP, WARM = range(10)
FORWARD, SHIFT_Y, SHIFT_Z, EDGE_Y, KIND = range(5)
THERM, QUART, HEAT, DECAY, STAY, AROUND = range(6)
KINDS = 2 * FREQ_GROUPS
SLAB, MODE = range(2)

SMEM = pl.BlockSpec(memory_space=pltpu.SMEM)
VMEM = pl.BlockSpec(memory_space=pltpu.VMEM)
PARAMS = pltpu.CompilerParams(vmem_limit_bytes=48 * 1024 * 1024)
ACROSS = math.cos(math.pi / 8) + math.sin(math.pi / 8)


def diagonal_of(speed, rate, cosine):
    sine = jnp.sqrt(1.0 - cosine * cosine)
    return speed * (cosine + sine * np.float32(ACROSS)) + rate + PSEUDO_RATE


def slot_tables(labels, speed, rate, storage, threshold, generation, slab, slabs, depth, width_z):
    band = labels // DIRS
    direction = labels % DIRS
    of_band = (band[None, :] == jnp.arange(FREQ_GROUPS, dtype=jnp.int32)[:, None]).astype(jnp.float32)
    speed, rate, storage, threshold, generation = (
        jnp.sum(of_band * value[:, None], axis=0) for value in (speed, rate, storage, threshold, generation)
    )
    polar = direction % 4
    outer = (polar == 0) | (polar == 3)
    forward = polar < 2
    cosine = jnp.where(outer, COSINES[0], COSINES[1])
    sine = jnp.sqrt(1.0 - cosine * cosine)
    azimuth = ((direction // 4).astype(jnp.float32) + 0.5) * (2.0 * math.pi / (DIRS // 4))
    vy = speed * sine * jnp.cos(azimuth)
    vz = speed * sine * jnp.sin(azimuth)
    diagonal = diagonal_of(speed, rate, cosine)
    ratio = speed * cosine / diagonal
    full = lax.integer_pow(ratio, depth)
    at_wall = jnp.where(forward, slab == 0, slab == slabs - 1)
    wall = storage * (1.0 + 1.0 / (4.0 * threshold**3))
    floats = jnp.stack(
        [
            PSEUDO_RATE / diagonal,
            jnp.abs(vy) / diagonal,
            jnp.abs(vz) / diagonal,
            ratio,
            jnp.where(at_wall, wall, 0.0),
            full,
            depth * full,
            (depth * (depth + 1) // 2) * full,
            lax.integer_pow(full, GROUP),
            generation / diagonal,
        ]
    )
    ints = jnp.stack(
        [
            forward.astype(jnp.int32),
            jnp.where(vy > 0, 1, 7).astype(jnp.int32),
            jnp.where(vz > 0, 1, width_z - 1).astype(jnp.int32),
            jnp.where(vy > 0, 0, 7).astype(jnp.int32),
            2 * band + jnp.where(outer, 0, 1),
        ]
    )
    return floats, ints


def kind_table(speed, rate, storage, threshold, generation):
    rows = []
    for cosine in COSINES:
        diagonal = diagonal_of(speed, rate, cosine)
        therm = rate * storage / diagonal
        quart = therm / (4.0 * threshold**3)
        across = jnp.sqrt(1.0 - cosine * cosine) * np.float32(2.0 * ACROSS)
        rows.append(
            jnp.stack(
                [
                    therm,
                    quart,
                    generation / diagonal,
                    speed * cosine / diagonal,
                    (DIRS // 4) * PSEUDO_RATE / diagonal,
                    across * speed / diagonal,
                ]
            )
        )
    return jnp.stack(rows, axis=2).reshape(6, KINDS)


def heat_matrices(kinds, slab, slabs, depth):
    cells = slabs * depth
    there = jnp.arange(cells, dtype=jnp.int32)
    decay = kinds[DECAY][:, None, None]
    per_cell = (DIRS // 4) / DIRS

    def side_by_side(weight, factor):
        sums = [jnp.sum((factor * kinds[row])[:, None, None] * weight, axis=0) for row in (THERM, QUART)]
        return jnp.concatenate(sums, axis=1)

    def between(here):
        far = jnp.abs(here[:, None] - there[None, :])
        n = far.astype(jnp.float32)
        return n, jnp.power(decay, n[None]) * jnp.where(far == 0, 2.0, 1.0)[None]

    _, everywhere = between(there)
    n, home = between(slab * depth + jnp.arange(depth, dtype=jnp.int32))
    twice = home * (n + 1.0)[None]
    one = jnp.full((KINDS,), per_cell, jnp.float32)
    once = side_by_side(home, one)
    stay = side_by_side(twice, kinds[STAY] / DIRS)
    around = side_by_side(twice, kinds[AROUND] / DIRS)
    before = jnp.stack([slab * depth - 1 - there, there - (slab + 1) * depth])
    n = before.astype(jnp.float32)[:, None, :]
    power = jnp.power(kinds[DECAY][None, :, None], jnp.maximum(n, 0.0))
    inflow = jnp.where(before[:, None, :] >= 0, power, 0.0)
    inflow = jnp.concatenate(
        [inflow * kinds[THERM][None, :, None], inflow * kinds[QUART][None, :, None]], axis=2
    )
    longer = inflow * (jnp.concatenate([n, n], axis=2) + 1.0)
    inflow, longer = (value.reshape(2 * KINDS, 2 * cells) for value in (inflow, longer))
    return (
        side_by_side(everywhere, one),
        jnp.concatenate([inflow, longer, stay, around], axis=0),
        jnp.concatenate([inflow, once], axis=0),
    )


def newton(density, kelvin, linear, quart):
    for _ in range(NEWTON):
        cube = kelvin * kelvin * kelvin
        residual = linear * kelvin + quart * (kelvin * cube) - density
        kelvin = kelvin - residual / (linear + 4.0 * quart * cube)
    return kelvin


def exact_dot(left, right):
    return jnp.dot(left, right, precision=lax.Precision.HIGHEST, preferred_element_type=jnp.float32)


def fourth(value):
    square = value * value
    return square * square


def add_up(values):
    while len(values) > 1:
        values = [a + b for a, b in zip(values[::2], values[1::2])]
    return values[0]


def stencil(low, high, c_self, c_y, c_z, shift_y, shift_z, at_edge):
    turned_low, turned_high = pltpu.roll(low, shift_y, 0), pltpu.roll(high, shift_y, 0)
    up_low = jnp.where(at_edge, turned_high, turned_low)
    up_high = jnp.where(at_edge, turned_low, turned_high)
    return (
        c_self * low + c_y * up_low + c_z * pltpu.roll(low, shift_z, 1),
        c_self * high + c_y * up_high + c_z * pltpu.roll(high, shift_z, 1),
    )


def course(ints, s, depth):
    forward = ints[FORWARD, s] == 1
    return jnp.where(forward, 0, depth - 1), jnp.where(forward, 1, -1)


def slot_stencil(floats, ints, s, row):
    at_edge = row == ints[EDGE_Y, s]
    c_self, c_y, c_z = floats[SELF, s], floats[UPY, s], floats[UPZ, s]
    shift_y, shift_z = ints[SHIFT_Y, s], ints[SHIFT_Z, s]
    return lambda low, high: stencil(low, high, c_self, c_y, c_z, shift_y, shift_z, at_edge)


def rows_of(s):
    at = pl.multiple_of(s * 16, 16)
    return pl.ds(at, 8), pl.ds(at + 8, 8)


K_SELF, K_LARGE, K_SMALL, K_RATIO, K_THERM, K_QUART, K_HEAT, K_WALL = range(8)


def fill_kinds(table, bands):
    speeds, rates, storages, thresholds, generations = bands
    for kind in range(KINDS):
        band, cosine = kind // 2, COSINES[kind % 2]
        sine = np.sqrt(np.float32(1.0) - cosine * cosine)
        speed, rate, storage, threshold, generation = (
            jnp.full((8, 128), ref[band], jnp.float32) for ref in (speeds, rates, storages, thresholds, generations)
        )
        inverse = 1.0 / (speed * float(cosine + sine * np.float32(ACROSS)) + rate + PSEUDO_RATE)
        quart = 1.0 / (4.0 * (threshold * threshold * threshold))
        across = speed * float(sine) * inverse
        therm = rate * storage * inverse
        rows = (
            PSEUDO_RATE * inverse,
            across * math.cos(math.pi / 8),
            across * math.sin(math.pi / 8),
            speed * float(cosine) * inverse,
            therm,
            therm * quart,
            generation * inverse,
            storage * (1.0 + quart),
        )
        for row, value in enumerate(rows):
            table[row, kind] = value


def sweeps_kernel(sizes, meta, labels, *refs):
    block, blocks, depth, width_y, slots, modes, group = sizes
    bands, refs = refs[:5], refs[5:]
    energy, flag, given, label_row, swept, quarter, *rest = refs
    faces, rest = rest[:group], rest[group:]
    keep, send, *planes, density, flat, sources, heat, table = rest
    out_one, turn_one, turn_two, out_two, turn_late, out_three = planes
    rows, own = width_y // modes, slots // group
    step = pl.program_id(0)
    slab, mode = meta[SLAB], meta[MODE]
    slabs = keep.shape[2] // depth

    @pl.when(step == 0)
    def _():
        fill_kinds(table, bands)
        for yy in range(rows):
            quarter[:, yy * 128 : (yy + 1) * 128] = given[pl.ds(mode * rows + yy, depth, stride=width_y), :]
        density[...] = jnp.zeros_like(density)

        def one_layer(x, carry):
            at = pl.multiple_of(x * 16, 16)
            for low in (0, 8):
                t = given[pl.ds(at + low, 8), :]
                power = fourth(t)
                hot = flag[pl.ds(at + low, 8), :].astype(jnp.float32)
                heat[x, low : low + 8, :] = hot
                for kind in range(KINDS):
                    value = table[K_THERM, kind] * t + table[K_QUART, kind] * power + table[K_HEAT, kind] * hot
                    sources[kind, x, low : low + 8, :] = value
            return carry

        lax.fori_loop(0, depth, one_layer, 0)

    row = lax.broadcasted_iota(jnp.int32, (8, 128), 0)

    def one_slot(i, carry):
        s = step * block + i
        label = labels[s]
        polar, turn_of = label % 4, (label // 4) % 8
        forward = polar < 2
        kind = 2 * (label // DIRS) + jnp.where((polar == 0) | (polar == 3), 0, 1)
        right, up = (turn_of < 2) | (turn_of > 5), turn_of < 4
        wide = (turn_of % 4 == 0) | (turn_of % 4 == 3)
        start, stride = jnp.where(forward, 0, depth - 1), jnp.where(forward, 1, -1)
        side = jnp.where(forward, 0, 1)
        at_wall = jnp.where(forward, slab == 0, slab == slabs - 1)
        c_self, ratio, warm = table[K_SELF, kind], table[K_RATIO, kind], table[K_HEAT, kind]
        c_y = table[jnp.where(wide, K_LARGE, K_SMALL), kind]
        c_z = table[jnp.where(wide, K_SMALL, K_LARGE), kind]
        wall = jnp.where(at_wall, 1.0, 0.0) * table[K_WALL, kind]
        shift_y, shift_z = jnp.where(right, 1, 7), jnp.where(up, 1, 127)
        at_edge = row == jnp.where(right, 0, 7)
        apply = lambda low, high: stencil(low, high, c_self, c_y, c_z, shift_y, shift_z, at_edge)
        xs = [start + stride * j for j in range(depth)]
        layers = [(energy[i, x, :8, :], energy[i, x, 8:, :]) for x in xs]
        last = []
        for turn in range(ITERS):
            total_low = total_high = wall
            for j, x in enumerate(xs):
                low, high = apply(*layers[j])
                if turn == 0:
                    low, high = low + sources[kind, x, :8, :], high + sources[kind, x, 8:, :]
                else:
                    low, high = low + warm * heat[x, :8, :], high + warm * heat[x, 8:, :]
                total_low = ratio * total_low + low
                total_high = ratio * total_high + high
                layers[j] = (total_low, total_high)
                density[turn, side, j, :8, :] += total_low
                density[turn, side, j, 8:, :] += total_high
                if turn == ITERS - 1:
                    swept[i, x, :8, :] = total_low
                    swept[i, x, 8:, :] = total_high
            last.append((total_low, total_high))
        turned = apply(*last[0])
        at_low, at_high = rows_of(s)
        values = (last[0], turned, apply(*turned), last[1], apply(*last[1]), last[2])
        for plane, (low, high) in zip(planes, values):
            plane[at_low, :] = low
            plane[at_high, :] = high
        return carry

    lax.fori_loop(0, block, one_slot, 0, unroll=2)

    @pl.when(step == blocks - 1)
    def _():
        for by in range(group):
            at = pl.ds(pl.multiple_of(((slab % group) ^ by) * own * 16, 16), own * 16)
            for index, plane in enumerate((turn_two, turn_late, out_three)):
                faces[by][index] = plane[at, :]
        for turn in range(ITERS):
            for x in range(depth):
                flat[turn, x * 16 : x * 16 + 16, :] = density[turn, 0, x] + density[turn, 1, depth - 1 - x]
        label = label_row[...]
        polar = label % 4
        kinds = 2 * (label // DIRS) + jnp.where((polar == 0) | (polar == 3), 0, 1)
        decay = jnp.ones((1, slots), jnp.float32)
        for kind in range(KINDS):
            decay = jnp.where(kinds == kind, table[K_RATIO, kind][:1, :slots], decay)
        x = lax.broadcasted_iota(jnp.int32, (slabs * depth, slots), 0)
        past = jnp.where(polar < 2, x - (slab * depth + depth - 1), slab * depth - x)
        n = past.astype(jnp.float32)
        weight = jnp.where(past > 0, jnp.exp(jnp.maximum(n, 0.0) * jnp.log(decay)), 0.0)
        weights = (weight, n * weight, (0.5 * n * (n + 1.0)) * weight)
        home = pl.ds(pl.multiple_of(slab * depth, 8), depth)
        for by in range(modes):
            ys = [(mode ^ by) * rows + yy for yy in range(rows)]
            pick = lambda plane, count: jnp.concatenate([plane[pl.ds(y, count, stride=width_y), :] for y in ys], axis=1)
            plain = exact_dot(weights[0], jnp.concatenate([pick(p, slots) for p in (out_one, out_two, out_three)], axis=1))
            once = exact_dot(weights[1], jnp.concatenate([pick(p, slots) for p in (turn_one, turn_late)], axis=1))
            twice = exact_dot(weights[2], pick(turn_two, slots))
            lanes = rows * 128
            target = (send if by % 2 else keep).at[by // 2]
            target[0] = plain[:, :lanes]
            target[1] = plain[:, lanes : 2 * lanes] + once[:, :lanes]
            target[2] = plain[:, 2 * lanes :] + once[:, lanes:] + twice
            for turn in range(ITERS):
                target[turn, home, :] += pick(flat.at[turn], depth)


def split_kernel(mine, other, keep, send):
    for index in range(mine.shape[0]):
        target = send if index % 2 else keep
        target[index // 2] = mine[index] + other[index]


def parts_kernel(depth, mine, other, parts):
    for turn in range(ITERS):
        total = mine[0, turn] + other[0, turn]
        for slab in range(parts.shape[0]):
            parts[slab, turn] = total[slab * depth : (slab + 1) * depth]


def totals_kernel(sums, parts, before, copies, late):
    slabs = parts.shape[0]
    one, two, three = (
        add_up([parts[slab, turn] for slab in range(slabs)]) * (1.0 / DIRS) for turn in range(ITERS)
    )
    late[...] = three
    kelvin = newton(one, before[...], sums[0], sums[1])
    for slab in range(slabs):
        copies[slab, 0] = kelvin
        copies[slab, 1] = two


def kelvins_kernel(depth, meta, sums, gathered, late, matrix_one, matrix_two, packed):
    slabs = gathered.shape[0]
    cells = slabs * depth
    one, two = (jnp.concatenate([gathered[slab, index] for slab in range(slabs)], axis=0) for index in range(2))
    first = exact_dot(matrix_one[...], jnp.concatenate([one, fourth(one)], axis=0))
    two = newton(two + first[:cells], one, sums[0], sums[1])
    second = exact_dot(matrix_two[...], jnp.concatenate([two, fourth(two)], axis=0))
    sided = 2 * KINDS
    packed[: 2 * sided, :] = first[cells : cells + 2 * sided]
    packed[2 * sided : 3 * sided, :] = second[:sided]
    base = 3 * sided
    packed[base : base + depth, :] = gathered[meta[SLAB], 0]
    stay = first[cells + 2 * sided : cells + 2 * sided + depth]
    around = first[cells + 2 * sided + depth :]
    own = jnp.zeros_like(around)
    for slab in range(slabs):
        own = jnp.where(meta[SLAB] == slab, two[slab * depth : (slab + 1) * depth], own)
    packed[base + depth : base + 2 * depth, :] = own
    packed[base + 2 * depth : base + 3 * depth, :] = late[...] + stay + second[sided:]
    packed[base + 3 * depth :, :] = around


def compose_kernel(own, group, meta, floats, ints, *refs):
    received, (_, composite, effective, ordered) = refs[:group], refs[group:]
    place = meta[SLAB] % group
    for by in range(group):
        ordered[place ^ by] = received[by][...]

    def one_slot(i, carry):
        s = place * own + i
        start, stride = course(ints, s, group)
        full, full_n, full_t = floats[FULL, s], floats[FULL_N, s], floats[FULL_T, s]
        at = pl.ds(pl.multiple_of(i * 16, 16), 16)
        one = two = three = jnp.zeros((16, 128), jnp.float32)
        for j in range(group):
            k = start + stride * j
            three = full * three + full_n * two + full_t * one + ordered[k, 2, at, :]
            two = full * two + full_n * one + ordered[k, 1, at, :]
            one = full * one + ordered[k, 0, at, :]
        for index, value in enumerate((one, two, three)):
            composite[index, at, :] = value
        return carry

    lax.fori_loop(0, own, one_slot, 0, unroll=4)
    effective[...] = ordered[...]


def enter_kernel(own, group, groups, depth, meta, floats, ints, effective, *refs):
    composites, rest = refs[:groups], refs[groups:]
    outs, (ordered, entered) = rest[:group], rest[group:]
    slab = meta[SLAB]
    place, mine = slab % group, slab // group
    for by in range(groups):
        ordered[mine ^ by] = composites[by][...]
    span = depth * group

    def one_slot(i, carry):
        s = place * own + i
        start, stride = course(ints, s, group)
        begin, leap = course(ints, s, groups)
        ahead = jnp.where(ints[FORWARD, s] == 1, mine, groups - 1 - mine)
        at = pl.ds(pl.multiple_of(i * 16, 16), 16)

        def push(values, full, full_n, full_t, added):
            one, two, three = values
            return (
                full * one + added[0],
                full * two + full_n * one + added[1],
                full * three + full_n * two + full_t * one + added[2],
            )

        values = (jnp.zeros((16, 128), jnp.float32),) * 3
        whole = floats[FULL_GROUP, s]
        for g in range(groups - 1):
            index = begin + leap * g
            added = [ordered[index, plane, at, :] for plane in range(3)]
            later = push(values, whole, span * whole, (span * (span + 1) // 2) * whole, added)
            values = tuple(jnp.where(g < ahead, a, b) for a, b in zip(later, values))
        full, full_n, full_t = floats[FULL, s], floats[FULL_N, s], floats[FULL_T, s]
        for j in range(group):
            k = start + stride * j
            for plane in range(3):
                entered[k, plane, at, :] = values[plane]
            if j < group - 1:
                values = push(values, full, full_n, full_t, [effective[k, plane, at, :] for plane in range(3)])
        return carry

    lax.fori_loop(0, own, one_slot, 0, unroll=2)
    for by in range(group):
        outs[by][...] = entered[place ^ by]


def warm_kernel(sizes, order, meta, floats, ints, kinds, sums, swept, *refs):
    block, depth, width_y, width_z, modes = sizes
    packs, refs = refs[:modes], refs[modes:]
    energy, kelvin, enter_one, enter_long, enter_two, second, added, own_one, own_two, plain, around = refs
    step = pl.program_id(0)
    rows = width_y // modes

    @pl.when(step == 0)
    def _():
        sided, base = 2 * KINDS, 6 * KINDS
        for pack, by in zip(packs, order):
            for yy in range(rows):
                y, lane = (meta[MODE] ^ by) * rows + yy, slice(yy * 128, (yy + 1) * 128)
                for index, target in enumerate((enter_one, enter_long, enter_two)):
                    target[pl.ds(y, sided, stride=width_y), :] = pack[index * sided : (index + 1) * sided, lane]
                scattered = pl.ds(y, depth, stride=width_y)
                own_one[scattered, :] = pack[base : base + depth, lane]
                own_two[scattered, :] = pack[base + depth : base + 2 * depth, lane]
                plain[y] = pack[base + 2 * depth : base + 3 * depth, lane]
                around[y] = pack[base + 3 * depth :, lane]
        for y in range(width_y):
            here = around[y]
            near = around[(y - 1) % width_y] + around[(y + 1) % width_y]
            near = near + (pltpu.roll(here, 1, 1) + pltpu.roll(here, width_z - 1, 1))
            scattered = pl.ds(y, depth, stride=width_y)
            kelvin[scattered, :] = newton(plain[y] + near, own_two[scattered, :], sums[0], sums[1])

        def one_kind(kind, carry):
            therm, quart, decay = kinds[THERM, kind], kinds[QUART, kind], kinds[DECAY, kind]
            ones, twos = [], []
            for x in range(depth):
                here = slice(x * 16, x * 16 + 16)
                t, u = own_one[here, :], own_two[here, :]
                ones.append(therm * t + quart * fourth(t))
                twos.append(therm * u + quart * fourth(u))
            for back in (0, KINDS):
                at = pl.ds(pl.multiple_of((kind + back) * 16, 16), 16)
                once, twice, new = enter_one[at, :], enter_long[at, :], enter_two[at, :]
                for j in range(depth):
                    x = depth - 1 - j if back else j
                    once = decay * once + ones[x]
                    twice = decay * twice + once
                    new = decay * new + twos[x]
                    second[kind + back, x] = twice
                    added[kind + back, x] = new
            return carry

        lax.fori_loop(0, KINDS, one_kind, 0)

    row = lax.broadcasted_iota(jnp.int32, (8, 128), 0)

    def one_slot(i, carry):
        s = step * block + i
        sided = ints[KIND, s] + KINDS * (1 - ints[FORWARD, s])
        apply = slot_stencil(floats, ints, s, row)
        for x in range(depth):
            low, high = apply(second[sided, x, :8, :], second[sided, x, 8:, :])
            energy[i, x, :8, :] = swept[i, x, :8, :] + (low + added[sided, x, :8, :])
            energy[i, x, 8:, :] = swept[i, x, 8:, :] + (high + added[sided, x, 8:, :])
        return carry

    lax.fori_loop(0, block, one_slot, 0, unroll=2)


def inflow_kernel(sizes, meta, floats, ints, warm, *refs):
    block, depth, own, group = sizes
    received, (energy, ordered) = refs[:group], refs[group:]
    step = pl.program_id(0)

    @pl.when(step == 0)
    def _():
        for by in range(group):
            ordered[(meta[SLAB] % group) ^ by] = received[by][...]

    def one_slot(i, carry):
        s = step * block + i
        start, stride = course(ints, s, depth)
        ratio = floats[RATIO, s]
        at = pl.ds(pl.multiple_of((s % own) * 16, 16), 16)
        one, two, three = (ordered[s // own, plane, at, :] for plane in range(ITERS))
        for j in range(depth):
            x = start + stride * j
            one = ratio * one
            two = ratio * two + one
            three = ratio * three + two
            energy[i, x] = warm[i, x] + three
        return carry

    lax.fori_loop(0, block, one_slot, 0, unroll=4)


def local(incoming_occupation, crystal_kelvin_given, generating_region_flag, labels, speed, rate, storage, threshold, generation):
    slots, depth, width_y, width_z = incoming_occupation.shape
    slabs, modes = lax.axis_size("slab"), lax.axis_size("mode")
    group, groups = GROUP, slabs // GROUP
    own = slots // group
    lanes = width_y // modes * width_z
    block = 8
    blocks = slots // block
    cells, all_x = depth * width_y, slabs * depth
    face_rows = own * width_y
    slab = lax.axis_index("slab").astype(jnp.int32)
    meta = jnp.stack([slab, lax.axis_index("mode").astype(jnp.int32)])
    floats, ints = slot_tables(labels, speed, rate, storage, threshold, generation, slab, slabs, depth, width_z)
    kinds = kind_table(speed, rate, storage, threshold, generation)
    everywhere, first_matrix, second_matrix = heat_matrices(kinds, slab, slabs, depth)
    sums = jnp.stack([jnp.sum(storage), jnp.sum(storage / (4.0 * threshold**3))])

    def shape(*dims):
        return jax.ShapeDtypeStruct(dims, jnp.float32)

    def whole(*dims):
        return pl.BlockSpec(dims, lambda i: (0,) * len(dims))

    def scratch(*dims):
        return pltpu.VMEM(dims, jnp.float32)

    def swap(array, axis, by):
        return lax.ppermute(array, axis, [(i, i ^ by) for i in range(lax.axis_size(axis))])

    def call(kernel, name, in_specs, out_shapes, *args, scratches=()):
        return pl.pallas_call(
            kernel,
            in_specs=in_specs,
            out_specs=[VMEM] * len(out_shapes),
            out_shape=out_shapes,
            scratch_shapes=list(scratches),
            compiler_params=PARAMS,
            name=name,
        )(*args)

    slot_block = pl.BlockSpec((block, depth, width_y, width_z), lambda i: (i, 0, 0, 0))
    slot_shape = shape(slots, depth, width_y, width_z)
    face = (3, face_rows, width_z)
    half = (modes // 2, ITERS, all_x, lanes)
    swept, quarter, *rest = pl.pallas_call(
        functools.partial(sweeps_kernel, (block, blocks, depth, width_y, slots, modes, group)),
        grid=(blocks,),
        in_specs=[SMEM] * 7 + [slot_block, whole(cells, width_z), whole(cells, width_z), whole(1, slots)],
        out_specs=[slot_block, whole(depth, lanes)] + [whole(*face)] * group + [whole(*half)] * 2,
        out_shape=[slot_shape, shape(depth, lanes)] + [shape(*face)] * group + [shape(*half)] * 2,
        scratch_shapes=[scratch(slots * width_y, width_z)] * 6
        + [
            scratch(ITERS, 2, depth, width_y, width_z),
            scratch(ITERS, cells, width_z),
            scratch(KINDS, depth, width_y, width_z),
            scratch(depth, width_y, width_z),
            scratch(8, KINDS, 8, width_z),
        ],
        compiler_params=PARAMS,
        name="sweeps",
    )(
        meta,
        labels,
        speed,
        rate,
        storage,
        threshold,
        generation,
        incoming_occupation,
        generating_region_flag.reshape(cells, width_z),
        crystal_kelvin_given.reshape(cells, width_z),
        labels.reshape(1, slots),
    )
    faces, (keep, send) = rest[:group], rest[group:]

    by = 1
    other = swap(send, "mode", by)
    received = [faces[0]] + [swap(faces[index], "slab", index) for index in range(1, group)]
    while 2 * by < modes:
        by *= 2
        now = (modes // (2 * by), ITERS, all_x, lanes)
        keep, send = call(split_kernel, "density_split", [VMEM] * 2, [shape(*now)] * 2, keep, other)
        other = swap(send, "mode", by)
    piece = (slabs, ITERS, depth, lanes)
    (parts,) = call(functools.partial(parts_kernel, depth), "density_parts", [VMEM] * 2, [shape(*piece)], keep, other)
    summed = lax.all_to_all(parts, "slab", 0, 0)

    composite, effective = call(
        functools.partial(compose_kernel, own, group),
        "compose",
        [SMEM] * 3 + [VMEM] * group + [pl.BlockSpec(memory_space=pl.ANY)],
        [shape(*face), shape(group, *face)],
        meta,
        floats,
        ints,
        *received,
        parts,
        scratches=[scratch(group, *face)],
    )
    summed, composite = lax.optimization_barrier((summed, composite))
    composites = [composite] + [swap(composite, "slab", index * group) for index in range(1, groups)]
    copies, late = call(
        totals_kernel,
        "density_totals",
        [SMEM] + [VMEM] * 2,
        [shape(slabs, 2, depth, lanes), shape(depth, lanes)],
        sums,
        summed,
        quarter,
    )
    gathered = lax.all_to_all(copies, "slab", 0, 0)
    entering = call(
        functools.partial(enter_kernel, own, group, groups, depth),
        "enter",
        [SMEM] * 3 + [VMEM] * (1 + groups),
        [shape(*face)] * group,
        meta,
        floats,
        ints,
        effective,
        *composites,
        scratches=[scratch(groups, *face), scratch(group, *face)],
    )
    gathered, entering = lax.optimization_barrier((gathered, entering))
    entering = [entering[0]] + [swap(entering[index], "slab", index) for index in range(1, group)]

    pack_shape = shape(6 * KINDS + 4 * depth, lanes)
    (packed,) = call(
        functools.partial(kelvins_kernel, depth),
        "kelvins",
        [SMEM] * 2 + [VMEM] * 4,
        [pack_shape],
        meta,
        sums,
        gathered,
        late,
        jnp.concatenate([everywhere, first_matrix], axis=0),
        second_matrix,
    )
    packs, order = [packed], [0]
    while by:
        packs = packs + [swap(pack, "mode", by) for pack in packs]
        order = order + [index ^ by for index in order]
        by //= 2

    warm, kelvin = pl.pallas_call(
        functools.partial(warm_kernel, (block, depth, width_y, width_z, modes), order),
        grid=(blocks,),
        in_specs=[SMEM] * 5 + [slot_block] + [whole(*pack_shape.shape)] * modes,
        out_specs=[slot_block, whole(cells, width_z)],
        out_shape=[slot_shape, shape(cells, width_z)],
        scratch_shapes=[scratch(2 * KINDS * width_y, width_z)] * 3
        + [scratch(2 * KINDS, depth, width_y, width_z)] * 2
        + [scratch(cells, width_z)] * 2
        + [scratch(width_y, depth, width_z)] * 2,
        compiler_params=PARAMS,
        name="warm",
    )(meta, floats, ints, kinds, sums, swept, *packs)
    energy = pl.pallas_call(
        functools.partial(inflow_kernel, (block, depth, own, group)),
        grid=(blocks,),
        in_specs=[SMEM] * 3 + [slot_block] + [whole(*face)] * group,
        out_specs=slot_block,
        out_shape=slot_shape,
        scratch_shapes=[scratch(group, *face)],
        compiler_params=PARAMS,
        name="inflow",
    )(meta, floats, ints, warm, *entering)
    return energy, kelvin.reshape(depth, width_y, width_z)


def solution(mesh):
    return jax.shard_map(
        local,
        mesh=mesh,
        in_specs=(
            P("mode", "slab", None, None),
            P("slab", None, None),
            P("slab", None, None),
            P("mode"),
            P(),
            P(),
            P(),
            P(),
            P(),
        ),
        out_specs=(P("mode", "slab", None, None), P("slab", None, None)),
        check_vma=False,
    )
```

```python
import functools
import math

import jax
import jax.numpy as jnp
import numpy as np
from jax import lax
from jax.experimental import pallas as pl
from jax.experimental.pallas import tpu as pltpu
from jax.sharding import PartitionSpec as P

FREQ_GROUPS = 8
DIRS = 32
ITERS = 3
NEWTON = 4
PSEUDO_RATE = 0.03
GROUP = 4
COSINES = (np.float32(0.99995), np.float32(0.9999))

SELF, UPY, UPZ, RATIO, WALL, FULL, FULL_N, FULL_T, FULL_GROUP, WARM = range(10)
FORWARD, SHIFT_Y, SHIFT_Z, EDGE_Y, KIND = range(5)
THERM, QUART, HEAT, DECAY, STAY, AROUND = range(6)
KINDS = 2 * FREQ_GROUPS
SLAB, MODE = range(2)

SMEM = pl.BlockSpec(memory_space=pltpu.SMEM)
VMEM = pl.BlockSpec(memory_space=pltpu.VMEM)
PARAMS = pltpu.CompilerParams(vmem_limit_bytes=48 * 1024 * 1024)
LARGE = pltpu.CompilerParams(vmem_limit_bytes=62 * 1024 * 1024)
ACROSS = math.cos(math.pi / 8) + math.sin(math.pi / 8)


def diagonal_of(speed, rate, cosine):
    sine = jnp.sqrt(1.0 - cosine * cosine)
    return speed * (cosine + sine * np.float32(ACROSS)) + rate + PSEUDO_RATE


def slot_tables(labels, speed, rate, storage, threshold, generation, slab, slabs, depth, width_z):
    band = labels // DIRS
    direction = labels % DIRS
    of_band = (band[None, :] == jnp.arange(FREQ_GROUPS, dtype=jnp.int32)[:, None]).astype(jnp.float32)
    speed, rate, storage, threshold, generation = (
        jnp.sum(of_band * value[:, None], axis=0) for value in (speed, rate, storage, threshold, generation)
    )
    polar = direction % 4
    outer = (polar == 0) | (polar == 3)
    forward = polar < 2
    cosine = jnp.where(outer, COSINES[0], COSINES[1])
    sine = jnp.sqrt(1.0 - cosine * cosine)
    azimuth = ((direction // 4).astype(jnp.float32) + 0.5) * (2.0 * math.pi / (DIRS // 4))
    vy = speed * sine * jnp.cos(azimuth)
    vz = speed * sine * jnp.sin(azimuth)
    diagonal = diagonal_of(speed, rate, cosine)
    ratio = speed * cosine / diagonal
    full = lax.integer_pow(ratio, depth)
    at_wall = jnp.where(forward, slab == 0, slab == slabs - 1)
    wall = storage * (1.0 + 1.0 / (4.0 * threshold**3))
    floats = jnp.stack(
        [
            PSEUDO_RATE / diagonal,
            jnp.abs(vy) / diagonal,
            jnp.abs(vz) / diagonal,
            ratio,
            jnp.where(at_wall, wall, 0.0),
            full,
            depth * full,
            (depth * (depth + 1) // 2) * full,
            lax.integer_pow(full, GROUP),
            generation / diagonal,
        ]
    )
    ints = jnp.stack(
        [
            forward.astype(jnp.int32),
            jnp.where(vy > 0, 1, 7).astype(jnp.int32),
            jnp.where(vz > 0, 1, width_z - 1).astype(jnp.int32),
            jnp.where(vy > 0, 0, 7).astype(jnp.int32),
            2 * band + jnp.where(outer, 0, 1),
        ]
    )
    return floats, ints


def kind_table(speed, rate, storage, threshold, generation):
    rows = []
    for cosine in COSINES:
        diagonal = diagonal_of(speed, rate, cosine)
        therm = rate * storage / diagonal
        quart = therm / (4.0 * threshold**3)
        across = jnp.sqrt(1.0 - cosine * cosine) * np.float32(2.0 * ACROSS)
        rows.append(
            jnp.stack(
                [
                    therm,
                    quart,
                    generation / diagonal,
                    speed * cosine / diagonal,
                    (DIRS // 4) * PSEUDO_RATE / diagonal,
                    across * speed / diagonal,
                ]
            )
        )
    return jnp.stack(rows, axis=2).reshape(6, KINDS)


def matrices_kernel(depth, meta, kinds, first, second):
    cells = first.shape[1] // 2
    slab = meta[SLAB]
    sided = 2 * KINDS
    per_cell = (DIRS // 4) / DIRS

    def places(rows):
        column = lax.broadcasted_iota(jnp.int32, (rows, 2 * cells), 1)
        quart = column >= cells
        return jnp.where(quart, column - cells, column), quart

    def distance(rows, base):
        there, quart = places(rows)
        far = jnp.abs(lax.broadcasted_iota(jnp.int32, (rows, 2 * cells), 0) + base - there)
        return far.astype(jnp.float32), jnp.where(far == 0, 2.0, 1.0), quart

    full, twice_full, quart_full = distance(cells, 0)
    home, twice_home, quart_home = distance(depth, slab * depth)
    there, quart_row = places(1)
    gaps = [value.astype(jnp.float32) for value in (slab * depth - 1 - there, there - (slab + 1) * depth)]
    everywhere = jnp.zeros((cells, 2 * cells), jnp.float32)
    once = stay = around = jnp.zeros((depth, 2 * cells), jnp.float32)
    for kind in range(KINDS):
        therm, quart = kinds[THERM, kind], kinds[QUART, kind]
        slope = jnp.log(jnp.full((1, 2 * cells), kinds[DECAY, kind], jnp.float32))
        everywhere += jnp.where(quart_full, quart, therm) * (jnp.exp(full * slope) * twice_full)
        weight = jnp.where(quart_home, quart, therm) * (jnp.exp(home * slope) * twice_home)
        once += weight
        weight = weight * (home + 1.0)
        stay += kinds[STAY, kind] * weight
        around += kinds[AROUND, kind] * weight
        for side, gap in enumerate(gaps):
            weight = jnp.where(quart_row, quart, therm) * jnp.exp(jnp.maximum(gap, 0.0) * slope)
            weight = jnp.where(gap >= 0, weight, 0.0)
            at = kind + side * KINDS
            first[cells + at : cells + at + 1, :] = weight
            first[cells + sided + at : cells + sided + at + 1, :] = weight * (gap + 1.0)
            second[at : at + 1, :] = weight
    first[:cells, :] = everywhere * per_cell
    base = cells + 2 * sided
    first[base : base + depth, :] = stay * (1.0 / DIRS)
    first[base + depth :, :] = around * (1.0 / DIRS)
    second[sided:, :] = once * per_cell


def newton(density, kelvin, linear, quart):
    for _ in range(NEWTON):
        cube = kelvin * kelvin * kelvin
        residual = linear * kelvin + quart * (kelvin * cube) - density
        kelvin = kelvin - residual / (linear + 4.0 * quart * cube)
    return kelvin


def exact_dot(left, right):
    return jnp.dot(left, right, precision=lax.Precision.HIGHEST, preferred_element_type=jnp.float32)


def fourth(value):
    square = value * value
    return square * square


def add_up(values):
    while len(values) > 1:
        values = [a + b for a, b in zip(values[::2], values[1::2])]
    return values[0]


def stencil(low, high, c_self, c_y, c_z, shift_y, shift_z, at_edge):
    turned_low, turned_high = pltpu.roll(low, shift_y, 0), pltpu.roll(high, shift_y, 0)
    up_low = jnp.where(at_edge, turned_high, turned_low)
    up_high = jnp.where(at_edge, turned_low, turned_high)
    return (
        c_self * low + c_y * up_low + c_z * pltpu.roll(low, shift_z, 1),
        c_self * high + c_y * up_high + c_z * pltpu.roll(high, shift_z, 1),
    )


def course(ints, s, depth):
    forward = ints[FORWARD, s] == 1
    return jnp.where(forward, 0, depth - 1), jnp.where(forward, 1, -1)


def slot_stencil(floats, ints, s, row):
    at_edge = row == ints[EDGE_Y, s]
    c_self, c_y, c_z = floats[SELF, s], floats[UPY, s], floats[UPZ, s]
    shift_y, shift_z = ints[SHIFT_Y, s], ints[SHIFT_Z, s]
    return lambda low, high: stencil(low, high, c_self, c_y, c_z, shift_y, shift_z, at_edge)


def rows_of(s):
    at = pl.multiple_of(s * 16, 16)
    return pl.ds(at, 8), pl.ds(at + 8, 8)


K_SELF, K_LARGE, K_SMALL, K_RATIO, K_THERM, K_QUART, K_HEAT, K_WALL = range(8)


def fill_kinds(table, bands):
    speeds, rates, storages, thresholds, generations = bands
    for kind in range(KINDS):
        band, cosine = kind // 2, COSINES[kind % 2]
        sine = np.sqrt(np.float32(1.0) - cosine * cosine)
        speed, rate, storage, threshold, generation = (
            jnp.full((8, 128), ref[band], jnp.float32) for ref in (speeds, rates, storages, thresholds, generations)
        )
        inverse = 1.0 / (speed * float(cosine + sine * np.float32(ACROSS)) + rate + PSEUDO_RATE)
        quart = 1.0 / (4.0 * (threshold * threshold * threshold))
        across = speed * float(sine) * inverse
        therm = rate * storage * inverse
        rows = (
            PSEUDO_RATE * inverse,
            across * math.cos(math.pi / 8),
            across * math.sin(math.pi / 8),
            speed * float(cosine) * inverse,
            therm,
            therm * quart,
            generation * inverse,
            storage * (1.0 + quart),
        )
        for row, value in enumerate(rows):
            table[row, kind] = value


def sweeps_kernel(sizes, meta, labels, *refs):
    block, blocks, depth, width_y, slots, modes, group = sizes
    bands, refs = refs[:5], refs[5:]
    energy, flag, given, label_row, swept, quarter, *rest = refs
    faces, rest = rest[:group], rest[group:]
    keep, send, *planes, density, flat, sources, heat, table = rest
    out_one, turn_one, turn_two, out_two, turn_late, out_three = planes
    rows, own = width_y // modes, slots // group
    step = pl.program_id(0)
    slab, mode = meta[SLAB], meta[MODE]
    slabs = keep.shape[2] // depth

    @pl.when(step == 0)
    def _():
        fill_kinds(table, bands)
        for yy in range(rows):
            quarter[:, yy * 128 : (yy + 1) * 128] = given[pl.ds(mode * rows + yy, depth, stride=width_y), :]
        density[...] = jnp.zeros_like(density)

        def one_layer(x, carry):
            at = pl.multiple_of(x * 16, 16)
            for low in (0, 8):
                t = given[pl.ds(at + low, 8), :]
                power = fourth(t)
                hot = flag[pl.ds(at + low, 8), :].astype(jnp.float32)
                heat[x, low : low + 8, :] = hot
                for kind in range(KINDS):
                    value = table[K_THERM, kind] * t + table[K_QUART, kind] * power + table[K_HEAT, kind] * hot
                    sources[kind, x, low : low + 8, :] = value
            return carry

        lax.fori_loop(0, depth, one_layer, 0)

    row = lax.broadcasted_iota(jnp.int32, (8, 128), 0)

    def one_slot(i, carry):
        s = step * block + i
        label = labels[s]
        polar, turn_of = label % 4, (label // 4) % 8
        forward = polar < 2
        kind = 2 * (label // DIRS) + jnp.where((polar == 0) | (polar == 3), 0, 1)
        right, up = (turn_of < 2) | (turn_of > 5), turn_of < 4
        wide = (turn_of % 4 == 0) | (turn_of % 4 == 3)
        start, stride = jnp.where(forward, 0, depth - 1), jnp.where(forward, 1, -1)
        side = jnp.where(forward, 0, 1)
        at_wall = jnp.where(forward, slab == 0, slab == slabs - 1)
        c_self, ratio, warm = table[K_SELF, kind], table[K_RATIO, kind], table[K_HEAT, kind]
        c_y = table[jnp.where(wide, K_LARGE, K_SMALL), kind]
        c_z = table[jnp.where(wide, K_SMALL, K_LARGE), kind]
        wall = jnp.where(at_wall, 1.0, 0.0) * table[K_WALL, kind]
        shift_y, shift_z = jnp.where(right, 1, 7), jnp.where(up, 1, 127)
        at_edge = row == jnp.where(right, 0, 7)
        apply = lambda low, high: stencil(low, high, c_self, c_y, c_z, shift_y, shift_z, at_edge)
        xs = [start + stride * j for j in range(depth)]
        layers = [(energy[i, x, :8, :], energy[i, x, 8:, :]) for x in xs]
        last = []
        for turn in range(ITERS):
            total_low = total_high = wall
            for j, x in enumerate(xs):
                low, high = apply(*layers[j])
                if turn == 0:
                    low, high = low + sources[kind, x, :8, :], high + sources[kind, x, 8:, :]
                else:
                    low, high = low + warm * heat[x, :8, :], high + warm * heat[x, 8:, :]
                total_low = ratio * total_low + low
                total_high = ratio * total_high + high
                layers[j] = (total_low, total_high)
                density[turn, side, j, :8, :] += total_low
                density[turn, side, j, 8:, :] += total_high
                if turn == ITERS - 1:
                    swept[i, x, :8, :] = total_low
                    swept[i, x, 8:, :] = total_high
            last.append((total_low, total_high))
        turned = apply(*last[0])
        at_low, at_high = rows_of(s)
        values = (last[0], turned, apply(*turned), last[1], apply(*last[1]), last[2])
        for plane, (low, high) in zip(planes, values):
            plane[at_low, :] = low
            plane[at_high, :] = high
        return carry

    lax.fori_loop(0, block, one_slot, 0, unroll=2)

    @pl.when(step == blocks - 1)
    def _():
        for by in range(group):
            at = pl.ds(pl.multiple_of(((slab % group) ^ by) * own * 16, 16), own * 16)
            for index, plane in enumerate((turn_two, turn_late, out_three)):
                faces[by][index] = plane[at, :]
        for turn in range(ITERS):
            for x in range(depth):
                flat[turn, x * 16 : x * 16 + 16, :] = density[turn, 0, x] + density[turn, 1, depth - 1 - x]
        label = label_row[...]
        polar = label % 4
        kinds = 2 * (label // DIRS) + jnp.where((polar == 0) | (polar == 3), 0, 1)
        decay = jnp.ones((1, slots), jnp.float32)
        for kind in range(KINDS):
            decay = jnp.where(kinds == kind, table[K_RATIO, kind][:1, :slots], decay)
        x = lax.broadcasted_iota(jnp.int32, (slabs * depth, slots), 0)
        past = jnp.where(polar < 2, x - (slab * depth + depth - 1), slab * depth - x)
        n = past.astype(jnp.float32)
        weight = jnp.where(past > 0, jnp.exp(jnp.maximum(n, 0.0) * jnp.log(decay)), 0.0)
        weights = (weight, n * weight, (0.5 * n * (n + 1.0)) * weight)
        home = pl.ds(pl.multiple_of(slab * depth, 8), depth)
        for by in range(modes):
            ys = [(mode ^ by) * rows + yy for yy in range(rows)]
            pick = lambda plane, count: jnp.concatenate([plane[pl.ds(y, count, stride=width_y), :] for y in ys], axis=1)
            plain = exact_dot(weights[0], jnp.concatenate([pick(p, slots) for p in (out_one, out_two, out_three)], axis=1))
            once = exact_dot(weights[1], jnp.concatenate([pick(p, slots) for p in (turn_one, turn_late)], axis=1))
            twice = exact_dot(weights[2], pick(turn_two, slots))
            lanes = rows * 128
            target = (send if by % 2 else keep).at[by // 2]
            target[0] = plain[:, :lanes]
            target[1] = plain[:, lanes : 2 * lanes] + once[:, :lanes]
            target[2] = plain[:, 2 * lanes :] + once[:, lanes:] + twice
            for turn in range(ITERS):
                target[turn, home, :] += pick(flat.at[turn], depth)


def split_kernel(mine, other, keep, send):
    for index in range(mine.shape[0]):
        target = send if index % 2 else keep
        target[index // 2] = mine[index] + other[index]


def parts_kernel(depth, mine, other, parts):
    for turn in range(ITERS):
        total = mine[0, turn] + other[0, turn]
        for slab in range(parts.shape[0]):
            parts[slab, turn] = total[slab * depth : (slab + 1) * depth]


def totals_kernel(sums, parts, before, copies, late):
    slabs = parts.shape[0]
    one, two, three = (
        add_up([parts[slab, turn] for slab in range(slabs)]) * (1.0 / DIRS) for turn in range(ITERS)
    )
    late[...] = three
    kelvin = newton(one, before[...], sums[0], sums[1])
    for slab in range(slabs):
        copies[slab, 0] = kelvin
        copies[slab, 1] = two


def kelvins_kernel(depth, meta, sums, gathered, late, matrix_one, matrix_two, packed):
    slabs = gathered.shape[0]
    cells = slabs * depth
    one, two = (jnp.concatenate([gathered[slab, index] for slab in range(slabs)], axis=0) for index in range(2))
    first = exact_dot(matrix_one[...], jnp.concatenate([one, fourth(one)], axis=0))
    two = newton(two + first[:cells], one, sums[0], sums[1])
    second = exact_dot(matrix_two[...], jnp.concatenate([two, fourth(two)], axis=0))
    sided = 2 * KINDS
    packed[: 2 * sided, :] = first[cells : cells + 2 * sided]
    packed[2 * sided : 3 * sided, :] = second[:sided]
    base = 3 * sided
    packed[base : base + depth, :] = gathered[meta[SLAB], 0]
    stay = first[cells + 2 * sided : cells + 2 * sided + depth]
    around = first[cells + 2 * sided + depth :]
    own = jnp.zeros_like(around)
    for slab in range(slabs):
        own = jnp.where(meta[SLAB] == slab, two[slab * depth : (slab + 1) * depth], own)
    packed[base + depth : base + 2 * depth, :] = own
    packed[base + 2 * depth : base + 3 * depth, :] = late[...] + stay + second[sided:]
    packed[base + 3 * depth :, :] = around


def compose_kernel(own, group, meta, floats, ints, *refs):
    received, (_, composite, effective, ordered) = refs[:group], refs[group:]
    place = meta[SLAB] % group
    for by in range(group):
        ordered[place ^ by] = received[by][...]

    def one_slot(i, carry):
        s = place * own + i
        start, stride = course(ints, s, group)
        full, full_n, full_t = floats[FULL, s], floats[FULL_N, s], floats[FULL_T, s]
        at = pl.ds(pl.multiple_of(i * 16, 16), 16)
        one = two = three = jnp.zeros((16, 128), jnp.float32)
        for j in range(group):
            k = start + stride * j
            three = full * three + full_n * two + full_t * one + ordered[k, 2, at, :]
            two = full * two + full_n * one + ordered[k, 1, at, :]
            one = full * one + ordered[k, 0, at, :]
        for index, value in enumerate((one, two, three)):
            composite[index, at, :] = value
        return carry

    lax.fori_loop(0, own, one_slot, 0, unroll=4)
    effective[...] = ordered[...]


def enter_kernel(own, group, groups, depth, meta, floats, ints, effective, *refs):
    composites, rest = refs[:groups], refs[groups:]
    outs, (ordered, entered) = rest[:group], rest[group:]
    slab = meta[SLAB]
    place, mine = slab % group, slab // group
    for by in range(groups):
        ordered[mine ^ by] = composites[by][...]
    span = depth * group

    def one_slot(i, carry):
        s = place * own + i
        start, stride = course(ints, s, group)
        begin, leap = course(ints, s, groups)
        ahead = jnp.where(ints[FORWARD, s] == 1, mine, groups - 1 - mine)
        at = pl.ds(pl.multiple_of(i * 16, 16), 16)

        def push(values, full, full_n, full_t, added):
            one, two, three = values
            return (
                full * one + added[0],
                full * two + full_n * one + added[1],
                full * three + full_n * two + full_t * one + added[2],
            )

        values = (jnp.zeros((16, 128), jnp.float32),) * 3
        whole = floats[FULL_GROUP, s]
        for g in range(groups - 1):
            index = begin + leap * g
            added = [ordered[index, plane, at, :] for plane in range(3)]
            later = push(values, whole, span * whole, (span * (span + 1) // 2) * whole, added)
            values = tuple(jnp.where(g < ahead, a, b) for a, b in zip(later, values))
        full, full_n, full_t = floats[FULL, s], floats[FULL_N, s], floats[FULL_T, s]
        for j in range(group):
            k = start + stride * j
            for plane in range(3):
                entered[k, plane, at, :] = values[plane]
            if j < group - 1:
                values = push(values, full, full_n, full_t, [effective[k, plane, at, :] for plane in range(3)])
        return carry

    lax.fori_loop(0, own, one_slot, 0, unroll=2)
    for by in range(group):
        outs[by][...] = entered[place ^ by]


def warm_kernel(sizes, order, meta, floats, ints, kinds, sums, swept, *refs):
    block, depth, width_y, width_z, modes = sizes
    packs, refs = refs[:modes], refs[modes:]
    energy, kelvin, enter_one, enter_long, enter_two, second, added, own_one, own_two, plain, around = refs
    step = pl.program_id(0)
    rows = width_y // modes

    @pl.when(step == 0)
    def _():
        sided, base = 2 * KINDS, 6 * KINDS
        for pack, by in zip(packs, order):
            for yy in range(rows):
                y, lane = (meta[MODE] ^ by) * rows + yy, slice(yy * 128, (yy + 1) * 128)
                for index, target in enumerate((enter_one, enter_long, enter_two)):
                    target[pl.ds(y, sided, stride=width_y), :] = pack[index * sided : (index + 1) * sided, lane]
                scattered = pl.ds(y, depth, stride=width_y)
                own_one[scattered, :] = pack[base : base + depth, lane]
                own_two[scattered, :] = pack[base + depth : base + 2 * depth, lane]
                plain[y] = pack[base + 2 * depth : base + 3 * depth, lane]
                around[y] = pack[base + 3 * depth :, lane]
        for y in range(width_y):
            here = around[y]
            near = around[(y - 1) % width_y] + around[(y + 1) % width_y]
            near = near + (pltpu.roll(here, 1, 1) + pltpu.roll(here, width_z - 1, 1))
            scattered = pl.ds(y, depth, stride=width_y)
            kelvin[scattered, :] = newton(plain[y] + near, own_two[scattered, :], sums[0], sums[1])

        def one_kind(kind, carry):
            therm, quart, decay = kinds[THERM, kind], kinds[QUART, kind], kinds[DECAY, kind]
            ones, twos = [], []
            for x in range(depth):
                here = slice(x * 16, x * 16 + 16)
                t, u = own_one[here, :], own_two[here, :]
                ones.append(therm * t + quart * fourth(t))
                twos.append(therm * u + quart * fourth(u))
            for back in (0, KINDS):
                at = pl.ds(pl.multiple_of((kind + back) * 16, 16), 16)
                once, twice, new = enter_one[at, :], enter_long[at, :], enter_two[at, :]
                for j in range(depth):
                    x = depth - 1 - j if back else j
                    once = decay * once + ones[x]
                    twice = decay * twice + once
                    new = decay * new + twos[x]
                    second[kind + back, x] = twice
                    added[kind + back, x] = new
            return carry

        lax.fori_loop(0, KINDS, one_kind, 0)

    row = lax.broadcasted_iota(jnp.int32, (8, 128), 0)

    def one_slot(i, carry):
        s = step * block + i
        sided = ints[KIND, s] + KINDS * (1 - ints[FORWARD, s])
        apply = slot_stencil(floats, ints, s, row)
        for x in range(depth):
            low, high = apply(second[sided, x, :8, :], second[sided, x, 8:, :])
            energy[i, x, :8, :] = swept[i, x, :8, :] + (low + added[sided, x, :8, :])
            energy[i, x, 8:, :] = swept[i, x, 8:, :] + (high + added[sided, x, 8:, :])
        return carry

    lax.fori_loop(0, block, one_slot, 0, unroll=2)


def inflow_kernel(sizes, meta, floats, ints, warm, *refs):
    block, depth, own, group = sizes
    received, (energy, ordered) = refs[:group], refs[group:]
    step = pl.program_id(0)

    @pl.when(step == 0)
    def _():
        for by in range(group):
            ordered[(meta[SLAB] % group) ^ by] = received[by][...]

    def one_slot(i, carry):
        s = step * block + i
        start, stride = course(ints, s, depth)
        ratio = floats[RATIO, s]
        at = pl.ds(pl.multiple_of((s % own) * 16, 16), 16)
        one, two, three = (ordered[s // own, plane, at, :] for plane in range(ITERS))
        for j in range(depth):
            x = start + stride * j
            one = ratio * one
            two = ratio * two + one
            three = ratio * three + two
            energy[i, x] = warm[i, x] + three
        return carry

    lax.fori_loop(0, block, one_slot, 0, unroll=4)


def local(incoming_occupation, crystal_kelvin_given, generating_region_flag, labels, speed, rate, storage, threshold, generation):
    slots, depth, width_y, width_z = incoming_occupation.shape
    slabs, modes = lax.axis_size("slab"), lax.axis_size("mode")
    group, groups = GROUP, slabs // GROUP
    own = slots // group
    lanes = width_y // modes * width_z
    block = 8
    blocks = slots // block
    cells, all_x = depth * width_y, slabs * depth
    face_rows = own * width_y
    slab = lax.axis_index("slab").astype(jnp.int32)
    meta = jnp.stack([slab, lax.axis_index("mode").astype(jnp.int32)])
    floats, ints = slot_tables(labels, speed, rate, storage, threshold, generation, slab, slabs, depth, width_z)
    kinds = kind_table(speed, rate, storage, threshold, generation)
    sums = jnp.stack([jnp.sum(storage), jnp.sum(storage / (4.0 * threshold**3))])

    def shape(*dims):
        return jax.ShapeDtypeStruct(dims, jnp.float32)

    def whole(*dims):
        return pl.BlockSpec(dims, lambda i: (0,) * len(dims))

    def scratch(*dims):
        return pltpu.VMEM(dims, jnp.float32)

    def swap(array, axis, by):
        return lax.ppermute(array, axis, [(i, i ^ by) for i in range(lax.axis_size(axis))])

    def call(kernel, name, in_specs, out_shapes, *args, scratches=()):
        return pl.pallas_call(
            kernel,
            in_specs=in_specs,
            out_specs=[VMEM] * len(out_shapes),
            out_shape=out_shapes,
            scratch_shapes=list(scratches),
            compiler_params=PARAMS,
            name=name,
        )(*args)

    slot_block = pl.BlockSpec((block, depth, width_y, width_z), lambda i: (i, 0, 0, 0))
    slot_shape = shape(slots, depth, width_y, width_z)
    face = (3, face_rows, width_z)
    half = (modes // 2, ITERS, all_x, lanes)
    swept, quarter, *rest = pl.pallas_call(
        functools.partial(sweeps_kernel, (block, blocks, depth, width_y, slots, modes, group)),
        grid=(blocks,),
        in_specs=[SMEM] * 7 + [slot_block, whole(cells, width_z), whole(cells, width_z), whole(1, slots)],
        out_specs=[slot_block, whole(depth, lanes)] + [whole(*face)] * group + [whole(*half)] * 2,
        out_shape=[slot_shape, shape(depth, lanes)] + [shape(*face)] * group + [shape(*half)] * 2,
        scratch_shapes=[scratch(slots * width_y, width_z)] * 6
        + [
            scratch(ITERS, 2, depth, width_y, width_z),
            scratch(ITERS, cells, width_z),
            scratch(KINDS, depth, width_y, width_z),
            scratch(depth, width_y, width_z),
            scratch(8, KINDS, 8, width_z),
        ],
        compiler_params=LARGE,
        name="sweeps",
    )(
        meta,
        labels,
        speed,
        rate,
        storage,
        threshold,
        generation,
        incoming_occupation,
        generating_region_flag.reshape(cells, width_z),
        crystal_kelvin_given.reshape(cells, width_z),
        labels.reshape(1, slots),
    )
    faces, (keep, send) = rest[:group], rest[group:]

    by = 1
    other = swap(send, "mode", by)
    received = [faces[0]] + [swap(faces[index], "slab", index) for index in range(1, group)]
    while 2 * by < modes:
        by *= 2
        now = (modes // (2 * by), ITERS, all_x, lanes)
        keep, send = call(split_kernel, "density_split", [VMEM] * 2, [shape(*now)] * 2, keep, other)
        other = swap(send, "mode", by)
    piece = (slabs, ITERS, depth, lanes)
    first_matrix, second_matrix = call(
        functools.partial(matrices_kernel, depth),
        "heat_matrices",
        [SMEM] * 2,
        [shape(all_x + 4 * KINDS + 2 * depth, 2 * all_x), shape(2 * KINDS + depth, 2 * all_x)],
        meta,
        kinds,
    )
    other, floats, ints, kinds, sums, first_matrix, second_matrix = lax.optimization_barrier(
        (other, floats, ints, kinds, sums, first_matrix, second_matrix)
    )
    (parts,) = call(functools.partial(parts_kernel, depth), "density_parts", [VMEM] * 2, [shape(*piece)], keep, other)
    summed = lax.all_to_all(parts, "slab", 0, 0)

    composite, effective = call(
        functools.partial(compose_kernel, own, group),
        "compose",
        [SMEM] * 3 + [VMEM] * group + [pl.BlockSpec(memory_space=pl.ANY)],
        [shape(*face), shape(group, *face)],
        meta,
        floats,
        ints,
        *received,
        parts,
        scratches=[scratch(group, *face)],
    )
    summed, composite = lax.optimization_barrier((summed, composite))
    composites = [composite] + [swap(composite, "slab", index * group) for index in range(1, groups)]
    copies, late = call(
        totals_kernel,
        "density_totals",
        [SMEM] + [VMEM] * 2,
        [shape(slabs, 2, depth, lanes), shape(depth, lanes)],
        sums,
        summed,
        quarter,
    )
    gathered = lax.all_to_all(copies, "slab", 0, 0)
    entering = call(
        functools.partial(enter_kernel, own, group, groups, depth),
        "enter",
        [SMEM] * 3 + [VMEM] * (1 + groups),
        [shape(*face)] * group,
        meta,
        floats,
        ints,
        effective,
        *composites,
        scratches=[scratch(groups, *face), scratch(group, *face)],
    )
    gathered, entering = lax.optimization_barrier((gathered, entering))
    entering = [entering[0]] + [swap(entering[index], "slab", index) for index in range(1, group)]

    pack_shape = shape(6 * KINDS + 4 * depth, lanes)
    (packed,) = call(
        functools.partial(kelvins_kernel, depth),
        "kelvins",
        [SMEM] * 2 + [VMEM] * 4,
        [pack_shape],
        meta,
        sums,
        gathered,
        late,
        first_matrix,
        second_matrix,
    )
    packs, order = [packed], [0]
    while by:
        packs = packs + [swap(pack, "mode", by) for pack in packs]
        order = order + [index ^ by for index in order]
        by //= 2

    warm, kelvin = pl.pallas_call(
        functools.partial(warm_kernel, (block, depth, width_y, width_z, modes), order),
        grid=(blocks,),
        in_specs=[SMEM] * 5 + [slot_block] + [whole(*pack_shape.shape)] * modes,
        out_specs=[slot_block, whole(cells, width_z)],
        out_shape=[slot_shape, shape(cells, width_z)],
        scratch_shapes=[scratch(2 * KINDS * width_y, width_z)] * 3
        + [scratch(2 * KINDS, depth, width_y, width_z)] * 2
        + [scratch(cells, width_z)] * 2
        + [scratch(width_y, depth, width_z)] * 2,
        compiler_params=PARAMS,
        name="warm",
    )(meta, floats, ints, kinds, sums, swept, *packs)
    energy = pl.pallas_call(
        functools.partial(inflow_kernel, (block, depth, own, group)),
        grid=(blocks,),
        in_specs=[SMEM] * 3 + [slot_block] + [whole(*face)] * group,
        out_specs=slot_block,
        out_shape=slot_shape,
        scratch_shapes=[scratch(group, *face)],
        compiler_params=PARAMS,
        name="inflow",
    )(meta, floats, ints, warm, *entering)
    return energy, kelvin.reshape(depth, width_y, width_z)


def solution(mesh):
    return jax.shard_map(
        local,
        mesh=mesh,
        in_specs=(
            P("mode", "slab", None, None),
            P("slab", None, None),
            P("slab", None, None),
            P("mode"),
            P(),
            P(),
            P(),
            P(),
            P(),
        ),
        out_specs=(P("mode", "slab", None, None), P("slab", None, None)),
        check_vma=False,
    )
```

```python
import functools
import math

import jax
import jax.numpy as jnp
import numpy as np
from jax import lax
from jax.experimental import pallas as pl
from jax.experimental.pallas import tpu as pltpu
from jax.sharding import PartitionSpec as P

FREQ_GROUPS = 8
DIRS = 32
ITERS = 3
NEWTON = 4
PSEUDO_RATE = 0.03
GROUP = 4
COSINES = (np.float32(0.99995), np.float32(0.9999))

SELF, UPY, UPZ, RATIO, WALL, FULL, FULL_N, FULL_T, FULL_GROUP, WARM = range(10)
FORWARD, SHIFT_Y, SHIFT_Z, EDGE_Y, KIND = range(5)
THERM, QUART, HEAT, DECAY, STAY, AROUND = range(6)
KINDS = 2 * FREQ_GROUPS
SLAB, MODE = range(2)

SMEM = pl.BlockSpec(memory_space=pltpu.SMEM)
VMEM = pl.BlockSpec(memory_space=pltpu.VMEM)
PARAMS = pltpu.CompilerParams(vmem_limit_bytes=48 * 1024 * 1024)
LARGE = pltpu.CompilerParams(vmem_limit_bytes=62 * 1024 * 1024)
ACROSS = math.cos(math.pi / 8) + math.sin(math.pi / 8)


def diagonal_of(speed, rate, cosine):
    sine = jnp.sqrt(1.0 - cosine * cosine)
    return speed * (cosine + sine * np.float32(ACROSS)) + rate + PSEUDO_RATE


def slot_tables(labels, speed, rate, storage, threshold, generation, slab, slabs, depth, width_z):
    band = labels // DIRS
    direction = labels % DIRS
    of_band = (band[None, :] == jnp.arange(FREQ_GROUPS, dtype=jnp.int32)[:, None]).astype(jnp.float32)
    speed, rate, storage, threshold, generation = (
        jnp.sum(of_band * value[:, None], axis=0) for value in (speed, rate, storage, threshold, generation)
    )
    polar = direction % 4
    outer = (polar == 0) | (polar == 3)
    forward = polar < 2
    cosine = jnp.where(outer, COSINES[0], COSINES[1])
    sine = jnp.sqrt(1.0 - cosine * cosine)
    azimuth = ((direction // 4).astype(jnp.float32) + 0.5) * (2.0 * math.pi / (DIRS // 4))
    vy = speed * sine * jnp.cos(azimuth)
    vz = speed * sine * jnp.sin(azimuth)
    diagonal = diagonal_of(speed, rate, cosine)
    ratio = speed * cosine / diagonal
    full = lax.integer_pow(ratio, depth)
    at_wall = jnp.where(forward, slab == 0, slab == slabs - 1)
    wall = storage * (1.0 + 1.0 / (4.0 * threshold**3))
    floats = jnp.stack(
        [
            PSEUDO_RATE / diagonal,
            jnp.abs(vy) / diagonal,
            jnp.abs(vz) / diagonal,
            ratio,
            jnp.where(at_wall, wall, 0.0),
            full,
            depth * full,
            (depth * (depth + 1) // 2) * full,
            lax.integer_pow(full, GROUP),
            generation / diagonal,
        ]
    )
    ints = jnp.stack(
        [
            forward.astype(jnp.int32),
            jnp.where(vy > 0, 1, 7).astype(jnp.int32),
            jnp.where(vz > 0, 1, width_z - 1).astype(jnp.int32),
            jnp.where(vy > 0, 0, 7).astype(jnp.int32),
            2 * band + jnp.where(outer, 0, 1),
        ]
    )
    return floats, ints


def kind_table(speed, rate, storage, threshold, generation):
    rows = []
    for cosine in COSINES:
        diagonal = diagonal_of(speed, rate, cosine)
        therm = rate * storage / diagonal
        quart = therm / (4.0 * threshold**3)
        across = jnp.sqrt(1.0 - cosine * cosine) * np.float32(2.0 * ACROSS)
        rows.append(
            jnp.stack(
                [
                    therm,
                    quart,
                    generation / diagonal,
                    speed * cosine / diagonal,
                    (DIRS // 4) * PSEUDO_RATE / diagonal,
                    across * speed / diagonal,
                ]
            )
        )
    return jnp.stack(rows, axis=2).reshape(6, KINDS)


def matrices_kernel(depth, meta, kinds, first, second):
    cells = first.shape[1] // 2
    slab = meta[SLAB]
    sided = 2 * KINDS
    per_cell = (DIRS // 4) / DIRS

    def places(rows):
        column = lax.broadcasted_iota(jnp.int32, (rows, 2 * cells), 1)
        quart = column >= cells
        return jnp.where(quart, column - cells, column), quart

    def distance(rows, base):
        there, quart = places(rows)
        far = jnp.abs(lax.broadcasted_iota(jnp.int32, (rows, 2 * cells), 0) + base - there)
        return far.astype(jnp.float32), jnp.where(far == 0, 2.0, 1.0), quart

    full, twice_full, quart_full = distance(cells, 0)
    home, twice_home, quart_home = distance(depth, slab * depth)
    there, quart_row = places(1)
    gaps = [value.astype(jnp.float32) for value in (slab * depth - 1 - there, there - (slab + 1) * depth)]
    everywhere = jnp.zeros((cells, 2 * cells), jnp.float32)
    once = stay = around = jnp.zeros((depth, 2 * cells), jnp.float32)
    for kind in range(KINDS):
        therm, quart = kinds[THERM, kind], kinds[QUART, kind]
        slope = jnp.log(jnp.full((1, 2 * cells), kinds[DECAY, kind], jnp.float32))
        everywhere += jnp.where(quart_full, quart, therm) * (jnp.exp(full * slope) * twice_full)
        weight = jnp.where(quart_home, quart, therm) * (jnp.exp(home * slope) * twice_home)
        once += weight
        weight = weight * (home + 1.0)
        stay += kinds[STAY, kind] * weight
        around += kinds[AROUND, kind] * weight
        for side, gap in enumerate(gaps):
            weight = jnp.where(quart_row, quart, therm) * jnp.exp(jnp.maximum(gap, 0.0) * slope)
            weight = jnp.where(gap >= 0, weight, 0.0)
            at = kind + side * KINDS
            first[cells + at : cells + at + 1, :] = weight
            first[cells + sided + at : cells + sided + at + 1, :] = weight * (gap + 1.0)
            second[at : at + 1, :] = weight
    first[:cells, :] = everywhere * per_cell
    base = cells + 2 * sided
    first[base : base + depth, :] = stay * (1.0 / DIRS)
    first[base + depth :, :] = around * (1.0 / DIRS)
    second[sided:, :] = once * per_cell


def newton(density, kelvin, linear, quart):
    for _ in range(NEWTON):
        cube = kelvin * kelvin * kelvin
        residual = linear * kelvin + quart * (kelvin * cube) - density
        kelvin = kelvin - residual / (linear + 4.0 * quart * cube)
    return kelvin


def exact_dot(left, right):
    return jnp.dot(left, right, precision=lax.Precision.HIGHEST, preferred_element_type=jnp.float32)


def fourth(value):
    square = value * value
    return square * square


def add_up(values):
    while len(values) > 1:
        values = [a + b for a, b in zip(values[::2], values[1::2])]
    return values[0]


def stencil(low, high, c_self, c_y, c_z, shift_y, shift_z, at_edge):
    turned_low, turned_high = pltpu.roll(low, shift_y, 0), pltpu.roll(high, shift_y, 0)
    up_low = jnp.where(at_edge, turned_high, turned_low)
    up_high = jnp.where(at_edge, turned_low, turned_high)
    return (
        c_self * low + c_y * up_low + c_z * pltpu.roll(low, shift_z, 1),
        c_self * high + c_y * up_high + c_z * pltpu.roll(high, shift_z, 1),
    )


def course(ints, s, depth):
    forward = ints[FORWARD, s] == 1
    return jnp.where(forward, 0, depth - 1), jnp.where(forward, 1, -1)


def slot_stencil(floats, ints, s, row):
    at_edge = row == ints[EDGE_Y, s]
    c_self, c_y, c_z = floats[SELF, s], floats[UPY, s], floats[UPZ, s]
    shift_y, shift_z = ints[SHIFT_Y, s], ints[SHIFT_Z, s]
    return lambda low, high: stencil(low, high, c_self, c_y, c_z, shift_y, shift_z, at_edge)


def rows_of(s):
    at = pl.multiple_of(s * 16, 16)
    return pl.ds(at, 8), pl.ds(at + 8, 8)


K_SELF, K_LARGE, K_SMALL, K_RATIO, K_THERM, K_QUART, K_HEAT, K_WALL = range(8)


def fill_kinds(table, bands):
    speeds, rates, storages, thresholds, generations = bands
    for kind in range(KINDS):
        band, cosine = kind // 2, COSINES[kind % 2]
        sine = np.sqrt(np.float32(1.0) - cosine * cosine)
        speed, rate, storage, threshold, generation = (
            jnp.full((8, 128), ref[band], jnp.float32) for ref in (speeds, rates, storages, thresholds, generations)
        )
        inverse = 1.0 / (speed * float(cosine + sine * np.float32(ACROSS)) + rate + PSEUDO_RATE)
        quart = 1.0 / (4.0 * (threshold * threshold * threshold))
        across = speed * float(sine) * inverse
        therm = rate * storage * inverse
        rows = (
            PSEUDO_RATE * inverse,
            across * math.cos(math.pi / 8),
            across * math.sin(math.pi / 8),
            speed * float(cosine) * inverse,
            therm,
            therm * quart,
            generation * inverse,
            storage * (1.0 + quart),
        )
        for row, value in enumerate(rows):
            table[row, kind] = value


def sweeps_kernel(sizes, meta, labels, *refs):
    block, blocks, depth, width_y, slots, modes, group = sizes
    bands, refs = refs[:5], refs[5:]
    energy, flag, given, label_row, swept, quarter, *rest = refs
    faces, rest = rest[:group], rest[group:]
    keep, send, *planes, density, flat, sources, heat, table = rest
    out_one, turn_one, turn_two, out_two, turn_late, out_three = planes
    rows, own = width_y // modes, slots // group
    step = pl.program_id(0)
    slab, mode = meta[SLAB], meta[MODE]
    slabs = keep.shape[2] // depth

    @pl.when(step == 0)
    def _():
        fill_kinds(table, bands)
        for yy in range(rows):
            quarter[:, yy * 128 : (yy + 1) * 128] = given[pl.ds(mode * rows + yy, depth, stride=width_y), :]
        density[...] = jnp.zeros_like(density)

        def one_layer(x, carry):
            at = pl.multiple_of(x * 16, 16)
            for low in (0, 8):
                t = given[pl.ds(at + low, 8), :]
                power = fourth(t)
                hot = flag[pl.ds(at + low, 8), :].astype(jnp.float32)
                heat[x, low : low + 8, :] = hot
                for kind in range(KINDS):
                    value = table[K_THERM, kind] * t + table[K_QUART, kind] * power + table[K_HEAT, kind] * hot
                    sources[kind, x, low : low + 8, :] = value
            return carry

        lax.fori_loop(0, depth, one_layer, 0)

    row = lax.broadcasted_iota(jnp.int32, (8, 128), 0)

    def one_slot(i, carry):
        s = step * block + i
        label = labels[s]
        polar, turn_of = label % 4, (label // 4) % 8
        forward = polar < 2
        kind = 2 * (label // DIRS) + jnp.where((polar == 0) | (polar == 3), 0, 1)
        right, up = (turn_of < 2) | (turn_of > 5), turn_of < 4
        wide = (turn_of % 4 == 0) | (turn_of % 4 == 3)
        start, stride = jnp.where(forward, 0, depth - 1), jnp.where(forward, 1, -1)
        side = jnp.where(forward, 0, 1)
        at_wall = jnp.where(forward, slab == 0, slab == slabs - 1)
        c_self, ratio, warm = table[K_SELF, kind], table[K_RATIO, kind], table[K_HEAT, kind]
        c_y = table[jnp.where(wide, K_LARGE, K_SMALL), kind]
        c_z = table[jnp.where(wide, K_SMALL, K_LARGE), kind]
        wall = jnp.where(at_wall, 1.0, 0.0) * table[K_WALL, kind]
        shift_y, shift_z = jnp.where(right, 1, 7), jnp.where(up, 1, 127)
        at_edge = row == jnp.where(right, 0, 7)
        apply = lambda low, high: stencil(low, high, c_self, c_y, c_z, shift_y, shift_z, at_edge)
        xs = [start + stride * j for j in range(depth)]
        layers = [(energy[i, x, :8, :], energy[i, x, 8:, :]) for x in xs]
        last = []
        for turn in range(ITERS):
            total_low = total_high = wall
            for j, x in enumerate(xs):
                low, high = apply(*layers[j])
                if turn == 0:
                    low, high = low + sources[kind, x, :8, :], high + sources[kind, x, 8:, :]
                else:
                    low, high = low + warm * heat[x, :8, :], high + warm * heat[x, 8:, :]
                total_low = ratio * total_low + low
                total_high = ratio * total_high + high
                layers[j] = (total_low, total_high)
                density[turn, side, j, :8, :] += total_low
                density[turn, side, j, 8:, :] += total_high
                if turn == ITERS - 1:
                    swept[i, x, :8, :] = total_low
                    swept[i, x, 8:, :] = total_high
            last.append((total_low, total_high))
        turned = apply(*last[0])
        at_low, at_high = rows_of(s)
        values = (last[0], turned, apply(*turned), last[1], apply(*last[1]), last[2])
        for plane, (low, high) in zip(planes, values):
            plane[at_low, :] = low
            plane[at_high, :] = high
        return carry

    lax.fori_loop(0, block, one_slot, 0, unroll=2)

    @pl.when(step == blocks - 1)
    def _():
        for by in range(group):
            at = pl.ds(pl.multiple_of(((slab % group) ^ by) * own * 16, 16), own * 16)
            for index, plane in enumerate((turn_two, turn_late, out_three)):
                faces[by][index] = plane[at, :]
        for turn in range(ITERS):
            for x in range(depth):
                flat[turn, x * 16 : x * 16 + 16, :] = density[turn, 0, x] + density[turn, 1, depth - 1 - x]
        label = label_row[...]
        polar = label % 4
        kinds = 2 * (label // DIRS) + jnp.where((polar == 0) | (polar == 3), 0, 1)
        decay = jnp.ones((1, slots), jnp.float32)
        for kind in range(KINDS):
            decay = jnp.where(kinds == kind, table[K_RATIO, kind][:1, :slots], decay)
        x = lax.broadcasted_iota(jnp.int32, (slabs * depth, slots), 0)
        past = jnp.where(polar < 2, x - (slab * depth + depth - 1), slab * depth - x)
        n = past.astype(jnp.float32)
        weight = jnp.where(past > 0, jnp.exp(jnp.maximum(n, 0.0) * jnp.log(decay)), 0.0)
        weights = (weight, n * weight, (0.5 * n * (n + 1.0)) * weight)
        home = pl.ds(pl.multiple_of(slab * depth, 8), depth)
        for by in range(modes):
            ys = [(mode ^ by) * rows + yy for yy in range(rows)]
            pick = lambda plane, count: jnp.concatenate([plane[pl.ds(y, count, stride=width_y), :] for y in ys], axis=1)
            plain = exact_dot(weights[0], jnp.concatenate([pick(p, slots) for p in (out_one, out_two, out_three)], axis=1))
            once = exact_dot(weights[1], jnp.concatenate([pick(p, slots) for p in (turn_one, turn_late)], axis=1))
            twice = exact_dot(weights[2], pick(turn_two, slots))
            lanes = rows * 128
            target = (send if by % 2 else keep).at[by // 2]
            target[0] = plain[:, :lanes]
            target[1] = plain[:, lanes : 2 * lanes] + once[:, :lanes]
            target[2] = plain[:, 2 * lanes :] + once[:, lanes:] + twice
            for turn in range(ITERS):
                target[turn, home, :] += pick(flat.at[turn], depth)


def split_kernel(mine, other, keep, send):
    for index in range(mine.shape[0]):
        target = send if index % 2 else keep
        target[index // 2] = mine[index] + other[index]


def parts_kernel(depth, mine, other, parts):
    for turn in range(ITERS):
        total = mine[0, turn] + other[0, turn]
        for slab in range(parts.shape[0]):
            parts[slab, turn] = total[slab * depth : (slab + 1) * depth]


def totals_kernel(sums, parts, before, copies, late):
    slabs = parts.shape[0]
    one, two, three = (
        add_up([parts[slab, turn] for slab in range(slabs)]) * (1.0 / DIRS) for turn in range(ITERS)
    )
    late[...] = three
    kelvin = newton(one, before[...], sums[0], sums[1])
    for slab in range(slabs):
        copies[slab, 0] = kelvin
        copies[slab, 1] = two


def kelvins_kernel(depth, meta, sums, gathered, late, matrix_one, matrix_two, packed):
    slabs = gathered.shape[0]
    cells = slabs * depth
    one, two = (jnp.concatenate([gathered[slab, index] for slab in range(slabs)], axis=0) for index in range(2))
    first = exact_dot(matrix_one[...], jnp.concatenate([one, fourth(one)], axis=0))
    two = newton(two + first[:cells], one, sums[0], sums[1])
    second = exact_dot(matrix_two[...], jnp.concatenate([two, fourth(two)], axis=0))
    sided = 2 * KINDS
    packed[: 2 * sided, :] = first[cells : cells + 2 * sided]
    packed[2 * sided : 3 * sided, :] = second[:sided]
    base = 3 * sided
    packed[base : base + depth, :] = gathered[meta[SLAB], 0]
    stay = first[cells + 2 * sided : cells + 2 * sided + depth]
    around = first[cells + 2 * sided + depth :]
    own = jnp.zeros_like(around)
    for slab in range(slabs):
        own = jnp.where(meta[SLAB] == slab, two[slab * depth : (slab + 1) * depth], own)
    packed[base + depth : base + 2 * depth, :] = own
    packed[base + 2 * depth : base + 3 * depth, :] = late[...] + stay + second[sided:]
    packed[base + 3 * depth :, :] = around


def compose_kernel(own, group, meta, floats, ints, *refs):
    received, (_, composite, effective, ordered) = refs[:group], refs[group:]
    place = meta[SLAB] % group
    for by in range(group):
        ordered[place ^ by] = received[by][...]

    def one_slot(i, carry):
        s = place * own + i
        start, stride = course(ints, s, group)
        full, full_n, full_t = floats[FULL, s], floats[FULL_N, s], floats[FULL_T, s]
        at = pl.ds(pl.multiple_of(i * 16, 16), 16)
        one = two = three = jnp.zeros((16, 128), jnp.float32)
        for j in range(group):
            k = start + stride * j
            three = full * three + full_n * two + full_t * one + ordered[k, 2, at, :]
            two = full * two + full_n * one + ordered[k, 1, at, :]
            one = full * one + ordered[k, 0, at, :]
        for index, value in enumerate((one, two, three)):
            composite[index, at, :] = value
        return carry

    lax.fori_loop(0, own, one_slot, 0, unroll=4)
    effective[...] = ordered[...]


def enter_kernel(own, group, groups, depth, meta, floats, ints, effective, *refs):
    composites, rest = refs[:groups], refs[groups:]
    outs, (ordered, entered) = rest[:group], rest[group:]
    slab = meta[SLAB]
    place, mine = slab % group, slab // group
    for by in range(groups):
        ordered[mine ^ by] = composites[by][...]
    span = depth * group

    def one_slot(i, carry):
        s = place * own + i
        start, stride = course(ints, s, group)
        begin, leap = course(ints, s, groups)
        ahead = jnp.where(ints[FORWARD, s] == 1, mine, groups - 1 - mine)
        at = pl.ds(pl.multiple_of(i * 16, 16), 16)

        def push(values, full, full_n, full_t, added):
            one, two, three = values
            return (
                full * one + added[0],
                full * two + full_n * one + added[1],
                full * three + full_n * two + full_t * one + added[2],
            )

        values = (jnp.zeros((16, 128), jnp.float32),) * 3
        whole = floats[FULL_GROUP, s]
        for g in range(groups - 1):
            index = begin + leap * g
            added = [ordered[index, plane, at, :] for plane in range(3)]
            later = push(values, whole, span * whole, (span * (span + 1) // 2) * whole, added)
            values = tuple(jnp.where(g < ahead, a, b) for a, b in zip(later, values))
        full, full_n, full_t = floats[FULL, s], floats[FULL_N, s], floats[FULL_T, s]
        for j in range(group):
            k = start + stride * j
            for plane in range(3):
                entered[k, plane, at, :] = values[plane]
            if j < group - 1:
                values = push(values, full, full_n, full_t, [effective[k, plane, at, :] for plane in range(3)])
        return carry

    lax.fori_loop(0, own, one_slot, 0, unroll=2)
    for by in range(group):
        outs[by][...] = entered[place ^ by]


def warm_kernel(sizes, order, meta, floats, ints, kinds, sums, swept, *refs):
    block, depth, width_y, width_z, modes = sizes
    packs, refs = refs[:modes], refs[modes:]
    energy, kelvin, enter_one, enter_long, enter_two, second, added, own_one, own_two, plain, around = refs
    step = pl.program_id(0)
    rows = width_y // modes

    @pl.when(step == 0)
    def _():
        sided, base = 2 * KINDS, 6 * KINDS
        for pack, by in zip(packs, order):
            for yy in range(rows):
                y, lane = (meta[MODE] ^ by) * rows + yy, slice(yy * 128, (yy + 1) * 128)
                for index, target in enumerate((enter_one, enter_long, enter_two)):
                    target[pl.ds(y, sided, stride=width_y), :] = pack[index * sided : (index + 1) * sided, lane]
                scattered = pl.ds(y, depth, stride=width_y)
                own_one[scattered, :] = pack[base : base + depth, lane]
                own_two[scattered, :] = pack[base + depth : base + 2 * depth, lane]
                plain[y] = pack[base + 2 * depth : base + 3 * depth, lane]
                around[y] = pack[base + 3 * depth :, lane]
        for y in range(width_y):
            here = around[y]
            near = around[(y - 1) % width_y] + around[(y + 1) % width_y]
            near = near + (pltpu.roll(here, 1, 1) + pltpu.roll(here, width_z - 1, 1))
            scattered = pl.ds(y, depth, stride=width_y)
            kelvin[scattered, :] = newton(plain[y] + near, own_two[scattered, :], sums[0], sums[1])

        def one_kind(kind, carry):
            therm, quart, decay = kinds[THERM, kind], kinds[QUART, kind], kinds[DECAY, kind]
            ones, twos = [], []
            for x in range(depth):
                here = slice(x * 16, x * 16 + 16)
                t, u = own_one[here, :], own_two[here, :]
                ones.append(therm * t + quart * fourth(t))
                twos.append(therm * u + quart * fourth(u))
            for back in (0, KINDS):
                at = pl.ds(pl.multiple_of((kind + back) * 16, 16), 16)
                once, twice, new = enter_one[at, :], enter_long[at, :], enter_two[at, :]
                for j in range(depth):
                    x = depth - 1 - j if back else j
                    once = decay * once + ones[x]
                    twice = decay * twice + once
                    new = decay * new + twos[x]
                    second[kind + back, x] = twice
                    added[kind + back, x] = new
            return carry

        lax.fori_loop(0, KINDS, one_kind, 0)

    row = lax.broadcasted_iota(jnp.int32, (8, 128), 0)

    def one_slot(i, carry):
        s = step * block + i
        sided = ints[KIND, s] + KINDS * (1 - ints[FORWARD, s])
        apply = slot_stencil(floats, ints, s, row)
        for x in range(depth):
            low, high = apply(second[sided, x, :8, :], second[sided, x, 8:, :])
            energy[i, x, :8, :] = swept[i, x, :8, :] + (low + added[sided, x, :8, :])
            energy[i, x, 8:, :] = swept[i, x, 8:, :] + (high + added[sided, x, 8:, :])
        return carry

    lax.fori_loop(0, block, one_slot, 0, unroll=2)


def inflow_kernel(sizes, meta, floats, ints, warm, *refs):
    block, depth, own, group = sizes
    received, (energy, ordered) = refs[:group], refs[group:]
    step = pl.program_id(0)

    @pl.when(step == 0)
    def _():
        for by in range(group):
            ordered[(meta[SLAB] % group) ^ by] = received[by][...]

    def one_slot(i, carry):
        s = step * block + i
        start, stride = course(ints, s, depth)
        ratio = floats[RATIO, s]
        at = pl.ds(pl.multiple_of((s % own) * 16, 16), 16)
        one, two, three = (ordered[s // own, plane, at, :] for plane in range(ITERS))
        for j in range(depth):
            x = start + stride * j
            one = ratio * one
            two = ratio * two + one
            three = ratio * three + two
            energy[i, x] = warm[i, x] + three
        return carry

    lax.fori_loop(0, block, one_slot, 0, unroll=4)


def local(incoming_occupation, crystal_kelvin_given, generating_region_flag, labels, speed, rate, storage, threshold, generation):
    slots, depth, width_y, width_z = incoming_occupation.shape
    slabs, modes = lax.axis_size("slab"), lax.axis_size("mode")
    group, groups = GROUP, slabs // GROUP
    own = slots // group
    lanes = width_y // modes * width_z
    block = 8
    blocks = slots // block
    cells, all_x = depth * width_y, slabs * depth
    face_rows = own * width_y
    slab = lax.axis_index("slab").astype(jnp.int32)
    meta = jnp.stack([slab, lax.axis_index("mode").astype(jnp.int32)])
    floats, ints = slot_tables(labels, speed, rate, storage, threshold, generation, slab, slabs, depth, width_z)
    kinds = kind_table(speed, rate, storage, threshold, generation)
    sums = jnp.stack([jnp.sum(storage), jnp.sum(storage / (4.0 * threshold**3))])

    def shape(*dims):
        return jax.ShapeDtypeStruct(dims, jnp.float32)

    def whole(*dims):
        return pl.BlockSpec(dims, lambda i: (0,) * len(dims))

    def scratch(*dims):
        return pltpu.VMEM(dims, jnp.float32)

    def swap(array, axis, by):
        return lax.ppermute(array, axis, [(i, i ^ by) for i in range(lax.axis_size(axis))])

    def call(kernel, name, in_specs, out_shapes, *args, scratches=()):
        return pl.pallas_call(
            kernel,
            in_specs=in_specs,
            out_specs=[VMEM] * len(out_shapes),
            out_shape=out_shapes,
            scratch_shapes=list(scratches),
            compiler_params=PARAMS,
            name=name,
        )(*args)

    slot_block = pl.BlockSpec((block, depth, width_y, width_z), lambda i: (i, 0, 0, 0))
    slot_shape = shape(slots, depth, width_y, width_z)
    face = (3, face_rows, width_z)
    half = (modes // 2, ITERS, all_x, lanes)
    swept, quarter, *rest = pl.pallas_call(
        functools.partial(sweeps_kernel, (block, blocks, depth, width_y, slots, modes, group)),
        grid=(blocks,),
        in_specs=[SMEM] * 7 + [slot_block, whole(cells, width_z), whole(cells, width_z), whole(1, slots)],
        out_specs=[slot_block, whole(depth, lanes)] + [whole(*face)] * group + [whole(*half)] * 2,
        out_shape=[slot_shape, shape(depth, lanes)] + [shape(*face)] * group + [shape(*half)] * 2,
        scratch_shapes=[scratch(slots * width_y, width_z)] * 6
        + [
            scratch(ITERS, 2, depth, width_y, width_z),
            scratch(ITERS, cells, width_z),
            scratch(KINDS, depth, width_y, width_z),
            scratch(depth, width_y, width_z),
            scratch(8, KINDS, 8, width_z),
        ],
        compiler_params=LARGE,
        name="sweeps",
    )(
        meta,
        labels,
        speed,
        rate,
        storage,
        threshold,
        generation,
        incoming_occupation,
        generating_region_flag.reshape(cells, width_z),
        crystal_kelvin_given.reshape(cells, width_z),
        labels.reshape(1, slots),
    )
    faces, (keep, send) = rest[:group], rest[group:]

    by = 1
    other = swap(send, "mode", by)
    received = [faces[0]] + [swap(faces[index], "slab", index) for index in range(1, group)]
    while 2 * by < modes:
        by *= 2
        now = (modes // (2 * by), ITERS, all_x, lanes)
        keep, send = call(split_kernel, "density_split", [VMEM] * 2, [shape(*now)] * 2, keep, other)
        other = swap(send, "mode", by)
    piece = (slabs, ITERS, depth, lanes)
    first_matrix, second_matrix = call(
        functools.partial(matrices_kernel, depth),
        "heat_matrices",
        [SMEM] * 2,
        [shape(all_x + 4 * KINDS + 2 * depth, 2 * all_x), shape(2 * KINDS + depth, 2 * all_x)],
        meta,
        kinds,
    )
    other, received[1:3], floats, ints, kinds, sums, first_matrix, second_matrix = lax.optimization_barrier(
        (other, received[1:3], floats, ints, kinds, sums, first_matrix, second_matrix)
    )
    (parts,) = call(functools.partial(parts_kernel, depth), "density_parts", [VMEM] * 2, [shape(*piece)], keep, other)
    summed = lax.all_to_all(parts, "slab", 0, 0)

    composite, effective = call(
        functools.partial(compose_kernel, own, group),
        "compose",
        [SMEM] * 3 + [VMEM] * group + [pl.BlockSpec(memory_space=pl.ANY)],
        [shape(*face), shape(group, *face)],
        meta,
        floats,
        ints,
        *received,
        parts,
        scratches=[scratch(group, *face)],
    )
    summed, composite = lax.optimization_barrier((summed, composite))
    composites = [composite] + [swap(composite, "slab", index * group) for index in range(1, groups)]
    copies, late = call(
        totals_kernel,
        "density_totals",
        [SMEM] + [VMEM] * 2,
        [shape(slabs, 2, depth, lanes), shape(depth, lanes)],
        sums,
        summed,
        quarter,
    )
    gathered = lax.all_to_all(copies, "slab", 0, 0)
    entering = call(
        functools.partial(enter_kernel, own, group, groups, depth),
        "enter",
        [SMEM] * 3 + [VMEM] * (1 + groups),
        [shape(*face)] * group,
        meta,
        floats,
        ints,
        effective,
        *composites,
        scratches=[scratch(groups, *face), scratch(group, *face)],
    )
    gathered, entering = lax.optimization_barrier((gathered, entering))
    entering = [entering[0]] + [swap(entering[index], "slab", index) for index in range(1, group)]

    pack_shape = shape(6 * KINDS + 4 * depth, lanes)
    (packed,) = call(
        functools.partial(kelvins_kernel, depth),
        "kelvins",
        [SMEM] * 2 + [VMEM] * 4,
        [pack_shape],
        meta,
        sums,
        gathered,
        late,
        first_matrix,
        second_matrix,
    )
    packs, order = [packed], [0]
    while by:
        packs = packs + [swap(pack, "mode", by) for pack in packs]
        order = order + [index ^ by for index in order]
        by //= 2

    warm, kelvin = pl.pallas_call(
        functools.partial(warm_kernel, (block, depth, width_y, width_z, modes), order),
        grid=(blocks,),
        in_specs=[SMEM] * 5 + [slot_block] + [whole(*pack_shape.shape)] * modes,
        out_specs=[slot_block, whole(cells, width_z)],
        out_shape=[slot_shape, shape(cells, width_z)],
        scratch_shapes=[scratch(2 * KINDS * width_y, width_z)] * 3
        + [scratch(2 * KINDS, depth, width_y, width_z)] * 2
        + [scratch(cells, width_z)] * 2
        + [scratch(width_y, depth, width_z)] * 2,
        compiler_params=PARAMS,
        name="warm",
    )(meta, floats, ints, kinds, sums, swept, *packs)
    energy = pl.pallas_call(
        functools.partial(inflow_kernel, (block, depth, own, group)),
        grid=(blocks,),
        in_specs=[SMEM] * 3 + [slot_block] + [whole(*face)] * group,
        out_specs=slot_block,
        out_shape=slot_shape,
        scratch_shapes=[scratch(group, *face)],
        compiler_params=PARAMS,
        name="inflow",
    )(meta, floats, ints, warm, *entering)
    return energy, kelvin.reshape(depth, width_y, width_z)


def solution(mesh):
    return jax.shard_map(
        local,
        mesh=mesh,
        in_specs=(
            P("mode", "slab", None, None),
            P("slab", None, None),
            P("slab", None, None),
            P("mode"),
            P(),
            P(),
            P(),
            P(),
            P(),
        ),
        out_specs=(P("mode", "slab", None, None), P("slab", None, None)),
        check_vma=False,
    )
```

```python
import functools
import math

import jax
import jax.numpy as jnp
import numpy as np
from jax import lax
from jax.experimental import pallas as pl
from jax.experimental.pallas import tpu as pltpu
from jax.sharding import PartitionSpec as P

FREQ_GROUPS = 8
DIRS = 32
ITERS = 3
NEWTON = 4
PSEUDO_RATE = 0.03
GROUP = 4
COSINES = (np.float32(0.99995), np.float32(0.9999))

SELF, UPY, UPZ, RATIO, WALL, FULL, FULL_N, FULL_T, FULL_GROUP, WARM = range(10)
FORWARD, SHIFT_Y, SHIFT_Z, EDGE_Y, KIND = range(5)
THERM, QUART, HEAT, DECAY, STAY, AROUND = range(6)
KINDS = 2 * FREQ_GROUPS
SLAB, MODE = range(2)

SMEM = pl.BlockSpec(memory_space=pltpu.SMEM)
VMEM = pl.BlockSpec(memory_space=pltpu.VMEM)
PARAMS = pltpu.CompilerParams(vmem_limit_bytes=48 * 1024 * 1024)
LARGE = pltpu.CompilerParams(vmem_limit_bytes=62 * 1024 * 1024)
ACROSS = math.cos(math.pi / 8) + math.sin(math.pi / 8)


def diagonal_of(speed, rate, cosine):
    sine = jnp.sqrt(1.0 - cosine * cosine)
    return speed * (cosine + sine * np.float32(ACROSS)) + rate + PSEUDO_RATE


def slot_tables(labels, speed, rate, storage, threshold, generation, slab, slabs, depth, width_z):
    band = labels // DIRS
    direction = labels % DIRS
    of_band = (band[None, :] == jnp.arange(FREQ_GROUPS, dtype=jnp.int32)[:, None]).astype(jnp.float32)
    speed, rate, storage, threshold, generation = (
        jnp.sum(of_band * value[:, None], axis=0) for value in (speed, rate, storage, threshold, generation)
    )
    polar = direction % 4
    outer = (polar == 0) | (polar == 3)
    forward = polar < 2
    cosine = jnp.where(outer, COSINES[0], COSINES[1])
    sine = jnp.sqrt(1.0 - cosine * cosine)
    azimuth = ((direction // 4).astype(jnp.float32) + 0.5) * (2.0 * math.pi / (DIRS // 4))
    vy = speed * sine * jnp.cos(azimuth)
    vz = speed * sine * jnp.sin(azimuth)
    diagonal = diagonal_of(speed, rate, cosine)
    ratio = speed * cosine / diagonal
    full = lax.integer_pow(ratio, depth)
    at_wall = jnp.where(forward, slab == 0, slab == slabs - 1)
    wall = storage * (1.0 + 1.0 / (4.0 * threshold**3))
    floats = jnp.stack(
        [
            PSEUDO_RATE / diagonal,
            jnp.abs(vy) / diagonal,
            jnp.abs(vz) / diagonal,
            ratio,
            jnp.where(at_wall, wall, 0.0),
            full,
            depth * full,
            (depth * (depth + 1) // 2) * full,
            lax.integer_pow(full, GROUP),
            generation / diagonal,
        ]
    )
    ints = jnp.stack(
        [
            forward.astype(jnp.int32),
            jnp.where(vy > 0, 1, 7).astype(jnp.int32),
            jnp.where(vz > 0, 1, width_z - 1).astype(jnp.int32),
            jnp.where(vy > 0, 0, 7).astype(jnp.int32),
            2 * band + jnp.where(outer, 0, 1),
        ]
    )
    return floats, ints


def kind_table(speed, rate, storage, threshold, generation):
    rows = []
    for cosine in COSINES:
        diagonal = diagonal_of(speed, rate, cosine)
        therm = rate * storage / diagonal
        quart = therm / (4.0 * threshold**3)
        across = jnp.sqrt(1.0 - cosine * cosine) * np.float32(2.0 * ACROSS)
        rows.append(
            jnp.stack(
                [
                    therm,
                    quart,
                    generation / diagonal,
                    speed * cosine / diagonal,
                    (DIRS // 4) * PSEUDO_RATE / diagonal,
                    across * speed / diagonal,
                ]
            )
        )
    return jnp.stack(rows, axis=2).reshape(6, KINDS)


def matrices_kernel(depth, meta, kinds, first, second):
    cells = first.shape[1] // 2
    slab = meta[SLAB]
    sided = 2 * KINDS
    per_cell = (DIRS // 4) / DIRS

    def places(rows):
        column = lax.broadcasted_iota(jnp.int32, (rows, 2 * cells), 1)
        quart = column >= cells
        return jnp.where(quart, column - cells, column), quart

    def distance(rows, base):
        there, quart = places(rows)
        far = jnp.abs(lax.broadcasted_iota(jnp.int32, (rows, 2 * cells), 0) + base - there)
        return far.astype(jnp.float32), jnp.where(far == 0, 2.0, 1.0), quart

    full, twice_full, quart_full = distance(cells, 0)
    home, twice_home, quart_home = distance(depth, slab * depth)
    there, quart_row = places(1)
    gaps = [value.astype(jnp.float32) for value in (slab * depth - 1 - there, there - (slab + 1) * depth)]
    everywhere = jnp.zeros((cells, 2 * cells), jnp.float32)
    once = stay = around = jnp.zeros((depth, 2 * cells), jnp.float32)
    for kind in range(KINDS):
        therm, quart = kinds[THERM, kind], kinds[QUART, kind]
        slope = jnp.log(jnp.full((1, 2 * cells), kinds[DECAY, kind], jnp.float32))
        everywhere += jnp.where(quart_full, quart, therm) * (jnp.exp(full * slope) * twice_full)
        weight = jnp.where(quart_home, quart, therm) * (jnp.exp(home * slope) * twice_home)
        once += weight
        weight = weight * (home + 1.0)
        stay += kinds[STAY, kind] * weight
        around += kinds[AROUND, kind] * weight
        for side, gap in enumerate(gaps):
            weight = jnp.where(quart_row, quart, therm) * jnp.exp(jnp.maximum(gap, 0.0) * slope)
            weight = jnp.where(gap >= 0, weight, 0.0)
            at = kind + side * KINDS
            first[cells + at : cells + at + 1, :] = weight
            first[cells + sided + at : cells + sided + at + 1, :] = weight * (gap + 1.0)
            second[at : at + 1, :] = weight
    first[:cells, :] = everywhere * per_cell
    base = cells + 2 * sided
    first[base : base + depth, :] = stay * (1.0 / DIRS)
    first[base + depth :, :] = around * (1.0 / DIRS)
    second[sided:, :] = once * per_cell


def newton(density, kelvin, linear, quart):
    for _ in range(NEWTON):
        cube = kelvin * kelvin * kelvin
        residual = linear * kelvin + quart * (kelvin * cube) - density
        kelvin = kelvin - residual / (linear + 4.0 * quart * cube)
    return kelvin


def exact_dot(left, right):
    return jnp.dot(left, right, precision=lax.Precision.HIGHEST, preferred_element_type=jnp.float32)


def fourth(value):
    square = value * value
    return square * square


def add_up(values):
    while len(values) > 1:
        values = [a + b for a, b in zip(values[::2], values[1::2])]
    return values[0]


def stencil(low, high, c_self, c_y, c_z, shift_y, shift_z, at_edge):
    turned_low, turned_high = pltpu.roll(low, shift_y, 0), pltpu.roll(high, shift_y, 0)
    up_low = jnp.where(at_edge, turned_high, turned_low)
    up_high = jnp.where(at_edge, turned_low, turned_high)
    return (
        c_self * low + c_y * up_low + c_z * pltpu.roll(low, shift_z, 1),
        c_self * high + c_y * up_high + c_z * pltpu.roll(high, shift_z, 1),
    )


def course(ints, s, depth):
    forward = ints[FORWARD, s] == 1
    return jnp.where(forward, 0, depth - 1), jnp.where(forward, 1, -1)


def slot_stencil(floats, ints, s, row):
    at_edge = row == ints[EDGE_Y, s]
    c_self, c_y, c_z = floats[SELF, s], floats[UPY, s], floats[UPZ, s]
    shift_y, shift_z = ints[SHIFT_Y, s], ints[SHIFT_Z, s]
    return lambda low, high: stencil(low, high, c_self, c_y, c_z, shift_y, shift_z, at_edge)


def rows_of(s):
    at = pl.multiple_of(s * 16, 16)
    return pl.ds(at, 8), pl.ds(at + 8, 8)


K_SELF, K_LARGE, K_SMALL, K_RATIO, K_THERM, K_QUART, K_HEAT, K_WALL = range(8)


def fill_kinds(table, bands):
    speeds, rates, storages, thresholds, generations = bands
    for kind in range(KINDS):
        band, cosine = kind // 2, COSINES[kind % 2]
        sine = np.sqrt(np.float32(1.0) - cosine * cosine)
        speed, rate, storage, threshold, generation = (
            jnp.full((8, 128), ref[band], jnp.float32) for ref in (speeds, rates, storages, thresholds, generations)
        )
        inverse = 1.0 / (speed * float(cosine + sine * np.float32(ACROSS)) + rate + PSEUDO_RATE)
        quart = 1.0 / (4.0 * (threshold * threshold * threshold))
        across = speed * float(sine) * inverse
        therm = rate * storage * inverse
        rows = (
            PSEUDO_RATE * inverse,
            across * math.cos(math.pi / 8),
            across * math.sin(math.pi / 8),
            speed * float(cosine) * inverse,
            therm,
            therm * quart,
            generation * inverse,
            storage * (1.0 + quart),
        )
        for row, value in enumerate(rows):
            table[row, kind] = value


def sweeps_kernel(sizes, meta, labels, *refs):
    block, blocks, depth, width_y, slots, modes, group = sizes
    bands, refs = refs[:5], refs[5:]
    energy, flag, given, label_row, swept, quarter, *rest = refs
    faces, rest = rest[:group], rest[group:]
    keep, send, *planes, density, flat, sources, heat, table = rest
    out_one, turn_one, turn_two, out_two, turn_late, out_three = planes
    rows, own = width_y // modes, slots // group
    step = pl.program_id(0)
    slab, mode = meta[SLAB], meta[MODE]
    slabs = keep.shape[2] // depth

    @pl.when(step == 0)
    def _():
        fill_kinds(table, bands)
        for yy in range(rows):
            quarter[:, yy * 128 : (yy + 1) * 128] = given[pl.ds(mode * rows + yy, depth, stride=width_y), :]
        density[...] = jnp.zeros_like(density)

        def one_layer(x, carry):
            at = pl.multiple_of(x * 16, 16)
            for low in (0, 8):
                t = given[pl.ds(at + low, 8), :]
                power = fourth(t)
                hot = flag[pl.ds(at + low, 8), :].astype(jnp.float32)
                heat[x, low : low + 8, :] = hot
                for kind in range(KINDS):
                    value = table[K_THERM, kind] * t + table[K_QUART, kind] * power + table[K_HEAT, kind] * hot
                    sources[kind, x, low : low + 8, :] = value
            return carry

        lax.fori_loop(0, depth, one_layer, 0)

    row = lax.broadcasted_iota(jnp.int32, (8, 128), 0)

    def one_slot(i, carry):
        s = step * block + i
        label = labels[s]
        polar, turn_of = label % 4, (label // 4) % 8
        forward = polar < 2
        kind = 2 * (label // DIRS) + jnp.where((polar == 0) | (polar == 3), 0, 1)
        right, up = (turn_of < 2) | (turn_of > 5), turn_of < 4
        wide = (turn_of % 4 == 0) | (turn_of % 4 == 3)
        start, stride = jnp.where(forward, 0, depth - 1), jnp.where(forward, 1, -1)
        side = jnp.where(forward, 0, 1)
        at_wall = jnp.where(forward, slab == 0, slab == slabs - 1)
        c_self, ratio, warm = table[K_SELF, kind], table[K_RATIO, kind], table[K_HEAT, kind]
        c_y = table[jnp.where(wide, K_LARGE, K_SMALL), kind]
        c_z = table[jnp.where(wide, K_SMALL, K_LARGE), kind]
        wall = jnp.where(at_wall, 1.0, 0.0) * table[K_WALL, kind]
        shift_y, shift_z = jnp.where(right, 1, 7), jnp.where(up, 1, 127)
        at_edge = row == jnp.where(right, 0, 7)
        apply = lambda low, high: stencil(low, high, c_self, c_y, c_z, shift_y, shift_z, at_edge)
        xs = [start + stride * j for j in range(depth)]
        layers = [(energy[i, x, :8, :], energy[i, x, 8:, :]) for x in xs]
        last = []
        for turn in range(ITERS):
            total_low = total_high = wall
            for j, x in enumerate(xs):
                low, high = apply(*layers[j])
                if turn == 0:
                    low, high = low + sources[kind, x, :8, :], high + sources[kind, x, 8:, :]
                else:
                    low, high = low + warm * heat[x, :8, :], high + warm * heat[x, 8:, :]
                total_low = ratio * total_low + low
                total_high = ratio * total_high + high
                layers[j] = (total_low, total_high)
                density[turn, side, j, :8, :] += total_low
                density[turn, side, j, 8:, :] += total_high
                if turn == ITERS - 1:
                    swept[i, x, :8, :] = total_low
                    swept[i, x, 8:, :] = total_high
            last.append((total_low, total_high))
        turned = apply(*last[0])
        at_low, at_high = rows_of(s)
        values = (last[0], turned, apply(*turned), last[1], apply(*last[1]), last[2])
        for plane, (low, high) in zip(planes, values):
            plane[at_low, :] = low
            plane[at_high, :] = high
        return carry

    lax.fori_loop(0, block, one_slot, 0, unroll=2)

    @pl.when(step == blocks - 1)
    def _():
        for by in range(group):
            at = pl.ds(pl.multiple_of(((slab % group) ^ by) * own * 16, 16), own * 16)
            for index, plane in enumerate((turn_two, turn_late, out_three)):
                faces[by][index] = plane[at, :]
        for turn in range(ITERS):
            for x in range(depth):
                flat[turn, x * 16 : x * 16 + 16, :] = density[turn, 0, x] + density[turn, 1, depth - 1 - x]
        label = label_row[...]
        polar = label % 4
        kinds = 2 * (label // DIRS) + jnp.where((polar == 0) | (polar == 3), 0, 1)
        decay = jnp.ones((1, slots), jnp.float32)
        for kind in range(KINDS):
            decay = jnp.where(kinds == kind, table[K_RATIO, kind][:1, :slots], decay)
        x = lax.broadcasted_iota(jnp.int32, (slabs * depth, slots), 0)
        past = jnp.where(polar < 2, x - (slab * depth + depth - 1), slab * depth - x)
        n = past.astype(jnp.float32)
        weight = jnp.where(past > 0, jnp.exp(jnp.maximum(n, 0.0) * jnp.log(decay)), 0.0)
        weights = (weight, n * weight, (0.5 * n * (n + 1.0)) * weight)
        home = pl.ds(pl.multiple_of(slab * depth, 8), depth)
        for by in range(modes):
            ys = [(mode ^ by) * rows + yy for yy in range(rows)]
            pick = lambda plane, count: jnp.concatenate([plane[pl.ds(y, count, stride=width_y), :] for y in ys], axis=1)
            plain = exact_dot(weights[0], jnp.concatenate([pick(p, slots) for p in (out_one, out_two, out_three)], axis=1))
            once = exact_dot(weights[1], jnp.concatenate([pick(p, slots) for p in (turn_one, turn_late)], axis=1))
            twice = exact_dot(weights[2], pick(turn_two, slots))
            lanes = rows * 128
            target = (send if by % 2 else keep).at[by // 2]
            target[0] = plain[:, :lanes]
            target[1] = plain[:, lanes : 2 * lanes] + once[:, :lanes]
            target[2] = plain[:, 2 * lanes :] + once[:, lanes:] + twice
            for turn in range(ITERS):
                target[turn, home, :] += pick(flat.at[turn], depth)


def split_kernel(mine, other, keep, send):
    for index in range(mine.shape[0]):
        target = send if index % 2 else keep
        target[index // 2] = mine[index] + other[index]


def parts_kernel(depth, mine, other, parts):
    for turn in range(ITERS):
        total = mine[0, turn] + other[0, turn]
        for slab in range(parts.shape[0]):
            parts[slab, turn] = total[slab * depth : (slab + 1) * depth]


def totals_kernel(sums, parts, before, copies, late):
    slabs = parts.shape[0]
    one, two, three = (
        add_up([parts[slab, turn] for slab in range(slabs)]) * (1.0 / DIRS) for turn in range(ITERS)
    )
    late[...] = three
    kelvin = newton(one, before[...], sums[0], sums[1])
    for slab in range(slabs):
        copies[slab, 0] = kelvin
        copies[slab, 1] = two


def kelvins_kernel(depth, meta, sums, gathered, late, matrix_one, matrix_two, packed):
    slabs = gathered.shape[0]
    cells = slabs * depth
    one, two = (jnp.concatenate([gathered[slab, index] for slab in range(slabs)], axis=0) for index in range(2))
    first = exact_dot(matrix_one[...], jnp.concatenate([one, fourth(one)], axis=0))
    two = newton(two + first[:cells], one, sums[0], sums[1])
    second = exact_dot(matrix_two[...], jnp.concatenate([two, fourth(two)], axis=0))
    sided = 2 * KINDS
    packed[: 2 * sided, :] = first[cells : cells + 2 * sided]
    packed[2 * sided : 3 * sided, :] = second[:sided]
    base = 3 * sided
    packed[base : base + depth, :] = gathered[meta[SLAB], 0]
    stay = first[cells + 2 * sided : cells + 2 * sided + depth]
    around = first[cells + 2 * sided + depth :]
    own = jnp.zeros_like(around)
    for slab in range(slabs):
        own = jnp.where(meta[SLAB] == slab, two[slab * depth : (slab + 1) * depth], own)
    packed[base + depth : base + 2 * depth, :] = own
    packed[base + 2 * depth : base + 3 * depth, :] = late[...] + stay + second[sided:]
    packed[base + 3 * depth :, :] = around


def compose_kernel(own, group, meta, floats, ints, *refs):
    received, (composite, effective, ordered) = refs[:group], refs[group:]
    place = meta[SLAB] % group
    for by in range(group):
        ordered[place ^ by] = received[by][...]

    def one_slot(i, carry):
        s = place * own + i
        start, stride = course(ints, s, group)
        full, full_n, full_t = floats[FULL, s], floats[FULL_N, s], floats[FULL_T, s]
        at = pl.ds(pl.multiple_of(i * 16, 16), 16)
        one = two = three = jnp.zeros((16, 128), jnp.float32)
        for j in range(group):
            k = start + stride * j
            three = full * three + full_n * two + full_t * one + ordered[k, 2, at, :]
            two = full * two + full_n * one + ordered[k, 1, at, :]
            one = full * one + ordered[k, 0, at, :]
        for index, value in enumerate((one, two, three)):
            composite[index, at, :] = value
        return carry

    lax.fori_loop(0, own, one_slot, 0, unroll=4)
    effective[...] = ordered[...]


def enter_kernel(own, group, groups, depth, meta, floats, ints, effective, *refs):
    composites, rest = refs[:groups], refs[groups:]
    outs, (ordered, entered) = rest[:group], rest[group:]
    slab = meta[SLAB]
    place, mine = slab % group, slab // group
    for by in range(groups):
        ordered[mine ^ by] = composites[by][...]
    span = depth * group

    def one_slot(i, carry):
        s = place * own + i
        start, stride = course(ints, s, group)
        begin, leap = course(ints, s, groups)
        ahead = jnp.where(ints[FORWARD, s] == 1, mine, groups - 1 - mine)
        at = pl.ds(pl.multiple_of(i * 16, 16), 16)

        def push(values, full, full_n, full_t, added):
            one, two, three = values
            return (
                full * one + added[0],
                full * two + full_n * one + added[1],
                full * three + full_n * two + full_t * one + added[2],
            )

        values = (jnp.zeros((16, 128), jnp.float32),) * 3
        whole = floats[FULL_GROUP, s]
        for g in range(groups - 1):
            index = begin + leap * g
            added = [ordered[index, plane, at, :] for plane in range(3)]
            later = push(values, whole, span * whole, (span * (span + 1) // 2) * whole, added)
            values = tuple(jnp.where(g < ahead, a, b) for a, b in zip(later, values))
        full, full_n, full_t = floats[FULL, s], floats[FULL_N, s], floats[FULL_T, s]
        for j in range(group):
            k = start + stride * j
            for plane in range(3):
                entered[k, plane, at, :] = values[plane]
            if j < group - 1:
                values = push(values, full, full_n, full_t, [effective[k, plane, at, :] for plane in range(3)])
        return carry

    lax.fori_loop(0, own, one_slot, 0, unroll=2)
    for by in range(group):
        outs[by][...] = entered[place ^ by]


def warm_kernel(sizes, order, meta, floats, ints, kinds, sums, swept, *refs):
    block, depth, width_y, width_z, modes = sizes
    packs, refs = refs[:modes], refs[modes:]
    energy, kelvin, enter_one, enter_long, enter_two, second, added, own_one, own_two, plain, around = refs
    step = pl.program_id(0)
    rows = width_y // modes

    @pl.when(step == 0)
    def _():
        sided, base = 2 * KINDS, 6 * KINDS
        for pack, by in zip(packs, order):
            for yy in range(rows):
                y, lane = (meta[MODE] ^ by) * rows + yy, slice(yy * 128, (yy + 1) * 128)
                for index, target in enumerate((enter_one, enter_long, enter_two)):
                    target[pl.ds(y, sided, stride=width_y), :] = pack[index * sided : (index + 1) * sided, lane]
                scattered = pl.ds(y, depth, stride=width_y)
                own_one[scattered, :] = pack[base : base + depth, lane]
                own_two[scattered, :] = pack[base + depth : base + 2 * depth, lane]
                plain[y] = pack[base + 2 * depth : base + 3 * depth, lane]
                around[y] = pack[base + 3 * depth :, lane]
        for y in range(width_y):
            here = around[y]
            near = around[(y - 1) % width_y] + around[(y + 1) % width_y]
            near = near + (pltpu.roll(here, 1, 1) + pltpu.roll(here, width_z - 1, 1))
            scattered = pl.ds(y, depth, stride=width_y)
            kelvin[scattered, :] = newton(plain[y] + near, own_two[scattered, :], sums[0], sums[1])

        def one_kind(kind, carry):
            therm, quart, decay = kinds[THERM, kind], kinds[QUART, kind], kinds[DECAY, kind]
            ones, twos = [], []
            for x in range(depth):
                here = slice(x * 16, x * 16 + 16)
                t, u = own_one[here, :], own_two[here, :]
                ones.append(therm * t + quart * fourth(t))
                twos.append(therm * u + quart * fourth(u))
            for back in (0, KINDS):
                at = pl.ds(pl.multiple_of((kind + back) * 16, 16), 16)
                once, twice, new = enter_one[at, :], enter_long[at, :], enter_two[at, :]
                for j in range(depth):
                    x = depth - 1 - j if back else j
                    once = decay * once + ones[x]
                    twice = decay * twice + once
                    new = decay * new + twos[x]
                    second[kind + back, x] = twice
                    added[kind + back, x] = new
            return carry

        lax.fori_loop(0, KINDS, one_kind, 0)

    row = lax.broadcasted_iota(jnp.int32, (8, 128), 0)

    def one_slot(i, carry):
        s = step * block + i
        sided = ints[KIND, s] + KINDS * (1 - ints[FORWARD, s])
        apply = slot_stencil(floats, ints, s, row)
        for x in range(depth):
            low, high = apply(second[sided, x, :8, :], second[sided, x, 8:, :])
            energy[i, x, :8, :] = swept[i, x, :8, :] + (low + added[sided, x, :8, :])
            energy[i, x, 8:, :] = swept[i, x, 8:, :] + (high + added[sided, x, 8:, :])
        return carry

    lax.fori_loop(0, block, one_slot, 0, unroll=2)


def inflow_kernel(sizes, meta, floats, ints, warm, *refs):
    block, depth, own, group = sizes
    received, (energy, ordered) = refs[:group], refs[group:]
    step = pl.program_id(0)

    @pl.when(step == 0)
    def _():
        for by in range(group):
            ordered[(meta[SLAB] % group) ^ by] = received[by][...]

    def one_slot(i, carry):
        s = step * block + i
        start, stride = course(ints, s, depth)
        ratio = floats[RATIO, s]
        at = pl.ds(pl.multiple_of((s % own) * 16, 16), 16)
        one, two, three = (ordered[s // own, plane, at, :] for plane in range(ITERS))
        for j in range(depth):
            x = start + stride * j
            one = ratio * one
            two = ratio * two + one
            three = ratio * three + two
            energy[i, x] = warm[i, x] + three
        return carry

    lax.fori_loop(0, block, one_slot, 0, unroll=4)


def local(incoming_occupation, crystal_kelvin_given, generating_region_flag, labels, speed, rate, storage, threshold, generation):
    slots, depth, width_y, width_z = incoming_occupation.shape
    slabs, modes = lax.axis_size("slab"), lax.axis_size("mode")
    group, groups = GROUP, slabs // GROUP
    own = slots // group
    lanes = width_y // modes * width_z
    block = 8
    blocks = slots // block
    cells, all_x = depth * width_y, slabs * depth
    face_rows = own * width_y
    slab = lax.axis_index("slab").astype(jnp.int32)
    meta = jnp.stack([slab, lax.axis_index("mode").astype(jnp.int32)])
    floats, ints = slot_tables(labels, speed, rate, storage, threshold, generation, slab, slabs, depth, width_z)
    kinds = kind_table(speed, rate, storage, threshold, generation)
    sums = jnp.stack([jnp.sum(storage), jnp.sum(storage / (4.0 * threshold**3))])

    def shape(*dims):
        return jax.ShapeDtypeStruct(dims, jnp.float32)

    def whole(*dims):
        return pl.BlockSpec(dims, lambda i: (0,) * len(dims))

    def scratch(*dims):
        return pltpu.VMEM(dims, jnp.float32)

    def swap(array, axis, by):
        return lax.ppermute(array, axis, [(i, i ^ by) for i in range(lax.axis_size(axis))])

    def call(kernel, name, in_specs, out_shapes, *args, scratches=()):
        return pl.pallas_call(
            kernel,
            in_specs=in_specs,
            out_specs=[VMEM] * len(out_shapes),
            out_shape=out_shapes,
            scratch_shapes=list(scratches),
            compiler_params=PARAMS,
            name=name,
        )(*args)

    slot_block = pl.BlockSpec((block, depth, width_y, width_z), lambda i: (i, 0, 0, 0))
    slot_shape = shape(slots, depth, width_y, width_z)
    face = (3, face_rows, width_z)
    half = (modes // 2, ITERS, all_x, lanes)
    swept, quarter, *rest = pl.pallas_call(
        functools.partial(sweeps_kernel, (block, blocks, depth, width_y, slots, modes, group)),
        grid=(blocks,),
        in_specs=[SMEM] * 7 + [slot_block, whole(cells, width_z), whole(cells, width_z), whole(1, slots)],
        out_specs=[slot_block, whole(depth, lanes)] + [whole(*face)] * group + [whole(*half)] * 2,
        out_shape=[slot_shape, shape(depth, lanes)] + [shape(*face)] * group + [shape(*half)] * 2,
        scratch_shapes=[scratch(slots * width_y, width_z)] * 6
        + [
            scratch(ITERS, 2, depth, width_y, width_z),
            scratch(ITERS, cells, width_z),
            scratch(KINDS, depth, width_y, width_z),
            scratch(depth, width_y, width_z),
            scratch(8, KINDS, 8, width_z),
        ],
        compiler_params=LARGE,
        name="sweeps",
    )(
        meta,
        labels,
        speed,
        rate,
        storage,
        threshold,
        generation,
        incoming_occupation,
        generating_region_flag.reshape(cells, width_z),
        crystal_kelvin_given.reshape(cells, width_z),
        labels.reshape(1, slots),
    )
    faces, (keep, send) = rest[:group], rest[group:]

    by = 1
    other = swap(send, "mode", by)
    received = [faces[0]] + [swap(faces[index], "slab", index) for index in range(1, group)]
    while 2 * by < modes:
        by *= 2
        now = (modes // (2 * by), ITERS, all_x, lanes)
        keep, send = call(split_kernel, "density_split", [VMEM] * 2, [shape(*now)] * 2, keep, other)
        other = swap(send, "mode", by)
    piece = (slabs, ITERS, depth, lanes)
    first_matrix, second_matrix = call(
        functools.partial(matrices_kernel, depth),
        "heat_matrices",
        [SMEM] * 2,
        [shape(all_x + 4 * KINDS + 2 * depth, 2 * all_x), shape(2 * KINDS + depth, 2 * all_x)],
        meta,
        kinds,
    )
    composite, effective = call(
        functools.partial(compose_kernel, own, group),
        "compose",
        [SMEM] * 3 + [VMEM] * group,
        [shape(*face), shape(group, *face)],
        meta,
        floats,
        ints,
        *received,
        scratches=[scratch(group, *face)],
    )
    other, composite, floats, ints, kinds, sums, first_matrix, second_matrix = lax.optimization_barrier(
        (other, composite, floats, ints, kinds, sums, first_matrix, second_matrix)
    )
    composites = [composite] + [swap(composite, "slab", index * group) for index in range(1, groups)]
    (parts,) = call(functools.partial(parts_kernel, depth), "density_parts", [VMEM] * 2, [shape(*piece)], keep, other)
    summed = lax.all_to_all(parts, "slab", 0, 0)

    copies, late = call(
        totals_kernel,
        "density_totals",
        [SMEM] + [VMEM] * 2,
        [shape(slabs, 2, depth, lanes), shape(depth, lanes)],
        sums,
        summed,
        quarter,
    )
    gathered = lax.all_to_all(copies, "slab", 0, 0)
    entering = call(
        functools.partial(enter_kernel, own, group, groups, depth),
        "enter",
        [SMEM] * 3 + [VMEM] * (1 + groups),
        [shape(*face)] * group,
        meta,
        floats,
        ints,
        effective,
        *composites,
        scratches=[scratch(groups, *face), scratch(group, *face)],
    )
    gathered, entering = lax.optimization_barrier((gathered, entering))
    entering = [entering[0]] + [swap(entering[index], "slab", index) for index in range(1, group)]

    pack_shape = shape(6 * KINDS + 4 * depth, lanes)
    (packed,) = call(
        functools.partial(kelvins_kernel, depth),
        "kelvins",
        [SMEM] * 2 + [VMEM] * 4,
        [pack_shape],
        meta,
        sums,
        gathered,
        late,
        first_matrix,
        second_matrix,
    )
    packs, order = [packed], [0]
    while by:
        packs = packs + [swap(pack, "mode", by) for pack in packs]
        order = order + [index ^ by for index in order]
        by //= 2

    warm, kelvin = pl.pallas_call(
        functools.partial(warm_kernel, (block, depth, width_y, width_z, modes), order),
        grid=(blocks,),
        in_specs=[SMEM] * 5 + [slot_block] + [whole(*pack_shape.shape)] * modes,
        out_specs=[slot_block, whole(cells, width_z)],
        out_shape=[slot_shape, shape(cells, width_z)],
        scratch_shapes=[scratch(2 * KINDS * width_y, width_z)] * 3
        + [scratch(2 * KINDS, depth, width_y, width_z)] * 2
        + [scratch(cells, width_z)] * 2
        + [scratch(width_y, depth, width_z)] * 2,
        compiler_params=PARAMS,
        name="warm",
    )(meta, floats, ints, kinds, sums, swept, *packs)
    energy = pl.pallas_call(
        functools.partial(inflow_kernel, (block, depth, own, group)),
        grid=(blocks,),
        in_specs=[SMEM] * 3 + [slot_block] + [whole(*face)] * group,
        out_specs=slot_block,
        out_shape=slot_shape,
        scratch_shapes=[scratch(group, *face)],
        compiler_params=PARAMS,
        name="inflow",
    )(meta, floats, ints, warm, *entering)
    return energy, kelvin.reshape(depth, width_y, width_z)


def solution(mesh):
    return jax.shard_map(
        local,
        mesh=mesh,
        in_specs=(
            P("mode", "slab", None, None),
            P("slab", None, None),
            P("slab", None, None),
            P("mode"),
            P(),
            P(),
            P(),
            P(),
            P(),
        ),
        out_specs=(P("mode", "slab", None, None), P("slab", None, None)),
        check_vma=False,
    )
```

```python
import functools
import math

import jax
import jax.numpy as jnp
import numpy as np
from jax import lax
from jax.experimental import pallas as pl
from jax.experimental.pallas import tpu as pltpu
from jax.sharding import PartitionSpec as P

FREQ_GROUPS = 8
DIRS = 32
ITERS = 3
NEWTON = 4
PSEUDO_RATE = 0.03
GROUP = 4
COSINES = (np.float32(0.99995), np.float32(0.9999))

SELF, UPY, UPZ, RATIO, WALL, FULL, FULL_N, FULL_T, FULL_GROUP, WARM = range(10)
FORWARD, SHIFT_Y, SHIFT_Z, EDGE_Y, KIND = range(5)
THERM, QUART, HEAT, DECAY, STAY, AROUND = range(6)
KINDS = 2 * FREQ_GROUPS
SLAB, MODE = range(2)

SMEM = pl.BlockSpec(memory_space=pltpu.SMEM)
VMEM = pl.BlockSpec(memory_space=pltpu.VMEM)
PARAMS = pltpu.CompilerParams(vmem_limit_bytes=48 * 1024 * 1024)
LARGE = pltpu.CompilerParams(vmem_limit_bytes=62 * 1024 * 1024)
ACROSS = math.cos(math.pi / 8) + math.sin(math.pi / 8)


def diagonal_of(speed, rate, cosine):
    sine = jnp.sqrt(1.0 - cosine * cosine)
    return speed * (cosine + sine * np.float32(ACROSS)) + rate + PSEUDO_RATE


def slot_tables(labels, speed, rate, storage, threshold, generation, slab, slabs, depth, width_z):
    band = labels // DIRS
    direction = labels % DIRS
    of_band = (band[None, :] == jnp.arange(FREQ_GROUPS, dtype=jnp.int32)[:, None]).astype(jnp.float32)
    speed, rate, storage, threshold, generation = (
        jnp.sum(of_band * value[:, None], axis=0) for value in (speed, rate, storage, threshold, generation)
    )
    polar = direction % 4
    outer = (polar == 0) | (polar == 3)
    forward = polar < 2
    cosine = jnp.where(outer, COSINES[0], COSINES[1])
    sine = jnp.sqrt(1.0 - cosine * cosine)
    azimuth = ((direction // 4).astype(jnp.float32) + 0.5) * (2.0 * math.pi / (DIRS // 4))
    vy = speed * sine * jnp.cos(azimuth)
    vz = speed * sine * jnp.sin(azimuth)
    diagonal = diagonal_of(speed, rate, cosine)
    ratio = speed * cosine / diagonal
    full = lax.integer_pow(ratio, depth)
    at_wall = jnp.where(forward, slab == 0, slab == slabs - 1)
    wall = storage * (1.0 + 1.0 / (4.0 * threshold**3))
    floats = jnp.stack(
        [
            PSEUDO_RATE / diagonal,
            jnp.abs(vy) / diagonal,
            jnp.abs(vz) / diagonal,
            ratio,
            jnp.where(at_wall, wall, 0.0),
            full,
            depth * full,
            (depth * (depth + 1) // 2) * full,
            lax.integer_pow(full, GROUP),
            generation / diagonal,
        ]
    )
    ints = jnp.stack(
        [
            forward.astype(jnp.int32),
            jnp.where(vy > 0, 1, 7).astype(jnp.int32),
            jnp.where(vz > 0, 1, width_z - 1).astype(jnp.int32),
            jnp.where(vy > 0, 0, 7).astype(jnp.int32),
            2 * band + jnp.where(outer, 0, 1),
        ]
    )
    return floats, ints


def kind_table(speed, rate, storage, threshold, generation):
    rows = []
    for cosine in COSINES:
        diagonal = diagonal_of(speed, rate, cosine)
        therm = rate * storage / diagonal
        quart = therm / (4.0 * threshold**3)
        across = jnp.sqrt(1.0 - cosine * cosine) * np.float32(2.0 * ACROSS)
        rows.append(
            jnp.stack(
                [
                    therm,
                    quart,
                    generation / diagonal,
                    speed * cosine / diagonal,
                    (DIRS // 4) * PSEUDO_RATE / diagonal,
                    across * speed / diagonal,
                ]
            )
        )
    return jnp.stack(rows, axis=2).reshape(6, KINDS)


def matrices_kernel(depth, meta, kinds, first, second):
    cells = first.shape[1] // 2
    slab = meta[SLAB]
    sided = 2 * KINDS
    per_cell = (DIRS // 4) / DIRS

    def places(rows):
        column = lax.broadcasted_iota(jnp.int32, (rows, 2 * cells), 1)
        quart = column >= cells
        return jnp.where(quart, column - cells, column), quart

    def distance(rows, base):
        there, quart = places(rows)
        far = jnp.abs(lax.broadcasted_iota(jnp.int32, (rows, 2 * cells), 0) + base - there)
        return far.astype(jnp.float32), jnp.where(far == 0, 2.0, 1.0), quart

    full, twice_full, quart_full = distance(cells, 0)
    home, twice_home, quart_home = distance(depth, slab * depth)
    there, quart_row = places(1)
    gaps = [value.astype(jnp.float32) for value in (slab * depth - 1 - there, there - (slab + 1) * depth)]
    everywhere = jnp.zeros((cells, 2 * cells), jnp.float32)
    once = stay = around = jnp.zeros((depth, 2 * cells), jnp.float32)
    for kind in range(KINDS):
        therm, quart = kinds[THERM, kind], kinds[QUART, kind]
        slope = jnp.log(jnp.full((1, 2 * cells), kinds[DECAY, kind], jnp.float32))
        everywhere += jnp.where(quart_full, quart, therm) * (jnp.exp(full * slope) * twice_full)
        weight = jnp.where(quart_home, quart, therm) * (jnp.exp(home * slope) * twice_home)
        once += weight
        weight = weight * (home + 1.0)
        stay += kinds[STAY, kind] * weight
        around += kinds[AROUND, kind] * weight
        for side, gap in enumerate(gaps):
            weight = jnp.where(quart_row, quart, therm) * jnp.exp(jnp.maximum(gap, 0.0) * slope)
            weight = jnp.where(gap >= 0, weight, 0.0)
            at = kind + side * KINDS
            first[cells + at : cells + at + 1, :] = weight
            first[cells + sided + at : cells + sided + at + 1, :] = weight * (gap + 1.0)
            second[at : at + 1, :] = weight
    first[:cells, :] = everywhere * per_cell
    base = cells + 2 * sided
    first[base : base + depth, :] = stay * (1.0 / DIRS)
    first[base + depth :, :] = around * (1.0 / DIRS)
    second[sided:, :] = once * per_cell


def newton(density, kelvin, linear, quart):
    for _ in range(NEWTON):
        cube = kelvin * kelvin * kelvin
        residual = linear * kelvin + quart * (kelvin * cube) - density
        kelvin = kelvin - residual / (linear + 4.0 * quart * cube)
    return kelvin


def exact_dot(left, right):
    return jnp.dot(left, right, precision=lax.Precision.HIGHEST, preferred_element_type=jnp.float32)


def fourth(value):
    square = value * value
    return square * square


def add_up(values):
    while len(values) > 1:
        values = [a + b for a, b in zip(values[::2], values[1::2])]
    return values[0]


def stencil(low, high, c_self, c_y, c_z, shift_y, shift_z, at_edge):
    turned_low, turned_high = pltpu.roll(low, shift_y, 0), pltpu.roll(high, shift_y, 0)
    up_low = jnp.where(at_edge, turned_high, turned_low)
    up_high = jnp.where(at_edge, turned_low, turned_high)
    return (
        c_self * low + c_y * up_low + c_z * pltpu.roll(low, shift_z, 1),
        c_self * high + c_y * up_high + c_z * pltpu.roll(high, shift_z, 1),
    )


def course(ints, s, depth):
    forward = ints[FORWARD, s] == 1
    return jnp.where(forward, 0, depth - 1), jnp.where(forward, 1, -1)


def slot_stencil(floats, ints, s, row):
    at_edge = row == ints[EDGE_Y, s]
    c_self, c_y, c_z = floats[SELF, s], floats[UPY, s], floats[UPZ, s]
    shift_y, shift_z = ints[SHIFT_Y, s], ints[SHIFT_Z, s]
    return lambda low, high: stencil(low, high, c_self, c_y, c_z, shift_y, shift_z, at_edge)


def rows_of(s):
    at = pl.multiple_of(s * 16, 16)
    return pl.ds(at, 8), pl.ds(at + 8, 8)


K_SELF, K_LARGE, K_SMALL, K_RATIO, K_THERM, K_QUART, K_HEAT, K_WALL = range(8)


def fill_kinds(table, bands):
    speeds, rates, storages, thresholds, generations = bands
    for kind in range(KINDS):
        band, cosine = kind // 2, COSINES[kind % 2]
        sine = np.sqrt(np.float32(1.0) - cosine * cosine)
        speed, rate, storage, threshold, generation = (
            jnp.full((8, 128), ref[band], jnp.float32) for ref in (speeds, rates, storages, thresholds, generations)
        )
        inverse = 1.0 / (speed * float(cosine + sine * np.float32(ACROSS)) + rate + PSEUDO_RATE)
        quart = 1.0 / (4.0 * (threshold * threshold * threshold))
        across = speed * float(sine) * inverse
        therm = rate * storage * inverse
        rows = (
            PSEUDO_RATE * inverse,
            across * math.cos(math.pi / 8),
            across * math.sin(math.pi / 8),
            speed * float(cosine) * inverse,
            therm,
            therm * quart,
            generation * inverse,
            storage * (1.0 + quart),
        )
        for row, value in enumerate(rows):
            table[row, kind] = value


def sweeps_kernel(sizes, meta, labels, *refs):
    block, blocks, depth, width_y, slots, modes, group = sizes
    bands, refs = refs[:5], refs[5:]
    energy, flag, given, label_row, swept, quarter, *rest = refs
    faces, rest = rest[:group], rest[group:]
    keep, send, *planes, density, flat, sources, heat, table = rest
    out_one, turn_one, turn_two, out_two, turn_late, out_three = planes
    rows, own = width_y // modes, slots // group
    step = pl.program_id(0)
    slab, mode = meta[SLAB], meta[MODE]
    slabs = keep.shape[2] // depth

    @pl.when(step == 0)
    def _():
        fill_kinds(table, bands)
        for yy in range(rows):
            quarter[:, yy * 128 : (yy + 1) * 128] = given[pl.ds(mode * rows + yy, depth, stride=width_y), :]
        density[...] = jnp.zeros_like(density)

        def one_layer(x, carry):
            at = pl.multiple_of(x * 16, 16)
            for low in (0, 8):
                t = given[pl.ds(at + low, 8), :]
                power = fourth(t)
                hot = flag[pl.ds(at + low, 8), :].astype(jnp.float32)
                heat[x, low : low + 8, :] = hot
                for kind in range(KINDS):
                    value = table[K_THERM, kind] * t + table[K_QUART, kind] * power + table[K_HEAT, kind] * hot
                    sources[kind, x, low : low + 8, :] = value
            return carry

        lax.fori_loop(0, depth, one_layer, 0)

    row = lax.broadcasted_iota(jnp.int32, (8, 128), 0)

    def one_slot(i, carry):
        s = step * block + i
        label = labels[s]
        polar, turn_of = label % 4, (label // 4) % 8
        forward = polar < 2
        kind = 2 * (label // DIRS) + jnp.where((polar == 0) | (polar == 3), 0, 1)
        right, up = (turn_of < 2) | (turn_of > 5), turn_of < 4
        wide = (turn_of % 4 == 0) | (turn_of % 4 == 3)
        start, stride = jnp.where(forward, 0, depth - 1), jnp.where(forward, 1, -1)
        side = jnp.where(forward, 0, 1)
        at_wall = jnp.where(forward, slab == 0, slab == slabs - 1)
        c_self, ratio, warm = table[K_SELF, kind], table[K_RATIO, kind], table[K_HEAT, kind]
        c_y = table[jnp.where(wide, K_LARGE, K_SMALL), kind]
        c_z = table[jnp.where(wide, K_SMALL, K_LARGE), kind]
        wall = jnp.where(at_wall, 1.0, 0.0) * table[K_WALL, kind]
        shift_y, shift_z = jnp.where(right, 1, 7), jnp.where(up, 1, 127)
        at_edge = row == jnp.where(right, 0, 7)
        apply = lambda low, high: stencil(low, high, c_self, c_y, c_z, shift_y, shift_z, at_edge)
        xs = [start + stride * j for j in range(depth)]
        layers = [(energy[i, x, :8, :], energy[i, x, 8:, :]) for x in xs]
        last = []
        for turn in range(ITERS):
            total_low = total_high = wall
            for j, x in enumerate(xs):
                low, high = apply(*layers[j])
                if turn == 0:
                    low, high = low + sources[kind, x, :8, :], high + sources[kind, x, 8:, :]
                else:
                    low, high = low + warm * heat[x, :8, :], high + warm * heat[x, 8:, :]
                total_low = ratio * total_low + low
                total_high = ratio * total_high + high
                layers[j] = (total_low, total_high)
                density[turn, side, j, :8, :] += total_low
                density[turn, side, j, 8:, :] += total_high
                if turn == ITERS - 1:
                    swept[i, x, :8, :] = total_low
                    swept[i, x, 8:, :] = total_high
            last.append((total_low, total_high))
        turned = apply(*last[0])
        at_low, at_high = rows_of(s)
        values = (last[0], turned, apply(*turned), last[1], apply(*last[1]), last[2])
        for plane, (low, high) in zip(planes, values):
            plane[at_low, :] = low
            plane[at_high, :] = high
        return carry

    lax.fori_loop(0, block, one_slot, 0, unroll=2)

    @pl.when(step == blocks - 1)
    def _():
        for by in range(group):
            at = pl.ds(pl.multiple_of(((slab % group) ^ by) * own * 16, 16), own * 16)
            for index, plane in enumerate((turn_two, turn_late, out_three)):
                faces[by][index] = plane[at, :]
        for turn in range(ITERS):
            for x in range(depth):
                flat[turn, x * 16 : x * 16 + 16, :] = density[turn, 0, x] + density[turn, 1, depth - 1 - x]
        label = label_row[...]
        polar = label % 4
        kinds = 2 * (label // DIRS) + jnp.where((polar == 0) | (polar == 3), 0, 1)
        decay = jnp.ones((1, slots), jnp.float32)
        for kind in range(KINDS):
            decay = jnp.where(kinds == kind, table[K_RATIO, kind][:1, :slots], decay)
        x = lax.broadcasted_iota(jnp.int32, (slabs * depth, slots), 0)
        past = jnp.where(polar < 2, x - (slab * depth + depth - 1), slab * depth - x)
        n = past.astype(jnp.float32)
        weight = jnp.where(past > 0, jnp.exp(jnp.maximum(n, 0.0) * jnp.log(decay)), 0.0)
        weights = (weight, n * weight, (0.5 * n * (n + 1.0)) * weight)
        home = pl.ds(pl.multiple_of(slab * depth, 8), depth)
        for by in range(modes):
            ys = [(mode ^ by) * rows + yy for yy in range(rows)]
            pick = lambda plane, count: jnp.concatenate([plane[pl.ds(y, count, stride=width_y), :] for y in ys], axis=1)
            plain = exact_dot(weights[0], jnp.concatenate([pick(p, slots) for p in (out_one, out_two, out_three)], axis=1))
            once = exact_dot(weights[1], jnp.concatenate([pick(p, slots) for p in (turn_one, turn_late)], axis=1))
            twice = exact_dot(weights[2], pick(turn_two, slots))
            lanes = rows * 128
            target = (send if by % 2 else keep).at[by // 2]
            target[0] = plain[:, :lanes]
            target[1] = plain[:, lanes : 2 * lanes] + once[:, :lanes]
            target[2] = plain[:, 2 * lanes :] + once[:, lanes:] + twice
            for turn in range(ITERS):
                target[turn, home, :] += pick(flat.at[turn], depth)


def split_kernel(mine, other, keep, send):
    for index in range(mine.shape[0]):
        target = send if index % 2 else keep
        target[index // 2] = mine[index] + other[index]


def parts_kernel(depth, mine, other, parts):
    for turn in range(ITERS):
        total = mine[0, turn] + other[0, turn]
        for slab in range(parts.shape[0]):
            parts[slab, turn] = total[slab * depth : (slab + 1) * depth]


def totals_kernel(sums, parts, before, copies, late):
    slabs = parts.shape[0]
    one, two, three = (
        add_up([parts[slab, turn] for slab in range(slabs)]) * (1.0 / DIRS) for turn in range(ITERS)
    )
    late[...] = three
    kelvin = newton(one, before[...], sums[0], sums[1])
    for slab in range(slabs):
        copies[slab, 0] = kelvin
        copies[slab, 1] = two


def kelvins_kernel(depth, meta, sums, gathered, late, matrix_one, matrix_two, packed):
    slabs = gathered.shape[0]
    cells = slabs * depth
    one, two = (jnp.concatenate([gathered[slab, index] for slab in range(slabs)], axis=0) for index in range(2))
    first = exact_dot(matrix_one[...], jnp.concatenate([one, fourth(one)], axis=0))
    two = newton(two + first[:cells], one, sums[0], sums[1])
    second = exact_dot(matrix_two[...], jnp.concatenate([two, fourth(two)], axis=0))
    sided = 2 * KINDS
    packed[: 2 * sided, :] = first[cells : cells + 2 * sided]
    packed[2 * sided : 3 * sided, :] = second[:sided]
    base = 3 * sided
    packed[base : base + depth, :] = gathered[meta[SLAB], 0]
    stay = first[cells + 2 * sided : cells + 2 * sided + depth]
    around = first[cells + 2 * sided + depth :]
    own = jnp.zeros_like(around)
    for slab in range(slabs):
        own = jnp.where(meta[SLAB] == slab, two[slab * depth : (slab + 1) * depth], own)
    packed[base + depth : base + 2 * depth, :] = own
    packed[base + 2 * depth : base + 3 * depth, :] = late[...] + stay + second[sided:]
    packed[base + 3 * depth :, :] = around


def compose_kernel(own, group, meta, floats, ints, *refs):
    received, (composite, effective, ordered) = refs[:group], refs[group:]
    place = meta[SLAB] % group
    for by in range(group):
        ordered[place ^ by] = received[by][...]

    def one_slot(i, carry):
        s = place * own + i
        start, stride = course(ints, s, group)
        full, full_n, full_t = floats[FULL, s], floats[FULL_N, s], floats[FULL_T, s]
        at = pl.ds(pl.multiple_of(i * 16, 16), 16)
        one = two = three = jnp.zeros((16, 128), jnp.float32)
        for j in range(group):
            k = start + stride * j
            three = full * three + full_n * two + full_t * one + ordered[k, 2, at, :]
            two = full * two + full_n * one + ordered[k, 1, at, :]
            one = full * one + ordered[k, 0, at, :]
        for index, value in enumerate((one, two, three)):
            composite[index, at, :] = value
        return carry

    lax.fori_loop(0, own, one_slot, 0, unroll=4)
    effective[...] = ordered[...]


def enter_kernel(own, group, groups, depth, meta, floats, ints, effective, *refs):
    composites, rest = refs[:groups], refs[groups:]
    outs, (ordered, entered) = rest[:group], rest[group:]
    slab = meta[SLAB]
    place, mine = slab % group, slab // group
    for by in range(groups):
        ordered[mine ^ by] = composites[by][...]
    span = depth * group

    def one_slot(i, carry):
        s = place * own + i
        start, stride = course(ints, s, group)
        begin, leap = course(ints, s, groups)
        ahead = jnp.where(ints[FORWARD, s] == 1, mine, groups - 1 - mine)
        at = pl.ds(pl.multiple_of(i * 16, 16), 16)

        def push(values, full, full_n, full_t, added):
            one, two, three = values
            return (
                full * one + added[0],
                full * two + full_n * one + added[1],
                full * three + full_n * two + full_t * one + added[2],
            )

        values = (jnp.zeros((16, 128), jnp.float32),) * 3
        whole = floats[FULL_GROUP, s]
        for g in range(groups - 1):
            index = begin + leap * g
            added = [ordered[index, plane, at, :] for plane in range(3)]
            later = push(values, whole, span * whole, (span * (span + 1) // 2) * whole, added)
            values = tuple(jnp.where(g < ahead, a, b) for a, b in zip(later, values))
        full, full_n, full_t = floats[FULL, s], floats[FULL_N, s], floats[FULL_T, s]
        for j in range(group):
            k = start + stride * j
            for plane in range(3):
                entered[k, plane, at, :] = values[plane]
            if j < group - 1:
                values = push(values, full, full_n, full_t, [effective[k, plane, at, :] for plane in range(3)])
        return carry

    lax.fori_loop(0, own, one_slot, 0, unroll=2)
    for by in range(group):
        outs[by][...] = entered[place ^ by]


def warm_kernel(sizes, order, meta, floats, ints, kinds, sums, swept, *refs):
    block, depth, width_y, width_z, modes = sizes
    packs, refs = refs[:modes], refs[modes:]
    energy, kelvin, enter_one, enter_long, enter_two, second, added, own_one, own_two, plain, around = refs
    step = pl.program_id(0)
    rows = width_y // modes

    @pl.when(step == 0)
    def _():
        sided, base = 2 * KINDS, 6 * KINDS
        for pack, by in zip(packs, order):
            for yy in range(rows):
                y, lane = (meta[MODE] ^ by) * rows + yy, slice(yy * 128, (yy + 1) * 128)
                for index, target in enumerate((enter_one, enter_long, enter_two)):
                    target[pl.ds(y, sided, stride=width_y), :] = pack[index * sided : (index + 1) * sided, lane]
                scattered = pl.ds(y, depth, stride=width_y)
                own_one[scattered, :] = pack[base : base + depth, lane]
                own_two[scattered, :] = pack[base + depth : base + 2 * depth, lane]
                plain[y] = pack[base + 2 * depth : base + 3 * depth, lane]
                around[y] = pack[base + 3 * depth :, lane]
        for y in range(width_y):
            here = around[y]
            near = around[(y - 1) % width_y] + around[(y + 1) % width_y]
            near = near + (pltpu.roll(here, 1, 1) + pltpu.roll(here, width_z - 1, 1))
            scattered = pl.ds(y, depth, stride=width_y)
            kelvin[scattered, :] = newton(plain[y] + near, own_two[scattered, :], sums[0], sums[1])

        def one_kind(kind, carry):
            therm, quart, decay = kinds[THERM, kind], kinds[QUART, kind], kinds[DECAY, kind]
            ones, twos = [], []
            for x in range(depth):
                here = slice(x * 16, x * 16 + 16)
                t, u = own_one[here, :], own_two[here, :]
                ones.append(therm * t + quart * fourth(t))
                twos.append(therm * u + quart * fourth(u))
            for back in (0, KINDS):
                at = pl.ds(pl.multiple_of((kind + back) * 16, 16), 16)
                once, twice, new = enter_one[at, :], enter_long[at, :], enter_two[at, :]
                for j in range(depth):
                    x = depth - 1 - j if back else j
                    once = decay * once + ones[x]
                    twice = decay * twice + once
                    new = decay * new + twos[x]
                    second[kind + back, x] = twice
                    added[kind + back, x] = new
            return carry

        lax.fori_loop(0, KINDS, one_kind, 0)

    row = lax.broadcasted_iota(jnp.int32, (8, 128), 0)

    def one_slot(i, carry):
        s = step * block + i
        sided = ints[KIND, s] + KINDS * (1 - ints[FORWARD, s])
        apply = slot_stencil(floats, ints, s, row)
        for x in range(depth):
            low, high = apply(second[sided, x, :8, :], second[sided, x, 8:, :])
            energy[i, x, :8, :] = swept[i, x, :8, :] + (low + added[sided, x, :8, :])
            energy[i, x, 8:, :] = swept[i, x, 8:, :] + (high + added[sided, x, 8:, :])
        return carry

    lax.fori_loop(0, block, one_slot, 0, unroll=2)


def inflow_kernel(sizes, meta, floats, ints, warm, *refs):
    block, depth, own, group = sizes
    received, (energy, ordered) = refs[:group], refs[group:]
    step = pl.program_id(0)

    @pl.when(step == 0)
    def _():
        for by in range(group):
            ordered[(meta[SLAB] % group) ^ by] = received[by][...]

    def one_slot(i, carry):
        s = step * block + i
        start, stride = course(ints, s, depth)
        ratio = floats[RATIO, s]
        at = pl.ds(pl.multiple_of((s % own) * 16, 16), 16)
        one, two, three = (ordered[s // own, plane, at, :] for plane in range(ITERS))
        for j in range(depth):
            x = start + stride * j
            one = ratio * one
            two = ratio * two + one
            three = ratio * three + two
            energy[i, x] = warm[i, x] + three
        return carry

    lax.fori_loop(0, block, one_slot, 0, unroll=4)


def local(incoming_occupation, crystal_kelvin_given, generating_region_flag, labels, speed, rate, storage, threshold, generation):
    slots, depth, width_y, width_z = incoming_occupation.shape
    slabs, modes = lax.axis_size("slab"), lax.axis_size("mode")
    group, groups = GROUP, slabs // GROUP
    own = slots // group
    lanes = width_y // modes * width_z
    block = 8
    blocks = slots // block
    cells, all_x = depth * width_y, slabs * depth
    face_rows = own * width_y
    slab = lax.axis_index("slab").astype(jnp.int32)
    meta = jnp.stack([slab, lax.axis_index("mode").astype(jnp.int32)])
    floats, ints = slot_tables(labels, speed, rate, storage, threshold, generation, slab, slabs, depth, width_z)
    kinds = kind_table(speed, rate, storage, threshold, generation)
    sums = jnp.stack([jnp.sum(storage), jnp.sum(storage / (4.0 * threshold**3))])

    def shape(*dims):
        return jax.ShapeDtypeStruct(dims, jnp.float32)

    def whole(*dims):
        return pl.BlockSpec(dims, lambda i: (0,) * len(dims))

    def scratch(*dims):
        return pltpu.VMEM(dims, jnp.float32)

    def swap(array, axis, by):
        return lax.ppermute(array, axis, [(i, i ^ by) for i in range(lax.axis_size(axis))])

    def call(kernel, name, in_specs, out_shapes, *args, scratches=()):
        return pl.pallas_call(
            kernel,
            in_specs=in_specs,
            out_specs=[VMEM] * len(out_shapes),
            out_shape=out_shapes,
            scratch_shapes=list(scratches),
            compiler_params=PARAMS,
            name=name,
        )(*args)

    slot_block = pl.BlockSpec((block, depth, width_y, width_z), lambda i: (i, 0, 0, 0))
    slot_shape = shape(slots, depth, width_y, width_z)
    face = (3, face_rows, width_z)
    half = (modes // 2, ITERS, all_x, lanes)
    swept, quarter, *rest = pl.pallas_call(
        functools.partial(sweeps_kernel, (block, blocks, depth, width_y, slots, modes, group)),
        grid=(blocks,),
        in_specs=[SMEM] * 7 + [slot_block, whole(cells, width_z), whole(cells, width_z), whole(1, slots)],
        out_specs=[slot_block, whole(depth, lanes)] + [whole(*face)] * group + [whole(*half)] * 2,
        out_shape=[slot_shape, shape(depth, lanes)] + [shape(*face)] * group + [shape(*half)] * 2,
        scratch_shapes=[scratch(slots * width_y, width_z)] * 6
        + [
            scratch(ITERS, 2, depth, width_y, width_z),
            scratch(ITERS, cells, width_z),
            scratch(KINDS, depth, width_y, width_z),
            scratch(depth, width_y, width_z),
            scratch(8, KINDS, 8, width_z),
        ],
        compiler_params=LARGE,
        name="sweeps",
    )(
        meta,
        labels,
        speed,
        rate,
        storage,
        threshold,
        generation,
        incoming_occupation,
        generating_region_flag.reshape(cells, width_z),
        crystal_kelvin_given.reshape(cells, width_z),
        labels.reshape(1, slots),
    )
    faces, (keep, send) = rest[:group], rest[group:]

    by = 1
    other = swap(send, "mode", by)
    received = [faces[0]] + [swap(faces[index], "slab", index) for index in range(1, group)]
    while 2 * by < modes:
        by *= 2
        now = (modes // (2 * by), ITERS, all_x, lanes)
        keep, send = call(split_kernel, "density_split", [VMEM] * 2, [shape(*now)] * 2, keep, other)
        other = swap(send, "mode", by)
    piece = (slabs, ITERS, depth, lanes)
    first_matrix, second_matrix = call(
        functools.partial(matrices_kernel, depth),
        "heat_matrices",
        [SMEM] * 2,
        [shape(all_x + 4 * KINDS + 2 * depth, 2 * all_x), shape(2 * KINDS + depth, 2 * all_x)],
        meta,
        kinds,
    )
    composite, effective = call(
        functools.partial(compose_kernel, own, group),
        "compose",
        [SMEM] * 3 + [VMEM] * group,
        [shape(*face), shape(group, *face)],
        meta,
        floats,
        ints,
        *received,
        scratches=[scratch(group, *face)],
    )
    other, composite, floats, ints, kinds, sums, first_matrix, second_matrix = lax.optimization_barrier(
        (other, composite, floats, ints, kinds, sums, first_matrix, second_matrix)
    )
    composites = [composite] + [swap(composite, "slab", index * group) for index in range(1, groups)]
    (parts,) = call(functools.partial(parts_kernel, depth), "density_parts", [VMEM] * 2, [shape(*piece)], keep, other)
    summed = lax.all_to_all(parts, "slab", 0, 0)
    summed, composites = lax.optimization_barrier((summed, composites))

    entering = call(
        functools.partial(enter_kernel, own, group, groups, depth),
        "enter",
        [SMEM] * 3 + [VMEM] * (1 + groups),
        [shape(*face)] * group,
        meta,
        floats,
        ints,
        effective,
        *composites,
        scratches=[scratch(groups, *face), scratch(group, *face)],
    )
    copies, late = call(
        totals_kernel,
        "density_totals",
        [SMEM] + [VMEM] * 2,
        [shape(slabs, 2, depth, lanes), shape(depth, lanes)],
        sums,
        summed,
        quarter,
    )
    gathered = lax.all_to_all(copies, "slab", 0, 0)
    entering = [entering[0]] + [swap(entering[index], "slab", index) for index in range(1, group)]

    pack_shape = shape(6 * KINDS + 4 * depth, lanes)
    (packed,) = call(
        functools.partial(kelvins_kernel, depth),
        "kelvins",
        [SMEM] * 2 + [VMEM] * 4,
        [pack_shape],
        meta,
        sums,
        gathered,
        late,
        first_matrix,
        second_matrix,
    )
    packs, order = [packed], [0]
    while by:
        packs = packs + [swap(pack, "mode", by) for pack in packs]
        order = order + [index ^ by for index in order]
        by //= 2

    warm, kelvin = pl.pallas_call(
        functools.partial(warm_kernel, (block, depth, width_y, width_z, modes), order),
        grid=(blocks,),
        in_specs=[SMEM] * 5 + [slot_block] + [whole(*pack_shape.shape)] * modes,
        out_specs=[slot_block, whole(cells, width_z)],
        out_shape=[slot_shape, shape(cells, width_z)],
        scratch_shapes=[scratch(2 * KINDS * width_y, width_z)] * 3
        + [scratch(2 * KINDS, depth, width_y, width_z)] * 2
        + [scratch(cells, width_z)] * 2
        + [scratch(width_y, depth, width_z)] * 2,
        compiler_params=PARAMS,
        name="warm",
    )(meta, floats, ints, kinds, sums, swept, *packs)
    energy = pl.pallas_call(
        functools.partial(inflow_kernel, (block, depth, own, group)),
        grid=(blocks,),
        in_specs=[SMEM] * 3 + [slot_block] + [whole(*face)] * group,
        out_specs=slot_block,
        out_shape=slot_shape,
        scratch_shapes=[scratch(group, *face)],
        compiler_params=PARAMS,
        name="inflow",
    )(meta, floats, ints, warm, *entering)
    return energy, kelvin.reshape(depth, width_y, width_z)


def solution(mesh):
    return jax.shard_map(
        local,
        mesh=mesh,
        in_specs=(
            P("mode", "slab", None, None),
            P("slab", None, None),
            P("slab", None, None),
            P("mode"),
            P(),
            P(),
            P(),
            P(),
            P(),
        ),
        out_specs=(P("mode", "slab", None, None), P("slab", None, None)),
        check_vma=False,
    )
```

```python
import functools
import math

import jax
import jax.numpy as jnp
import numpy as np
from jax import lax
from jax.experimental import pallas as pl
from jax.experimental.pallas import tpu as pltpu
from jax.sharding import PartitionSpec as P

FREQ_GROUPS = 8
DIRS = 32
ITERS = 3
NEWTON = 4
PSEUDO_RATE = 0.03
GROUP = 4
COSINES = (np.float32(0.99995), np.float32(0.9999))

SELF, UPY, UPZ, RATIO, WALL, FULL, FULL_N, FULL_T, FULL_GROUP, WARM = range(10)
FORWARD, SHIFT_Y, SHIFT_Z, EDGE_Y, KIND = range(5)
THERM, QUART, HEAT, DECAY, STAY, AROUND = range(6)
KINDS = 2 * FREQ_GROUPS
SLAB, MODE = range(2)

SMEM = pl.BlockSpec(memory_space=pltpu.SMEM)
VMEM = pl.BlockSpec(memory_space=pltpu.VMEM)
PARAMS = pltpu.CompilerParams(vmem_limit_bytes=48 * 1024 * 1024)
LARGE = pltpu.CompilerParams(vmem_limit_bytes=62 * 1024 * 1024)
ACROSS = math.cos(math.pi / 8) + math.sin(math.pi / 8)


def diagonal_of(speed, rate, cosine):
    sine = jnp.sqrt(1.0 - cosine * cosine)
    return speed * (cosine + sine * np.float32(ACROSS)) + rate + PSEUDO_RATE


def slot_tables(labels, speed, rate, storage, threshold, generation, slab, slabs, depth, width_z):
    band = labels // DIRS
    direction = labels % DIRS
    of_band = (band[None, :] == jnp.arange(FREQ_GROUPS, dtype=jnp.int32)[:, None]).astype(jnp.float32)
    speed, rate, storage, threshold, generation = (
        jnp.sum(of_band * value[:, None], axis=0) for value in (speed, rate, storage, threshold, generation)
    )
    polar = direction % 4
    outer = (polar == 0) | (polar == 3)
    forward = polar < 2
    cosine = jnp.where(outer, COSINES[0], COSINES[1])
    sine = jnp.sqrt(1.0 - cosine * cosine)
    azimuth = ((direction // 4).astype(jnp.float32) + 0.5) * (2.0 * math.pi / (DIRS // 4))
    vy = speed * sine * jnp.cos(azimuth)
    vz = speed * sine * jnp.sin(azimuth)
    diagonal = diagonal_of(speed, rate, cosine)
    ratio = speed * cosine / diagonal
    full = lax.integer_pow(ratio, depth)
    at_wall = jnp.where(forward, slab == 0, slab == slabs - 1)
    wall = storage * (1.0 + 1.0 / (4.0 * threshold**3))
    floats = jnp.stack(
        [
            PSEUDO_RATE / diagonal,
            jnp.abs(vy) / diagonal,
            jnp.abs(vz) / diagonal,
            ratio,
            jnp.where(at_wall, wall, 0.0),
            full,
            depth * full,
            (depth * (depth + 1) // 2) * full,
            lax.integer_pow(full, GROUP),
            generation / diagonal,
        ]
    )
    ints = jnp.stack(
        [
            forward.astype(jnp.int32),
            jnp.where(vy > 0, 1, 7).astype(jnp.int32),
            jnp.where(vz > 0, 1, width_z - 1).astype(jnp.int32),
            jnp.where(vy > 0, 0, 7).astype(jnp.int32),
            2 * band + jnp.where(outer, 0, 1),
        ]
    )
    return floats, ints


def kind_table(speed, rate, storage, threshold, generation):
    rows = []
    for cosine in COSINES:
        diagonal = diagonal_of(speed, rate, cosine)
        therm = rate * storage / diagonal
        quart = therm / (4.0 * threshold**3)
        across = jnp.sqrt(1.0 - cosine * cosine) * np.float32(2.0 * ACROSS)
        rows.append(
            jnp.stack(
                [
                    therm,
                    quart,
                    generation / diagonal,
                    speed * cosine / diagonal,
                    (DIRS // 4) * PSEUDO_RATE / diagonal,
                    across * speed / diagonal,
                ]
            )
        )
    return jnp.stack(rows, axis=2).reshape(6, KINDS)


def matrices_kernel(depth, meta, kinds, first, second):
    cells = first.shape[1] // 2
    slab = meta[SLAB]
    sided = 2 * KINDS
    per_cell = (DIRS // 4) / DIRS

    def places(rows):
        column = lax.broadcasted_iota(jnp.int32, (rows, 2 * cells), 1)
        quart = column >= cells
        return jnp.where(quart, column - cells, column), quart

    def distance(rows, base):
        there, quart = places(rows)
        far = jnp.abs(lax.broadcasted_iota(jnp.int32, (rows, 2 * cells), 0) + base - there)
        return far.astype(jnp.float32), jnp.where(far == 0, 2.0, 1.0), quart

    full, twice_full, quart_full = distance(cells, 0)
    home, twice_home, quart_home = distance(depth, slab * depth)
    there, quart_row = places(1)
    gaps = [value.astype(jnp.float32) for value in (slab * depth - 1 - there, there - (slab + 1) * depth)]
    everywhere = jnp.zeros((cells, 2 * cells), jnp.float32)
    once = stay = around = jnp.zeros((depth, 2 * cells), jnp.float32)
    for kind in range(KINDS):
        therm, quart = kinds[THERM, kind], kinds[QUART, kind]
        slope = jnp.log(jnp.full((1, 2 * cells), kinds[DECAY, kind], jnp.float32))
        everywhere += jnp.where(quart_full, quart, therm) * (jnp.exp(full * slope) * twice_full)
        weight = jnp.where(quart_home, quart, therm) * (jnp.exp(home * slope) * twice_home)
        once += weight
        weight = weight * (home + 1.0)
        stay += kinds[STAY, kind] * weight
        around += kinds[AROUND, kind] * weight
        for side, gap in enumerate(gaps):
            weight = jnp.where(quart_row, quart, therm) * jnp.exp(jnp.maximum(gap, 0.0) * slope)
            weight = jnp.where(gap >= 0, weight, 0.0)
            at = kind + side * KINDS
            first[cells + at : cells + at + 1, :] = weight
            first[cells + sided + at : cells + sided + at + 1, :] = weight * (gap + 1.0)
            second[at : at + 1, :] = weight
    first[:cells, :] = everywhere * per_cell
    base = cells + 2 * sided
    first[base : base + depth, :] = stay * (1.0 / DIRS)
    first[base + depth :, :] = around * (1.0 / DIRS)
    second[sided:, :] = once * per_cell


def newton(density, kelvin, linear, quart):
    for _ in range(NEWTON):
        cube = kelvin * kelvin * kelvin
        residual = linear * kelvin + quart * (kelvin * cube) - density
        kelvin = kelvin - residual / (linear + 4.0 * quart * cube)
    return kelvin


def exact_dot(left, right):
    return jnp.dot(left, right, precision=lax.Precision.HIGHEST, preferred_element_type=jnp.float32)


def fourth(value):
    square = value * value
    return square * square


def add_up(values):
    while len(values) > 1:
        values = [a + b for a, b in zip(values[::2], values[1::2])]
    return values[0]


def stencil(low, high, c_self, c_y, c_z, shift_y, shift_z, at_edge):
    turned_low, turned_high = pltpu.roll(low, shift_y, 0), pltpu.roll(high, shift_y, 0)
    up_low = jnp.where(at_edge, turned_high, turned_low)
    up_high = jnp.where(at_edge, turned_low, turned_high)
    return (
        c_self * low + c_y * up_low + c_z * pltpu.roll(low, shift_z, 1),
        c_self * high + c_y * up_high + c_z * pltpu.roll(high, shift_z, 1),
    )


def course(ints, s, depth):
    forward = ints[FORWARD, s] == 1
    return jnp.where(forward, 0, depth - 1), jnp.where(forward, 1, -1)


def slot_stencil(floats, ints, s, row):
    at_edge = row == ints[EDGE_Y, s]
    c_self, c_y, c_z = floats[SELF, s], floats[UPY, s], floats[UPZ, s]
    shift_y, shift_z = ints[SHIFT_Y, s], ints[SHIFT_Z, s]
    return lambda low, high: stencil(low, high, c_self, c_y, c_z, shift_y, shift_z, at_edge)


def rows_of(s):
    at = pl.multiple_of(s * 16, 16)
    return pl.ds(at, 8), pl.ds(at + 8, 8)


K_SELF, K_LARGE, K_SMALL, K_RATIO, K_THERM, K_QUART, K_HEAT, K_WALL = range(8)


def fill_kinds(table, bands):
    speeds, rates, storages, thresholds, generations = bands
    for kind in range(KINDS):
        band, cosine = kind // 2, COSINES[kind % 2]
        sine = np.sqrt(np.float32(1.0) - cosine * cosine)
        speed, rate, storage, threshold, generation = (
            jnp.full((8, 128), ref[band], jnp.float32) for ref in (speeds, rates, storages, thresholds, generations)
        )
        inverse = 1.0 / (speed * float(cosine + sine * np.float32(ACROSS)) + rate + PSEUDO_RATE)
        quart = 1.0 / (4.0 * (threshold * threshold * threshold))
        across = speed * float(sine) * inverse
        therm = rate * storage * inverse
        rows = (
            PSEUDO_RATE * inverse,
            across * math.cos(math.pi / 8),
            across * math.sin(math.pi / 8),
            speed * float(cosine) * inverse,
            therm,
            therm * quart,
            generation * inverse,
            storage * (1.0 + quart),
        )
        for row, value in enumerate(rows):
            table[row, kind] = value


def sweeps_kernel(sizes, meta, labels, *refs):
    block, blocks, depth, width_y, slots, modes, group = sizes
    bands, refs = refs[:5], refs[5:]
    energy, flag, given, label_row, swept, quarter, *rest = refs
    faces, rest = rest[:group], rest[group:]
    keep, send, *planes, density, flat, sources, heat, table = rest
    out_one, turn_one, turn_two, out_two, turn_late, out_three = planes
    rows, own = width_y // modes, slots // group
    step = pl.program_id(0)
    slab, mode = meta[SLAB], meta[MODE]
    slabs = keep.shape[2] // depth

    @pl.when(step == 0)
    def _():
        fill_kinds(table, bands)
        for yy in range(rows):
            quarter[:, yy * 128 : (yy + 1) * 128] = given[pl.ds(mode * rows + yy, depth, stride=width_y), :]
        density[...] = jnp.zeros_like(density)

        def one_layer(x, carry):
            at = pl.multiple_of(x * 16, 16)
            for low in (0, 8):
                t = given[pl.ds(at + low, 8), :]
                power = fourth(t)
                hot = flag[pl.ds(at + low, 8), :].astype(jnp.float32)
                heat[x, low : low + 8, :] = hot
                for kind in range(KINDS):
                    value = table[K_THERM, kind] * t + table[K_QUART, kind] * power + table[K_HEAT, kind] * hot
                    sources[kind, x, low : low + 8, :] = value
            return carry

        lax.fori_loop(0, depth, one_layer, 0)

    row = lax.broadcasted_iota(jnp.int32, (8, 128), 0)

    def of_slot(i):
        s = step * block + i
        label = labels[s]
        polar, turn_of = label % 4, (label // 4) % 8
        forward = polar < 2
        kind = 2 * (label // DIRS) + jnp.where((polar == 0) | (polar == 3), 0, 1)
        right, up = (turn_of < 2) | (turn_of > 5), turn_of < 4
        wide = (turn_of % 4 == 0) | (turn_of % 4 == 3)
        start, stride = jnp.where(forward, 0, depth - 1), jnp.where(forward, 1, -1)
        at_wall = jnp.where(forward, slab == 0, slab == slabs - 1)
        c_self = table[K_SELF, kind]
        c_y = table[jnp.where(wide, K_LARGE, K_SMALL), kind]
        c_z = table[jnp.where(wide, K_SMALL, K_LARGE), kind]
        wall = jnp.where(at_wall, 1.0, 0.0) * table[K_WALL, kind]
        shift_y, shift_z = jnp.where(right, 1, 7), jnp.where(up, 1, 127)
        at_edge = row == jnp.where(right, 0, 7)
        apply = lambda low, high: stencil(low, high, c_self, c_y, c_z, shift_y, shift_z, at_edge)
        xs = [start + stride * j for j in range(depth)]
        return s, forward, kind, wall, apply, xs

    def one_pair(pair, carry):
        pair = [2 * pair, 2 * pair + 1]
        slots_of = [of_slot(i) for i in pair]
        layers = [[(energy[i, x, :8, :], energy[i, x, 8:, :]) for x in of[-1]] for i, of in zip(pair, slots_of)]
        lasts = [[], []]
        for turn in range(ITERS):
            for which, (s, forward, kind, wall, apply, xs) in enumerate(slots_of):
                ratio = table[K_RATIO, kind]
                warm = table[K_HEAT, kind] if turn else None
                total_low = total_high = wall
                for j, x in enumerate(xs):
                    low, high = apply(*layers[which][j])
                    if turn == 0:
                        low, high = low + sources[kind, x, :8, :], high + sources[kind, x, 8:, :]
                    else:
                        low, high = low + warm * heat[x, :8, :], high + warm * heat[x, 8:, :]
                    total_low = ratio * total_low + low
                    total_high = ratio * total_high + high
                    layers[which][j] = (total_low, total_high)
                lasts[which].append((total_low, total_high))
            for x in range(depth):
                for half, here in enumerate((slice(0, 8), slice(8, 16))):
                    values = [
                        jnp.where(of[1], layer[x][half], layer[depth - 1 - x][half]) for of, layer in zip(slots_of, layers)
                    ]
                    density[turn, x, here, :] += values[0] + values[1]
                    if turn == ITERS - 1:
                        for i, value in zip(pair, values):
                            swept[i, x, here, :] = value
        for (s, _, _, _, apply, _), last in zip(slots_of, lasts):
            turned = apply(*last[0])
            at_low, at_high = rows_of(s)
            values = (last[0], turned, apply(*turned), last[1], apply(*last[1]), last[2])
            for plane, (low, high) in zip(planes, values):
                plane[at_low, :] = low
                plane[at_high, :] = high
        return carry

    lax.fori_loop(0, block // 2, one_pair, 0)

    @pl.when(step == blocks - 1)
    def _():
        for by in range(group):
            at = pl.ds(pl.multiple_of(((slab % group) ^ by) * own * 16, 16), own * 16)
            for index, plane in enumerate((turn_two, turn_late, out_three)):
                faces[by][index] = plane[at, :]
        for turn in range(ITERS):
            for x in range(depth):
                flat[turn, x * 16 : x * 16 + 16, :] = density[turn, x]
        label = label_row[...]
        polar = label % 4
        kinds = 2 * (label // DIRS) + jnp.where((polar == 0) | (polar == 3), 0, 1)
        decay = jnp.ones((1, slots), jnp.float32)
        for kind in range(KINDS):
            decay = jnp.where(kinds == kind, table[K_RATIO, kind][:1, :slots], decay)
        x = lax.broadcasted_iota(jnp.int32, (slabs * depth, slots), 0)
        past = jnp.where(polar < 2, x - (slab * depth + depth - 1), slab * depth - x)
        n = past.astype(jnp.float32)
        weight = jnp.where(past > 0, jnp.exp(jnp.maximum(n, 0.0) * jnp.log(decay)), 0.0)
        weights = (weight, n * weight, (0.5 * n * (n + 1.0)) * weight)
        home = pl.ds(pl.multiple_of(slab * depth, 8), depth)
        for by in range(modes):
            ys = [(mode ^ by) * rows + yy for yy in range(rows)]
            pick = lambda plane, count: jnp.concatenate([plane[pl.ds(y, count, stride=width_y), :] for y in ys], axis=1)
            plain = exact_dot(weights[0], jnp.concatenate([pick(p, slots) for p in (out_one, out_two, out_three)], axis=1))
            once = exact_dot(weights[1], jnp.concatenate([pick(p, slots) for p in (turn_one, turn_late)], axis=1))
            twice = exact_dot(weights[2], pick(turn_two, slots))
            lanes = rows * 128
            target = (send if by % 2 else keep).at[by // 2]
            target[0] = plain[:, :lanes]
            target[1] = plain[:, lanes : 2 * lanes] + once[:, :lanes]
            target[2] = plain[:, 2 * lanes :] + once[:, lanes:] + twice
            for turn in range(ITERS):
                target[turn, home, :] += pick(flat.at[turn], depth)


def split_kernel(mine, other, keep, send):
    for index in range(mine.shape[0]):
        target = send if index % 2 else keep
        target[index // 2] = mine[index] + other[index]


def parts_kernel(depth, mine, other, parts):
    for turn in range(ITERS):
        total = mine[0, turn] + other[0, turn]
        for slab in range(parts.shape[0]):
            parts[slab, turn] = total[slab * depth : (slab + 1) * depth]


def totals_kernel(sums, parts, before, copies, late):
    slabs = parts.shape[0]
    one, two, three = (
        add_up([parts[slab, turn] for slab in range(slabs)]) * (1.0 / DIRS) for turn in range(ITERS)
    )
    late[...] = three
    kelvin = newton(one, before[...], sums[0], sums[1])
    for slab in range(slabs):
        copies[slab, 0] = kelvin
        copies[slab, 1] = two


def kelvins_kernel(depth, meta, sums, gathered, late, matrix_one, matrix_two, packed):
    slabs = gathered.shape[0]
    cells = slabs * depth
    one, two = (jnp.concatenate([gathered[slab, index] for slab in range(slabs)], axis=0) for index in range(2))
    first = exact_dot(matrix_one[...], jnp.concatenate([one, fourth(one)], axis=0))
    two = newton(two + first[:cells], one, sums[0], sums[1])
    second = exact_dot(matrix_two[...], jnp.concatenate([two, fourth(two)], axis=0))
    sided = 2 * KINDS
    packed[: 2 * sided, :] = first[cells : cells + 2 * sided]
    packed[2 * sided : 3 * sided, :] = second[:sided]
    base = 3 * sided
    packed[base : base + depth, :] = gathered[meta[SLAB], 0]
    stay = first[cells + 2 * sided : cells + 2 * sided + depth]
    around = first[cells + 2 * sided + depth :]
    own = jnp.zeros_like(around)
    for slab in range(slabs):
        own = jnp.where(meta[SLAB] == slab, two[slab * depth : (slab + 1) * depth], own)
    packed[base + depth : base + 2 * depth, :] = own
    packed[base + 2 * depth : base + 3 * depth, :] = late[...] + stay + second[sided:]
    packed[base + 3 * depth :, :] = around


def compose_kernel(own, group, meta, floats, ints, *refs):
    received, (composite, effective, ordered) = refs[:group], refs[group:]
    place = meta[SLAB] % group
    for by in range(group):
        ordered[place ^ by] = received[by][...]

    def one_slot(i, carry):
        s = place * own + i
        start, stride = course(ints, s, group)
        full, full_n, full_t = floats[FULL, s], floats[FULL_N, s], floats[FULL_T, s]
        at = pl.ds(pl.multiple_of(i * 16, 16), 16)
        one = two = three = jnp.zeros((16, 128), jnp.float32)
        for j in range(group):
            k = start + stride * j
            three = full * three + full_n * two + full_t * one + ordered[k, 2, at, :]
            two = full * two + full_n * one + ordered[k, 1, at, :]
            one = full * one + ordered[k, 0, at, :]
        for index, value in enumerate((one, two, three)):
            composite[index, at, :] = value
        return carry

    lax.fori_loop(0, own, one_slot, 0, unroll=4)
    effective[...] = ordered[...]


def enter_kernel(own, group, groups, depth, meta, floats, ints, effective, *refs):
    composites, rest = refs[:groups], refs[groups:]
    outs, (ordered, entered) = rest[:group], rest[group:]
    slab = meta[SLAB]
    place, mine = slab % group, slab // group
    for by in range(groups):
        ordered[mine ^ by] = composites[by][...]
    span = depth * group

    def one_slot(i, carry):
        s = place * own + i
        start, stride = course(ints, s, group)
        begin, leap = course(ints, s, groups)
        ahead = jnp.where(ints[FORWARD, s] == 1, mine, groups - 1 - mine)
        at = pl.ds(pl.multiple_of(i * 16, 16), 16)

        def push(values, full, full_n, full_t, added):
            one, two, three = values
            return (
                full * one + added[0],
                full * two + full_n * one + added[1],
                full * three + full_n * two + full_t * one + added[2],
            )

        values = (jnp.zeros((16, 128), jnp.float32),) * 3
        whole = floats[FULL_GROUP, s]
        for g in range(groups - 1):
            index = begin + leap * g
            added = [ordered[index, plane, at, :] for plane in range(3)]
            later = push(values, whole, span * whole, (span * (span + 1) // 2) * whole, added)
            values = tuple(jnp.where(g < ahead, a, b) for a, b in zip(later, values))
        full, full_n, full_t = floats[FULL, s], floats[FULL_N, s], floats[FULL_T, s]
        for j in range(group):
            k = start + stride * j
            for plane in range(3):
                entered[k, plane, at, :] = values[plane]
            if j < group - 1:
                values = push(values, full, full_n, full_t, [effective[k, plane, at, :] for plane in range(3)])
        return carry

    lax.fori_loop(0, own, one_slot, 0, unroll=2)
    for by in range(group):
        outs[by][...] = entered[place ^ by]


def warm_kernel(sizes, order, meta, floats, ints, kinds, sums, swept, *refs):
    block, depth, width_y, width_z, modes = sizes
    packs, refs = refs[:modes], refs[modes:]
    energy, kelvin, enter_one, enter_long, enter_two, second, added, own_one, own_two, plain, around = refs
    step = pl.program_id(0)
    rows = width_y // modes

    @pl.when(step == 0)
    def _():
        sided, base = 2 * KINDS, 6 * KINDS
        for pack, by in zip(packs, order):
            for yy in range(rows):
                y, lane = (meta[MODE] ^ by) * rows + yy, slice(yy * 128, (yy + 1) * 128)
                for index, target in enumerate((enter_one, enter_long, enter_two)):
                    target[pl.ds(y, sided, stride=width_y), :] = pack[index * sided : (index + 1) * sided, lane]
                scattered = pl.ds(y, depth, stride=width_y)
                own_one[scattered, :] = pack[base : base + depth, lane]
                own_two[scattered, :] = pack[base + depth : base + 2 * depth, lane]
                plain[y] = pack[base + 2 * depth : base + 3 * depth, lane]
                around[y] = pack[base + 3 * depth :, lane]
        for y in range(width_y):
            here = around[y]
            near = around[(y - 1) % width_y] + around[(y + 1) % width_y]
            near = near + (pltpu.roll(here, 1, 1) + pltpu.roll(here, width_z - 1, 1))
            scattered = pl.ds(y, depth, stride=width_y)
            kelvin[scattered, :] = newton(plain[y] + near, own_two[scattered, :], sums[0], sums[1])

        def one_kind(kind, carry):
            therm, quart, decay = kinds[THERM, kind], kinds[QUART, kind], kinds[DECAY, kind]
            ones, twos = [], []
            for x in range(depth):
                here = slice(x * 16, x * 16 + 16)
                t, u = own_one[here, :], own_two[here, :]
                ones.append(therm * t + quart * fourth(t))
                twos.append(therm * u + quart * fourth(u))
            for back in (0, KINDS):
                at = pl.ds(pl.multiple_of((kind + back) * 16, 16), 16)
                once, twice, new = enter_one[at, :], enter_long[at, :], enter_two[at, :]
                for j in range(depth):
                    x = depth - 1 - j if back else j
                    once = decay * once + ones[x]
                    twice = decay * twice + once
                    new = decay * new + twos[x]
                    second[kind + back, x] = twice
                    added[kind + back, x] = new
            return carry

        lax.fori_loop(0, KINDS, one_kind, 0)

    row = lax.broadcasted_iota(jnp.int32, (8, 128), 0)

    def one_slot(i, carry):
        s = step * block + i
        sided = ints[KIND, s] + KINDS * (1 - ints[FORWARD, s])
        apply = slot_stencil(floats, ints, s, row)
        for x in range(depth):
            low, high = apply(second[sided, x, :8, :], second[sided, x, 8:, :])
            energy[i, x, :8, :] = swept[i, x, :8, :] + (low + added[sided, x, :8, :])
            energy[i, x, 8:, :] = swept[i, x, 8:, :] + (high + added[sided, x, 8:, :])
        return carry

    lax.fori_loop(0, block, one_slot, 0, unroll=2)


def inflow_kernel(sizes, meta, floats, ints, warm, *refs):
    block, depth, own, group = sizes
    received, (energy, ordered) = refs[:group], refs[group:]
    step = pl.program_id(0)

    @pl.when(step == 0)
    def _():
        for by in range(group):
            ordered[(meta[SLAB] % group) ^ by] = received[by][...]

    def one_slot(i, carry):
        s = step * block + i
        start, stride = course(ints, s, depth)
        ratio = floats[RATIO, s]
        at = pl.ds(pl.multiple_of((s % own) * 16, 16), 16)
        one, two, three = (ordered[s // own, plane, at, :] for plane in range(ITERS))
        for j in range(depth):
            x = start + stride * j
            one = ratio * one
            two = ratio * two + one
            three = ratio * three + two
            energy[i, x] = warm[i, x] + three
        return carry

    lax.fori_loop(0, block, one_slot, 0, unroll=4)


def local(incoming_occupation, crystal_kelvin_given, generating_region_flag, labels, speed, rate, storage, threshold, generation):
    slots, depth, width_y, width_z = incoming_occupation.shape
    slabs, modes = lax.axis_size("slab"), lax.axis_size("mode")
    group, groups = GROUP, slabs // GROUP
    own = slots // group
    lanes = width_y // modes * width_z
    block = 8
    blocks = slots // block
    cells, all_x = depth * width_y, slabs * depth
    face_rows = own * width_y
    slab = lax.axis_index("slab").astype(jnp.int32)
    meta = jnp.stack([slab, lax.axis_index("mode").astype(jnp.int32)])
    floats, ints = slot_tables(labels, speed, rate, storage, threshold, generation, slab, slabs, depth, width_z)
    kinds = kind_table(speed, rate, storage, threshold, generation)
    sums = jnp.stack([jnp.sum(storage), jnp.sum(storage / (4.0 * threshold**3))])

    def shape(*dims):
        return jax.ShapeDtypeStruct(dims, jnp.float32)

    def whole(*dims):
        return pl.BlockSpec(dims, lambda i: (0,) * len(dims))

    def scratch(*dims):
        return pltpu.VMEM(dims, jnp.float32)

    def swap(array, axis, by):
        return lax.ppermute(array, axis, [(i, i ^ by) for i in range(lax.axis_size(axis))])

    def call(kernel, name, in_specs, out_shapes, *args, scratches=()):
        return pl.pallas_call(
            kernel,
            in_specs=in_specs,
            out_specs=[VMEM] * len(out_shapes),
            out_shape=out_shapes,
            scratch_shapes=list(scratches),
            compiler_params=PARAMS,
            name=name,
        )(*args)

    slot_block = pl.BlockSpec((block, depth, width_y, width_z), lambda i: (i, 0, 0, 0))
    slot_shape = shape(slots, depth, width_y, width_z)
    face = (3, face_rows, width_z)
    half = (modes // 2, ITERS, all_x, lanes)
    swept, quarter, *rest = pl.pallas_call(
        functools.partial(sweeps_kernel, (block, blocks, depth, width_y, slots, modes, group)),
        grid=(blocks,),
        in_specs=[SMEM] * 7 + [slot_block, whole(cells, width_z), whole(cells, width_z), whole(1, slots)],
        out_specs=[slot_block, whole(depth, lanes)] + [whole(*face)] * group + [whole(*half)] * 2,
        out_shape=[slot_shape, shape(depth, lanes)] + [shape(*face)] * group + [shape(*half)] * 2,
        scratch_shapes=[scratch(slots * width_y, width_z)] * 6
        + [
            scratch(ITERS, depth, width_y, width_z),
            scratch(ITERS, cells, width_z),
            scratch(KINDS, depth, width_y, width_z),
            scratch(depth, width_y, width_z),
            scratch(8, KINDS, 8, width_z),
        ],
        compiler_params=LARGE,
        name="sweeps",
    )(
        meta,
        labels,
        speed,
        rate,
        storage,
        threshold,
        generation,
        incoming_occupation,
        generating_region_flag.reshape(cells, width_z),
        crystal_kelvin_given.reshape(cells, width_z),
        labels.reshape(1, slots),
    )
    faces, (keep, send) = rest[:group], rest[group:]

    by = 1
    other = swap(send, "mode", by)
    received = [faces[0]] + [swap(faces[index], "slab", index) for index in range(1, group)]
    while 2 * by < modes:
        by *= 2
        now = (modes // (2 * by), ITERS, all_x, lanes)
        keep, send = call(split_kernel, "density_split", [VMEM] * 2, [shape(*now)] * 2, keep, other)
        other = swap(send, "mode", by)
    piece = (slabs, ITERS, depth, lanes)
    first_matrix, second_matrix = call(
        functools.partial(matrices_kernel, depth),
        "heat_matrices",
        [SMEM] * 2,
        [shape(all_x + 4 * KINDS + 2 * depth, 2 * all_x), shape(2 * KINDS + depth, 2 * all_x)],
        meta,
        kinds,
    )
    composite, effective = call(
        functools.partial(compose_kernel, own, group),
        "compose",
        [SMEM] * 3 + [VMEM] * group,
        [shape(*face), shape(group, *face)],
        meta,
        floats,
        ints,
        *received,
        scratches=[scratch(group, *face)],
    )
    other, composite, floats, ints, kinds, sums, first_matrix, second_matrix = lax.optimization_barrier(
        (other, composite, floats, ints, kinds, sums, first_matrix, second_matrix)
    )
    composites = [composite] + [swap(composite, "slab", index * group) for index in range(1, groups)]
    (parts,) = call(functools.partial(parts_kernel, depth), "density_parts", [VMEM] * 2, [shape(*piece)], keep, other)
    summed = lax.all_to_all(parts, "slab", 0, 0)
    summed, composites = lax.optimization_barrier((summed, composites))

    entering = call(
        functools.partial(enter_kernel, own, group, groups, depth),
        "enter",
        [SMEM] * 3 + [VMEM] * (1 + groups),
        [shape(*face)] * group,
        meta,
        floats,
        ints,
        effective,
        *composites,
        scratches=[scratch(groups, *face), scratch(group, *face)],
    )
    copies, late = call(
        totals_kernel,
        "density_totals",
        [SMEM] + [VMEM] * 2,
        [shape(slabs, 2, depth, lanes), shape(depth, lanes)],
        sums,
        summed,
        quarter,
    )
    copies, entering = lax.optimization_barrier((copies, entering))
    gathered = lax.all_to_all(copies, "slab", 0, 0)
    entering = [entering[0]] + [swap(entering[index], "slab", index) for index in range(1, group)]
    gathered, entering[1:3] = lax.optimization_barrier((gathered, entering[1:3]))

    pack_shape = shape(6 * KINDS + 4 * depth, lanes)
    (packed,) = call(
        functools.partial(kelvins_kernel, depth),
        "kelvins",
        [SMEM] * 2 + [VMEM] * 4,
        [pack_shape],
        meta,
        sums,
        gathered,
        late,
        first_matrix,
        second_matrix,
    )
    packs, order = [packed], [0]
    while by:
        packs = packs + [swap(pack, "mode", by) for pack in packs]
        order = order + [index ^ by for index in order]
        by //= 2

    warm, kelvin = pl.pallas_call(
        functools.partial(warm_kernel, (block, depth, width_y, width_z, modes), order),
        grid=(blocks,),
        in_specs=[SMEM] * 5 + [slot_block] + [whole(*pack_shape.shape)] * modes,
        out_specs=[slot_block, whole(cells, width_z)],
        out_shape=[slot_shape, shape(cells, width_z)],
        scratch_shapes=[scratch(2 * KINDS * width_y, width_z)] * 3
        + [scratch(2 * KINDS, depth, width_y, width_z)] * 2
        + [scratch(cells, width_z)] * 2
        + [scratch(width_y, depth, width_z)] * 2,
        compiler_params=PARAMS,
        name="warm",
    )(meta, floats, ints, kinds, sums, swept, *packs)
    energy = pl.pallas_call(
        functools.partial(inflow_kernel, (block, depth, own, group)),
        grid=(blocks,),
        in_specs=[SMEM] * 3 + [slot_block] + [whole(*face)] * group,
        out_specs=slot_block,
        out_shape=slot_shape,
        scratch_shapes=[scratch(group, *face)],
        compiler_params=PARAMS,
        name="inflow",
    )(meta, floats, ints, warm, *entering)
    return energy, kelvin.reshape(depth, width_y, width_z)


def solution(mesh):
    return jax.shard_map(
        local,
        mesh=mesh,
        in_specs=(
            P("mode", "slab", None, None),
            P("slab", None, None),
            P("slab", None, None),
            P("mode"),
            P(),
            P(),
            P(),
            P(),
            P(),
        ),
        out_specs=(P("mode", "slab", None, None), P("slab", None, None)),
        check_vma=False,
    )
```

```python
import functools
import math

import jax
import jax.numpy as jnp
import numpy as np
from jax import lax
from jax.experimental import pallas as pl
from jax.experimental.pallas import tpu as pltpu
from jax.sharding import PartitionSpec as P

FREQ_GROUPS = 8
DIRS = 32
ITERS = 3
NEWTON = 4
PSEUDO_RATE = 0.03
GROUP = 4
COSINES = (np.float32(0.99995), np.float32(0.9999))

SELF, UPY, UPZ, RATIO, WALL, FULL, FULL_N, FULL_T, FULL_GROUP, WARM = range(10)
FORWARD, SHIFT_Y, SHIFT_Z, EDGE_Y, KIND = range(5)
THERM, QUART, HEAT, DECAY, STAY, AROUND = range(6)
KINDS = 2 * FREQ_GROUPS
SLAB, MODE = range(2)

SMEM = pl.BlockSpec(memory_space=pltpu.SMEM)
VMEM = pl.BlockSpec(memory_space=pltpu.VMEM)
PARAMS = pltpu.CompilerParams(vmem_limit_bytes=48 * 1024 * 1024)
LARGE = pltpu.CompilerParams(vmem_limit_bytes=62 * 1024 * 1024)
ACROSS = math.cos(math.pi / 8) + math.sin(math.pi / 8)


def diagonal_of(speed, rate, cosine):
    sine = jnp.sqrt(1.0 - cosine * cosine)
    return speed * (cosine + sine * np.float32(ACROSS)) + rate + PSEUDO_RATE


def slot_tables(labels, speed, rate, storage, threshold, generation, slab, slabs, depth, width_z):
    band = labels // DIRS
    direction = labels % DIRS
    of_band = (band[None, :] == jnp.arange(FREQ_GROUPS, dtype=jnp.int32)[:, None]).astype(jnp.float32)
    speed, rate, storage, threshold, generation = (
        jnp.sum(of_band * value[:, None], axis=0) for value in (speed, rate, storage, threshold, generation)
    )
    polar = direction % 4
    outer = (polar == 0) | (polar == 3)
    forward = polar < 2
    cosine = jnp.where(outer, COSINES[0], COSINES[1])
    sine = jnp.sqrt(1.0 - cosine * cosine)
    azimuth = ((direction // 4).astype(jnp.float32) + 0.5) * (2.0 * math.pi / (DIRS // 4))
    vy = speed * sine * jnp.cos(azimuth)
    vz = speed * sine * jnp.sin(azimuth)
    diagonal = diagonal_of(speed, rate, cosine)
    ratio = speed * cosine / diagonal
    full = lax.integer_pow(ratio, depth)
    at_wall = jnp.where(forward, slab == 0, slab == slabs - 1)
    wall = storage * (1.0 + 1.0 / (4.0 * threshold**3))
    floats = jnp.stack(
        [
            PSEUDO_RATE / diagonal,
            jnp.abs(vy) / diagonal,
            jnp.abs(vz) / diagonal,
            ratio,
            jnp.where(at_wall, wall, 0.0),
            full,
            depth * full,
            (depth * (depth + 1) // 2) * full,
            lax.integer_pow(full, GROUP),
            generation / diagonal,
        ]
    )
    ints = jnp.stack(
        [
            forward.astype(jnp.int32),
            jnp.where(vy > 0, 1, 7).astype(jnp.int32),
            jnp.where(vz > 0, 1, width_z - 1).astype(jnp.int32),
            jnp.where(vy > 0, 0, 7).astype(jnp.int32),
            2 * band + jnp.where(outer, 0, 1),
        ]
    )
    return floats, ints


def kind_table(speed, rate, storage, threshold, generation):
    rows = []
    for cosine in COSINES:
        diagonal = diagonal_of(speed, rate, cosine)
        therm = rate * storage / diagonal
        quart = therm / (4.0 * threshold**3)
        across = jnp.sqrt(1.0 - cosine * cosine) * np.float32(2.0 * ACROSS)
        rows.append(
            jnp.stack(
                [
                    therm,
                    quart,
                    generation / diagonal,
                    speed * cosine / diagonal,
                    (DIRS // 4) * PSEUDO_RATE / diagonal,
                    across * speed / diagonal,
                ]
            )
        )
    return jnp.stack(rows, axis=2).reshape(6, KINDS)


def matrices_kernel(depth, meta, kinds, first, second):
    cells = first.shape[1] // 2
    slab = meta[SLAB]
    sided = 2 * KINDS
    per_cell = (DIRS // 4) / DIRS

    def places(rows):
        column = lax.broadcasted_iota(jnp.int32, (rows, 2 * cells), 1)
        quart = column >= cells
        return jnp.where(quart, column - cells, column), quart

    def distance(rows, base):
        there, quart = places(rows)
        far = jnp.abs(lax.broadcasted_iota(jnp.int32, (rows, 2 * cells), 0) + base - there)
        return far.astype(jnp.float32), jnp.where(far == 0, 2.0, 1.0), quart

    full, twice_full, quart_full = distance(cells, 0)
    home, twice_home, quart_home = distance(depth, slab * depth)
    there, quart_row = places(1)
    gaps = [value.astype(jnp.float32) for value in (slab * depth - 1 - there, there - (slab + 1) * depth)]
    everywhere = jnp.zeros((cells, 2 * cells), jnp.float32)
    once = stay = around = jnp.zeros((depth, 2 * cells), jnp.float32)
    for kind in range(KINDS):
        therm, quart = kinds[THERM, kind], kinds[QUART, kind]
        slope = jnp.log(jnp.full((1, 2 * cells), kinds[DECAY, kind], jnp.float32))
        everywhere += jnp.where(quart_full, quart, therm) * (jnp.exp(full * slope) * twice_full)
        weight = jnp.where(quart_home, quart, therm) * (jnp.exp(home * slope) * twice_home)
        once += weight
        weight = weight * (home + 1.0)
        stay += kinds[STAY, kind] * weight
        around += kinds[AROUND, kind] * weight
        for side, gap in enumerate(gaps):
            weight = jnp.where(quart_row, quart, therm) * jnp.exp(jnp.maximum(gap, 0.0) * slope)
            weight = jnp.where(gap >= 0, weight, 0.0)
            at = kind + side * KINDS
            first[cells + at : cells + at + 1, :] = weight
            first[cells + sided + at : cells + sided + at + 1, :] = weight * (gap + 1.0)
            second[at : at + 1, :] = weight
    first[:cells, :] = everywhere * per_cell
    base = cells + 2 * sided
    first[base : base + depth, :] = stay * (1.0 / DIRS)
    first[base + depth :, :] = around * (1.0 / DIRS)
    second[sided:, :] = once * per_cell


def newton(density, kelvin, linear, quart):
    for _ in range(NEWTON):
        cube = kelvin * kelvin * kelvin
        residual = linear * kelvin + quart * (kelvin * cube) - density
        kelvin = kelvin - residual / (linear + 4.0 * quart * cube)
    return kelvin


def exact_dot(left, right):
    return jnp.dot(left, right, precision=lax.Precision.HIGHEST, preferred_element_type=jnp.float32)


def fourth(value):
    square = value * value
    return square * square


def add_up(values):
    while len(values) > 1:
        values = [a + b for a, b in zip(values[::2], values[1::2])]
    return values[0]


def stencil(low, high, c_self, c_y, c_z, shift_y, shift_z, at_edge):
    turned_low, turned_high = pltpu.roll(low, shift_y, 0), pltpu.roll(high, shift_y, 0)
    up_low = jnp.where(at_edge, turned_high, turned_low)
    up_high = jnp.where(at_edge, turned_low, turned_high)
    return (
        c_self * low + c_y * up_low + c_z * pltpu.roll(low, shift_z, 1),
        c_self * high + c_y * up_high + c_z * pltpu.roll(high, shift_z, 1),
    )


def course(ints, s, depth):
    forward = ints[FORWARD, s] == 1
    return jnp.where(forward, 0, depth - 1), jnp.where(forward, 1, -1)


def slot_stencil(floats, ints, s, row):
    at_edge = row == ints[EDGE_Y, s]
    c_self, c_y, c_z = floats[SELF, s], floats[UPY, s], floats[UPZ, s]
    shift_y, shift_z = ints[SHIFT_Y, s], ints[SHIFT_Z, s]
    return lambda low, high: stencil(low, high, c_self, c_y, c_z, shift_y, shift_z, at_edge)


def rows_of(s):
    at = pl.multiple_of(s * 16, 16)
    return pl.ds(at, 8), pl.ds(at + 8, 8)


K_SELF, K_LARGE, K_SMALL, K_RATIO, K_THERM, K_QUART, K_HEAT, K_WALL = range(8)


def fill_kinds(table, bands):
    speeds, rates, storages, thresholds, generations = bands
    for kind in range(KINDS):
        band, cosine = kind // 2, COSINES[kind % 2]
        sine = np.sqrt(np.float32(1.0) - cosine * cosine)
        speed, rate, storage, threshold, generation = (
            jnp.full((8, 128), ref[band], jnp.float32) for ref in (speeds, rates, storages, thresholds, generations)
        )
        inverse = 1.0 / (speed * float(cosine + sine * np.float32(ACROSS)) + rate + PSEUDO_RATE)
        quart = 1.0 / (4.0 * (threshold * threshold * threshold))
        across = speed * float(sine) * inverse
        therm = rate * storage * inverse
        rows = (
            PSEUDO_RATE * inverse,
            across * math.cos(math.pi / 8),
            across * math.sin(math.pi / 8),
            speed * float(cosine) * inverse,
            therm,
            therm * quart,
            generation * inverse,
            storage * (1.0 + quart),
        )
        for row, value in enumerate(rows):
            table[row, kind] = value


def sweeps_kernel(sizes, meta, labels, *refs):
    block, blocks, depth, width_y, slots, modes, group = sizes
    bands, refs = refs[:5], refs[5:]
    energy, flag, given, label_row, swept, quarter, *rest = refs
    faces, rest = rest[:group], rest[group:]
    keep, send, *planes, density, flat, sources, heat, table = rest
    out_one, turn_one, turn_two, out_two, turn_late, out_three = planes
    rows, own = width_y // modes, slots // group
    step = pl.program_id(0)
    slab, mode = meta[SLAB], meta[MODE]
    slabs = keep.shape[2] // depth

    @pl.when(step == 0)
    def _():
        fill_kinds(table, bands)
        for yy in range(rows):
            quarter[:, yy * 128 : (yy + 1) * 128] = given[pl.ds(mode * rows + yy, depth, stride=width_y), :]
        density[...] = jnp.zeros_like(density)

        def one_layer(x, carry):
            at = pl.multiple_of(x * 16, 16)
            for low in (0, 8):
                t = given[pl.ds(at + low, 8), :]
                power = fourth(t)
                hot = flag[pl.ds(at + low, 8), :].astype(jnp.float32)
                heat[x, low : low + 8, :] = hot
                for kind in range(KINDS):
                    value = table[K_THERM, kind] * t + table[K_QUART, kind] * power + table[K_HEAT, kind] * hot
                    sources[kind, x, low : low + 8, :] = value
            return carry

        lax.fori_loop(0, depth, one_layer, 0)

    row = lax.broadcasted_iota(jnp.int32, (8, 128), 0)

    def of_slot(i):
        s = step * block + i
        label = labels[s]
        polar, turn_of = label % 4, (label // 4) % 8
        forward = polar < 2
        kind = 2 * (label // DIRS) + jnp.where((polar == 0) | (polar == 3), 0, 1)
        right, up = (turn_of < 2) | (turn_of > 5), turn_of < 4
        wide = (turn_of % 4 == 0) | (turn_of % 4 == 3)
        start, stride = jnp.where(forward, 0, depth - 1), jnp.where(forward, 1, -1)
        at_wall = jnp.where(forward, slab == 0, slab == slabs - 1)
        c_self = table[K_SELF, kind]
        c_y = table[jnp.where(wide, K_LARGE, K_SMALL), kind]
        c_z = table[jnp.where(wide, K_SMALL, K_LARGE), kind]
        wall = jnp.where(at_wall, 1.0, 0.0) * table[K_WALL, kind]
        shift_y, shift_z = jnp.where(right, 1, 7), jnp.where(up, 1, 127)
        at_edge = row == jnp.where(right, 0, 7)
        apply = lambda low, high: stencil(low, high, c_self, c_y, c_z, shift_y, shift_z, at_edge)
        xs = [start + stride * j for j in range(depth)]
        return s, forward, kind, wall, apply, xs

    def one_pair(pair, carry):
        pair = [2 * pair, 2 * pair + 1]
        slots_of = [of_slot(i) for i in pair]
        layers = [[(energy[i, x, :8, :], energy[i, x, 8:, :]) for x in of[-1]] for i, of in zip(pair, slots_of)]
        lasts = [[], []]
        for turn in range(ITERS):
            for which, (s, forward, kind, wall, apply, xs) in enumerate(slots_of):
                ratio = table[K_RATIO, kind]
                warm = table[K_HEAT, kind] if turn else None
                total_low = total_high = wall
                for j, x in enumerate(xs):
                    low, high = apply(*layers[which][j])
                    if turn == 0:
                        low, high = low + sources[kind, x, :8, :], high + sources[kind, x, 8:, :]
                    else:
                        low, high = low + warm * heat[x, :8, :], high + warm * heat[x, 8:, :]
                    total_low = ratio * total_low + low
                    total_high = ratio * total_high + high
                    layers[which][j] = (total_low, total_high)
                lasts[which].append((total_low, total_high))
            for x in range(depth):
                for half, here in enumerate((slice(0, 8), slice(8, 16))):
                    values = [
                        jnp.where(of[1], layer[x][half], layer[depth - 1 - x][half]) for of, layer in zip(slots_of, layers)
                    ]
                    density[turn, x, here, :] += values[0] + values[1]
                    if turn == ITERS - 1:
                        for i, value in zip(pair, values):
                            swept[i, x, here, :] = value
        for (s, _, _, _, apply, _), last in zip(slots_of, lasts):
            turned = apply(*last[0])
            at_low, at_high = rows_of(s)
            values = (last[0], turned, apply(*turned), last[1], apply(*last[1]), last[2])
            for plane, (low, high) in zip(planes, values):
                plane[at_low, :] = low
                plane[at_high, :] = high
        return carry

    lax.fori_loop(0, block // 2, one_pair, 0)

    @pl.when(step == blocks - 1)
    def _():
        for by in range(group):
            at = pl.ds(pl.multiple_of(((slab % group) ^ by) * own * 16, 16), own * 16)
            for index, plane in enumerate((turn_two, turn_late, out_three)):
                faces[by][index] = plane[at, :]
        for turn in range(ITERS):
            for x in range(depth):
                flat[turn, x * 16 : x * 16 + 16, :] = density[turn, x]
        label = label_row[...]
        polar = label % 4
        kinds = 2 * (label // DIRS) + jnp.where((polar == 0) | (polar == 3), 0, 1)
        decay = jnp.ones((1, slots), jnp.float32)
        for kind in range(KINDS):
            decay = jnp.where(kinds == kind, table[K_RATIO, kind][:1, :slots], decay)
        x = lax.broadcasted_iota(jnp.int32, (slabs * depth, slots), 0)
        past = jnp.where(polar < 2, x - (slab * depth + depth - 1), slab * depth - x)
        n = past.astype(jnp.float32)
        weight = jnp.where(past > 0, jnp.exp(jnp.maximum(n, 0.0) * jnp.log(decay)), 0.0)
        weights = (weight, n * weight, (0.5 * n * (n + 1.0)) * weight)
        home = pl.ds(pl.multiple_of(slab * depth, 8), depth)
        for by in range(modes):
            ys = [(mode ^ by) * rows + yy for yy in range(rows)]
            pick = lambda plane, count: jnp.concatenate([plane[pl.ds(y, count, stride=width_y), :] for y in ys], axis=1)
            plain = exact_dot(weights[0], jnp.concatenate([pick(p, slots) for p in (out_one, out_two, out_three)], axis=1))
            once = exact_dot(weights[1], jnp.concatenate([pick(p, slots) for p in (turn_one, turn_late)], axis=1))
            twice = exact_dot(weights[2], pick(turn_two, slots))
            lanes = rows * 128
            target = (send if by % 2 else keep).at[by // 2]
            target[0] = plain[:, :lanes]
            target[1] = plain[:, lanes : 2 * lanes] + once[:, :lanes]
            target[2] = plain[:, 2 * lanes :] + once[:, lanes:] + twice
            for turn in range(ITERS):
                target[turn, home, :] += pick(flat.at[turn], depth)


def split_kernel(mine, other, keep, send):
    for index in range(mine.shape[0]):
        target = send if index % 2 else keep
        target[index // 2] = mine[index] + other[index]


def parts_kernel(depth, mine, other, parts):
    for turn in range(ITERS):
        total = mine[0, turn] + other[0, turn]
        for slab in range(parts.shape[0]):
            parts[slab, turn] = total[slab * depth : (slab + 1) * depth]


def totals_kernel(sums, parts, before, copies, late):
    slabs = parts.shape[0]
    one, two, three = (
        add_up([parts[slab, turn] for slab in range(slabs)]) * (1.0 / DIRS) for turn in range(ITERS)
    )
    late[...] = three
    kelvin = newton(one, before[...], sums[0], sums[1])
    for slab in range(slabs):
        copies[slab, 0] = kelvin
        copies[slab, 1] = two


def kelvins_kernel(depth, meta, sums, gathered, late, matrix_one, matrix_two, packed):
    slabs = gathered.shape[0]
    cells = slabs * depth
    one, two = (jnp.concatenate([gathered[slab, index] for slab in range(slabs)], axis=0) for index in range(2))
    first = exact_dot(matrix_one[...], jnp.concatenate([one, fourth(one)], axis=0))
    two = newton(two + first[:cells], one, sums[0], sums[1])
    second = exact_dot(matrix_two[...], jnp.concatenate([two, fourth(two)], axis=0))
    sided = 2 * KINDS
    packed[: 2 * sided, :] = first[cells : cells + 2 * sided]
    packed[2 * sided : 3 * sided, :] = second[:sided]
    base = 3 * sided
    packed[base : base + depth, :] = gathered[meta[SLAB], 0]
    stay = first[cells + 2 * sided : cells + 2 * sided + depth]
    around = first[cells + 2 * sided + depth :]
    own = jnp.zeros_like(around)
    for slab in range(slabs):
        own = jnp.where(meta[SLAB] == slab, two[slab * depth : (slab + 1) * depth], own)
    packed[base + depth : base + 2 * depth, :] = own
    packed[base + 2 * depth : base + 3 * depth, :] = late[...] + stay + second[sided:]
    packed[base + 3 * depth :, :] = around


def compose_kernel(own, group, meta, floats, ints, *refs):
    received, (first, others, effective, ordered) = refs[:group], refs[group:]
    place = meta[SLAB] % group
    for by in range(group):
        ordered[place ^ by] = received[by][...]

    def one_slot(i, carry):
        s = place * own + i
        start, stride = course(ints, s, group)
        full, full_n, full_t = floats[FULL, s], floats[FULL_N, s], floats[FULL_T, s]
        at = pl.ds(pl.multiple_of(i * 16, 16), 16)
        one = two = three = jnp.zeros((16, 128), jnp.float32)
        for j in range(group):
            k = start + stride * j
            three = full * three + full_n * two + full_t * one + ordered[k, 2, at, :]
            two = full * two + full_n * one + ordered[k, 1, at, :]
            one = full * one + ordered[k, 0, at, :]
        first[at, :] = one
        others[0, at, :] = two
        others[1, at, :] = three
        return carry

    lax.fori_loop(0, own, one_slot, 0, unroll=4)
    effective[...] = ordered[...]


def enter_kernel(own, group, groups, depth, meta, floats, ints, effective, *refs):
    firsts, others, rest = refs[:groups], refs[groups : 2 * groups], refs[2 * groups :]
    outs, (ordered, entered) = rest[:group], rest[group:]
    slab = meta[SLAB]
    place, mine = slab % group, slab // group
    for by in range(groups):
        ordered[mine ^ by, 0] = firsts[by][...]
        ordered[mine ^ by, 1:] = others[by][...]
    span = depth * group

    def one_slot(i, carry):
        s = place * own + i
        start, stride = course(ints, s, group)
        begin, leap = course(ints, s, groups)
        ahead = jnp.where(ints[FORWARD, s] == 1, mine, groups - 1 - mine)
        at = pl.ds(pl.multiple_of(i * 16, 16), 16)

        def push(values, full, full_n, full_t, added):
            one, two, three = values
            return (
                full * one + added[0],
                full * two + full_n * one + added[1],
                full * three + full_n * two + full_t * one + added[2],
            )

        values = (jnp.zeros((16, 128), jnp.float32),) * 3
        whole = floats[FULL_GROUP, s]
        for g in range(groups - 1):
            index = begin + leap * g
            added = [ordered[index, plane, at, :] for plane in range(3)]
            later = push(values, whole, span * whole, (span * (span + 1) // 2) * whole, added)
            values = tuple(jnp.where(g < ahead, a, b) for a, b in zip(later, values))
        full, full_n, full_t = floats[FULL, s], floats[FULL_N, s], floats[FULL_T, s]
        for j in range(group):
            k = start + stride * j
            for plane in range(3):
                entered[k, plane, at, :] = values[plane]
            if j < group - 1:
                values = push(values, full, full_n, full_t, [effective[k, plane, at, :] for plane in range(3)])
        return carry

    lax.fori_loop(0, own, one_slot, 0, unroll=2)
    for by in range(group):
        outs[by][...] = entered[place ^ by]


def warm_kernel(sizes, order, meta, floats, ints, kinds, sums, swept, *refs):
    block, depth, width_y, width_z, modes = sizes
    packs, refs = refs[:modes], refs[modes:]
    energy, kelvin, enter_one, enter_long, enter_two, second, added, own_one, own_two, plain, around = refs
    step = pl.program_id(0)
    rows = width_y // modes

    @pl.when(step == 0)
    def _():
        sided, base = 2 * KINDS, 6 * KINDS
        for pack, by in zip(packs, order):
            for yy in range(rows):
                y, lane = (meta[MODE] ^ by) * rows + yy, slice(yy * 128, (yy + 1) * 128)
                for index, target in enumerate((enter_one, enter_long, enter_two)):
                    target[pl.ds(y, sided, stride=width_y), :] = pack[index * sided : (index + 1) * sided, lane]
                scattered = pl.ds(y, depth, stride=width_y)
                own_one[scattered, :] = pack[base : base + depth, lane]
                own_two[scattered, :] = pack[base + depth : base + 2 * depth, lane]
                plain[y] = pack[base + 2 * depth : base + 3 * depth, lane]
                around[y] = pack[base + 3 * depth :, lane]
        for y in range(width_y):
            here = around[y]
            near = around[(y - 1) % width_y] + around[(y + 1) % width_y]
            near = near + (pltpu.roll(here, 1, 1) + pltpu.roll(here, width_z - 1, 1))
            scattered = pl.ds(y, depth, stride=width_y)
            kelvin[scattered, :] = newton(plain[y] + near, own_two[scattered, :], sums[0], sums[1])

        def one_kind(kind, carry):
            therm, quart, decay = kinds[THERM, kind], kinds[QUART, kind], kinds[DECAY, kind]
            ones, twos = [], []
            for x in range(depth):
                here = slice(x * 16, x * 16 + 16)
                t, u = own_one[here, :], own_two[here, :]
                ones.append(therm * t + quart * fourth(t))
                twos.append(therm * u + quart * fourth(u))
            for back in (0, KINDS):
                at = pl.ds(pl.multiple_of((kind + back) * 16, 16), 16)
                once, twice, new = enter_one[at, :], enter_long[at, :], enter_two[at, :]
                for j in range(depth):
                    x = depth - 1 - j if back else j
                    once = decay * once + ones[x]
                    twice = decay * twice + once
                    new = decay * new + twos[x]
                    second[kind + back, x] = twice
                    added[kind + back, x] = new
            return carry

        lax.fori_loop(0, KINDS, one_kind, 0)

    row = lax.broadcasted_iota(jnp.int32, (8, 128), 0)

    def one_slot(i, carry):
        s = step * block + i
        sided = ints[KIND, s] + KINDS * (1 - ints[FORWARD, s])
        apply = slot_stencil(floats, ints, s, row)
        for x in range(depth):
            low, high = apply(second[sided, x, :8, :], second[sided, x, 8:, :])
            energy[i, x, :8, :] = swept[i, x, :8, :] + (low + added[sided, x, :8, :])
            energy[i, x, 8:, :] = swept[i, x, 8:, :] + (high + added[sided, x, 8:, :])
        return carry

    lax.fori_loop(0, block, one_slot, 0, unroll=2)


def inflow_kernel(sizes, meta, floats, ints, warm, *refs):
    block, depth, own, group = sizes
    received, (energy, ordered) = refs[:group], refs[group:]
    step = pl.program_id(0)

    @pl.when(step == 0)
    def _():
        for by in range(group):
            ordered[(meta[SLAB] % group) ^ by] = received[by][...]

    def one_slot(i, carry):
        s = step * block + i
        start, stride = course(ints, s, depth)
        ratio = floats[RATIO, s]
        at = pl.ds(pl.multiple_of((s % own) * 16, 16), 16)
        one, two, three = (ordered[s // own, plane, at, :] for plane in range(ITERS))
        for j in range(depth):
            x = start + stride * j
            one = ratio * one
            two = ratio * two + one
            three = ratio * three + two
            energy[i, x] = warm[i, x] + three
        return carry

    lax.fori_loop(0, block, one_slot, 0, unroll=4)


def local(incoming_occupation, crystal_kelvin_given, generating_region_flag, labels, speed, rate, storage, threshold, generation):
    slots, depth, width_y, width_z = incoming_occupation.shape
    slabs, modes = lax.axis_size("slab"), lax.axis_size("mode")
    group, groups = GROUP, slabs // GROUP
    own = slots // group
    lanes = width_y // modes * width_z
    block = 8
    blocks = slots // block
    cells, all_x = depth * width_y, slabs * depth
    face_rows = own * width_y
    slab = lax.axis_index("slab").astype(jnp.int32)
    meta = jnp.stack([slab, lax.axis_index("mode").astype(jnp.int32)])
    floats, ints = slot_tables(labels, speed, rate, storage, threshold, generation, slab, slabs, depth, width_z)
    kinds = kind_table(speed, rate, storage, threshold, generation)
    sums = jnp.stack([jnp.sum(storage), jnp.sum(storage / (4.0 * threshold**3))])

    def shape(*dims):
        return jax.ShapeDtypeStruct(dims, jnp.float32)

    def whole(*dims):
        return pl.BlockSpec(dims, lambda i: (0,) * len(dims))

    def scratch(*dims):
        return pltpu.VMEM(dims, jnp.float32)

    def swap(array, axis, by):
        return lax.ppermute(array, axis, [(i, i ^ by) for i in range(lax.axis_size(axis))])

    def call(kernel, name, in_specs, out_shapes, *args, scratches=()):
        return pl.pallas_call(
            kernel,
            in_specs=in_specs,
            out_specs=[VMEM] * len(out_shapes),
            out_shape=out_shapes,
            scratch_shapes=list(scratches),
            compiler_params=PARAMS,
            name=name,
        )(*args)

    slot_block = pl.BlockSpec((block, depth, width_y, width_z), lambda i: (i, 0, 0, 0))
    slot_shape = shape(slots, depth, width_y, width_z)
    face = (3, face_rows, width_z)
    half = (modes // 2, ITERS, all_x, lanes)
    swept, quarter, *rest = pl.pallas_call(
        functools.partial(sweeps_kernel, (block, blocks, depth, width_y, slots, modes, group)),
        grid=(blocks,),
        in_specs=[SMEM] * 7 + [slot_block, whole(cells, width_z), whole(cells, width_z), whole(1, slots)],
        out_specs=[slot_block, whole(depth, lanes)] + [whole(*face)] * group + [whole(*half)] * 2,
        out_shape=[slot_shape, shape(depth, lanes)] + [shape(*face)] * group + [shape(*half)] * 2,
        scratch_shapes=[scratch(slots * width_y, width_z)] * 6
        + [
            scratch(ITERS, depth, width_y, width_z),
            scratch(ITERS, cells, width_z),
            scratch(KINDS, depth, width_y, width_z),
            scratch(depth, width_y, width_z),
            scratch(8, KINDS, 8, width_z),
        ],
        compiler_params=LARGE,
        name="sweeps",
    )(
        meta,
        labels,
        speed,
        rate,
        storage,
        threshold,
        generation,
        incoming_occupation,
        generating_region_flag.reshape(cells, width_z),
        crystal_kelvin_given.reshape(cells, width_z),
        labels.reshape(1, slots),
    )
    faces, (keep, send) = rest[:group], rest[group:]

    by = 1
    other = swap(send, "mode", by)
    received = [faces[0]] + [swap(faces[index], "slab", index) for index in range(1, group)]
    while 2 * by < modes:
        by *= 2
        now = (modes // (2 * by), ITERS, all_x, lanes)
        keep, send = call(split_kernel, "density_split", [VMEM] * 2, [shape(*now)] * 2, keep, other)
        other = swap(send, "mode", by)
    piece = (slabs, ITERS, depth, lanes)
    first_matrix, second_matrix = call(
        functools.partial(matrices_kernel, depth),
        "heat_matrices",
        [SMEM] * 2,
        [shape(all_x + 4 * KINDS + 2 * depth, 2 * all_x), shape(2 * KINDS + depth, 2 * all_x)],
        meta,
        kinds,
    )
    first, others, effective = call(
        functools.partial(compose_kernel, own, group),
        "compose",
        [SMEM] * 3 + [VMEM] * group,
        [shape(*face[1:]), shape(2, *face[1:]), shape(group, *face)],
        meta,
        floats,
        ints,
        *received,
        scratches=[scratch(group, *face)],
    )
    other, first, others, floats, ints, kinds, sums, first_matrix, second_matrix = lax.optimization_barrier(
        (other, first, others, floats, ints, kinds, sums, first_matrix, second_matrix)
    )
    firsts, others = (
        [value] + [swap(value, "slab", index * group) for index in range(1, groups)] for value in (first, others)
    )
    (parts,) = call(functools.partial(parts_kernel, depth), "density_parts", [VMEM] * 2, [shape(*piece)], keep, other)
    summed = lax.all_to_all(parts, "slab", 0, 0)
    summed, firsts = lax.optimization_barrier((summed, firsts))

    copies, late = call(
        totals_kernel,
        "density_totals",
        [SMEM] + [VMEM] * 2,
        [shape(slabs, 2, depth, lanes), shape(depth, lanes)],
        sums,
        summed,
        quarter,
    )
    gathered = lax.all_to_all(copies, "slab", 0, 0)
    entering = call(
        functools.partial(enter_kernel, own, group, groups, depth),
        "enter",
        [SMEM] * 3 + [VMEM] * (1 + 2 * groups),
        [shape(*face)] * group,
        meta,
        floats,
        ints,
        effective,
        *firsts,
        *others,
        scratches=[scratch(groups, *face), scratch(group, *face)],
    )
    entering = [entering[0]] + [swap(entering[index], "slab", index) for index in range(1, group)]

    pack_shape = shape(6 * KINDS + 4 * depth, lanes)
    (packed,) = call(
        functools.partial(kelvins_kernel, depth),
        "kelvins",
        [SMEM] * 2 + [VMEM] * 4,
        [pack_shape],
        meta,
        sums,
        gathered,
        late,
        first_matrix,
        second_matrix,
    )
    packs, order = [packed], [0]
    while by:
        packs = packs + [swap(pack, "mode", by) for pack in packs]
        order = order + [index ^ by for index in order]
        by //= 2

    warm, kelvin = pl.pallas_call(
        functools.partial(warm_kernel, (block, depth, width_y, width_z, modes), order),
        grid=(blocks,),
        in_specs=[SMEM] * 5 + [slot_block] + [whole(*pack_shape.shape)] * modes,
        out_specs=[slot_block, whole(cells, width_z)],
        out_shape=[slot_shape, shape(cells, width_z)],
        scratch_shapes=[scratch(2 * KINDS * width_y, width_z)] * 3
        + [scratch(2 * KINDS, depth, width_y, width_z)] * 2
        + [scratch(cells, width_z)] * 2
        + [scratch(width_y, depth, width_z)] * 2,
        compiler_params=PARAMS,
        name="warm",
    )(meta, floats, ints, kinds, sums, swept, *packs)
    energy = pl.pallas_call(
        functools.partial(inflow_kernel, (block, depth, own, group)),
        grid=(blocks,),
        in_specs=[SMEM] * 3 + [slot_block] + [whole(*face)] * group,
        out_specs=slot_block,
        out_shape=slot_shape,
        scratch_shapes=[scratch(group, *face)],
        compiler_params=PARAMS,
        name="inflow",
    )(meta, floats, ints, warm, *entering)
    return energy, kelvin.reshape(depth, width_y, width_z)


def solution(mesh):
    return jax.shard_map(
        local,
        mesh=mesh,
        in_specs=(
            P("mode", "slab", None, None),
            P("slab", None, None),
            P("slab", None, None),
            P("mode"),
            P(),
            P(),
            P(),
            P(),
            P(),
        ),
        out_specs=(P("mode", "slab", None, None), P("slab", None, None)),
        check_vma=False,
    )
```

```python
import functools
import math

import jax
import jax.numpy as jnp
import numpy as np
from jax import lax
from jax.experimental import pallas as pl
from jax.experimental.pallas import tpu as pltpu
from jax.sharding import PartitionSpec as P

FREQ_GROUPS = 8
DIRS = 32
ITERS = 3
NEWTON = 4
PSEUDO_RATE = 0.03
GROUP = 4
COSINES = (np.float32(0.99995), np.float32(0.9999))

SELF, UPY, UPZ, RATIO, WALL, FULL, FULL_N, FULL_T, FULL_GROUP, WARM = range(10)
FORWARD, SHIFT_Y, SHIFT_Z, EDGE_Y, KIND = range(5)
THERM, QUART, HEAT, DECAY, STAY, AROUND = range(6)
KINDS = 2 * FREQ_GROUPS
SLAB, MODE = range(2)

SMEM = pl.BlockSpec(memory_space=pltpu.SMEM)
VMEM = pl.BlockSpec(memory_space=pltpu.VMEM)
PARAMS = pltpu.CompilerParams(vmem_limit_bytes=48 * 1024 * 1024)
LARGE = pltpu.CompilerParams(vmem_limit_bytes=62 * 1024 * 1024)
ACROSS = math.cos(math.pi / 8) + math.sin(math.pi / 8)


def diagonal_of(speed, rate, cosine):
    sine = jnp.sqrt(1.0 - cosine * cosine)
    return speed * (cosine + sine * np.float32(ACROSS)) + rate + PSEUDO_RATE


def slot_tables(labels, speed, rate, storage, threshold, generation, slab, slabs, depth, width_z):
    band = labels // DIRS
    direction = labels % DIRS
    of_band = (band[None, :] == jnp.arange(FREQ_GROUPS, dtype=jnp.int32)[:, None]).astype(jnp.float32)
    speed, rate, storage, threshold, generation = (
        jnp.sum(of_band * value[:, None], axis=0) for value in (speed, rate, storage, threshold, generation)
    )
    polar = direction % 4
    outer = (polar == 0) | (polar == 3)
    forward = polar < 2
    cosine = jnp.where(outer, COSINES[0], COSINES[1])
    sine = jnp.sqrt(1.0 - cosine * cosine)
    azimuth = ((direction // 4).astype(jnp.float32) + 0.5) * (2.0 * math.pi / (DIRS // 4))
    vy = speed * sine * jnp.cos(azimuth)
    vz = speed * sine * jnp.sin(azimuth)
    diagonal = diagonal_of(speed, rate, cosine)
    ratio = speed * cosine / diagonal
    full = lax.integer_pow(ratio, depth)
    at_wall = jnp.where(forward, slab == 0, slab == slabs - 1)
    wall = storage * (1.0 + 1.0 / (4.0 * threshold**3))
    floats = jnp.stack(
        [
            PSEUDO_RATE / diagonal,
            jnp.abs(vy) / diagonal,
            jnp.abs(vz) / diagonal,
            ratio,
            jnp.where(at_wall, wall, 0.0),
            full,
            depth * full,
            (depth * (depth + 1) // 2) * full,
            lax.integer_pow(full, GROUP),
            generation / diagonal,
        ]
    )
    ints = jnp.stack(
        [
            forward.astype(jnp.int32),
            jnp.where(vy > 0, 1, 7).astype(jnp.int32),
            jnp.where(vz > 0, 1, width_z - 1).astype(jnp.int32),
            jnp.where(vy > 0, 0, 7).astype(jnp.int32),
            2 * band + jnp.where(outer, 0, 1),
        ]
    )
    return floats, ints


def kind_table(speed, rate, storage, threshold, generation):
    rows = []
    for cosine in COSINES:
        diagonal = diagonal_of(speed, rate, cosine)
        therm = rate * storage / diagonal
        quart = therm / (4.0 * threshold**3)
        across = jnp.sqrt(1.0 - cosine * cosine) * np.float32(2.0 * ACROSS)
        rows.append(
            jnp.stack(
                [
                    therm,
                    quart,
                    generation / diagonal,
                    speed * cosine / diagonal,
                    (DIRS // 4) * PSEUDO_RATE / diagonal,
                    across * speed / diagonal,
                ]
            )
        )
    return jnp.stack(rows, axis=2).reshape(6, KINDS)


def matrices_kernel(depth, meta, kinds, first, second):
    cells = first.shape[1] // 2
    slab = meta[SLAB]
    sided = 2 * KINDS
    per_cell = (DIRS // 4) / DIRS

    def places(rows):
        column = lax.broadcasted_iota(jnp.int32, (rows, 2 * cells), 1)
        quart = column >= cells
        return jnp.where(quart, column - cells, column), quart

    def distance(rows, base):
        there, quart = places(rows)
        far = jnp.abs(lax.broadcasted_iota(jnp.int32, (rows, 2 * cells), 0) + base - there)
        return far.astype(jnp.float32), jnp.where(far == 0, 2.0, 1.0), quart

    full, twice_full, quart_full = distance(cells, 0)
    home, twice_home, quart_home = distance(depth, slab * depth)
    there, quart_row = places(1)
    gaps = [value.astype(jnp.float32) for value in (slab * depth - 1 - there, there - (slab + 1) * depth)]
    everywhere = jnp.zeros((cells, 2 * cells), jnp.float32)
    once = stay = around = jnp.zeros((depth, 2 * cells), jnp.float32)
    for kind in range(KINDS):
        therm, quart = kinds[THERM, kind], kinds[QUART, kind]
        slope = jnp.log(jnp.full((1, 2 * cells), kinds[DECAY, kind], jnp.float32))
        everywhere += jnp.where(quart_full, quart, therm) * (jnp.exp(full * slope) * twice_full)
        weight = jnp.where(quart_home, quart, therm) * (jnp.exp(home * slope) * twice_home)
        once += weight
        weight = weight * (home + 1.0)
        stay += kinds[STAY, kind] * weight
        around += kinds[AROUND, kind] * weight
        for side, gap in enumerate(gaps):
            weight = jnp.where(quart_row, quart, therm) * jnp.exp(jnp.maximum(gap, 0.0) * slope)
            weight = jnp.where(gap >= 0, weight, 0.0)
            at = kind + side * KINDS
            first[cells + at : cells + at + 1, :] = weight
            first[cells + sided + at : cells + sided + at + 1, :] = weight * (gap + 1.0)
            second[at : at + 1, :] = weight
    first[:cells, :] = everywhere * per_cell
    base = cells + 2 * sided
    first[base : base + depth, :] = stay * (1.0 / DIRS)
    first[base + depth :, :] = around * (1.0 / DIRS)
    second[sided:, :] = once * per_cell


def newton(density, kelvin, linear, quart):
    for _ in range(NEWTON):
        cube = kelvin * kelvin * kelvin
        residual = linear * kelvin + quart * (kelvin * cube) - density
        kelvin = kelvin - residual / (linear + 4.0 * quart * cube)
    return kelvin


def exact_dot(left, right):
    return jnp.dot(left, right, precision=lax.Precision.HIGHEST, preferred_element_type=jnp.float32)


def fourth(value):
    square = value * value
    return square * square


def add_up(values):
    while len(values) > 1:
        values = [a + b for a, b in zip(values[::2], values[1::2])]
    return values[0]


def stencil(low, high, c_self, c_y, c_z, shift_y, shift_z, at_edge):
    turned_low, turned_high = pltpu.roll(low, shift_y, 0), pltpu.roll(high, shift_y, 0)
    up_low = jnp.where(at_edge, turned_high, turned_low)
    up_high = jnp.where(at_edge, turned_low, turned_high)
    return (
        c_self * low + c_y * up_low + c_z * pltpu.roll(low, shift_z, 1),
        c_self * high + c_y * up_high + c_z * pltpu.roll(high, shift_z, 1),
    )


def course(ints, s, depth):
    forward = ints[FORWARD, s] == 1
    return jnp.where(forward, 0, depth - 1), jnp.where(forward, 1, -1)


def slot_stencil(floats, ints, s, row):
    at_edge = row == ints[EDGE_Y, s]
    c_self, c_y, c_z = floats[SELF, s], floats[UPY, s], floats[UPZ, s]
    shift_y, shift_z = ints[SHIFT_Y, s], ints[SHIFT_Z, s]
    return lambda low, high: stencil(low, high, c_self, c_y, c_z, shift_y, shift_z, at_edge)


def rows_of(s):
    at = pl.multiple_of(s * 16, 16)
    return pl.ds(at, 8), pl.ds(at + 8, 8)


K_SELF, K_LARGE, K_SMALL, K_RATIO, K_THERM, K_QUART, K_HEAT, K_WALL = range(8)


def fill_kinds(table, bands):
    speeds, rates, storages, thresholds, generations = bands
    for kind in range(KINDS):
        band, cosine = kind // 2, COSINES[kind % 2]
        sine = np.sqrt(np.float32(1.0) - cosine * cosine)
        speed, rate, storage, threshold, generation = (
            jnp.full((8, 128), ref[band], jnp.float32) for ref in (speeds, rates, storages, thresholds, generations)
        )
        inverse = 1.0 / (speed * float(cosine + sine * np.float32(ACROSS)) + rate + PSEUDO_RATE)
        quart = 1.0 / (4.0 * (threshold * threshold * threshold))
        across = speed * float(sine) * inverse
        therm = rate * storage * inverse
        rows = (
            PSEUDO_RATE * inverse,
            across * math.cos(math.pi / 8),
            across * math.sin(math.pi / 8),
            speed * float(cosine) * inverse,
            therm,
            therm * quart,
            generation * inverse,
            storage * (1.0 + quart),
        )
        for row, value in enumerate(rows):
            table[row, kind] = value


def sweeps_kernel(sizes, meta, labels, *refs):
    block, blocks, depth, width_y, slots, modes, group = sizes
    bands, refs = refs[:5], refs[5:]
    energy, flag, given, label_row, swept, quarter, *rest = refs
    faces, rest = rest[:group], rest[group:]
    keep, send, *planes, density, flat, sources, heat, table = rest
    out_one, turn_one, turn_two, out_two, turn_late, out_three = planes
    rows, own = width_y // modes, slots // group
    step = pl.program_id(0)
    slab, mode = meta[SLAB], meta[MODE]
    slabs = keep.shape[2] // depth

    @pl.when(step == 0)
    def _():
        fill_kinds(table, bands)
        for yy in range(rows):
            quarter[:, yy * 128 : (yy + 1) * 128] = given[pl.ds(mode * rows + yy, depth, stride=width_y), :]
        density[...] = jnp.zeros_like(density)

        def one_layer(x, carry):
            at = pl.multiple_of(x * 16, 16)
            for low in (0, 8):
                t = given[pl.ds(at + low, 8), :]
                power = fourth(t)
                hot = flag[pl.ds(at + low, 8), :].astype(jnp.float32)
                heat[x, low : low + 8, :] = hot
                for kind in range(KINDS):
                    value = table[K_THERM, kind] * t + table[K_QUART, kind] * power + table[K_HEAT, kind] * hot
                    sources[kind, x, low : low + 8, :] = value
            return carry

        lax.fori_loop(0, depth, one_layer, 0)

    row = lax.broadcasted_iota(jnp.int32, (8, 128), 0)

    def one_slot(i, carry):
        s = step * block + i
        label = labels[s]
        polar, turn_of = label % 4, (label // 4) % 8
        forward = polar < 2
        kind = 2 * (label // DIRS) + jnp.where((polar == 0) | (polar == 3), 0, 1)
        right, up = (turn_of < 2) | (turn_of > 5), turn_of < 4
        wide = (turn_of % 4 == 0) | (turn_of % 4 == 3)
        start, stride = jnp.where(forward, 0, depth - 1), jnp.where(forward, 1, -1)
        at_wall = jnp.where(forward, slab == 0, slab == slabs - 1)
        xs = [start + stride * j for j in range(depth)]

        def body(shift_y, shift_z):
            c_self, ratio, warm = table[K_SELF, kind], table[K_RATIO, kind], table[K_HEAT, kind]
            c_y = table[jnp.where(wide, K_LARGE, K_SMALL), kind]
            c_z = table[jnp.where(wide, K_SMALL, K_LARGE), kind]
            wall = jnp.where(at_wall, 1.0, 0.0) * table[K_WALL, kind]
            at_edge = row == (0 if shift_y == 1 else 7)
            apply = lambda low, high: stencil(low, high, c_self, c_y, c_z, shift_y, shift_z, at_edge)
            layers = [(energy[i, x, :8, :], energy[i, x, 8:, :]) for x in xs]
            last = []
            for turn in range(ITERS):
                total_low = total_high = wall
                for j, x in enumerate(xs):
                    low, high = apply(*layers[j])
                    if turn == 0:
                        low, high = low + sources[kind, x, :8, :], high + sources[kind, x, 8:, :]
                    else:
                        low, high = low + warm * heat[x, :8, :], high + warm * heat[x, 8:, :]
                    total_low = ratio * total_low + low
                    total_high = ratio * total_high + high
                    layers[j] = (total_low, total_high)
                last.append((total_low, total_high))
                for x in range(depth):
                    for half, here in enumerate((slice(0, 8), slice(8, 16))):
                        value = jnp.where(forward, layers[x][half], layers[depth - 1 - x][half])
                        density[turn, x, here, :] += value
                        if turn == ITERS - 1:
                            swept[i, x, here, :] = value
            turned = apply(*last[0])
            at_low, at_high = rows_of(s)
            values = (last[0], turned, apply(*turned), last[1], apply(*last[1]), last[2])
            for plane, (low, high) in zip(planes, values):
                plane[at_low, :] = low
                plane[at_high, :] = high

        for y_sign, shift_y in ((right, 1), (~right, 7)):
            for z_sign, shift_z in ((up, 1), (~up, 127)):
                pl.when(y_sign & z_sign)(functools.partial(body, shift_y, shift_z))
        return carry

    lax.fori_loop(0, block, one_slot, 0)

    @pl.when(step == blocks - 1)
    def _():
        for by in range(group):
            at = pl.ds(pl.multiple_of(((slab % group) ^ by) * own * 16, 16), own * 16)
            for index, plane in enumerate((turn_two, turn_late, out_three)):
                faces[by][index] = plane[at, :]
        for turn in range(ITERS):
            for x in range(depth):
                flat[turn, x * 16 : x * 16 + 16, :] = density[turn, x]
        label = label_row[...]
        polar = label % 4
        kinds = 2 * (label // DIRS) + jnp.where((polar == 0) | (polar == 3), 0, 1)
        decay = jnp.ones((1, slots), jnp.float32)
        for kind in range(KINDS):
            decay = jnp.where(kinds == kind, table[K_RATIO, kind][:1, :slots], decay)
        x = lax.broadcasted_iota(jnp.int32, (slabs * depth, slots), 0)
        past = jnp.where(polar < 2, x - (slab * depth + depth - 1), slab * depth - x)
        n = past.astype(jnp.float32)
        weight = jnp.where(past > 0, jnp.exp(jnp.maximum(n, 0.0) * jnp.log(decay)), 0.0)
        weights = (weight, n * weight, (0.5 * n * (n + 1.0)) * weight)
        home = pl.ds(pl.multiple_of(slab * depth, 8), depth)
        for by in range(modes):
            ys = [(mode ^ by) * rows + yy for yy in range(rows)]
            pick = lambda plane, count: jnp.concatenate([plane[pl.ds(y, count, stride=width_y), :] for y in ys], axis=1)
            plain = exact_dot(weights[0], jnp.concatenate([pick(p, slots) for p in (out_one, out_two, out_three)], axis=1))
            once = exact_dot(weights[1], jnp.concatenate([pick(p, slots) for p in (turn_one, turn_late)], axis=1))
            twice = exact_dot(weights[2], pick(turn_two, slots))
            lanes = rows * 128
            target = (send if by % 2 else keep).at[by // 2]
            target[0] = plain[:, :lanes]
            target[1] = plain[:, lanes : 2 * lanes] + once[:, :lanes]
            target[2] = plain[:, 2 * lanes :] + once[:, lanes:] + twice
            for turn in range(ITERS):
                target[turn, home, :] += pick(flat.at[turn], depth)


def split_kernel(mine, other, keep, send):
    for index in range(mine.shape[0]):
        target = send if index % 2 else keep
        target[index // 2] = mine[index] + other[index]


def parts_kernel(depth, mine, other, parts):
    for turn in range(ITERS):
        total = mine[0, turn] + other[0, turn]
        for slab in range(parts.shape[0]):
            parts[slab, turn] = total[slab * depth : (slab + 1) * depth]


def totals_kernel(sums, parts, before, copies, late):
    slabs = parts.shape[0]
    one, two, three = (
        add_up([parts[slab, turn] for slab in range(slabs)]) * (1.0 / DIRS) for turn in range(ITERS)
    )
    late[...] = three
    kelvin = newton(one, before[...], sums[0], sums[1])
    for slab in range(slabs):
        copies[slab, 0] = kelvin
        copies[slab, 1] = two


def kelvins_kernel(depth, meta, sums, gathered, late, matrix_one, matrix_two, packed):
    slabs = gathered.shape[0]
    cells = slabs * depth
    one, two = (jnp.concatenate([gathered[slab, index] for slab in range(slabs)], axis=0) for index in range(2))
    first = exact_dot(matrix_one[...], jnp.concatenate([one, fourth(one)], axis=0))
    two = newton(two + first[:cells], one, sums[0], sums[1])
    second = exact_dot(matrix_two[...], jnp.concatenate([two, fourth(two)], axis=0))
    sided = 2 * KINDS
    packed[: 2 * sided, :] = first[cells : cells + 2 * sided]
    packed[2 * sided : 3 * sided, :] = second[:sided]
    base = 3 * sided
    packed[base : base + depth, :] = gathered[meta[SLAB], 0]
    stay = first[cells + 2 * sided : cells + 2 * sided + depth]
    around = first[cells + 2 * sided + depth :]
    own = jnp.zeros_like(around)
    for slab in range(slabs):
        own = jnp.where(meta[SLAB] == slab, two[slab * depth : (slab + 1) * depth], own)
    packed[base + depth : base + 2 * depth, :] = own
    packed[base + 2 * depth : base + 3 * depth, :] = late[...] + stay + second[sided:]
    packed[base + 3 * depth :, :] = around


def compose_kernel(own, group, meta, floats, ints, *refs):
    received, (first, others, effective, ordered) = refs[:group], refs[group:]
    place = meta[SLAB] % group
    for by in range(group):
        ordered[place ^ by] = received[by][...]

    def one_slot(i, carry):
        s = place * own + i
        start, stride = course(ints, s, group)
        full, full_n, full_t = floats[FULL, s], floats[FULL_N, s], floats[FULL_T, s]
        at = pl.ds(pl.multiple_of(i * 16, 16), 16)
        one = two = three = jnp.zeros((16, 128), jnp.float32)
        for j in range(group):
            k = start + stride * j
            three = full * three + full_n * two + full_t * one + ordered[k, 2, at, :]
            two = full * two + full_n * one + ordered[k, 1, at, :]
            one = full * one + ordered[k, 0, at, :]
        first[at, :] = one
        others[0, at, :] = two
        others[1, at, :] = three
        return carry

    lax.fori_loop(0, own, one_slot, 0, unroll=4)
    effective[...] = ordered[...]


def enter_kernel(own, group, groups, depth, meta, floats, ints, effective, *refs):
    firsts, others, rest = refs[:groups], refs[groups : 2 * groups], refs[2 * groups :]
    outs, (ordered, entered) = rest[:group], rest[group:]
    slab = meta[SLAB]
    place, mine = slab % group, slab // group
    for by in range(groups):
        ordered[mine ^ by, 0] = firsts[by][...]
        ordered[mine ^ by, 1:] = others[by][...]
    span = depth * group

    def one_slot(i, carry):
        s = place * own + i
        start, stride = course(ints, s, group)
        begin, leap = course(ints, s, groups)
        ahead = jnp.where(ints[FORWARD, s] == 1, mine, groups - 1 - mine)
        at = pl.ds(pl.multiple_of(i * 16, 16), 16)

        def push(values, full, full_n, full_t, added):
            one, two, three = values
            return (
                full * one + added[0],
                full * two + full_n * one + added[1],
                full * three + full_n * two + full_t * one + added[2],
            )

        values = (jnp.zeros((16, 128), jnp.float32),) * 3
        whole = floats[FULL_GROUP, s]
        for g in range(groups - 1):
            index = begin + leap * g
            added = [ordered[index, plane, at, :] for plane in range(3)]
            later = push(values, whole, span * whole, (span * (span + 1) // 2) * whole, added)
            values = tuple(jnp.where(g < ahead, a, b) for a, b in zip(later, values))
        full, full_n, full_t = floats[FULL, s], floats[FULL_N, s], floats[FULL_T, s]
        for j in range(group):
            k = start + stride * j
            for plane in range(3):
                entered[k, plane, at, :] = values[plane]
            if j < group - 1:
                values = push(values, full, full_n, full_t, [effective[k, plane, at, :] for plane in range(3)])
        return carry

    lax.fori_loop(0, own, one_slot, 0, unroll=2)
    for by in range(group):
        outs[by][...] = entered[place ^ by]


def warm_kernel(sizes, order, meta, floats, ints, kinds, sums, swept, *refs):
    block, depth, width_y, width_z, modes = sizes
    packs, refs = refs[:modes], refs[modes:]
    energy, kelvin, enter_one, enter_long, enter_two, second, added, own_one, own_two, plain, around = refs
    step = pl.program_id(0)
    rows = width_y // modes

    @pl.when(step == 0)
    def _():
        sided, base = 2 * KINDS, 6 * KINDS
        for pack, by in zip(packs, order):
            for yy in range(rows):
                y, lane = (meta[MODE] ^ by) * rows + yy, slice(yy * 128, (yy + 1) * 128)
                for index, target in enumerate((enter_one, enter_long, enter_two)):
                    target[pl.ds(y, sided, stride=width_y), :] = pack[index * sided : (index + 1) * sided, lane]
                scattered = pl.ds(y, depth, stride=width_y)
                own_one[scattered, :] = pack[base : base + depth, lane]
                own_two[scattered, :] = pack[base + depth : base + 2 * depth, lane]
                plain[y] = pack[base + 2 * depth : base + 3 * depth, lane]
                around[y] = pack[base + 3 * depth :, lane]
        for y in range(width_y):
            here = around[y]
            near = around[(y - 1) % width_y] + around[(y + 1) % width_y]
            near = near + (pltpu.roll(here, 1, 1) + pltpu.roll(here, width_z - 1, 1))
            scattered = pl.ds(y, depth, stride=width_y)
            kelvin[scattered, :] = newton(plain[y] + near, own_two[scattered, :], sums[0], sums[1])

        def one_kind(kind, carry):
            therm, quart, decay = kinds[THERM, kind], kinds[QUART, kind], kinds[DECAY, kind]
            ones, twos = [], []
            for x in range(depth):
                here = slice(x * 16, x * 16 + 16)
                t, u = own_one[here, :], own_two[here, :]
                ones.append(therm * t + quart * fourth(t))
                twos.append(therm * u + quart * fourth(u))
            for back in (0, KINDS):
                at = pl.ds(pl.multiple_of((kind + back) * 16, 16), 16)
                once, twice, new = enter_one[at, :], enter_long[at, :], enter_two[at, :]
                for j in range(depth):
                    x = depth - 1 - j if back else j
                    once = decay * once + ones[x]
                    twice = decay * twice + once
                    new = decay * new + twos[x]
                    second[kind + back, x] = twice
                    added[kind + back, x] = new
            return carry

        lax.fori_loop(0, KINDS, one_kind, 0)

    row = lax.broadcasted_iota(jnp.int32, (8, 128), 0)

    def one_slot(i, carry):
        s = step * block + i
        sided = ints[KIND, s] + KINDS * (1 - ints[FORWARD, s])
        apply = slot_stencil(floats, ints, s, row)
        for x in range(depth):
            low, high = apply(second[sided, x, :8, :], second[sided, x, 8:, :])
            energy[i, x, :8, :] = swept[i, x, :8, :] + (low + added[sided, x, :8, :])
            energy[i, x, 8:, :] = swept[i, x, 8:, :] + (high + added[sided, x, 8:, :])
        return carry

    lax.fori_loop(0, block, one_slot, 0, unroll=2)


def inflow_kernel(first, sizes, meta, floats, ints, warm, *refs):
    block, depth, own, group = sizes
    received, (energy, ordered) = refs[:-2], refs[-2:]
    step = pl.program_id(0)
    per_home = own // block
    home = (meta[SLAB] % group) ^ (step // per_home + first)

    @pl.when(step == 0)
    def _():
        for index, ref in enumerate(received):
            ordered[index] = ref[...]

    def one_slot(i, carry):
        inside = (step % per_home) * block + i
        s = home * own + inside
        start, stride = course(ints, s, depth)
        ratio = floats[RATIO, s]
        at = pl.ds(pl.multiple_of(inside * 16, 16), 16)
        one, two, three = (ordered[step // per_home, plane, at, :] for plane in range(ITERS))
        for j in range(depth):
            x = start + stride * j
            one = ratio * one
            two = ratio * two + one
            three = ratio * three + two
            energy[i, x] = warm[i, x] + three
        return carry

    lax.fori_loop(0, block, one_slot, 0, unroll=4)


def local(incoming_occupation, crystal_kelvin_given, generating_region_flag, labels, speed, rate, storage, threshold, generation):
    slots, depth, width_y, width_z = incoming_occupation.shape
    slabs, modes = lax.axis_size("slab"), lax.axis_size("mode")
    group, groups = GROUP, slabs // GROUP
    own = slots // group
    lanes = width_y // modes * width_z
    block = 8
    blocks = slots // block
    cells, all_x = depth * width_y, slabs * depth
    face_rows = own * width_y
    slab = lax.axis_index("slab").astype(jnp.int32)
    meta = jnp.stack([slab, lax.axis_index("mode").astype(jnp.int32)])
    floats, ints = slot_tables(labels, speed, rate, storage, threshold, generation, slab, slabs, depth, width_z)
    kinds = kind_table(speed, rate, storage, threshold, generation)
    sums = jnp.stack([jnp.sum(storage), jnp.sum(storage / (4.0 * threshold**3))])

    def shape(*dims):
        return jax.ShapeDtypeStruct(dims, jnp.float32)

    def whole(*dims):
        return pl.BlockSpec(dims, lambda i: (0,) * len(dims))

    def scratch(*dims):
        return pltpu.VMEM(dims, jnp.float32)

    def swap(array, axis, by):
        return lax.ppermute(array, axis, [(i, i ^ by) for i in range(lax.axis_size(axis))])

    def call(kernel, name, in_specs, out_shapes, *args, scratches=()):
        return pl.pallas_call(
            kernel,
            in_specs=in_specs,
            out_specs=[VMEM] * len(out_shapes),
            out_shape=out_shapes,
            scratch_shapes=list(scratches),
            compiler_params=PARAMS,
            name=name,
        )(*args)

    slot_block = pl.BlockSpec((block, depth, width_y, width_z), lambda i: (i, 0, 0, 0))
    slot_shape = shape(slots, depth, width_y, width_z)
    face = (3, face_rows, width_z)
    half = (modes // 2, ITERS, all_x, lanes)
    swept, quarter, *rest = pl.pallas_call(
        functools.partial(sweeps_kernel, (block, blocks, depth, width_y, slots, modes, group)),
        grid=(blocks,),
        in_specs=[SMEM] * 7 + [slot_block, whole(cells, width_z), whole(cells, width_z), whole(1, slots)],
        out_specs=[slot_block, whole(depth, lanes)] + [whole(*face)] * group + [whole(*half)] * 2,
        out_shape=[slot_shape, shape(depth, lanes)] + [shape(*face)] * group + [shape(*half)] * 2,
        scratch_shapes=[scratch(slots * width_y, width_z)] * 6
        + [
            scratch(ITERS, depth, width_y, width_z),
            scratch(ITERS, cells, width_z),
            scratch(KINDS, depth, width_y, width_z),
            scratch(depth, width_y, width_z),
            scratch(8, KINDS, 8, width_z),
        ],
        compiler_params=LARGE,
        name="sweeps",
    )(
        meta,
        labels,
        speed,
        rate,
        storage,
        threshold,
        generation,
        incoming_occupation,
        generating_region_flag.reshape(cells, width_z),
        crystal_kelvin_given.reshape(cells, width_z),
        labels.reshape(1, slots),
    )
    faces, (keep, send) = rest[:group], rest[group:]

    by = 1
    other = swap(send, "mode", by)
    received = [faces[0]] + [swap(faces[index], "slab", index) for index in range(1, group)]
    while 2 * by < modes:
        by *= 2
        now = (modes // (2 * by), ITERS, all_x, lanes)
        keep, send = call(split_kernel, "density_split", [VMEM] * 2, [shape(*now)] * 2, keep, other)
        other = swap(send, "mode", by)
    piece = (slabs, ITERS, depth, lanes)
    first_matrix, second_matrix = call(
        functools.partial(matrices_kernel, depth),
        "heat_matrices",
        [SMEM] * 2,
        [shape(all_x + 4 * KINDS + 2 * depth, 2 * all_x), shape(2 * KINDS + depth, 2 * all_x)],
        meta,
        kinds,
    )
    first, others, effective = call(
        functools.partial(compose_kernel, own, group),
        "compose",
        [SMEM] * 3 + [VMEM] * group,
        [shape(*face[1:]), shape(2, *face[1:]), shape(group, *face)],
        meta,
        floats,
        ints,
        *received,
        scratches=[scratch(group, *face)],
    )
    other, first, others, floats, ints, kinds, sums, first_matrix, second_matrix = lax.optimization_barrier(
        (other, first, others, floats, ints, kinds, sums, first_matrix, second_matrix)
    )
    firsts, others = (
        [value] + [swap(value, "slab", index * group) for index in range(1, groups)] for value in (first, others)
    )
    (parts,) = call(functools.partial(parts_kernel, depth), "density_parts", [VMEM] * 2, [shape(*piece)], keep, other)
    summed = lax.all_to_all(parts, "slab", 0, 0)
    summed, firsts = lax.optimization_barrier((summed, firsts))

    copies, late = call(
        totals_kernel,
        "density_totals",
        [SMEM] + [VMEM] * 2,
        [shape(slabs, 2, depth, lanes), shape(depth, lanes)],
        sums,
        summed,
        quarter,
    )
    gathered = lax.all_to_all(copies, "slab", 0, 0)
    entering = call(
        functools.partial(enter_kernel, own, group, groups, depth),
        "enter",
        [SMEM] * 3 + [VMEM] * (1 + 2 * groups),
        [shape(*face)] * group,
        meta,
        floats,
        ints,
        effective,
        *firsts,
        *others,
        scratches=[scratch(groups, *face), scratch(group, *face)],
    )
    entering = [entering[0]] + [swap(entering[index], "slab", index) for index in range(1, group)]

    pack_shape = shape(6 * KINDS + 4 * depth, lanes)
    (packed,) = call(
        functools.partial(kelvins_kernel, depth),
        "kelvins",
        [SMEM] * 2 + [VMEM] * 4,
        [pack_shape],
        meta,
        sums,
        gathered,
        late,
        first_matrix,
        second_matrix,
    )
    packs, order = [packed], [0]
    while by:
        packs = packs + [swap(pack, "mode", by) for pack in packs]
        order = order + [index ^ by for index in order]
        by //= 2

    warm, kelvin = pl.pallas_call(
        functools.partial(warm_kernel, (block, depth, width_y, width_z, modes), order),
        grid=(blocks,),
        in_specs=[SMEM] * 5 + [slot_block] + [whole(*pack_shape.shape)] * modes,
        out_specs=[slot_block, whole(cells, width_z)],
        out_shape=[slot_shape, shape(cells, width_z)],
        scratch_shapes=[scratch(2 * KINDS * width_y, width_z)] * 3
        + [scratch(2 * KINDS, depth, width_y, width_z)] * 2
        + [scratch(cells, width_z)] * 2
        + [scratch(width_y, depth, width_z)] * 2,
        compiler_params=PARAMS,
        name="warm",
    )(meta, floats, ints, kinds, sums, swept, *packs)
    def add_inflow(first, received, energy):
        per_home = own // block

        def place(i, meta, floats, ints):
            home = (meta[SLAB] % group) ^ (i // per_home + first)
            return home * per_home + i % per_home, 0, 0, 0

        home_block = pl.BlockSpec((block, depth, width_y, width_z), place)
        face_block = pl.BlockSpec(face, lambda i, *_: (0, 0, 0))
        return pl.pallas_call(
            functools.partial(inflow_kernel, first, (block, depth, own, group)),
            grid_spec=pltpu.PrefetchScalarGridSpec(
                num_scalar_prefetch=3,
                grid=(per_home * len(received),),
                in_specs=[home_block] + [face_block] * len(received),
                out_specs=home_block,
                scratch_shapes=[scratch(len(received), *face)],
            ),
            out_shape=slot_shape,
            input_output_aliases={3: 0},
            compiler_params=PARAMS,
            name=f"inflow_{first}",
        )(meta, floats, ints, energy, *received)

    energy = add_inflow(0, entering[:-1], warm)
    energy = add_inflow(group - 1, entering[-1:], energy)
    return energy, kelvin.reshape(depth, width_y, width_z)


def solution(mesh):
    return jax.shard_map(
        local,
        mesh=mesh,
        in_specs=(
            P("mode", "slab", None, None),
            P("slab", None, None),
            P("slab", None, None),
            P("mode"),
            P(),
            P(),
            P(),
            P(),
            P(),
        ),
        out_specs=(P("mode", "slab", None, None), P("slab", None, None)),
        check_vma=False,
    )
```

```python
import functools
import math

import jax
import jax.numpy as jnp
import numpy as np
from jax import lax
from jax.experimental import pallas as pl
from jax.experimental.pallas import tpu as pltpu
from jax.sharding import PartitionSpec as P

FREQ_GROUPS = 8
DIRS = 32
ITERS = 3
NEWTON = 4
PSEUDO_RATE = 0.03
GROUP = 4
COSINES = (np.float32(0.99995), np.float32(0.9999))

SELF, UPY, UPZ, RATIO, WALL, FULL, FULL_N, FULL_T, FULL_GROUP, WARM = range(10)
FORWARD, SHIFT_Y, SHIFT_Z, EDGE_Y, KIND = range(5)
THERM, QUART, HEAT, DECAY, STAY, AROUND = range(6)
KINDS = 2 * FREQ_GROUPS
SLAB, MODE = range(2)

SMEM = pl.BlockSpec(memory_space=pltpu.SMEM)
VMEM = pl.BlockSpec(memory_space=pltpu.VMEM)
PARAMS = pltpu.CompilerParams(vmem_limit_bytes=48 * 1024 * 1024)
LARGE = pltpu.CompilerParams(vmem_limit_bytes=62 * 1024 * 1024)
ACROSS = math.cos(math.pi / 8) + math.sin(math.pi / 8)


def diagonal_of(speed, rate, cosine):
    sine = jnp.sqrt(1.0 - cosine * cosine)
    return speed * (cosine + sine * np.float32(ACROSS)) + rate + PSEUDO_RATE


def slot_tables(labels, speed, rate, storage, threshold, generation, slab, slabs, depth, width_z):
    band = labels // DIRS
    direction = labels % DIRS
    of_band = (band[None, :] == jnp.arange(FREQ_GROUPS, dtype=jnp.int32)[:, None]).astype(jnp.float32)
    speed, rate, storage, threshold, generation = (
        jnp.sum(of_band * value[:, None], axis=0) for value in (speed, rate, storage, threshold, generation)
    )
    polar = direction % 4
    outer = (polar == 0) | (polar == 3)
    forward = polar < 2
    cosine = jnp.where(outer, COSINES[0], COSINES[1])
    sine = jnp.sqrt(1.0 - cosine * cosine)
    azimuth = ((direction // 4).astype(jnp.float32) + 0.5) * (2.0 * math.pi / (DIRS // 4))
    vy = speed * sine * jnp.cos(azimuth)
    vz = speed * sine * jnp.sin(azimuth)
    diagonal = diagonal_of(speed, rate, cosine)
    ratio = speed * cosine / diagonal
    full = lax.integer_pow(ratio, depth)
    at_wall = jnp.where(forward, slab == 0, slab == slabs - 1)
    wall = storage * (1.0 + 1.0 / (4.0 * threshold**3))
    floats = jnp.stack(
        [
            PSEUDO_RATE / diagonal,
            jnp.abs(vy) / diagonal,
            jnp.abs(vz) / diagonal,
            ratio,
            jnp.where(at_wall, wall, 0.0),
            full,
            depth * full,
            (depth * (depth + 1) // 2) * full,
            lax.integer_pow(full, GROUP),
            generation / diagonal,
        ]
    )
    ints = jnp.stack(
        [
            forward.astype(jnp.int32),
            jnp.where(vy > 0, 1, 7).astype(jnp.int32),
            jnp.where(vz > 0, 1, width_z - 1).astype(jnp.int32),
            jnp.where(vy > 0, 0, 7).astype(jnp.int32),
            2 * band + jnp.where(outer, 0, 1),
        ]
    )
    return floats, ints


def kind_table(speed, rate, storage, threshold, generation):
    rows = []
    for cosine in COSINES:
        diagonal = diagonal_of(speed, rate, cosine)
        therm = rate * storage / diagonal
        quart = therm / (4.0 * threshold**3)
        across = jnp.sqrt(1.0 - cosine * cosine) * np.float32(2.0 * ACROSS)
        rows.append(
            jnp.stack(
                [
                    therm,
                    quart,
                    generation / diagonal,
                    speed * cosine / diagonal,
                    (DIRS // 4) * PSEUDO_RATE / diagonal,
                    across * speed / diagonal,
                ]
            )
        )
    return jnp.stack(rows, axis=2).reshape(6, KINDS)


def matrices_kernel(depth, meta, kinds, first, second):
    cells = first.shape[1] // 2
    slab = meta[SLAB]
    sided = 2 * KINDS
    per_cell = (DIRS // 4) / DIRS

    def places(rows):
        column = lax.broadcasted_iota(jnp.int32, (rows, 2 * cells), 1)
        quart = column >= cells
        return jnp.where(quart, column - cells, column), quart

    def distance(rows, base):
        there, quart = places(rows)
        far = jnp.abs(lax.broadcasted_iota(jnp.int32, (rows, 2 * cells), 0) + base - there)
        return far.astype(jnp.float32), jnp.where(far == 0, 2.0, 1.0), quart

    full, twice_full, quart_full = distance(cells, 0)
    home, twice_home, quart_home = distance(depth, slab * depth)
    there, quart_row = places(1)
    gaps = [value.astype(jnp.float32) for value in (slab * depth - 1 - there, there - (slab + 1) * depth)]
    everywhere = jnp.zeros((cells, 2 * cells), jnp.float32)
    once = stay = around = jnp.zeros((depth, 2 * cells), jnp.float32)
    for kind in range(KINDS):
        therm, quart = kinds[THERM, kind], kinds[QUART, kind]
        slope = jnp.log(jnp.full((1, 2 * cells), kinds[DECAY, kind], jnp.float32))
        everywhere += jnp.where(quart_full, quart, therm) * (jnp.exp(full * slope) * twice_full)
        weight = jnp.where(quart_home, quart, therm) * (jnp.exp(home * slope) * twice_home)
        once += weight
        weight = weight * (home + 1.0)
        stay += kinds[STAY, kind] * weight
        around += kinds[AROUND, kind] * weight
        for side, gap in enumerate(gaps):
            weight = jnp.where(quart_row, quart, therm) * jnp.exp(jnp.maximum(gap, 0.0) * slope)
            weight = jnp.where(gap >= 0, weight, 0.0)
            at = kind + side * KINDS
            first[cells + at : cells + at + 1, :] = weight
            first[cells + sided + at : cells + sided + at + 1, :] = weight * (gap + 1.0)
            second[at : at + 1, :] = weight
    first[:cells, :] = everywhere * per_cell
    base = cells + 2 * sided
    first[base : base + depth, :] = stay * (1.0 / DIRS)
    first[base + depth :, :] = around * (1.0 / DIRS)
    second[sided:, :] = once * per_cell


def newton(density, kelvin, linear, quart):
    for _ in range(NEWTON):
        cube = kelvin * kelvin * kelvin
        residual = linear * kelvin + quart * (kelvin * cube) - density
        kelvin = kelvin - residual / (linear + 4.0 * quart * cube)
    return kelvin


def exact_dot(left, right):
    return jnp.dot(left, right, precision=lax.Precision.HIGHEST, preferred_element_type=jnp.float32)


def fourth(value):
    square = value * value
    return square * square


def add_up(values):
    while len(values) > 1:
        values = [a + b for a, b in zip(values[::2], values[1::2])]
    return values[0]


def stencil(low, high, c_self, c_y, c_z, shift_y, shift_z, at_edge):
    turned_low, turned_high = pltpu.roll(low, shift_y, 0), pltpu.roll(high, shift_y, 0)
    up_low = jnp.where(at_edge, turned_high, turned_low)
    up_high = jnp.where(at_edge, turned_low, turned_high)
    return (
        c_self * low + c_y * up_low + c_z * pltpu.roll(low, shift_z, 1),
        c_self * high + c_y * up_high + c_z * pltpu.roll(high, shift_z, 1),
    )


def course(ints, s, depth):
    forward = ints[FORWARD, s] == 1
    return jnp.where(forward, 0, depth - 1), jnp.where(forward, 1, -1)


def slot_stencil(floats, ints, s, row):
    at_edge = row == ints[EDGE_Y, s]
    c_self, c_y, c_z = floats[SELF, s], floats[UPY, s], floats[UPZ, s]
    shift_y, shift_z = ints[SHIFT_Y, s], ints[SHIFT_Z, s]
    return lambda low, high: stencil(low, high, c_self, c_y, c_z, shift_y, shift_z, at_edge)


def rows_of(s):
    at = pl.multiple_of(s * 16, 16)
    return pl.ds(at, 8), pl.ds(at + 8, 8)


K_SELF, K_LARGE, K_SMALL, K_RATIO, K_THERM, K_QUART, K_HEAT, K_WALL = range(8)


def fill_kinds(table, bands):
    speeds, rates, storages, thresholds, generations = bands
    for kind in range(KINDS):
        band, cosine = kind // 2, COSINES[kind % 2]
        sine = np.sqrt(np.float32(1.0) - cosine * cosine)
        speed, rate, storage, threshold, generation = (
            jnp.full((8, 128), ref[band], jnp.float32) for ref in (speeds, rates, storages, thresholds, generations)
        )
        inverse = 1.0 / (speed * float(cosine + sine * np.float32(ACROSS)) + rate + PSEUDO_RATE)
        quart = 1.0 / (4.0 * (threshold * threshold * threshold))
        across = speed * float(sine) * inverse
        therm = rate * storage * inverse
        rows = (
            PSEUDO_RATE * inverse,
            across * math.cos(math.pi / 8),
            across * math.sin(math.pi / 8),
            speed * float(cosine) * inverse,
            therm,
            therm * quart,
            generation * inverse,
            storage * (1.0 + quart),
        )
        for row, value in enumerate(rows):
            table[row, kind] = value


def sweeps_kernel(sizes, meta, labels, *refs):
    block, blocks, depth, width_y, slots, modes, group = sizes
    bands, refs = refs[:5], refs[5:]
    energy, flag, given, label_row, swept, quarter, *rest = refs
    faces, rest = rest[:group], rest[group:]
    keep, send, *planes, density, flat, sources, heat, table = rest
    out_one, turn_one, turn_two, out_two, turn_late, out_three = planes
    rows, own = width_y // modes, slots // group
    step = pl.program_id(0)
    slab, mode = meta[SLAB], meta[MODE]
    slabs = keep.shape[2] // depth

    @pl.when(step == 0)
    def _():
        fill_kinds(table, bands)
        for yy in range(rows):
            quarter[:, yy * 128 : (yy + 1) * 128] = given[pl.ds(mode * rows + yy, depth, stride=width_y), :]
        density[...] = jnp.zeros_like(density)

        def one_layer(x, carry):
            at = pl.multiple_of(x * 16, 16)
            for low in (0, 8):
                t = given[pl.ds(at + low, 8), :]
                power = fourth(t)
                hot = flag[pl.ds(at + low, 8), :].astype(jnp.float32)
                heat[x, low : low + 8, :] = hot
                for kind in range(KINDS):
                    value = table[K_THERM, kind] * t + table[K_QUART, kind] * power + table[K_HEAT, kind] * hot
                    sources[kind, x, low : low + 8, :] = value
            return carry

        lax.fori_loop(0, depth, one_layer, 0)

    row = lax.broadcasted_iota(jnp.int32, (8, 128), 0)

    def of_slot(i):
        s = step * block + i
        label = labels[s]
        polar, turn_of = label % 4, (label // 4) % 8
        forward = polar < 2
        kind = 2 * (label // DIRS) + jnp.where((polar == 0) | (polar == 3), 0, 1)
        right, up = (turn_of < 2) | (turn_of > 5), turn_of < 4
        wide = (turn_of % 4 == 0) | (turn_of % 4 == 3)
        start, stride = jnp.where(forward, 0, depth - 1), jnp.where(forward, 1, -1)
        at_wall = jnp.where(forward, slab == 0, slab == slabs - 1)
        c_self = table[K_SELF, kind]
        c_y = table[jnp.where(wide, K_LARGE, K_SMALL), kind]
        c_z = table[jnp.where(wide, K_SMALL, K_LARGE), kind]
        wall = jnp.where(at_wall, 1.0, 0.0) * table[K_WALL, kind]
        shift_y, shift_z = jnp.where(right, 1, 7), jnp.where(up, 1, 127)
        at_edge = row == jnp.where(right, 0, 7)
        apply = lambda low, high: stencil(low, high, c_self, c_y, c_z, shift_y, shift_z, at_edge)
        xs = [start + stride * j for j in range(depth)]
        return s, forward, kind, wall, apply, xs

    def one_pair(pair, carry):
        pair = [2 * pair, 2 * pair + 1]
        slots_of = [of_slot(i) for i in pair]
        layers = [[(energy[i, x, :8, :], energy[i, x, 8:, :]) for x in of[-1]] for i, of in zip(pair, slots_of)]
        lasts = [[], []]
        for turn in range(ITERS):
            for which, (s, forward, kind, wall, apply, xs) in enumerate(slots_of):
                ratio = table[K_RATIO, kind]
                warm = table[K_HEAT, kind] if turn else None
                total_low = total_high = wall
                for j, x in enumerate(xs):
                    low, high = apply(*layers[which][j])
                    if turn == 0:
                        low, high = low + sources[kind, x, :8, :], high + sources[kind, x, 8:, :]
                    else:
                        low, high = low + warm * heat[x, :8, :], high + warm * heat[x, 8:, :]
                    total_low = ratio * total_low + low
                    total_high = ratio * total_high + high
                    layers[which][j] = (total_low, total_high)
                lasts[which].append((total_low, total_high))
            for x in range(depth):
                for half, here in enumerate((slice(0, 8), slice(8, 16))):
                    values = [
                        jnp.where(of[1], layer[x][half], layer[depth - 1 - x][half]) for of, layer in zip(slots_of, layers)
                    ]
                    density[turn, x, here, :] += values[0] + values[1]
                    if turn == ITERS - 1:
                        for i, value in zip(pair, values):
                            swept[i, x, here, :] = value
        for (s, _, _, _, apply, _), last in zip(slots_of, lasts):
            turned = apply(*last[0])
            at_low, at_high = rows_of(s)
            values = (last[0], turned, apply(*turned), last[1], apply(*last[1]), last[2])
            for plane, (low, high) in zip(planes, values):
                plane[at_low, :] = low
                plane[at_high, :] = high
        return carry

    lax.fori_loop(0, block // 2, one_pair, 0, unroll=2)

    @pl.when(step == blocks - 1)
    def _():
        for by in range(group):
            at = pl.ds(pl.multiple_of(((slab % group) ^ by) * own * 16, 16), own * 16)
            for index, plane in enumerate((turn_two, turn_late, out_three)):
                faces[by][index] = plane[at, :]
        for turn in range(ITERS):
            for x in range(depth):
                flat[turn, x * 16 : x * 16 + 16, :] = density[turn, x]
        label = label_row[...]
        polar = label % 4
        kinds = 2 * (label // DIRS) + jnp.where((polar == 0) | (polar == 3), 0, 1)
        decay = jnp.ones((1, slots), jnp.float32)
        for kind in range(KINDS):
            decay = jnp.where(kinds == kind, table[K_RATIO, kind][:1, :slots], decay)
        x = lax.broadcasted_iota(jnp.int32, (slabs * depth, slots), 0)
        past = jnp.where(polar < 2, x - (slab * depth + depth - 1), slab * depth - x)
        n = past.astype(jnp.float32)
        weight = jnp.where(past > 0, jnp.exp(jnp.maximum(n, 0.0) * jnp.log(decay)), 0.0)
        weights = (weight, n * weight, (0.5 * n * (n + 1.0)) * weight)
        home = pl.ds(pl.multiple_of(slab * depth, 8), depth)
        for by in range(modes):
            ys = [(mode ^ by) * rows + yy for yy in range(rows)]
            pick = lambda plane, count: jnp.concatenate([plane[pl.ds(y, count, stride=width_y), :] for y in ys], axis=1)
            plain = exact_dot(weights[0], jnp.concatenate([pick(p, slots) for p in (out_one, out_two, out_three)], axis=1))
            once = exact_dot(weights[1], jnp.concatenate([pick(p, slots) for p in (turn_one, turn_late)], axis=1))
            twice = exact_dot(weights[2], pick(turn_two, slots))
            lanes = rows * 128
            target = (send if by % 2 else keep).at[by // 2]
            target[0] = plain[:, :lanes]
            target[1] = plain[:, lanes : 2 * lanes] + once[:, :lanes]
            target[2] = plain[:, 2 * lanes :] + once[:, lanes:] + twice
            for turn in range(ITERS):
                target[turn, home, :] += pick(flat.at[turn], depth)


def split_kernel(mine, other, keep, send):
    for index in range(mine.shape[0]):
        target = send if index % 2 else keep
        target[index // 2] = mine[index] + other[index]


def parts_kernel(depth, mine, other, parts):
    for turn in range(ITERS):
        total = mine[0, turn] + other[0, turn]
        for slab in range(parts.shape[0]):
            parts[slab, turn] = total[slab * depth : (slab + 1) * depth]


def totals_kernel(sums, parts, before, copies, late):
    slabs = parts.shape[0]
    one, two, three = (
        add_up([parts[slab, turn] for slab in range(slabs)]) * (1.0 / DIRS) for turn in range(ITERS)
    )
    late[...] = three
    kelvin = newton(one, before[...], sums[0], sums[1])
    for slab in range(slabs):
        copies[slab, 0] = kelvin
        copies[slab, 1] = two


def kelvins_kernel(depth, meta, sums, gathered, late, matrix_one, matrix_two, packed):
    slabs = gathered.shape[0]
    cells = slabs * depth
    one, two = (jnp.concatenate([gathered[slab, index] for slab in range(slabs)], axis=0) for index in range(2))
    first = exact_dot(matrix_one[...], jnp.concatenate([one, fourth(one)], axis=0))
    two = newton(two + first[:cells], one, sums[0], sums[1])
    second = exact_dot(matrix_two[...], jnp.concatenate([two, fourth(two)], axis=0))
    sided = 2 * KINDS
    packed[: 2 * sided, :] = first[cells : cells + 2 * sided]
    packed[2 * sided : 3 * sided, :] = second[:sided]
    base = 3 * sided
    packed[base : base + depth, :] = gathered[meta[SLAB], 0]
    stay = first[cells + 2 * sided : cells + 2 * sided + depth]
    around = first[cells + 2 * sided + depth :]
    own = jnp.zeros_like(around)
    for slab in range(slabs):
        own = jnp.where(meta[SLAB] == slab, two[slab * depth : (slab + 1) * depth], own)
    packed[base + depth : base + 2 * depth, :] = own
    packed[base + 2 * depth : base + 3 * depth, :] = late[...] + stay + second[sided:]
    packed[base + 3 * depth :, :] = around


def compose_kernel(own, group, meta, floats, ints, *refs):
    received, (first, others, effective, ordered) = refs[:group], refs[group:]
    place = meta[SLAB] % group
    for by in range(group):
        ordered[place ^ by] = received[by][...]

    def one_slot(i, carry):
        s = place * own + i
        start, stride = course(ints, s, group)
        full, full_n, full_t = floats[FULL, s], floats[FULL_N, s], floats[FULL_T, s]
        at = pl.ds(pl.multiple_of(i * 16, 16), 16)
        one = two = three = jnp.zeros((16, 128), jnp.float32)
        for j in range(group):
            k = start + stride * j
            three = full * three + full_n * two + full_t * one + ordered[k, 2, at, :]
            two = full * two + full_n * one + ordered[k, 1, at, :]
            one = full * one + ordered[k, 0, at, :]
        first[at, :] = one
        others[0, at, :] = two
        others[1, at, :] = three
        return carry

    lax.fori_loop(0, own, one_slot, 0, unroll=4)
    effective[...] = ordered[...]


def enter_kernel(own, group, groups, depth, meta, floats, ints, effective, *refs):
    firsts, others, rest = refs[:groups], refs[groups : 2 * groups], refs[2 * groups :]
    outs, (ordered, entered) = rest[:group], rest[group:]
    slab = meta[SLAB]
    place, mine = slab % group, slab // group
    for by in range(groups):
        ordered[mine ^ by, 0] = firsts[by][...]
        ordered[mine ^ by, 1:] = others[by][...]
    span = depth * group

    def one_slot(i, carry):
        s = place * own + i
        start, stride = course(ints, s, group)
        begin, leap = course(ints, s, groups)
        ahead = jnp.where(ints[FORWARD, s] == 1, mine, groups - 1 - mine)
        at = pl.ds(pl.multiple_of(i * 16, 16), 16)

        def push(values, full, full_n, full_t, added):
            one, two, three = values
            return (
                full * one + added[0],
                full * two + full_n * one + added[1],
                full * three + full_n * two + full_t * one + added[2],
            )

        values = (jnp.zeros((16, 128), jnp.float32),) * 3
        whole = floats[FULL_GROUP, s]
        for g in range(groups - 1):
            index = begin + leap * g
            added = [ordered[index, plane, at, :] for plane in range(3)]
            later = push(values, whole, span * whole, (span * (span + 1) // 2) * whole, added)
            values = tuple(jnp.where(g < ahead, a, b) for a, b in zip(later, values))
        full, full_n, full_t = floats[FULL, s], floats[FULL_N, s], floats[FULL_T, s]
        for j in range(group):
            k = start + stride * j
            for plane in range(3):
                entered[k, plane, at, :] = values[plane]
            if j < group - 1:
                values = push(values, full, full_n, full_t, [effective[k, plane, at, :] for plane in range(3)])
        return carry

    lax.fori_loop(0, own, one_slot, 0, unroll=2)
    for by in range(group):
        outs[by][...] = entered[place ^ by]


def warm_kernel(sizes, order, meta, floats, ints, kinds, sums, swept, *refs):
    block, depth, width_y, width_z, modes = sizes
    packs, refs = refs[:modes], refs[modes:]
    energy, kelvin, enter_one, enter_long, enter_two, second, added, own_one, own_two, plain, around = refs
    step = pl.program_id(0)
    rows = width_y // modes

    @pl.when(step == 0)
    def _():
        sided, base = 2 * KINDS, 6 * KINDS
        for pack, by in zip(packs, order):
            for yy in range(rows):
                y, lane = (meta[MODE] ^ by) * rows + yy, slice(yy * 128, (yy + 1) * 128)
                for index, target in enumerate((enter_one, enter_long, enter_two)):
                    target[pl.ds(y, sided, stride=width_y), :] = pack[index * sided : (index + 1) * sided, lane]
                scattered = pl.ds(y, depth, stride=width_y)
                own_one[scattered, :] = pack[base : base + depth, lane]
                own_two[scattered, :] = pack[base + depth : base + 2 * depth, lane]
                plain[y] = pack[base + 2 * depth : base + 3 * depth, lane]
                around[y] = pack[base + 3 * depth :, lane]
        for y in range(width_y):
            here = around[y]
            near = around[(y - 1) % width_y] + around[(y + 1) % width_y]
            near = near + (pltpu.roll(here, 1, 1) + pltpu.roll(here, width_z - 1, 1))
            scattered = pl.ds(y, depth, stride=width_y)
            kelvin[scattered, :] = newton(plain[y] + near, own_two[scattered, :], sums[0], sums[1])

        def one_kind(kind, carry):
            therm, quart, decay = kinds[THERM, kind], kinds[QUART, kind], kinds[DECAY, kind]
            ones, twos = [], []
            for x in range(depth):
                here = slice(x * 16, x * 16 + 16)
                t, u = own_one[here, :], own_two[here, :]
                ones.append(therm * t + quart * fourth(t))
                twos.append(therm * u + quart * fourth(u))
            for back in (0, KINDS):
                at = pl.ds(pl.multiple_of((kind + back) * 16, 16), 16)
                once, twice, new = enter_one[at, :], enter_long[at, :], enter_two[at, :]
                for j in range(depth):
                    x = depth - 1 - j if back else j
                    once = decay * once + ones[x]
                    twice = decay * twice + once
                    new = decay * new + twos[x]
                    second[kind + back, x] = twice
                    added[kind + back, x] = new
            return carry

        lax.fori_loop(0, KINDS, one_kind, 0)

    row = lax.broadcasted_iota(jnp.int32, (8, 128), 0)

    def one_slot(i, carry):
        s = step * block + i
        sided = ints[KIND, s] + KINDS * (1 - ints[FORWARD, s])
        apply = slot_stencil(floats, ints, s, row)
        for x in range(depth):
            low, high = apply(second[sided, x, :8, :], second[sided, x, 8:, :])
            energy[i, x, :8, :] = swept[i, x, :8, :] + (low + added[sided, x, :8, :])
            energy[i, x, 8:, :] = swept[i, x, 8:, :] + (high + added[sided, x, 8:, :])
        return carry

    lax.fori_loop(0, block, one_slot, 0, unroll=2)


def inflow_kernel(sizes, meta, floats, ints, warm, *refs):
    block, depth, own, group = sizes
    received, (energy, ordered) = refs[:group], refs[group:]
    step = pl.program_id(0)

    @pl.when(step == 0)
    def _():
        for by in range(group):
            ordered[(meta[SLAB] % group) ^ by] = received[by][...]

    def one_slot(i, carry):
        s = step * block + i
        start, stride = course(ints, s, depth)
        ratio = floats[RATIO, s]
        at = pl.ds(pl.multiple_of((s % own) * 16, 16), 16)
        one, two, three = (ordered[s // own, plane, at, :] for plane in range(ITERS))
        for j in range(depth):
            x = start + stride * j
            one = ratio * one
            two = ratio * two + one
            three = ratio * three + two
            energy[i, x] = warm[i, x] + three
        return carry

    lax.fori_loop(0, block, one_slot, 0, unroll=4)


def local(incoming_occupation, crystal_kelvin_given, generating_region_flag, labels, speed, rate, storage, threshold, generation):
    slots, depth, width_y, width_z = incoming_occupation.shape
    slabs, modes = lax.axis_size("slab"), lax.axis_size("mode")
    group, groups = GROUP, slabs // GROUP
    own = slots // group
    lanes = width_y // modes * width_z
    block = 8
    blocks = slots // block
    cells, all_x = depth * width_y, slabs * depth
    face_rows = own * width_y
    slab = lax.axis_index("slab").astype(jnp.int32)
    meta = jnp.stack([slab, lax.axis_index("mode").astype(jnp.int32)])
    floats, ints = slot_tables(labels, speed, rate, storage, threshold, generation, slab, slabs, depth, width_z)
    kinds = kind_table(speed, rate, storage, threshold, generation)
    sums = jnp.stack([jnp.sum(storage), jnp.sum(storage / (4.0 * threshold**3))])

    def shape(*dims):
        return jax.ShapeDtypeStruct(dims, jnp.float32)

    def whole(*dims):
        return pl.BlockSpec(dims, lambda i: (0,) * len(dims))

    def scratch(*dims):
        return pltpu.VMEM(dims, jnp.float32)

    def swap(array, axis, by):
        return lax.ppermute(array, axis, [(i, i ^ by) for i in range(lax.axis_size(axis))])

    def call(kernel, name, in_specs, out_shapes, *args, scratches=()):
        return pl.pallas_call(
            kernel,
            in_specs=in_specs,
            out_specs=[VMEM] * len(out_shapes),
            out_shape=out_shapes,
            scratch_shapes=list(scratches),
            compiler_params=LARGE if name in ("density_parts", "density_totals", "enter", "kelvins") else PARAMS,
            name=name,
        )(*args)

    slot_block = pl.BlockSpec((block, depth, width_y, width_z), lambda i: (i, 0, 0, 0))
    slot_shape = shape(slots, depth, width_y, width_z)
    face = (3, face_rows, width_z)
    half = (modes // 2, ITERS, all_x, lanes)
    swept, quarter, *rest = pl.pallas_call(
        functools.partial(sweeps_kernel, (block, blocks, depth, width_y, slots, modes, group)),
        grid=(blocks,),
        in_specs=[SMEM] * 7 + [slot_block, whole(cells, width_z), whole(cells, width_z), whole(1, slots)],
        out_specs=[slot_block, whole(depth, lanes)] + [whole(*face)] * group + [whole(*half)] * 2,
        out_shape=[slot_shape, shape(depth, lanes)] + [shape(*face)] * group + [shape(*half)] * 2,
        scratch_shapes=[scratch(slots * width_y, width_z)] * 6
        + [
            scratch(ITERS, depth, width_y, width_z),
            scratch(ITERS, cells, width_z),
            scratch(KINDS, depth, width_y, width_z),
            scratch(depth, width_y, width_z),
            scratch(8, KINDS, 8, width_z),
        ],
        compiler_params=LARGE,
        name="sweeps",
    )(
        meta,
        labels,
        speed,
        rate,
        storage,
        threshold,
        generation,
        incoming_occupation,
        generating_region_flag.reshape(cells, width_z),
        crystal_kelvin_given.reshape(cells, width_z),
        labels.reshape(1, slots),
    )
    faces, (keep, send) = rest[:group], rest[group:]

    by = 1
    other = swap(send, "mode", by)
    received = [faces[0]] + [swap(faces[index], "slab", index) for index in range(1, group)]
    while 2 * by < modes:
        by *= 2
        now = (modes // (2 * by), ITERS, all_x, lanes)
        keep, send = call(split_kernel, "density_split", [VMEM] * 2, [shape(*now)] * 2, keep, other)
        other = swap(send, "mode", by)
    piece = (slabs, ITERS, depth, lanes)
    first_matrix, second_matrix = call(
        functools.partial(matrices_kernel, depth),
        "heat_matrices",
        [SMEM] * 2,
        [shape(all_x + 4 * KINDS + 2 * depth, 2 * all_x), shape(2 * KINDS + depth, 2 * all_x)],
        meta,
        kinds,
    )
    first, others, effective = call(
        functools.partial(compose_kernel, own, group),
        "compose",
        [SMEM] * 3 + [VMEM] * group,
        [shape(*face[1:]), shape(2, *face[1:]), shape(group, *face)],
        meta,
        floats,
        ints,
        *received,
        scratches=[scratch(group, *face)],
    )
    other, first, others, floats, ints, kinds, sums, first_matrix, second_matrix = lax.optimization_barrier(
        (other, first, others, floats, ints, kinds, sums, first_matrix, second_matrix)
    )
    firsts, others = (
        [value] + [swap(value, "slab", index * group) for index in range(1, groups)] for value in (first, others)
    )
    (parts,) = call(functools.partial(parts_kernel, depth), "density_parts", [VMEM] * 2, [shape(*piece)], keep, other)
    summed = lax.all_to_all(parts, "slab", 0, 0)
    summed, firsts = lax.optimization_barrier((summed, firsts))

    copies, late = call(
        totals_kernel,
        "density_totals",
        [SMEM] + [VMEM] * 2,
        [shape(slabs, 2, depth, lanes), shape(depth, lanes)],
        sums,
        summed,
        quarter,
    )
    gathered = lax.all_to_all(copies, "slab", 0, 0)
    entering = call(
        functools.partial(enter_kernel, own, group, groups, depth),
        "enter",
        [SMEM] * 3 + [VMEM] * (1 + 2 * groups),
        [shape(*face)] * group,
        meta,
        floats,
        ints,
        effective,
        *firsts,
        *others,
        scratches=[scratch(groups, *face), scratch(group, *face)],
    )
    entering = [entering[0]] + [swap(entering[index], "slab", index) for index in range(1, group)]

    pack_shape = shape(6 * KINDS + 4 * depth, lanes)
    (packed,) = call(
        functools.partial(kelvins_kernel, depth),
        "kelvins",
        [SMEM] * 2 + [VMEM] * 4,
        [pack_shape],
        meta,
        sums,
        gathered,
        late,
        first_matrix,
        second_matrix,
    )
    packs, order = [packed], [0]
    while by:
        packs = packs + [swap(pack, "mode", by) for pack in packs]
        order = order + [index ^ by for index in order]
        by //= 2

    warm, kelvin = pl.pallas_call(
        functools.partial(warm_kernel, (block, depth, width_y, width_z, modes), order),
        grid=(blocks,),
        in_specs=[SMEM] * 5 + [slot_block] + [whole(*pack_shape.shape)] * modes,
        out_specs=[slot_block, whole(cells, width_z)],
        out_shape=[slot_shape, shape(cells, width_z)],
        scratch_shapes=[scratch(2 * KINDS * width_y, width_z)] * 3
        + [scratch(2 * KINDS, depth, width_y, width_z)] * 2
        + [scratch(cells, width_z)] * 2
        + [scratch(width_y, depth, width_z)] * 2,
        compiler_params=PARAMS,
        name="warm",
    )(meta, floats, ints, kinds, sums, swept, *packs)
    energy = pl.pallas_call(
        functools.partial(inflow_kernel, (block, depth, own, group)),
        grid=(blocks,),
        in_specs=[SMEM] * 3 + [slot_block] + [whole(*face)] * group,
        out_specs=slot_block,
        out_shape=slot_shape,
        scratch_shapes=[scratch(group, *face)],
        compiler_params=PARAMS,
        name="inflow",
    )(meta, floats, ints, warm, *entering)
    return energy, kelvin.reshape(depth, width_y, width_z)


def solution(mesh):
    return jax.shard_map(
        local,
        mesh=mesh,
        in_specs=(
            P("mode", "slab", None, None),
            P("slab", None, None),
            P("slab", None, None),
            P("mode"),
            P(),
            P(),
            P(),
            P(),
            P(),
        ),
        out_specs=(P("mode", "slab", None, None), P("slab", None, None)),
        check_vma=False,
    )
```

```python
import functools
import math

import jax
import jax.numpy as jnp
import numpy as np
from jax import lax
from jax.experimental import pallas as pl
from jax.experimental.pallas import tpu as pltpu
from jax.sharding import PartitionSpec as P

FREQ_GROUPS = 8
DIRS = 32
ITERS = 3
NEWTON = 4
PSEUDO_RATE = 0.03
GROUP = 4
COSINES = (np.float32(0.99995), np.float32(0.9999))

SELF, UPY, UPZ, RATIO, WALL, FULL, FULL_N, FULL_T, FULL_GROUP, WARM = range(10)
FORWARD, SHIFT_Y, SHIFT_Z, EDGE_Y, KIND = range(5)
THERM, QUART, HEAT, DECAY, STAY, AROUND = range(6)
KINDS = 2 * FREQ_GROUPS
SLAB, MODE = range(2)

SMEM = pl.BlockSpec(memory_space=pltpu.SMEM)
VMEM = pl.BlockSpec(memory_space=pltpu.VMEM)
PARAMS = pltpu.CompilerParams(vmem_limit_bytes=48 * 1024 * 1024)
LARGE = pltpu.CompilerParams(vmem_limit_bytes=62 * 1024 * 1024)
ACROSS = math.cos(math.pi / 8) + math.sin(math.pi / 8)


def diagonal_of(speed, rate, cosine):
    sine = jnp.sqrt(1.0 - cosine * cosine)
    return speed * (cosine + sine * np.float32(ACROSS)) + rate + PSEUDO_RATE


def slot_tables(labels, speed, rate, storage, threshold, generation, slab, slabs, depth, width_z):
    band = labels // DIRS
    direction = labels % DIRS
    of_band = (band[None, :] == jnp.arange(FREQ_GROUPS, dtype=jnp.int32)[:, None]).astype(jnp.float32)
    speed, rate, storage, threshold, generation = (
        jnp.sum(of_band * value[:, None], axis=0) for value in (speed, rate, storage, threshold, generation)
    )
    polar = direction % 4
    outer = (polar == 0) | (polar == 3)
    forward = polar < 2
    cosine = jnp.where(outer, COSINES[0], COSINES[1])
    sine = jnp.sqrt(1.0 - cosine * cosine)
    azimuth = ((direction // 4).astype(jnp.float32) + 0.5) * (2.0 * math.pi / (DIRS // 4))
    vy = speed * sine * jnp.cos(azimuth)
    vz = speed * sine * jnp.sin(azimuth)
    diagonal = diagonal_of(speed, rate, cosine)
    ratio = speed * cosine / diagonal
    full = lax.integer_pow(ratio, depth)
    at_wall = jnp.where(forward, slab == 0, slab == slabs - 1)
    wall = storage * (1.0 + 1.0 / (4.0 * threshold**3))
    floats = jnp.stack(
        [
            PSEUDO_RATE / diagonal,
            jnp.abs(vy) / diagonal,
            jnp.abs(vz) / diagonal,
            ratio,
            jnp.where(at_wall, wall, 0.0),
            full,
            depth * full,
            (depth * (depth + 1) // 2) * full,
            lax.integer_pow(full, GROUP),
            generation / diagonal,
        ]
    )
    ints = jnp.stack(
        [
            forward.astype(jnp.int32),
            jnp.where(vy > 0, 1, 7).astype(jnp.int32),
            jnp.where(vz > 0, 1, width_z - 1).astype(jnp.int32),
            jnp.where(vy > 0, 0, 7).astype(jnp.int32),
            2 * band + jnp.where(outer, 0, 1),
        ]
    )
    return floats, ints


def kind_table(speed, rate, storage, threshold, generation):
    rows = []
    for cosine in COSINES:
        diagonal = diagonal_of(speed, rate, cosine)
        therm = rate * storage / diagonal
        quart = therm / (4.0 * threshold**3)
        across = jnp.sqrt(1.0 - cosine * cosine) * np.float32(2.0 * ACROSS)
        rows.append(
            jnp.stack(
                [
                    therm,
                    quart,
                    generation / diagonal,
                    speed * cosine / diagonal,
                    (DIRS // 4) * PSEUDO_RATE / diagonal,
                    across * speed / diagonal,
                ]
            )
        )
    return jnp.stack(rows, axis=2).reshape(6, KINDS)


def matrices_kernel(depth, meta, kinds, first, second):
    cells = first.shape[1] // 2
    slab = meta[SLAB]
    sided = 2 * KINDS
    per_cell = (DIRS // 4) / DIRS

    def places(rows):
        column = lax.broadcasted_iota(jnp.int32, (rows, 2 * cells), 1)
        quart = column >= cells
        return jnp.where(quart, column - cells, column), quart

    def distance(rows, base):
        there, quart = places(rows)
        far = jnp.abs(lax.broadcasted_iota(jnp.int32, (rows, 2 * cells), 0) + base - there)
        return far.astype(jnp.float32), jnp.where(far == 0, 2.0, 1.0), quart

    full, twice_full, quart_full = distance(cells, 0)
    home, twice_home, quart_home = distance(depth, slab * depth)
    there, quart_row = places(1)
    gaps = [value.astype(jnp.float32) for value in (slab * depth - 1 - there, there - (slab + 1) * depth)]
    everywhere = jnp.zeros((cells, 2 * cells), jnp.float32)
    once = stay = around = jnp.zeros((depth, 2 * cells), jnp.float32)
    for kind in range(KINDS):
        therm, quart = kinds[THERM, kind], kinds[QUART, kind]
        slope = jnp.log(jnp.full((1, 2 * cells), kinds[DECAY, kind], jnp.float32))
        everywhere += jnp.where(quart_full, quart, therm) * (jnp.exp(full * slope) * twice_full)
        weight = jnp.where(quart_home, quart, therm) * (jnp.exp(home * slope) * twice_home)
        once += weight
        weight = weight * (home + 1.0)
        stay += kinds[STAY, kind] * weight
        around += kinds[AROUND, kind] * weight
        for side, gap in enumerate(gaps):
            weight = jnp.where(quart_row, quart, therm) * jnp.exp(jnp.maximum(gap, 0.0) * slope)
            weight = jnp.where(gap >= 0, weight, 0.0)
            at = kind + side * KINDS
            first[cells + at : cells + at + 1, :] = weight
            first[cells + sided + at : cells + sided + at + 1, :] = weight * (gap + 1.0)
            second[at : at + 1, :] = weight
    first[:cells, :] = everywhere * per_cell
    base = cells + 2 * sided
    first[base : base + depth, :] = stay * (1.0 / DIRS)
    first[base + depth :, :] = around * (1.0 / DIRS)
    second[sided:, :] = once * per_cell


def newton(density, kelvin, linear, quart):
    for _ in range(NEWTON):
        cube = kelvin * kelvin * kelvin
        residual = linear * kelvin + quart * (kelvin * cube) - density
        kelvin = kelvin - residual / (linear + 4.0 * quart * cube)
    return kelvin


def exact_dot(left, right):
    return jnp.dot(left, right, precision=lax.Precision.HIGHEST, preferred_element_type=jnp.float32)


def fourth(value):
    square = value * value
    return square * square


def add_up(values):
    while len(values) > 1:
        values = [a + b for a, b in zip(values[::2], values[1::2])]
    return values[0]


def stencil(low, high, c_self, c_y, c_z, shift_y, shift_z, at_edge):
    turned_low, turned_high = pltpu.roll(low, shift_y, 0), pltpu.roll(high, shift_y, 0)
    up_low = jnp.where(at_edge, turned_high, turned_low)
    up_high = jnp.where(at_edge, turned_low, turned_high)
    return (
        c_self * low + c_y * up_low + c_z * pltpu.roll(low, shift_z, 1),
        c_self * high + c_y * up_high + c_z * pltpu.roll(high, shift_z, 1),
    )


def course(ints, s, depth):
    forward = ints[FORWARD, s] == 1
    return jnp.where(forward, 0, depth - 1), jnp.where(forward, 1, -1)


def slot_stencil(floats, ints, s, row):
    at_edge = row == ints[EDGE_Y, s]
    c_self, c_y, c_z = floats[SELF, s], floats[UPY, s], floats[UPZ, s]
    shift_y, shift_z = ints[SHIFT_Y, s], ints[SHIFT_Z, s]
    return lambda low, high: stencil(low, high, c_self, c_y, c_z, shift_y, shift_z, at_edge)


def rows_of(s):
    at = pl.multiple_of(s * 16, 16)
    return pl.ds(at, 8), pl.ds(at + 8, 8)


K_SELF, K_LARGE, K_SMALL, K_RATIO, K_THERM, K_QUART, K_HEAT, K_WALL = range(8)


def fill_kinds(table, bands):
    speeds, rates, storages, thresholds, generations = bands
    for kind in range(KINDS):
        band, cosine = kind // 2, COSINES[kind % 2]
        sine = np.sqrt(np.float32(1.0) - cosine * cosine)
        speed, rate, storage, threshold, generation = (
            jnp.full((8, 128), ref[band], jnp.float32) for ref in (speeds, rates, storages, thresholds, generations)
        )
        inverse = 1.0 / (speed * float(cosine + sine * np.float32(ACROSS)) + rate + PSEUDO_RATE)
        quart = 1.0 / (4.0 * (threshold * threshold * threshold))
        across = speed * float(sine) * inverse
        therm = rate * storage * inverse
        rows = (
            PSEUDO_RATE * inverse,
            across * math.cos(math.pi / 8),
            across * math.sin(math.pi / 8),
            speed * float(cosine) * inverse,
            therm,
            therm * quart,
            generation * inverse,
            storage * (1.0 + quart),
        )
        for row, value in enumerate(rows):
            table[row, kind] = value


def sweeps_kernel(sizes, meta, labels, *refs):
    block, blocks, depth, width_y, slots, modes, group = sizes
    bands, refs = refs[:5], refs[5:]
    energy, flag, given, label_row, swept, quarter, *rest = refs
    faces, rest = rest[:group], rest[group:]
    keep, send, *planes, density, flat, sources, heat, table = rest
    out_one, turn_one, turn_two, out_two, turn_late, out_three = planes
    rows, own = width_y // modes, slots // group
    step = pl.program_id(0)
    slab, mode = meta[SLAB], meta[MODE]
    slabs = keep.shape[2] // depth

    @pl.when(step == 0)
    def _():
        fill_kinds(table, bands)
        for yy in range(rows):
            quarter[:, yy * 128 : (yy + 1) * 128] = given[pl.ds(mode * rows + yy, depth, stride=width_y), :]
        density[...] = jnp.zeros_like(density)

        def one_layer(x, carry):
            at = pl.multiple_of(x * 16, 16)
            for low in (0, 8):
                t = given[pl.ds(at + low, 8), :]
                power = fourth(t)
                hot = flag[pl.ds(at + low, 8), :].astype(jnp.float32)
                heat[x, low : low + 8, :] = hot
                for kind in range(KINDS):
                    value = table[K_THERM, kind] * t + table[K_QUART, kind] * power + table[K_HEAT, kind] * hot
                    sources[kind, x, low : low + 8, :] = value
            return carry

        lax.fori_loop(0, depth, one_layer, 0)

    row = lax.broadcasted_iota(jnp.int32, (8, 128), 0)

    def of_slot(i):
        s = step * block + i
        label = labels[s]
        polar, turn_of = label % 4, (label // 4) % 8
        forward = polar < 2
        kind = 2 * (label // DIRS) + jnp.where((polar == 0) | (polar == 3), 0, 1)
        right, up = (turn_of < 2) | (turn_of > 5), turn_of < 4
        wide = (turn_of % 4 == 0) | (turn_of % 4 == 3)
        start, stride = jnp.where(forward, 0, depth - 1), jnp.where(forward, 1, -1)
        at_wall = jnp.where(forward, slab == 0, slab == slabs - 1)
        c_self = table[K_SELF, kind]
        c_y = table[jnp.where(wide, K_LARGE, K_SMALL), kind]
        c_z = table[jnp.where(wide, K_SMALL, K_LARGE), kind]
        wall = jnp.where(at_wall, 1.0, 0.0) * table[K_WALL, kind]
        shift_y, shift_z = jnp.where(right, 1, 7), jnp.where(up, 1, 127)
        at_edge = row == jnp.where(right, 0, 7)
        apply = lambda low, high: stencil(low, high, c_self, c_y, c_z, shift_y, shift_z, at_edge)
        xs = [start + stride * j for j in range(depth)]
        return s, forward, kind, wall, apply, xs

    def one_pair(pair, carry):
        pair = [2 * pair, 2 * pair + 1]
        slots_of = [of_slot(i) for i in pair]
        layers = [[(energy[i, x, :8, :], energy[i, x, 8:, :]) for x in of[-1]] for i, of in zip(pair, slots_of)]
        lasts = [[], []]
        for turn in range(ITERS):
            for which, (s, forward, kind, wall, apply, xs) in enumerate(slots_of):
                ratio = table[K_RATIO, kind]
                warm = table[K_HEAT, kind] if turn else None
                total_low = total_high = wall
                for j, x in enumerate(xs):
                    low, high = apply(*layers[which][j])
                    if turn == 0:
                        low, high = low + sources[kind, x, :8, :], high + sources[kind, x, 8:, :]
                    else:
                        low, high = low + warm * heat[x, :8, :], high + warm * heat[x, 8:, :]
                    total_low = ratio * total_low + low
                    total_high = ratio * total_high + high
                    layers[which][j] = (total_low, total_high)
                lasts[which].append((total_low, total_high))
            for x in range(depth):
                for half, here in enumerate((slice(0, 8), slice(8, 16))):
                    values = [
                        jnp.where(of[1], layer[x][half], layer[depth - 1 - x][half]) for of, layer in zip(slots_of, layers)
                    ]
                    density[turn, x, here, :] += values[0] + values[1]
                    if turn == ITERS - 1:
                        for i, value in zip(pair, values):
                            swept[i, x, here, :] = value
        for (s, _, _, _, apply, _), last in zip(slots_of, lasts):
            turned = apply(*last[0])
            at_low, at_high = rows_of(s)
            values = (last[0], turned, apply(*turned), last[1], apply(*last[1]), last[2])
            for plane, (low, high) in zip(planes, values):
                plane[at_low, :] = low
                plane[at_high, :] = high
        return carry

    lax.fori_loop(0, block // 2, one_pair, 0, unroll=2)

    @pl.when(step == blocks - 1)
    def _():
        for by in range(group):
            at = pl.ds(pl.multiple_of(((slab % group) ^ by) * own * 16, 16), own * 16)
            for index, plane in enumerate((turn_two, turn_late, out_three)):
                faces[by][index] = plane[at, :]
        for turn in range(ITERS):
            for x in range(depth):
                flat[turn, x * 16 : x * 16 + 16, :] = density[turn, x]
        label = label_row[...]
        polar = label % 4
        kinds = 2 * (label // DIRS) + jnp.where((polar == 0) | (polar == 3), 0, 1)
        decay = jnp.ones((1, slots), jnp.float32)
        for kind in range(KINDS):
            decay = jnp.where(kinds == kind, table[K_RATIO, kind][:1, :slots], decay)
        x = lax.broadcasted_iota(jnp.int32, (slabs * depth, slots), 0)
        past = jnp.where(polar < 2, x - (slab * depth + depth - 1), slab * depth - x)
        n = past.astype(jnp.float32)
        weight = jnp.where(past > 0, jnp.exp(jnp.maximum(n, 0.0) * jnp.log(decay)), 0.0)
        weights = (weight, n * weight, (0.5 * n * (n + 1.0)) * weight)
        home = pl.ds(pl.multiple_of(slab * depth, 8), depth)
        for by in range(modes):
            ys = [(mode ^ by) * rows + yy for yy in range(rows)]
            pick = lambda plane, count: jnp.concatenate([plane[pl.ds(y, count, stride=width_y), :] for y in ys], axis=1)
            plain = exact_dot(weights[0], jnp.concatenate([pick(p, slots) for p in (out_one, out_two, out_three)], axis=1))
            once = exact_dot(weights[1], jnp.concatenate([pick(p, slots) for p in (turn_one, turn_late)], axis=1))
            twice = exact_dot(weights[2], pick(turn_two, slots))
            lanes = rows * 128
            target = (send if by % 2 else keep).at[by // 2]
            target[0] = plain[:, :lanes]
            target[1] = plain[:, lanes : 2 * lanes] + once[:, :lanes]
            target[2] = plain[:, 2 * lanes :] + once[:, lanes:] + twice
            for turn in range(ITERS):
                target[turn, home, :] += pick(flat.at[turn], depth)


def split_kernel(mine, other, keep, send):
    for index in range(mine.shape[0]):
        target = send if index % 2 else keep
        target[index // 2] = mine[index] + other[index]


def parts_kernel(depth, mine, other, parts):
    for turn in range(ITERS):
        total = mine[0, turn] + other[0, turn]
        for slab in range(parts.shape[0]):
            parts[slab, turn] = total[slab * depth : (slab + 1) * depth]


def totals_kernel(sums, parts, before, copies, late):
    slabs = parts.shape[0]
    one, two, three = (
        add_up([parts[slab, turn] for slab in range(slabs)]) * (1.0 / DIRS) for turn in range(ITERS)
    )
    late[...] = three
    kelvin = newton(one, before[...], sums[0], sums[1])
    for slab in range(slabs):
        copies[slab, 0] = kelvin
        copies[slab, 1] = two


def kelvins_kernel(depth, meta, sums, gathered, late, matrix_one, matrix_two, packed):
    slabs = gathered.shape[0]
    cells = slabs * depth
    one, two = (jnp.concatenate([gathered[slab, index] for slab in range(slabs)], axis=0) for index in range(2))
    first = exact_dot(matrix_one[...], jnp.concatenate([one, fourth(one)], axis=0))
    two = newton(two + first[:cells], one, sums[0], sums[1])
    second = exact_dot(matrix_two[...], jnp.concatenate([two, fourth(two)], axis=0))
    sided = 2 * KINDS
    packed[: 2 * sided, :] = first[cells : cells + 2 * sided]
    packed[2 * sided : 3 * sided, :] = second[:sided]
    base = 3 * sided
    packed[base : base + depth, :] = gathered[meta[SLAB], 0]
    stay = first[cells + 2 * sided : cells + 2 * sided + depth]
    around = first[cells + 2 * sided + depth :]
    own = jnp.zeros_like(around)
    for slab in range(slabs):
        own = jnp.where(meta[SLAB] == slab, two[slab * depth : (slab + 1) * depth], own)
    packed[base + depth : base + 2 * depth, :] = own
    packed[base + 2 * depth : base + 3 * depth, :] = late[...] + stay + second[sided:]
    packed[base + 3 * depth :, :] = around


def compose_kernel(own, group, meta, floats, ints, *refs):
    received, (first, others, effective, ordered) = refs[:group], refs[group:]
    place = meta[SLAB] % group
    for by in range(group):
        ordered[place ^ by] = received[by][...]

    def one_slot(i, carry):
        s = place * own + i
        start, stride = course(ints, s, group)
        full, full_n, full_t = floats[FULL, s], floats[FULL_N, s], floats[FULL_T, s]
        at = pl.ds(pl.multiple_of(i * 16, 16), 16)
        one = two = three = jnp.zeros((16, 128), jnp.float32)
        for j in range(group):
            k = start + stride * j
            three = full * three + full_n * two + full_t * one + ordered[k, 2, at, :]
            two = full * two + full_n * one + ordered[k, 1, at, :]
            one = full * one + ordered[k, 0, at, :]
        first[at, :] = one
        others[0, at, :] = two
        others[1, at, :] = three
        return carry

    lax.fori_loop(0, own, one_slot, 0, unroll=4)
    effective[...] = ordered[...]


def enter_kernel(own, group, groups, depth, meta, floats, ints, effective, *refs):
    firsts, others, rest = refs[:groups], refs[groups : 2 * groups], refs[2 * groups :]
    outs, (ordered, entered) = rest[:group], rest[group:]
    slab = meta[SLAB]
    place, mine = slab % group, slab // group
    for by in range(groups):
        ordered[mine ^ by, 0] = firsts[by][...]
        ordered[mine ^ by, 1:] = others[by][...]
    span = depth * group

    def one_slot(i, carry):
        s = place * own + i
        start, stride = course(ints, s, group)
        begin, leap = course(ints, s, groups)
        ahead = jnp.where(ints[FORWARD, s] == 1, mine, groups - 1 - mine)
        at = pl.ds(pl.multiple_of(i * 16, 16), 16)

        def push(values, full, full_n, full_t, added):
            one, two, three = values
            return (
                full * one + added[0],
                full * two + full_n * one + added[1],
                full * three + full_n * two + full_t * one + added[2],
            )

        values = (jnp.zeros((16, 128), jnp.float32),) * 3
        whole = floats[FULL_GROUP, s]
        for g in range(groups - 1):
            index = begin + leap * g
            added = [ordered[index, plane, at, :] for plane in range(3)]
            later = push(values, whole, span * whole, (span * (span + 1) // 2) * whole, added)
            values = tuple(jnp.where(g < ahead, a, b) for a, b in zip(later, values))
        full, full_n, full_t = floats[FULL, s], floats[FULL_N, s], floats[FULL_T, s]
        for j in range(group):
            k = start + stride * j
            for plane in range(3):
                entered[k, plane, at, :] = values[plane]
            if j < group - 1:
                values = push(values, full, full_n, full_t, [effective[k, plane, at, :] for plane in range(3)])
        return carry

    lax.fori_loop(0, own, one_slot, 0, unroll=2)
    for by in range(group):
        outs[by][...] = entered[place ^ by]


def warm_kernel(sizes, order, meta, floats, ints, kinds, sums, swept, *refs):
    block, depth, width_y, width_z, modes = sizes
    packs, refs = refs[:modes], refs[modes:]
    energy, kelvin, enter_one, enter_long, enter_two, second, added, own_one, own_two, plain, around = refs
    step = pl.program_id(0)
    rows = width_y // modes

    @pl.when(step == 0)
    def _():
        sided, base = 2 * KINDS, 6 * KINDS
        for pack, by in zip(packs, order):
            for yy in range(rows):
                y, lane = (meta[MODE] ^ by) * rows + yy, slice(yy * 128, (yy + 1) * 128)
                for index, target in enumerate((enter_one, enter_long, enter_two)):
                    target[pl.ds(y, sided, stride=width_y), :] = pack[index * sided : (index + 1) * sided, lane]
                scattered = pl.ds(y, depth, stride=width_y)
                own_one[scattered, :] = pack[base : base + depth, lane]
                own_two[scattered, :] = pack[base + depth : base + 2 * depth, lane]
                plain[y] = pack[base + 2 * depth : base + 3 * depth, lane]
                around[y] = pack[base + 3 * depth :, lane]
        for y in range(width_y):
            here = around[y]
            near = around[(y - 1) % width_y] + around[(y + 1) % width_y]
            near = near + (pltpu.roll(here, 1, 1) + pltpu.roll(here, width_z - 1, 1))
            scattered = pl.ds(y, depth, stride=width_y)
            kelvin[scattered, :] = newton(plain[y] + near, own_two[scattered, :], sums[0], sums[1])

        def one_kind(kind, carry):
            therm, quart, decay = kinds[THERM, kind], kinds[QUART, kind], kinds[DECAY, kind]
            ones, twos = [], []
            for x in range(depth):
                here = slice(x * 16, x * 16 + 16)
                t, u = own_one[here, :], own_two[here, :]
                ones.append(therm * t + quart * fourth(t))
                twos.append(therm * u + quart * fourth(u))
            for back in (0, KINDS):
                at = pl.ds(pl.multiple_of((kind + back) * 16, 16), 16)
                once, twice, new = enter_one[at, :], enter_long[at, :], enter_two[at, :]
                for j in range(depth):
                    x = depth - 1 - j if back else j
                    once = decay * once + ones[x]
                    twice = decay * twice + once
                    new = decay * new + twos[x]
                    second[kind + back, x] = twice
                    added[kind + back, x] = new
            return carry

        lax.fori_loop(0, KINDS, one_kind, 0)

    row = lax.broadcasted_iota(jnp.int32, (8, 128), 0)

    def one_slot(i, carry):
        s = step * block + i
        sided = ints[KIND, s] + KINDS * (1 - ints[FORWARD, s])
        apply = slot_stencil(floats, ints, s, row)
        for x in range(depth):
            low, high = apply(second[sided, x, :8, :], second[sided, x, 8:, :])
            energy[i, x, :8, :] = swept[i, x, :8, :] + (low + added[sided, x, :8, :])
            energy[i, x, 8:, :] = swept[i, x, 8:, :] + (high + added[sided, x, 8:, :])
        return carry

    lax.fori_loop(0, block, one_slot, 0, unroll=2)


def inflow_kernel(sizes, meta, floats, ints, warm, *refs):
    block, depth, own, group = sizes
    received, (energy, ordered) = refs[:group], refs[group:]
    step = pl.program_id(0)

    @pl.when(step == 0)
    def _():
        for by in range(group):
            ordered[(meta[SLAB] % group) ^ by] = received[by][...]

    def one_slot(i, carry):
        s = step * block + i
        start, stride = course(ints, s, depth)
        ratio = floats[RATIO, s]
        at = pl.ds(pl.multiple_of((s % own) * 16, 16), 16)
        one, two, three = (ordered[s // own, plane, at, :] for plane in range(ITERS))
        for j in range(depth):
            x = start + stride * j
            one = ratio * one
            two = ratio * two + one
            three = ratio * three + two
            energy[i, x] = warm[i, x] + three
        return carry

    lax.fori_loop(0, block, one_slot, 0, unroll=4)


def local(incoming_occupation, crystal_kelvin_given, generating_region_flag, labels, speed, rate, storage, threshold, generation):
    slots, depth, width_y, width_z = incoming_occupation.shape
    slabs, modes = lax.axis_size("slab"), lax.axis_size("mode")
    group, groups = GROUP, slabs // GROUP
    own = slots // group
    lanes = width_y // modes * width_z
    block = 8
    blocks = slots // block
    cells, all_x = depth * width_y, slabs * depth
    face_rows = own * width_y
    slab = lax.axis_index("slab").astype(jnp.int32)
    meta = jnp.stack([slab, lax.axis_index("mode").astype(jnp.int32)])
    floats, ints = slot_tables(labels, speed, rate, storage, threshold, generation, slab, slabs, depth, width_z)
    kinds = kind_table(speed, rate, storage, threshold, generation)
    sums = jnp.stack([jnp.sum(storage), jnp.sum(storage / (4.0 * threshold**3))])

    def shape(*dims):
        return jax.ShapeDtypeStruct(dims, jnp.float32)

    def whole(*dims):
        return pl.BlockSpec(dims, lambda i: (0,) * len(dims))

    def scratch(*dims):
        return pltpu.VMEM(dims, jnp.float32)

    def swap(array, axis, by):
        return lax.ppermute(array, axis, [(i, i ^ by) for i in range(lax.axis_size(axis))])

    def call(kernel, name, in_specs, out_shapes, *args, scratches=()):
        return pl.pallas_call(
            kernel,
            in_specs=in_specs,
            out_specs=[VMEM] * len(out_shapes),
            out_shape=out_shapes,
            scratch_shapes=list(scratches),
            compiler_params=PARAMS,
            name=name,
        )(*args)

    slot_block = pl.BlockSpec((block, depth, width_y, width_z), lambda i: (i, 0, 0, 0))
    slot_shape = shape(slots, depth, width_y, width_z)
    face = (3, face_rows, width_z)
    half = (modes // 2, ITERS, all_x, lanes)
    swept, quarter, *rest = pl.pallas_call(
        functools.partial(sweeps_kernel, (block, blocks, depth, width_y, slots, modes, group)),
        grid=(blocks,),
        in_specs=[SMEM] * 7 + [slot_block, whole(cells, width_z), whole(cells, width_z), whole(1, slots)],
        out_specs=[slot_block, whole(depth, lanes)] + [whole(*face)] * group + [whole(*half)] * 2,
        out_shape=[slot_shape, shape(depth, lanes)] + [shape(*face)] * group + [shape(*half)] * 2,
        scratch_shapes=[scratch(slots * width_y, width_z)] * 6
        + [
            scratch(ITERS, depth, width_y, width_z),
            scratch(ITERS, cells, width_z),
            scratch(KINDS, depth, width_y, width_z),
            scratch(depth, width_y, width_z),
            scratch(8, KINDS, 8, width_z),
        ],
        compiler_params=LARGE,
        name="sweeps",
    )(
        meta,
        labels,
        speed,
        rate,
        storage,
        threshold,
        generation,
        incoming_occupation,
        generating_region_flag.reshape(cells, width_z),
        crystal_kelvin_given.reshape(cells, width_z),
        labels.reshape(1, slots),
    )
    faces, (keep, send) = rest[:group], rest[group:]

    by = 1
    other = swap(send, "mode", by)
    received = [faces[0]] + [swap(faces[index], "slab", index) for index in range(1, group)]
    while 2 * by < modes:
        by *= 2
        now = (modes // (2 * by), ITERS, all_x, lanes)
        keep, send = call(split_kernel, "density_split", [VMEM] * 2, [shape(*now)] * 2, keep, other)
        other = swap(send, "mode", by)
    piece = (slabs, ITERS, depth, lanes)
    first_matrix, second_matrix = call(
        functools.partial(matrices_kernel, depth),
        "heat_matrices",
        [SMEM] * 2,
        [shape(all_x + 4 * KINDS + 2 * depth, 2 * all_x), shape(2 * KINDS + depth, 2 * all_x)],
        meta,
        kinds,
    )
    first, others, effective = call(
        functools.partial(compose_kernel, own, group),
        "compose",
        [SMEM] * 3 + [VMEM] * group,
        [shape(*face[1:]), shape(2, *face[1:]), shape(group, *face)],
        meta,
        floats,
        ints,
        *received,
        scratches=[scratch(group, *face)],
    )
    other, first, others, floats, ints, kinds, sums, first_matrix, second_matrix = lax.optimization_barrier(
        (other, first, others, floats, ints, kinds, sums, first_matrix, second_matrix)
    )
    firsts, others = (
        [value] + [swap(value, "slab", index * group) for index in range(1, groups)] for value in (first, others)
    )
    (parts,) = call(functools.partial(parts_kernel, depth), "density_parts", [VMEM] * 2, [shape(*piece)], keep, other)
    summed = lax.all_to_all(parts, "slab", 0, 0)
    summed, firsts = lax.optimization_barrier((summed, firsts))

    copies, late = call(
        totals_kernel,
        "density_totals",
        [SMEM] + [VMEM] * 2,
        [shape(slabs, 2, depth, lanes), shape(depth, lanes)],
        sums,
        summed,
        quarter,
    )
    gathered = lax.all_to_all(copies, "slab", 0, 0)
    entering = call(
        functools.partial(enter_kernel, own, group, groups, depth),
        "enter",
        [SMEM] * 3 + [VMEM] * (1 + 2 * groups),
        [shape(*face)] * group,
        meta,
        floats,
        ints,
        effective,
        *firsts,
        *others,
        scratches=[scratch(groups, *face), scratch(group, *face)],
    )
    entering = [entering[0]] + [swap(entering[index], "slab", index) for index in range(1, group)]

    pack_shape = shape(6 * KINDS + 4 * depth, lanes)
    (packed,) = call(
        functools.partial(kelvins_kernel, depth),
        "kelvins",
        [SMEM] * 2 + [VMEM] * 4,
        [pack_shape],
        meta,
        sums,
        gathered,
        late,
        first_matrix,
        second_matrix,
    )
    packs, order = [packed], [0]
    while by:
        packs = packs + [swap(pack, "mode", by) for pack in packs]
        order = order + [index ^ by for index in order]
        by //= 2

    warm, kelvin = pl.pallas_call(
        functools.partial(warm_kernel, (block, depth, width_y, width_z, modes), order),
        grid=(blocks,),
        in_specs=[SMEM] * 5 + [slot_block] + [whole(*pack_shape.shape)] * modes,
        out_specs=[slot_block, whole(cells, width_z)],
        out_shape=[slot_shape, shape(cells, width_z)],
        scratch_shapes=[scratch(2 * KINDS * width_y, width_z)] * 3
        + [scratch(2 * KINDS, depth, width_y, width_z)] * 2
        + [scratch(cells, width_z)] * 2
        + [scratch(width_y, depth, width_z)] * 2,
        compiler_params=PARAMS,
        name="warm",
    )(meta, floats, ints, kinds, sums, swept, *packs)
    energy = pl.pallas_call(
        functools.partial(inflow_kernel, (block, depth, own, group)),
        grid=(blocks,),
        in_specs=[SMEM] * 3 + [slot_block] + [whole(*face)] * group,
        out_specs=slot_block,
        out_shape=slot_shape,
        scratch_shapes=[scratch(group, *face)],
        compiler_params=PARAMS,
        name="inflow",
    )(meta, floats, ints, warm, *entering)
    return energy, kelvin.reshape(depth, width_y, width_z)


def solution(mesh):
    return jax.shard_map(
        local,
        mesh=mesh,
        in_specs=(
            P("mode", "slab", None, None),
            P("slab", None, None),
            P("slab", None, None),
            P("mode"),
            P(),
            P(),
            P(),
            P(),
            P(),
        ),
        out_specs=(P("mode", "slab", None, None), P("slab", None, None)),
        check_vma=False,
    )
```

```python
import functools
import math

import jax
import jax.numpy as jnp
import numpy as np
from jax import lax
from jax.experimental import pallas as pl
from jax.experimental.pallas import tpu as pltpu
from jax.sharding import PartitionSpec as P

FREQ_GROUPS = 8
DIRS = 32
ITERS = 3
NEWTON = 4
PSEUDO_RATE = 0.03
GROUP = 4
COSINES = (np.float32(0.99995), np.float32(0.9999))

SELF, UPY, UPZ, RATIO, WALL, FULL, FULL_N, FULL_T, FULL_GROUP, WARM = range(10)
FORWARD, SHIFT_Y, SHIFT_Z, EDGE_Y, KIND = range(5)
THERM, QUART, HEAT, DECAY, STAY, AROUND = range(6)
KINDS = 2 * FREQ_GROUPS
SLAB, MODE = range(2)

SMEM = pl.BlockSpec(memory_space=pltpu.SMEM)
VMEM = pl.BlockSpec(memory_space=pltpu.VMEM)
PARAMS = pltpu.CompilerParams(vmem_limit_bytes=48 * 1024 * 1024)
LARGE = pltpu.CompilerParams(vmem_limit_bytes=62 * 1024 * 1024)
ACROSS = math.cos(math.pi / 8) + math.sin(math.pi / 8)


def diagonal_of(speed, rate, cosine):
    sine = jnp.sqrt(1.0 - cosine * cosine)
    return speed * (cosine + sine * np.float32(ACROSS)) + rate + PSEUDO_RATE


def slot_tables(labels, speed, rate, storage, threshold, generation, slab, slabs, depth, width_z):
    band = labels // DIRS
    direction = labels % DIRS
    of_band = (band[None, :] == jnp.arange(FREQ_GROUPS, dtype=jnp.int32)[:, None]).astype(jnp.float32)
    speed, rate, storage, threshold, generation = (
        jnp.sum(of_band * value[:, None], axis=0) for value in (speed, rate, storage, threshold, generation)
    )
    polar = direction % 4
    outer = (polar == 0) | (polar == 3)
    forward = polar < 2
    cosine = jnp.where(outer, COSINES[0], COSINES[1])
    sine = jnp.sqrt(1.0 - cosine * cosine)
    azimuth = ((direction // 4).astype(jnp.float32) + 0.5) * (2.0 * math.pi / (DIRS // 4))
    vy = speed * sine * jnp.cos(azimuth)
    vz = speed * sine * jnp.sin(azimuth)
    diagonal = diagonal_of(speed, rate, cosine)
    ratio = speed * cosine / diagonal
    full = lax.integer_pow(ratio, depth)
    at_wall = jnp.where(forward, slab == 0, slab == slabs - 1)
    wall = storage * (1.0 + 1.0 / (4.0 * threshold**3))
    floats = jnp.stack(
        [
            PSEUDO_RATE / diagonal,
            jnp.abs(vy) / diagonal,
            jnp.abs(vz) / diagonal,
            ratio,
            jnp.where(at_wall, wall, 0.0),
            full,
            depth * full,
            (depth * (depth + 1) // 2) * full,
            lax.integer_pow(full, GROUP),
            generation / diagonal,
        ]
    )
    ints = jnp.stack(
        [
            forward.astype(jnp.int32),
            jnp.where(vy > 0, 1, 7).astype(jnp.int32),
            jnp.where(vz > 0, 1, width_z - 1).astype(jnp.int32),
            jnp.where(vy > 0, 0, 7).astype(jnp.int32),
            2 * band + jnp.where(outer, 0, 1),
        ]
    )
    return floats, ints


def kind_table(speed, rate, storage, threshold, generation):
    rows = []
    for cosine in COSINES:
        diagonal = diagonal_of(speed, rate, cosine)
        therm = rate * storage / diagonal
        quart = therm / (4.0 * threshold**3)
        across = jnp.sqrt(1.0 - cosine * cosine) * np.float32(2.0 * ACROSS)
        rows.append(
            jnp.stack(
                [
                    therm,
                    quart,
                    generation / diagonal,
                    speed * cosine / diagonal,
                    (DIRS // 4) * PSEUDO_RATE / diagonal,
                    across * speed / diagonal,
                ]
            )
        )
    return jnp.stack(rows, axis=2).reshape(6, KINDS)


def matrices_kernel(depth, meta, kinds, first, second):
    cells = first.shape[1] // 2
    slab = meta[SLAB]
    sided = 2 * KINDS
    per_cell = (DIRS // 4) / DIRS

    def places(rows):
        column = lax.broadcasted_iota(jnp.int32, (rows, 2 * cells), 1)
        quart = column >= cells
        return jnp.where(quart, column - cells, column), quart

    def distance(rows, base):
        there, quart = places(rows)
        far = jnp.abs(lax.broadcasted_iota(jnp.int32, (rows, 2 * cells), 0) + base - there)
        return far.astype(jnp.float32), jnp.where(far == 0, 2.0, 1.0), quart

    full, twice_full, quart_full = distance(cells, 0)
    home, twice_home, quart_home = distance(depth, slab * depth)
    there, quart_row = places(1)
    gaps = [value.astype(jnp.float32) for value in (slab * depth - 1 - there, there - (slab + 1) * depth)]
    everywhere = jnp.zeros((cells, 2 * cells), jnp.float32)
    once = stay = around = jnp.zeros((depth, 2 * cells), jnp.float32)
    for kind in range(KINDS):
        therm, quart = kinds[THERM, kind], kinds[QUART, kind]
        slope = jnp.log(jnp.full((1, 2 * cells), kinds[DECAY, kind], jnp.float32))
        everywhere += jnp.where(quart_full, quart, therm) * (jnp.exp(full * slope) * twice_full)
        weight = jnp.where(quart_home, quart, therm) * (jnp.exp(home * slope) * twice_home)
        once += weight
        weight = weight * (home + 1.0)
        stay += kinds[STAY, kind] * weight
        around += kinds[AROUND, kind] * weight
        for side, gap in enumerate(gaps):
            weight = jnp.where(quart_row, quart, therm) * jnp.exp(jnp.maximum(gap, 0.0) * slope)
            weight = jnp.where(gap >= 0, weight, 0.0)
            at = kind + side * KINDS
            first[cells + at : cells + at + 1, :] = weight
            first[cells + sided + at : cells + sided + at + 1, :] = weight * (gap + 1.0)
            second[at : at + 1, :] = weight
    first[:cells, :] = everywhere * per_cell
    base = cells + 2 * sided
    first[base : base + depth, :] = stay * (1.0 / DIRS)
    first[base + depth :, :] = around * (1.0 / DIRS)
    second[sided:, :] = once * per_cell


def newton(density, kelvin, linear, quart):
    for _ in range(NEWTON):
        cube = kelvin * kelvin * kelvin
        residual = linear * kelvin + quart * (kelvin * cube) - density
        kelvin = kelvin - residual / (linear + 4.0 * quart * cube)
    return kelvin


def exact_dot(left, right):
    return jnp.dot(left, right, precision=lax.Precision.HIGHEST, preferred_element_type=jnp.float32)


def fourth(value):
    square = value * value
    return square * square


def add_up(values):
    while len(values) > 1:
        values = [a + b for a, b in zip(values[::2], values[1::2])]
    return values[0]


def stencil(low, high, c_self, c_y, c_z, shift_y, shift_z, at_edge):
    turned_low, turned_high = pltpu.roll(low, shift_y, 0), pltpu.roll(high, shift_y, 0)
    up_low = jnp.where(at_edge, turned_high, turned_low)
    up_high = jnp.where(at_edge, turned_low, turned_high)
    return (
        c_self * low + c_y * up_low + c_z * pltpu.roll(low, shift_z, 1),
        c_self * high + c_y * up_high + c_z * pltpu.roll(high, shift_z, 1),
    )


def course(ints, s, depth):
    forward = ints[FORWARD, s] == 1
    return jnp.where(forward, 0, depth - 1), jnp.where(forward, 1, -1)


def slot_stencil(floats, ints, s, row):
    at_edge = row == ints[EDGE_Y, s]
    c_self, c_y, c_z = floats[SELF, s], floats[UPY, s], floats[UPZ, s]
    shift_y, shift_z = ints[SHIFT_Y, s], ints[SHIFT_Z, s]
    return lambda low, high: stencil(low, high, c_self, c_y, c_z, shift_y, shift_z, at_edge)


def rows_of(s):
    at = pl.multiple_of(s * 16, 16)
    return pl.ds(at, 8), pl.ds(at + 8, 8)


K_SELF, K_LARGE, K_SMALL, K_RATIO, K_THERM, K_QUART, K_HEAT, K_WALL = range(8)


def fill_kinds(table, bands):
    speeds, rates, storages, thresholds, generations = bands
    for kind in range(KINDS):
        band, cosine = kind // 2, COSINES[kind % 2]
        sine = np.sqrt(np.float32(1.0) - cosine * cosine)
        speed, rate, storage, threshold, generation = (
            jnp.full((8, 128), ref[band], jnp.float32) for ref in (speeds, rates, storages, thresholds, generations)
        )
        inverse = 1.0 / (speed * float(cosine + sine * np.float32(ACROSS)) + rate + PSEUDO_RATE)
        quart = 1.0 / (4.0 * (threshold * threshold * threshold))
        across = speed * float(sine) * inverse
        therm = rate * storage * inverse
        rows = (
            PSEUDO_RATE * inverse,
            across * math.cos(math.pi / 8),
            across * math.sin(math.pi / 8),
            speed * float(cosine) * inverse,
            therm,
            therm * quart,
            generation * inverse,
            storage * (1.0 + quart),
        )
        for row, value in enumerate(rows):
            table[row, kind] = value


def sweeps_kernel(sizes, meta, labels, *refs):
    block, blocks, depth, width_y, slots, modes, group = sizes
    bands, refs = refs[:5], refs[5:]
    energy, flag, given, label_row, swept, quarter, *rest = refs
    faces, rest = rest[:group], rest[group:]
    keep, send, *planes, density, flat, sources, heat, table = rest
    out_one, turn_one, turn_two, out_two, turn_late, out_three = planes
    rows, own = width_y // modes, slots // group
    step = pl.program_id(0)
    slab, mode = meta[SLAB], meta[MODE]
    slabs = keep.shape[2] // depth

    @pl.when(step == 0)
    def _():
        fill_kinds(table, bands)
        for yy in range(rows):
            quarter[:, yy * 128 : (yy + 1) * 128] = given[pl.ds(mode * rows + yy, depth, stride=width_y), :]
        density[...] = jnp.zeros_like(density)

        def one_layer(x, carry):
            at = pl.multiple_of(x * 16, 16)
            for low in (0, 8):
                t = given[pl.ds(at + low, 8), :]
                power = fourth(t)
                hot = flag[pl.ds(at + low, 8), :].astype(jnp.float32)
                heat[x, low : low + 8, :] = hot
                for kind in range(KINDS):
                    value = table[K_THERM, kind] * t + table[K_QUART, kind] * power + table[K_HEAT, kind] * hot
                    sources[kind, x, low : low + 8, :] = value
            return carry

        lax.fori_loop(0, depth, one_layer, 0)

    row = lax.broadcasted_iota(jnp.int32, (8, 128), 0)

    def of_slot(i):
        s = step * block + i
        label = labels[s]
        polar, turn_of = label % 4, (label // 4) % 8
        forward = polar < 2
        kind = 2 * (label // DIRS) + jnp.where((polar == 0) | (polar == 3), 0, 1)
        right, up = (turn_of < 2) | (turn_of > 5), turn_of < 4
        wide = (turn_of % 4 == 0) | (turn_of % 4 == 3)
        start, stride = jnp.where(forward, 0, depth - 1), jnp.where(forward, 1, -1)
        at_wall = jnp.where(forward, slab == 0, slab == slabs - 1)
        c_self = table[K_SELF, kind]
        c_y = table[jnp.where(wide, K_LARGE, K_SMALL), kind]
        c_z = table[jnp.where(wide, K_SMALL, K_LARGE), kind]
        wall = jnp.where(at_wall, 1.0, 0.0) * table[K_WALL, kind]
        shift_y, shift_z = jnp.where(right, 1, 7), jnp.where(up, 1, 127)
        at_edge = row == jnp.where(right, 0, 7)
        apply = lambda low, high: stencil(low, high, c_self, c_y, c_z, shift_y, shift_z, at_edge)
        xs = [start + stride * j for j in range(depth)]
        return s, forward, kind, wall, apply, xs

    def one_pair(pair, carry):
        pair = [2 * pair, 2 * pair + 1]
        slots_of = [of_slot(i) for i in pair]
        layers = [[(energy[i, x, :8, :], energy[i, x, 8:, :]) for x in of[-1]] for i, of in zip(pair, slots_of)]
        lasts = [[], []]
        for turn in range(ITERS):
            for which, (s, forward, kind, wall, apply, xs) in enumerate(slots_of):
                ratio = table[K_RATIO, kind]
                warm = table[K_HEAT, kind] if turn else None
                total_low = total_high = wall
                for j, x in enumerate(xs):
                    low, high = apply(*layers[which][j])
                    if turn == 0:
                        low, high = low + sources[kind, x, :8, :], high + sources[kind, x, 8:, :]
                    else:
                        low, high = low + warm * heat[x, :8, :], high + warm * heat[x, 8:, :]
                    total_low = ratio * total_low + low
                    total_high = ratio * total_high + high
                    layers[which][j] = (total_low, total_high)
                lasts[which].append((total_low, total_high))
            for x in range(depth):
                for half, here in enumerate((slice(0, 8), slice(8, 16))):
                    values = [
                        jnp.where(of[1], layer[x][half], layer[depth - 1 - x][half]) for of, layer in zip(slots_of, layers)
                    ]
                    density[turn, x, here, :] += values[0] + values[1]
                    if turn == ITERS - 1:
                        for i, value in zip(pair, values):
                            swept[i, x, here, :] = value
        for (s, _, _, _, apply, _), last in zip(slots_of, lasts):
            turned = apply(*last[0])
            at_low, at_high = rows_of(s)
            values = (last[0], turned, apply(*turned), last[1], apply(*last[1]), last[2])
            for plane, (low, high) in zip(planes, values):
                plane[at_low, :] = low
                plane[at_high, :] = high
        return carry

    lax.fori_loop(0, block // 2, one_pair, 0, unroll=4)

    @pl.when(step == blocks - 1)
    def _():
        for by in range(group):
            at = pl.ds(pl.multiple_of(((slab % group) ^ by) * own * 16, 16), own * 16)
            for index, plane in enumerate((turn_two, turn_late, out_three)):
                faces[by][index] = plane[at, :]
        for turn in range(ITERS):
            for x in range(depth):
                flat[turn, x * 16 : x * 16 + 16, :] = density[turn, x]
        label = label_row[...]
        polar = label % 4
        kinds = 2 * (label // DIRS) + jnp.where((polar == 0) | (polar == 3), 0, 1)
        decay = jnp.ones((1, slots), jnp.float32)
        for kind in range(KINDS):
            decay = jnp.where(kinds == kind, table[K_RATIO, kind][:1, :slots], decay)
        x = lax.broadcasted_iota(jnp.int32, (slabs * depth, slots), 0)
        past = jnp.where(polar < 2, x - (slab * depth + depth - 1), slab * depth - x)
        n = past.astype(jnp.float32)
        weight = jnp.where(past > 0, jnp.exp(jnp.maximum(n, 0.0) * jnp.log(decay)), 0.0)
        weights = (weight, n * weight, (0.5 * n * (n + 1.0)) * weight)
        home = pl.ds(pl.multiple_of(slab * depth, 8), depth)
        for by in range(modes):
            ys = [(mode ^ by) * rows + yy for yy in range(rows)]
            pick = lambda plane, count: jnp.concatenate([plane[pl.ds(y, count, stride=width_y), :] for y in ys], axis=1)
            plain = exact_dot(weights[0], jnp.concatenate([pick(p, slots) for p in (out_one, out_two, out_three)], axis=1))
            once = exact_dot(weights[1], jnp.concatenate([pick(p, slots) for p in (turn_one, turn_late)], axis=1))
            twice = exact_dot(weights[2], pick(turn_two, slots))
            lanes = rows * 128
            target = (send if by % 2 else keep).at[by // 2]
            target[0] = plain[:, :lanes]
            target[1] = plain[:, lanes : 2 * lanes] + once[:, :lanes]
            target[2] = plain[:, 2 * lanes :] + once[:, lanes:] + twice
            for turn in range(ITERS):
                target[turn, home, :] += pick(flat.at[turn], depth)


def split_kernel(mine, other, keep, send):
    for index in range(mine.shape[0]):
        target = send if index % 2 else keep
        target[index // 2] = mine[index] + other[index]


def parts_kernel(depth, mine, other, parts):
    for turn in range(ITERS):
        total = mine[0, turn] + other[0, turn]
        for slab in range(parts.shape[0]):
            parts[slab, turn] = total[slab * depth : (slab + 1) * depth]


def totals_kernel(sums, parts, before, copies, late):
    slabs = parts.shape[0]
    one, two, three = (
        add_up([parts[slab, turn] for slab in range(slabs)]) * (1.0 / DIRS) for turn in range(ITERS)
    )
    late[...] = three
    kelvin = newton(one, before[...], sums[0], sums[1])
    for slab in range(slabs):
        copies[slab, 0] = kelvin
        copies[slab, 1] = two


def kelvins_kernel(depth, meta, sums, gathered, late, matrix_one, matrix_two, packed):
    slabs = gathered.shape[0]
    cells = slabs * depth
    one, two = (jnp.concatenate([gathered[slab, index] for slab in range(slabs)], axis=0) for index in range(2))
    first = exact_dot(matrix_one[...], jnp.concatenate([one, fourth(one)], axis=0))
    two = newton(two + first[:cells], one, sums[0], sums[1])
    second = exact_dot(matrix_two[...], jnp.concatenate([two, fourth(two)], axis=0))
    sided = 2 * KINDS
    packed[: 2 * sided, :] = first[cells : cells + 2 * sided]
    packed[2 * sided : 3 * sided, :] = second[:sided]
    base = 3 * sided
    packed[base : base + depth, :] = gathered[meta[SLAB], 0]
    stay = first[cells + 2 * sided : cells + 2 * sided + depth]
    around = first[cells + 2 * sided + depth :]
    own = jnp.zeros_like(around)
    for slab in range(slabs):
        own = jnp.where(meta[SLAB] == slab, two[slab * depth : (slab + 1) * depth], own)
    packed[base + depth : base + 2 * depth, :] = own
    packed[base + 2 * depth : base + 3 * depth, :] = late[...] + stay + second[sided:]
    packed[base + 3 * depth :, :] = around


def compose_kernel(own, group, meta, floats, ints, *refs):
    received, (first, others, effective, ordered) = refs[:group], refs[group:]
    place = meta[SLAB] % group
    for by in range(group):
        ordered[place ^ by] = received[by][...]

    def one_slot(i, carry):
        s = place * own + i
        start, stride = course(ints, s, group)
        full, full_n, full_t = floats[FULL, s], floats[FULL_N, s], floats[FULL_T, s]
        at = pl.ds(pl.multiple_of(i * 16, 16), 16)
        one = two = three = jnp.zeros((16, 128), jnp.float32)
        for j in range(group):
            k = start + stride * j
            three = full * three + full_n * two + full_t * one + ordered[k, 2, at, :]
            two = full * two + full_n * one + ordered[k, 1, at, :]
            one = full * one + ordered[k, 0, at, :]
        first[at, :] = one
        others[0, at, :] = two
        others[1, at, :] = three
        return carry

    lax.fori_loop(0, own, one_slot, 0, unroll=4)
    effective[...] = ordered[...]


def enter_kernel(own, group, groups, depth, meta, floats, ints, effective, *refs):
    firsts, others, rest = refs[:groups], refs[groups : 2 * groups], refs[2 * groups :]
    outs, (ordered, entered) = rest[:group], rest[group:]
    slab = meta[SLAB]
    place, mine = slab % group, slab // group
    for by in range(groups):
        ordered[mine ^ by, 0] = firsts[by][...]
        ordered[mine ^ by, 1:] = others[by][...]
    span = depth * group

    def one_slot(i, carry):
        s = place * own + i
        start, stride = course(ints, s, group)
        begin, leap = course(ints, s, groups)
        ahead = jnp.where(ints[FORWARD, s] == 1, mine, groups - 1 - mine)
        at = pl.ds(pl.multiple_of(i * 16, 16), 16)

        def push(values, full, full_n, full_t, added):
            one, two, three = values
            return (
                full * one + added[0],
                full * two + full_n * one + added[1],
                full * three + full_n * two + full_t * one + added[2],
            )

        values = (jnp.zeros((16, 128), jnp.float32),) * 3
        whole = floats[FULL_GROUP, s]
        for g in range(groups - 1):
            index = begin + leap * g
            added = [ordered[index, plane, at, :] for plane in range(3)]
            later = push(values, whole, span * whole, (span * (span + 1) // 2) * whole, added)
            values = tuple(jnp.where(g < ahead, a, b) for a, b in zip(later, values))
        full, full_n, full_t = floats[FULL, s], floats[FULL_N, s], floats[FULL_T, s]
        for j in range(group):
            k = start + stride * j
            for plane in range(3):
                entered[k, plane, at, :] = values[plane]
            if j < group - 1:
                values = push(values, full, full_n, full_t, [effective[k, plane, at, :] for plane in range(3)])
        return carry

    lax.fori_loop(0, own, one_slot, 0, unroll=2)
    for by in range(group):
        outs[by][...] = entered[place ^ by]


def warm_kernel(sizes, order, meta, floats, ints, kinds, sums, swept, *refs):
    block, depth, width_y, width_z, modes = sizes
    packs, refs = refs[:modes], refs[modes:]
    energy, kelvin, enter_one, enter_long, enter_two, second, added, own_one, own_two, plain, around = refs
    step = pl.program_id(0)
    rows = width_y // modes

    @pl.when(step == 0)
    def _():
        sided, base = 2 * KINDS, 6 * KINDS
        for pack, by in zip(packs, order):
            for yy in range(rows):
                y, lane = (meta[MODE] ^ by) * rows + yy, slice(yy * 128, (yy + 1) * 128)
                for index, target in enumerate((enter_one, enter_long, enter_two)):
                    target[pl.ds(y, sided, stride=width_y), :] = pack[index * sided : (index + 1) * sided, lane]
                scattered = pl.ds(y, depth, stride=width_y)
                own_one[scattered, :] = pack[base : base + depth, lane]
                own_two[scattered, :] = pack[base + depth : base + 2 * depth, lane]
                plain[y] = pack[base + 2 * depth : base + 3 * depth, lane]
                around[y] = pack[base + 3 * depth :, lane]
        for y in range(width_y):
            here = around[y]
            near = around[(y - 1) % width_y] + around[(y + 1) % width_y]
            near = near + (pltpu.roll(here, 1, 1) + pltpu.roll(here, width_z - 1, 1))
            scattered = pl.ds(y, depth, stride=width_y)
            kelvin[scattered, :] = newton(plain[y] + near, own_two[scattered, :], sums[0], sums[1])

        def one_kind(kind, carry):
            therm, quart, decay = kinds[THERM, kind], kinds[QUART, kind], kinds[DECAY, kind]
            ones, twos = [], []
            for x in range(depth):
                here = slice(x * 16, x * 16 + 16)
                t, u = own_one[here, :], own_two[here, :]
                ones.append(therm * t + quart * fourth(t))
                twos.append(therm * u + quart * fourth(u))
            for back in (0, KINDS):
                at = pl.ds(pl.multiple_of((kind + back) * 16, 16), 16)
                once, twice, new = enter_one[at, :], enter_long[at, :], enter_two[at, :]
                for j in range(depth):
                    x = depth - 1 - j if back else j
                    once = decay * once + ones[x]
                    twice = decay * twice + once
                    new = decay * new + twos[x]
                    second[kind + back, x] = twice
                    added[kind + back, x] = new
            return carry

        lax.fori_loop(0, KINDS, one_kind, 0)

    row = lax.broadcasted_iota(jnp.int32, (8, 128), 0)

    def one_slot(i, carry):
        s = step * block + i
        sided = ints[KIND, s] + KINDS * (1 - ints[FORWARD, s])
        apply = slot_stencil(floats, ints, s, row)
        for x in range(depth):
            low, high = apply(second[sided, x, :8, :], second[sided, x, 8:, :])
            energy[i, x, :8, :] = swept[i, x, :8, :] + (low + added[sided, x, :8, :])
            energy[i, x, 8:, :] = swept[i, x, 8:, :] + (high + added[sided, x, 8:, :])
        return carry

    lax.fori_loop(0, block, one_slot, 0, unroll=2)


def inflow_kernel(sizes, meta, floats, ints, warm, *refs):
    block, depth, own, group = sizes
    received, (energy, ordered) = refs[:group], refs[group:]
    step = pl.program_id(0)

    @pl.when(step == 0)
    def _():
        for by in range(group):
            ordered[(meta[SLAB] % group) ^ by] = received[by][...]

    def one_slot(i, carry):
        s = step * block + i
        start, stride = course(ints, s, depth)
        ratio = floats[RATIO, s]
        at = pl.ds(pl.multiple_of((s % own) * 16, 16), 16)
        one, two, three = (ordered[s // own, plane, at, :] for plane in range(ITERS))
        for j in range(depth):
            x = start + stride * j
            one = ratio * one
            two = ratio * two + one
            three = ratio * three + two
            energy[i, x] = warm[i, x] + three
        return carry

    lax.fori_loop(0, block, one_slot, 0, unroll=4)


def local(incoming_occupation, crystal_kelvin_given, generating_region_flag, labels, speed, rate, storage, threshold, generation):
    slots, depth, width_y, width_z = incoming_occupation.shape
    slabs, modes = lax.axis_size("slab"), lax.axis_size("mode")
    group, groups = GROUP, slabs // GROUP
    own = slots // group
    lanes = width_y // modes * width_z
    block = 8
    blocks = slots // block
    cells, all_x = depth * width_y, slabs * depth
    face_rows = own * width_y
    slab = lax.axis_index("slab").astype(jnp.int32)
    meta = jnp.stack([slab, lax.axis_index("mode").astype(jnp.int32)])
    floats, ints = slot_tables(labels, speed, rate, storage, threshold, generation, slab, slabs, depth, width_z)
    kinds = kind_table(speed, rate, storage, threshold, generation)
    sums = jnp.stack([jnp.sum(storage), jnp.sum(storage / (4.0 * threshold**3))])

    def shape(*dims):
        return jax.ShapeDtypeStruct(dims, jnp.float32)

    def whole(*dims):
        return pl.BlockSpec(dims, lambda i: (0,) * len(dims))

    def scratch(*dims):
        return pltpu.VMEM(dims, jnp.float32)

    def swap(array, axis, by):
        return lax.ppermute(array, axis, [(i, i ^ by) for i in range(lax.axis_size(axis))])

    def call(kernel, name, in_specs, out_shapes, *args, scratches=()):
        return pl.pallas_call(
            kernel,
            in_specs=in_specs,
            out_specs=[VMEM] * len(out_shapes),
            out_shape=out_shapes,
            scratch_shapes=list(scratches),
            compiler_params=PARAMS,
            name=name,
        )(*args)

    slot_block = pl.BlockSpec((block, depth, width_y, width_z), lambda i: (i, 0, 0, 0))
    slot_shape = shape(slots, depth, width_y, width_z)
    face = (3, face_rows, width_z)
    half = (modes // 2, ITERS, all_x, lanes)
    swept, quarter, *rest = pl.pallas_call(
        functools.partial(sweeps_kernel, (block, blocks, depth, width_y, slots, modes, group)),
        grid=(blocks,),
        in_specs=[SMEM] * 7 + [slot_block, whole(cells, width_z), whole(cells, width_z), whole(1, slots)],
        out_specs=[slot_block, whole(depth, lanes)] + [whole(*face)] * group + [whole(*half)] * 2,
        out_shape=[slot_shape, shape(depth, lanes)] + [shape(*face)] * group + [shape(*half)] * 2,
        scratch_shapes=[scratch(slots * width_y, width_z)] * 6
        + [
            scratch(ITERS, depth, width_y, width_z),
            scratch(ITERS, cells, width_z),
            scratch(KINDS, depth, width_y, width_z),
            scratch(depth, width_y, width_z),
            scratch(8, KINDS, 8, width_z),
        ],
        compiler_params=LARGE,
        name="sweeps",
    )(
        meta,
        labels,
        speed,
        rate,
        storage,
        threshold,
        generation,
        incoming_occupation,
        generating_region_flag.reshape(cells, width_z),
        crystal_kelvin_given.reshape(cells, width_z),
        labels.reshape(1, slots),
    )
    faces, (keep, send) = rest[:group], rest[group:]

    by = 1
    other = swap(send, "mode", by)
    received = [faces[0]] + [swap(faces[index], "slab", index) for index in range(1, group)]
    while 2 * by < modes:
        by *= 2
        now = (modes // (2 * by), ITERS, all_x, lanes)
        keep, send = call(split_kernel, "density_split", [VMEM] * 2, [shape(*now)] * 2, keep, other)
        other = swap(send, "mode", by)
    piece = (slabs, ITERS, depth, lanes)
    first_matrix, second_matrix = call(
        functools.partial(matrices_kernel, depth),
        "heat_matrices",
        [SMEM] * 2,
        [shape(all_x + 4 * KINDS + 2 * depth, 2 * all_x), shape(2 * KINDS + depth, 2 * all_x)],
        meta,
        kinds,
    )
    first, others, effective = call(
        functools.partial(compose_kernel, own, group),
        "compose",
        [SMEM] * 3 + [VMEM] * group,
        [shape(*face[1:]), shape(2, *face[1:]), shape(group, *face)],
        meta,
        floats,
        ints,
        *received,
        scratches=[scratch(group, *face)],
    )
    other, first, others, floats, ints, kinds, sums, first_matrix, second_matrix = lax.optimization_barrier(
        (other, first, others, floats, ints, kinds, sums, first_matrix, second_matrix)
    )
    firsts, others = (
        [value] + [swap(value, "slab", index * group) for index in range(1, groups)] for value in (first, others)
    )
    (parts,) = call(functools.partial(parts_kernel, depth), "density_parts", [VMEM] * 2, [shape(*piece)], keep, other)
    summed = lax.all_to_all(parts, "slab", 0, 0)
    summed, firsts = lax.optimization_barrier((summed, firsts))

    copies, late = call(
        totals_kernel,
        "density_totals",
        [SMEM] + [VMEM] * 2,
        [shape(slabs, 2, depth, lanes), shape(depth, lanes)],
        sums,
        summed,
        quarter,
    )
    gathered = lax.all_to_all(copies, "slab", 0, 0)
    entering = call(
        functools.partial(enter_kernel, own, group, groups, depth),
        "enter",
        [SMEM] * 3 + [VMEM] * (1 + 2 * groups),
        [shape(*face)] * group,
        meta,
        floats,
        ints,
        effective,
        *firsts,
        *others,
        scratches=[scratch(groups, *face), scratch(group, *face)],
    )
    entering = [entering[0]] + [swap(entering[index], "slab", index) for index in range(1, group)]

    pack_shape = shape(6 * KINDS + 4 * depth, lanes)
    (packed,) = call(
        functools.partial(kelvins_kernel, depth),
        "kelvins",
        [SMEM] * 2 + [VMEM] * 4,
        [pack_shape],
        meta,
        sums,
        gathered,
        late,
        first_matrix,
        second_matrix,
    )
    packs, order = [packed], [0]
    while by:
        packs = packs + [swap(pack, "mode", by) for pack in packs]
        order = order + [index ^ by for index in order]
        by //= 2

    warm, kelvin = pl.pallas_call(
        functools.partial(warm_kernel, (block, depth, width_y, width_z, modes), order),
        grid=(blocks,),
        in_specs=[SMEM] * 5 + [slot_block] + [whole(*pack_shape.shape)] * modes,
        out_specs=[slot_block, whole(cells, width_z)],
        out_shape=[slot_shape, shape(cells, width_z)],
        scratch_shapes=[scratch(2 * KINDS * width_y, width_z)] * 3
        + [scratch(2 * KINDS, depth, width_y, width_z)] * 2
        + [scratch(cells, width_z)] * 2
        + [scratch(width_y, depth, width_z)] * 2,
        compiler_params=PARAMS,
        name="warm",
    )(meta, floats, ints, kinds, sums, swept, *packs)
    energy = pl.pallas_call(
        functools.partial(inflow_kernel, (block, depth, own, group)),
        grid=(blocks,),
        in_specs=[SMEM] * 3 + [slot_block] + [whole(*face)] * group,
        out_specs=slot_block,
        out_shape=slot_shape,
        scratch_shapes=[scratch(group, *face)],
        compiler_params=PARAMS,
        name="inflow",
    )(meta, floats, ints, warm, *entering)
    return energy, kelvin.reshape(depth, width_y, width_z)


def solution(mesh):
    return jax.shard_map(
        local,
        mesh=mesh,
        in_specs=(
            P("mode", "slab", None, None),
            P("slab", None, None),
            P("slab", None, None),
            P("mode"),
            P(),
            P(),
            P(),
            P(),
            P(),
        ),
        out_specs=(P("mode", "slab", None, None), P("slab", None, None)),
        check_vma=False,
    )
```
